32 devices in a mesh: dp: 8 (over z, x), mp: 4 (over y, core).
Axes of the slice: x: 2, y: 2, z: 4, core: 2. Of those that a mesh axis runs over, the one named last changes fastest.
Arguments:
- byte_states: bfloat16 [2048, 8, 512], P('mp', 'dp'), may hold values from -6 to 6
- word_start: int32 [2048, 8], P(None, 'dp'), may hold values from 0 to 1, as said below
- bucket_ids: int32 [4095], replicated, may hold values from 0 to 31
- conv_two: float32 [2, 512], P(None, 'mp'), may hold values from -3 to 3
- conv_three: float32 [3, 512], P(None, 'mp'), may hold values from -3 to 3
- conv_four: float32 [4, 512], P(None, 'mp'), may hold values from -3 to 3
- join_weight: bfloat16 [512, 512], P('mp'), may hold values from -0.25 to 0.25
- norm_gain: float32 [512], replicated, may hold values from 0.5 to 1.5
- query_weight: bfloat16 [512, 512], P(None, 'mp'), may hold values from -0.125 to 0.125
- key_weight: bfloat16 [512, 512], P(None, 'mp'), may hold values from -0.125 to 0.125
- value_weight: bfloat16 [512, 512], P(None, 'mp'), may hold values from -0.25 to 0.25
- position_bias: float32 [32, 8], P(None, 'mp'), may hold values from -4 to 4
- out_weight: bfloat16 [512, 512], P('mp'), may hold values from -1 to 1
- ffn_gain: float32 [512], replicated, may hold values from 0.5 to 1.5
- gate_weight: bfloat16 [512, 2048], P(None, 'mp'), may hold values from -0.25 to 0.25
- up_weight: bfloat16 [512, 2048], P(None, 'mp'), may hold values from -0.25 to 0.25
- down_weight: bfloat16 [2048, 512], P('mp'), may hold values from -0.125 to 0.125
- out_grad: bfloat16 [2048, 8, 512], P('mp', 'dp'), may hold values from -6 to 6
Outputs:
- out_states: float32 [2048, 8, 512], P('mp', 'dp')
- input_grad: float32 [2048, 8, 512], P('mp', 'dp')
- conv_two_grad: float32 [2, 512], P(None, 'mp')
- conv_three_grad: float32 [3, 512], P(None, 'mp')
- conv_four_grad: float32 [4, 512], P(None, 'mp')
- join_weight_grad: float32 [512, 512], P('mp')
- norm_gain_grad: float32 [512], replicated
- query_weight_grad: float32 [512, 512], P(None, 'mp')
- key_weight_grad: float32 [512, 512], P(None, 'mp')
- value_weight_grad: float32 [512, 512], P(None, 'mp')
- position_bias_grad: float32 [32, 8], P(None, 'mp')
- out_weight_grad: float32 [512, 512], P('mp')
- ffn_gain_grad: float32 [512], replicated
- gate_weight_grad: float32 [512, 2048], P(None, 'mp')
- up_weight_grad: float32 [512, 2048], P(None, 'mp')
- down_weight_grad: float32 [2048, 512], P('mp')
The draws below stay inside these ranges and needn't reach their ends.
Inputs may be any that keep to these rules, and one draw needn't show every extreme that they name: word_start[0, s] = 1 for every sequence s; the number of words may differ from sequence to sequence.
All inputs are finite; a program needn't handle non-finite values.
Results may differ from the reference program's by a relative error of at most 0.017.
The reference program's roundings to bfloat16 on the way count: a program that leaves them out, or rounds other values in their place, can miss the bound.
Values may be sent and summed in bfloat16 or wider, within the bound.
A program may use at most 128 MiB of HBM per device.

```python
import jax
import jax.numpy as jnp
from jax import lax

D = 512
H = 8
FF = 2048
NB = 32
LEN = 2048
BATCH = 8


def draw_word_start(key, part):
    key = jax.random.fold_in(key, 11)
    rate_key, mark_key = jax.random.split(key)
    spacing = jax.random.randint(rate_key, (1, BATCH), 2, 12)
    marks = jax.random.randint(mark_key, (LEN, BATCH), 0, 1 << 20)
    starts = (marks % spacing == 0).astype(jnp.int32)
    return starts.at[0].set(1)


def with_ends(drawn, stream_key, low, largest):
    longest = drawn.shape.index(max(drawn.shape))
    spots = []
    for shift in (0, 1):
        where = [jax.random.randint(jax.random.fold_in(stream_key, axis), (), 0, length) for axis, length in enumerate(drawn.shape)]
        where[longest] = (where[longest] + shift) % drawn.shape[longest]
        spots.append(tuple(where))
    return drawn.at[spots[0]].set(low).at[spots[1]].set(largest)


def level_of(own_key, extent, shards, low, largest):
    def one(dim, shards_of):
        steps = jax.random.uniform(jax.random.fold_in(jax.random.fold_in(own_key, 6), dim), (shards_of,), jnp.float32, low / len(shards), largest / len(shards))
        return jnp.repeat(jnp.exp(steps), extent[dim] // shards_of).reshape((-1,) + (1,) * (len(extent) - dim - 1))

    loudness = one(*shards[0])
    for cut in shards[1:]:
        loudness = loudness * one(*cut)
    return loudness


def gaussian(rng, dims, width, bound, cuts=(), held_as=jnp.bfloat16):
    entries = jax.random.normal(rng, dims, jnp.float32) * width
    if len(cuts) > 0:
        entries = level_of(rng, dims, cuts, -0.22, 0.18) * entries
    return jnp.clip(entries, min=-bound, max=bound).astype(held_as)


def setup_inputs(seed: int = 0) -> dict:
    seeds = jax.random.split(jax.random.key(seed), 19)
    byte_states = gaussian(seeds[0], (LEN, BATCH, D), 1.0, 6.0, ((0, 4), (1, 8)))
    word_start = draw_word_start(jax.random.fold_in(seeds[18], 71), 0)
    bucket_ids = with_ends(jax.random.randint(seeds[2], (2 * LEN - 1,), 0, NB), jax.random.fold_in(seeds[2], 1), 0, NB - 1).astype(jnp.int32)
    conv_two = gaussian(seeds[3], (2, D), 0.5, 3.0, ((1, 4),), jnp.float32)
    conv_three = gaussian(seeds[4], (3, D), 0.5, 3.0, ((1, 4),), jnp.float32)
    conv_four = gaussian(seeds[5], (4, D), 0.5, 3.0, ((1, 4),), jnp.float32)
    join_weight = gaussian(seeds[6], (D, D), D ** -0.5, 0.25, ((0, 4),))
    norm_gain = jnp.clip(1.0 + 0.1 * jax.random.normal(seeds[7], (D,), jnp.float32), 0.5, 1.5)
    query_weight = gaussian(seeds[8], (D, D), (4 * D) ** -0.5, 0.125, ((1, 4),))
    key_weight = gaussian(seeds[9], (D, D), (4 * D) ** -0.5, 0.125, ((1, 4),))
    value_weight = gaussian(seeds[10], (D, D), D ** -0.5, 0.25, ((1, 4),))
    position_bias = gaussian(seeds[11], (NB, H), 1.0, 4.0, ((1, 4),), jnp.float32)
    out_weight = gaussian(seeds[12], (D, D), (D // 16) ** -0.5, 1.0, ((0, 4),))
    ffn_gain = jnp.clip(1.0 + 0.1 * jax.random.normal(seeds[13], (D,), jnp.float32), 0.5, 1.5)
    gate_weight = gaussian(seeds[14], (D, FF), D ** -0.5, 0.25, ((1, 4),))
    up_weight = gaussian(seeds[15], (D, FF), D ** -0.5, 0.25, ((1, 4),))
    down_weight = gaussian(seeds[16], (FF, D), FF ** -0.5, 0.125, ((0, 4),))
    out_grad = gaussian(seeds[17], (LEN, BATCH, D), 1.0, 6.0, ((0, 4), (1, 8)))
    return dict(byte_states=byte_states, word_start=word_start, bucket_ids=bucket_ids, conv_two=conv_two, conv_three=conv_three, conv_four=conv_four, join_weight=join_weight, norm_gain=norm_gain, query_weight=query_weight, key_weight=key_weight, value_weight=value_weight, position_bias=position_bias, out_weight=out_weight, ffn_gain=ffn_gain, gate_weight=gate_weight, up_weight=up_weight, down_weight=down_weight, out_grad=out_grad)


EPSILON = 1e-06
HIGHEST = lax.Precision.HIGHEST

@jax.custom_vjp
def low(v):
    return lax.optimization_barrier(v.astype(jnp.bfloat16)).astype(jnp.float32)

@jax.custom_vjp
def low_back(v):
    return v

def low_keep(v):
    return (low(v), None)

def low_pass(kept, grad):
    return (grad,)

def back_keep(v):
    return (v, None)

def back_low(kept, grad):
    return (low(grad),)
low.defvjp(low_keep, low_pass)
low_back.defvjp(back_keep, back_low)

def both_low(values):
    return low(low_back(values))

def rms_scale(values, gain):
    return values * lax.rsqrt(lax.optimization_barrier(jnp.mean(values * values, axis=-1, keepdims=True)) + EPSILON) * gain

def shifted(values, steps):
    return jnp.pad(values, ((steps, 0), (0, 0)))[:values.shape[0]]

def block_forward(states, params, word_ids, counts, bucket_table):
    conv_two, conv_three, conv_four, join_weight, norm_gain, query_weight, key_weight, value_weight, position_bias, out_weight, ffn_gain, gate_weight, up_weight, down_weight = params
    length = states.shape[0]
    pooled = jax.ops.segment_sum(states, word_ids, num_segments=length) / jnp.maximum(counts, 1.0)[:, None]
    word_total = jnp.zeros_like(pooled)
    for conv_taps in (conv_two, conv_three, conv_four):
        for lag_steps in range(conv_taps.shape[0]):
            word_total = word_total + conv_taps[lag_steps] * shifted(pooled, lag_steps)
    word_mix = low(word_total)
    joined_rows = low_back(jnp.dot(word_mix[word_ids], join_weight, precision=HIGHEST))
    residual = states + joined_rows
    normed = low(rms_scale(residual, norm_gain))
    head_count = position_bias.shape[1]
    head_width = query_weight.shape[1] // head_count

    def project(weight):
        made = both_low(jnp.dot(normed, weight, precision=HIGHEST))
        return made.reshape(length, head_count, head_width).transpose(1, 0, 2)
    queries = project(query_weight)
    keys_all = project(key_weight)
    values_all = project(value_weight)

    def head_attend(inputs):
        query_rows, key_rows, value_rows, column = inputs
        scores = low_back(jnp.dot(query_rows, key_rows.T, precision=HIGHEST) + column[bucket_table])
        attn_probs = jax.nn.softmax(scores, axis=-1)
        return both_low(jnp.dot(low(attn_probs), value_rows, precision=HIGHEST))
    attended = lax.map(jax.checkpoint(head_attend), (queries, keys_all, values_all, position_bias.T))
    attended = attended.transpose(1, 0, 2).reshape(length, head_count * head_width)
    middle = residual + low_back(jnp.dot(attended, out_weight, precision=HIGHEST))
    normed_two = low(rms_scale(middle, ffn_gain))
    gate_value = low_back(jnp.dot(normed_two, gate_weight, precision=HIGHEST))
    up_value = low_back(jnp.dot(normed_two, up_weight, precision=HIGHEST))
    hidden = low(jax.nn.gelu(gate_value, approximate=True) * up_value)
    return middle + low_back(jnp.dot(hidden, down_weight, precision=HIGHEST))

def reference(byte_states, word_start, bucket_ids, conv_two, conv_three, conv_four, join_weight, norm_gain, query_weight, key_weight, value_weight, position_bias, out_weight, ffn_gain, gate_weight, up_weight, down_weight, out_grad):
    params = tuple((weight.astype(jnp.float32) for weight in (conv_two, conv_three, conv_four, join_weight, norm_gain, query_weight, key_weight, value_weight, position_bias, out_weight, ffn_gain, gate_weight, up_weight, down_weight)))
    length = byte_states.shape[0]
    word_ids = (jnp.cumsum(word_start, axis=0) - 1).astype(jnp.int32)
    offsets = (jnp.arange(length)[None, :] - jnp.arange(length)[:, None] + length - 1).astype(jnp.int32)
    bucket_table = bucket_ids[offsets]

    def one_sequence(totals, inputs):
        states, seq_ids, cotangent = inputs
        counts = jax.ops.segment_sum(jnp.ones(seq_ids.shape, jnp.float32), seq_ids, num_segments=length)
        result, backward = jax.vjp(lambda given, weights: block_forward(given, weights, seq_ids, counts, bucket_table), states, params)
        state_grad, param_grads = backward(cotangent)
        totals = jax.tree.map(lambda first_term, second_term: first_term + second_term, totals, param_grads)
        return (totals, (result, state_grad))
    zero_grads = jax.tree.map(jnp.zeros_like, params)
    totals, (outputs, grads) = lax.scan(one_sequence, zero_grads, (byte_states.astype(jnp.float32).transpose(1, 0, 2), word_ids.T, out_grad.astype(jnp.float32).transpose(1, 0, 2)))
    conv_two_grad, conv_three_grad, conv_four_grad, join_weight_grad, norm_gain_grad, query_weight_grad, key_weight_grad, value_weight_grad, position_bias_grad, out_weight_grad, ffn_gain_grad, gate_weight_grad, up_weight_grad, down_weight_grad = totals
    return (outputs.transpose(1, 0, 2), grads.transpose(1, 0, 2), conv_two_grad, conv_three_grad, conv_four_grad, join_weight_grad, norm_gain_grad, query_weight_grad, key_weight_grad, value_weight_grad, position_bias_grad, out_weight_grad, ffn_gain_grad, gate_weight_grad, up_weight_grad, down_weight_grad)
```

```python
import functools

import jax
import jax.numpy as jnp
from jax import lax
from jax.experimental import pallas as pl
from jax.experimental.pallas import tpu as pltpu
from jax.sharding import PartitionSpec as P

EPSILON = 1e-06
HIGHEST = lax.Precision.HIGHEST
LOG2E = 1.4426950408889634
F32 = jnp.float32
BF16 = jnp.bfloat16
LANES = 128
VMEM_LIMIT = 56 << 20


def whole(count):
    return [pl.BlockSpec(memory_space=pltpu.VMEM)] * count


def params():
    return pltpu.CompilerParams(vmem_limit_bytes=VMEM_LIMIT)


def dot(lhs, rhs):
    return jnp.dot(lhs, rhs, preferred_element_type=F32)


def split(values):
    high = values.astype(BF16)
    return high, (values - high.astype(F32)).astype(BF16)


def bucket_hits(bucket_ref, buckets):
    span = bucket_ref.shape[1]
    rows = lax.broadcasted_iota(jnp.int32, (buckets, span), 0)
    return rows == jnp.broadcast_to(bucket_ref[...], (buckets, span))


def bias_table_kernel(bucket_ref, bias_ref, table_ref):
    span = bucket_ref.shape[1]
    hits = bucket_hits(bucket_ref, bias_ref.shape[0])
    for head in range(bias_ref.shape[1]):
        line = jnp.sum(jnp.where(hits, bias_ref[:, head : head + 1], 0.0), axis=0, keepdims=True)
        skew = pltpu.roll(
            jnp.broadcast_to(line * LOG2E, (LANES, span)), span - LANES + 1, 1, stride=1, stride_axis=0
        )
        for block in range(span // LANES - 1):
            cut = slice(block * LANES, (block + 1) * LANES)
            table_ref[head, cut, :] = skew[:, cut].T


def bias_table(bucket_row, bias):
    span = bucket_row.shape[1]
    return pl.pallas_call(
        bias_table_kernel,
        out_shape=jax.ShapeDtypeStruct((bias.shape[1], span - LANES, LANES), F32),
        in_specs=whole(2),
        out_specs=whole(1)[0],
        compiler_params=params(),
    )(bucket_row, bias)


def bias_grad_kernel(table_ref, bucket_ref, grad_ref):
    span = bucket_ref.shape[1]
    hits = bucket_hits(bucket_ref, grad_ref.shape[0])
    columns = []
    for head in range(table_ref.shape[0]):
        blocks = [
            table_ref[head, block * LANES : (block + 1) * LANES, :].T
            for block in range(span // LANES - 1)
        ]
        skew = jnp.concatenate(blocks + [jnp.zeros((LANES, LANES), F32)], axis=1)
        rows = LANES // 2
        while rows >= 8:
            skew = skew[:rows] + pltpu.roll(skew[rows:], span - rows, 1)
            rows //= 2
        line = jnp.zeros((1, span), F32)
        for row in range(8):
            line = line + pltpu.roll(skew[row : row + 1], LANES - 1 - row, 1)
        columns.append(jnp.sum(jnp.where(hits, line, 0.0), axis=1, keepdims=True))
    grad_ref[...] = jnp.concatenate(columns, axis=1)


def bias_grad_sums(table, bucket_row, buckets):
    return pl.pallas_call(
        bias_grad_kernel,
        out_shape=jax.ShapeDtypeStruct((buckets, table.shape[0]), F32),
        in_specs=whole(2),
        out_specs=whole(1)[0],
        compiler_params=params(),
    )(table, bucket_row)


def attend_kernel(
    width, wide, deep, query_ref, key_ref, value_ref, table_ref, out_ref, total_ref, score_ref
):
    heads, length = key_ref.shape[0], key_ref.shape[1]
    blocks = length // wide

    def step(index, carry):
        head, block = index // blocks, index % blocks
        begin = pl.multiple_of(block * wide, wide)
        rows = pl.ds(pl.multiple_of(head * width, width), width)
        scaled = query_ref[rows, pl.ds(begin, wide)].astype(F32) * LOG2E
        queries = jnp.concatenate(split(scaled), axis=0)
        peak = jnp.full((8, wide), -1e30, F32)
        for part in range(length // deep):
            cut = slice(part * deep, (part + 1) * deep)
            raw = dot(key_ref[head, cut, :], queries)
            columns = []
            for lane in range(0, wide, LANES):
                offset = pl.multiple_of(part * deep - begin - lane + length - LANES, LANES)
                columns.append(raw[:, lane : lane + LANES] + table_ref[head, pl.ds(offset, deep), :])
            scores = jnp.concatenate(columns, axis=1)
            score_ref[cut, :] = scores
            peak = jnp.maximum(peak, jnp.max(scores.reshape(deep // 8, 8, wide), axis=0))
        peak = jnp.max(peak, axis=0, keepdims=True)
        sums = jnp.zeros((8, wide), F32)
        made = jnp.zeros((width, wide), F32)
        for part in range(length // deep):
            cut = slice(part * deep, (part + 1) * deep)
            raised = jnp.exp2(score_ref[cut, :] - peak)
            sums = sums + jnp.sum(raised.reshape(deep // 8, 8, wide), axis=0)
            made = made + dot(value_ref[rows, cut], raised.astype(BF16))
        total = jnp.sum(sums, axis=0, keepdims=True)
        out_ref[rows, pl.ds(begin, wide)] = made / total
        total_ref[head, :, pl.ds(begin, wide)] = peak + jnp.log2(total)
        return carry

    lax.fori_loop(0, heads * blocks, step, 0)


def attend(queries, twice_keys, values, table, width):
    heads, length, _ = twice_keys.shape
    wide = deep = min(512, length)
    return pl.pallas_call(
        functools.partial(attend_kernel, width, wide, deep),
        out_shape=(
            jax.ShapeDtypeStruct(queries.shape, F32),
            jax.ShapeDtypeStruct((heads, 1, length), F32),
        ),
        in_specs=whole(4),
        out_specs=whole(2),
        scratch_shapes=[pltpu.VMEM((length, wide), F32)],
        compiler_params=params(),
    )(queries, twice_keys, values, table)


def attend_back_kernel(
    width,
    wide,
    deep,
    query_t_ref,
    query_ref,
    twice_key_ref,
    key_t_ref,
    value_ref,
    grad_t_ref,
    grad_ref,
    out_ref,
    total_ref,
    table_ref,
    query_grad_ref,
    key_grad_ref,
    value_grad_ref,
    table_grad_ref,
):
    heads, length = twice_key_ref.shape[0], twice_key_ref.shape[1]
    inner = heads * width
    blocks = length // wide
    key_grad_ref[...] = jnp.zeros_like(key_grad_ref)
    value_grad_ref[...] = jnp.zeros_like(value_grad_ref)
    table_grad_ref[...] = jnp.zeros_like(table_grad_ref)

    def step(index, carry):
        head, block = index // blocks, index % blocks
        begin = pl.multiple_of(block * wide, wide)
        span = pl.ds(begin, wide)
        rows = pl.ds(pl.multiple_of(head * width, width), width)
        scaled = query_t_ref[rows, span].astype(F32) * LOG2E
        queries = jnp.concatenate(split(scaled), axis=0)
        total = total_ref[head, :, span]
        grads = grad_t_ref[rows, span].astype(F32)
        dots = jnp.sum(grads * out_ref[rows, span], axis=0, keepdims=True)
        own_rows = lax.broadcasted_iota(jnp.int32, (inner, wide), 0) // width == head
        own_lanes = lax.broadcasted_iota(jnp.int32, (wide, inner), 1) // width == head
        grad_t_own = jnp.where(own_rows, grad_t_ref[:, span].astype(F32), 0.0).astype(BF16)
        query_own = jnp.where(own_lanes, query_ref[span, :].astype(F32), 0.0).astype(BF16)
        grad_own = jnp.where(own_lanes, grad_ref[span, :].astype(F32), 0.0).astype(BF16)
        query_grad = jnp.zeros((width, wide), F32)
        for part in range(length // deep):
            cut = slice(part * deep, (part + 1) * deep)
            raw = dot(twice_key_ref[head, cut, :], queries)
            raw_grad = dot(value_ref[cut, :], grad_t_own)
            probs, score_grads = [], []
            for lane in range(0, wide, LANES):
                piece = slice(lane, lane + LANES)
                offset = pl.multiple_of(part * deep - begin - lane + length - LANES, LANES)
                shift = table_ref[head, pl.ds(offset, deep), :]
                prob = jnp.exp2(raw[:, piece] + shift - total[:, piece])
                low = (prob * (raw_grad[:, piece] - dots[:, piece])).astype(BF16)
                table_grad_ref[head, pl.ds(offset, deep), :] += low.astype(F32)
                probs.append(prob.astype(BF16))
                score_grads.append(low)
            probs = jnp.concatenate(probs, axis=1)
            score_grads = jnp.concatenate(score_grads, axis=1)
            value_grad_ref[cut, :] += dot(probs, grad_own)
            key_grad_ref[cut, :] += dot(score_grads, query_own)
            query_grad = query_grad + dot(key_t_ref[rows, cut], score_grads)
        query_grad_ref[rows, span] = query_grad
        return carry

    lax.fori_loop(0, heads * blocks, step, 0)


def attend_back(queries_t, queries, twice_keys, keys_t, values, grads_t, grads, outs, totals, table, width):
    heads, length, _ = twice_keys.shape
    wide, deep = min(512, length), min(256, length)
    inner = heads * width
    return pl.pallas_call(
        functools.partial(attend_back_kernel, width, wide, deep),
        out_shape=(
            jax.ShapeDtypeStruct((inner, length), F32),
            jax.ShapeDtypeStruct((length, inner), F32),
            jax.ShapeDtypeStruct((length, inner), F32),
            jax.ShapeDtypeStruct(table.shape, F32),
        ),
        in_specs=whole(10),
        out_specs=whole(4),
        compiler_params=params(),
    )(queries_t, queries, twice_keys, keys_t, values, grads_t, grads, outs, totals, table)


def rms_scale(values, gain):
    return values * lax.rsqrt(jnp.mean(values * values, axis=-1, keepdims=True) + EPSILON) * gain


def gelu_tanh(values):
    return jax.nn.gelu(values, approximate=True)


def word_table(word_ids, length):
    matches = word_ids.T[:, None, :] == jnp.arange(length)[None, :, None]
    return matches.astype(jnp.bfloat16)


def word_sums_low(values, table):
    return jnp.einsum("bwt,tbc->wbc", table, values, preferred_element_type=jnp.float32)


def word_sums_wide(values, table):
    return jnp.einsum(
        "bwt,tbc->wbc",
        table.astype(jnp.float32),
        values,
        preferred_element_type=jnp.float32,
        precision=HIGHEST,
    )


def by_word_low(word_values, table):
    return jnp.einsum(
        "bwt,wbc->tbc", table, word_values, preferred_element_type=jnp.float32
    ).astype(jnp.bfloat16)


def by_word_wide(word_values, table):
    return jnp.einsum(
        "bwt,wbc->tbc",
        table.astype(jnp.float32),
        word_values,
        preferred_element_type=jnp.float32,
        precision=HIGHEST,
    )


def lagged(values, steps):
    if steps == 0:
        return values
    return jnp.pad(values, ((steps, 0), (0, 0), (0, 0)))[: values.shape[0]]


def leading(values, steps):
    return jnp.pad(values, ((0, steps), (0, 0), (0, 0)))[steps:]


def spread_rows(term, rows):
    return lax.psum_scatter(
        term(jnp.int32(0), rows * lax.axis_size("mp")), "mp", scatter_dimension=0, tiled=True
    )


def spread_grads(term, rows):
    return lax.psum_scatter(
        term(jnp.int32(0), rows * lax.axis_size("mp")), "mp", scatter_dimension=0, tiled=True
    )


def gather_normed(values):
    return lax.all_gather(values, "mp", axis=0, tiled=True)


def gather_grads(values):
    return lax.all_gather(values, "mp", axis=0, tiled=True)


def shards(
    byte_states,
    word_start,
    bucket_ids,
    conv_two,
    conv_three,
    conv_four,
    join_weight,
    norm_gain,
    query_weight,
    key_weight,
    value_weight,
    position_bias,
    out_weight,
    ffn_gain,
    gate_weight,
    up_weight,
    down_weight,
    out_grad,
):
    local_rows = byte_states.shape[0]
    batch_seqs = byte_states.shape[1]
    length = word_start.shape[0]
    head_count = position_bias.shape[1]
    head_width = query_weight.shape[1] // head_count
    inner = head_count * head_width
    word_ids = jnp.cumsum(word_start, axis=0) - 1
    table = word_table(word_ids, length)
    counts = jnp.sum(table.astype(jnp.float32), axis=2).T[:, :, None]
    divisor = jnp.maximum(counts, 1.0)
    channel_states = lax.all_to_all(byte_states, "mp", split_axis=2, concat_axis=0, tiled=True)
    pooled = word_sums_low(channel_states, table) / divisor
    merged_taps = [
        conv_two[0] + conv_three[0] + conv_four[0],
        conv_two[1] + conv_three[1] + conv_four[1],
        conv_three[2] + conv_four[2],
        conv_four[3],
    ]
    word_total = pooled * merged_taps[0]
    for lag_steps in range(1, 4):
        word_total = word_total + lagged(pooled, lag_steps) * merged_taps[lag_steps]
    word_mix = word_total.astype(jnp.bfloat16)
    byte_mix = by_word_low(word_mix, table)

    def joining_term(start, count):
        return jnp.einsum("tbc,cd->tbd", byte_mix, join_weight, preferred_element_type=jnp.float32)

    residual = byte_states.astype(jnp.float32) + spread_rows(joining_term, local_rows)
    normed_value, norm_back_one = jax.vjp(rms_scale, residual, norm_gain)
    normed = normed_value.astype(jnp.bfloat16)
    normed_full = gather_normed(normed)
    joint_weight = jnp.concatenate([query_weight, key_weight, value_weight], axis=1)
    joint = jnp.einsum(
        "tbd,de->tbe", normed_full, joint_weight, preferred_element_type=jnp.float32
    ).astype(jnp.bfloat16)
    queries = joint[:, 0, :inner]
    keys = joint[:, 0, inner : 2 * inner]
    values = joint[:, 0, 2 * inner :]
    bucket_row = jnp.pad(bucket_ids, (0, 1), constant_values=-1)[None]
    table_bias = bias_table(bucket_row, position_bias)
    queries_t = queries.T
    by_head = keys.reshape(length, head_count, head_width).transpose(1, 0, 2)
    twice_keys = jnp.concatenate([by_head, by_head], axis=2)
    outs, totals = attend(queries_t, twice_keys, values.T, table_bias, head_width)
    attended_flat = outs.astype(BF16).T[:, None, :]

    def attention_term(start, count):
        return jnp.einsum(
            "tbe,ed->tbd", attended_flat, out_weight, preferred_element_type=jnp.float32
        )

    middle = residual + spread_rows(attention_term, local_rows)
    normed_two_value, norm_back_two = jax.vjp(rms_scale, middle, ffn_gain)
    normed_two = normed_two_value.astype(jnp.bfloat16)
    gate_full, up_full, down_full = (gate_weight, up_weight, down_weight)
    ffn_input = gather_normed(normed_two)
    gate_value = jnp.einsum("tbd,df->tbf", ffn_input, gate_full, preferred_element_type=jnp.float32)
    up_value = jnp.einsum("tbd,df->tbf", ffn_input, up_full, preferred_element_type=jnp.float32)
    gelu_value, gelu_back = jax.vjp(gelu_tanh, gate_value)
    hidden = (gelu_value * up_value).astype(jnp.bfloat16)

    def ffn_term(start, count):
        return jnp.einsum("tbf,fd->tbd", hidden, down_full, preferred_element_type=jnp.float32)

    ffn_out = spread_rows(ffn_term, local_rows)
    out_states = middle + ffn_out
    grad_input = gather_grads(out_grad)
    d_hidden = jnp.einsum("tbd,fd->tbf", grad_input, down_full, preferred_element_type=jnp.float32)
    down_grad = jnp.einsum("tbf,tbd->fd", hidden, grad_input, preferred_element_type=jnp.float32)
    d_gate = gelu_back(d_hidden * up_value)[0].astype(jnp.bfloat16)
    d_up = (d_hidden * gelu_value).astype(jnp.bfloat16)
    gate_grad = jnp.einsum("tbd,tbf->df", ffn_input, d_gate, preferred_element_type=jnp.float32)
    up_grad = jnp.einsum("tbd,tbf->df", ffn_input, d_up, preferred_element_type=jnp.float32)

    def ffn_back_term(start, count):
        return jnp.einsum(
            "tbf,df->tbd", d_gate, gate_full, preferred_element_type=jnp.float32
        ) + jnp.einsum("tbf,df->tbd", d_up, up_full, preferred_element_type=jnp.float32)

    d_normed_two = spread_grads(ffn_back_term, local_rows)
    d_middle_part, ffn_gain_grad = norm_back_two(d_normed_two)
    d_middle = out_grad.astype(jnp.float32) + d_middle_part
    d_attn_full = gather_grads(d_middle.astype(jnp.bfloat16))
    out_weight_grad = jnp.einsum(
        "tbe,tbd->ed", attended_flat, d_attn_full, preferred_element_type=jnp.float32
    )
    d_attended = jnp.einsum(
        "tbd,ed->tbe", d_attn_full, out_weight, preferred_element_type=jnp.float32
    )
    d_attended = d_attended.astype(BF16)[:, 0, :]
    query_grad, key_grad, value_grad, table_grad = attend_back(
        queries_t,
        queries,
        twice_keys,
        keys.T,
        values,
        d_attended.T,
        d_attended,
        outs,
        totals,
        table_bias,
        head_width,
    )
    d_joint = jnp.concatenate(
        [query_grad.T.astype(BF16), key_grad.astype(BF16), value_grad.astype(BF16)], axis=1
    )[:, None, :]
    joint_grad = jnp.einsum("tbd,tbe->de", normed_full, d_joint, preferred_element_type=jnp.float32)
    bias_grad = bias_grad_sums(table_grad, bucket_row, position_bias.shape[0])

    def attention_back_term(start, count):
        return jnp.einsum("tbe,de->tbd", d_joint, joint_weight, preferred_element_type=jnp.float32)

    d_normed = spread_grads(attention_back_term, local_rows)
    d_residual_part, norm_gain_grad = norm_back_one(d_normed)
    d_residual = d_middle + d_residual_part
    d_joined_full = gather_grads(d_residual.astype(jnp.bfloat16))
    join_grad = jnp.einsum(
        "tbc,tbd->cd", byte_mix, d_joined_full, preferred_element_type=jnp.float32
    )
    d_byte_mix = jnp.einsum(
        "tbd,cd->tbc", d_joined_full, join_weight, preferred_element_type=jnp.float32
    )
    d_word_mix = word_sums_wide(d_byte_mix, table)
    tap_grads = [
        jnp.sum(lagged(pooled, lag_steps) * d_word_mix, axis=(0, 1)) for lag_steps in range(4)
    ]
    d_pooled = d_word_mix * merged_taps[0]
    for lag_steps in range(1, 4):
        d_pooled = d_pooled + leading(d_word_mix, lag_steps) * merged_taps[lag_steps]
    d_channel_bytes = by_word_wide(d_pooled / divisor, table)
    input_grad = d_residual + lax.all_to_all(
        d_channel_bytes, "mp", split_axis=0, concat_axis=2, tiled=True
    )
    summed = lax.psum(
        (
            jnp.stack(tap_grads[:2]),
            jnp.stack(tap_grads[:3]),
            jnp.stack(tap_grads),
            join_grad,
            joint_grad[:, :inner],
            joint_grad[:, inner : 2 * inner],
            joint_grad[:, 2 * inner :],
            bias_grad,
            out_weight_grad,
            gate_grad,
            up_grad,
            down_grad,
        ),
        "dp",
    )
    gain_totals = lax.psum((norm_gain_grad, ffn_gain_grad), ("dp", "mp"))
    (
        conv_two_grad,
        conv_three_grad,
        conv_four_grad,
        join_weight_grad,
        query_weight_grad,
        key_weight_grad,
        value_weight_grad,
        position_bias_grad,
        out_weight_total,
        gate_weight_grad,
        up_weight_grad,
        down_weight_grad,
    ) = summed
    return (
        out_states,
        input_grad,
        conv_two_grad,
        conv_three_grad,
        conv_four_grad,
        join_weight_grad,
        gain_totals[0],
        query_weight_grad,
        key_weight_grad,
        value_weight_grad,
        position_bias_grad,
        out_weight_total,
        gain_totals[1],
        gate_weight_grad,
        up_weight_grad,
        down_weight_grad,
    )


def solution(mesh):
    return jax.shard_map(
        shards,
        mesh=mesh,
        in_specs=(
            P("mp", "dp", None),
            P(None, "dp"),
            P(),
            P(None, "mp"),
            P(None, "mp"),
            P(None, "mp"),
            P("mp", None),
            P(),
            P(None, "mp"),
            P(None, "mp"),
            P(None, "mp"),
            P(None, "mp"),
            P("mp", None),
            P(),
            P(None, "mp"),
            P(None, "mp"),
            P("mp", None),
            P("mp", "dp", None),
        ),
        out_specs=(
            P("mp", "dp", None),
            P("mp", "dp", None),
            P(None, "mp"),
            P(None, "mp"),
            P(None, "mp"),
            P("mp", None),
            P(),
            P(None, "mp"),
            P(None, "mp"),
            P(None, "mp"),
            P(None, "mp"),
            P("mp", None),
            P(),
            P(None, "mp"),
            P(None, "mp"),
            P("mp", None),
        ),
        check_vma=False,
    )
```

```python
import functools

import jax
import jax.numpy as jnp
from jax import lax
from jax.experimental import pallas as pl
from jax.experimental.pallas import tpu as pltpu
from jax.sharding import PartitionSpec as P

EPSILON = 1e-06
LOG2E = 1.4426950408889634
GELU_SCALE = 0.7978845608028654
GELU_CUBE = 0.044715
F32 = jnp.float32
BF16 = jnp.bfloat16
LANES = 128
HALO = 3
VMEM_LIMIT = 56 << 20
MESH = pl.DeviceIdType.MESH


def whole(count):
    return [pl.BlockSpec(memory_space=pltpu.VMEM)] * count


def anywhere(count):
    return [pl.BlockSpec(memory_space=pl.ANY)] * count


def params(collective=None):
    return pltpu.CompilerParams(
        vmem_limit_bytes=VMEM_LIMIT, collective_id=collective, has_side_effects=collective is not None
    )


def like(shape, dtype):
    return jax.ShapeDtypeStruct(shape, dtype)


def dot(lhs, rhs):
    return jnp.dot(lhs, rhs, preferred_element_type=F32)


def dot_nt(lhs, rhs):
    return lax.dot_general(lhs, rhs, (((1,), (1,)), ((), ())), preferred_element_type=F32)


def dot_tn(lhs, rhs):
    return lax.dot_general(lhs, rhs, (((0,), (0,)), ((), ())), preferred_element_type=F32)


def split(values):
    high = values.astype(BF16)
    return high, (values - high.astype(F32)).astype(BF16)


def turned(values):
    return values.astype(F32).T.astype(BF16)


def ranks():
    me = lax.axis_index("mp")
    near = me + 1 - 2 * (me % 2)
    return me, near, (me + 2) % 4, (near + 2) % 4


def greet(peers):
    barrier = pltpu.get_barrier_semaphore()
    for peer in peers:
        pl.semaphore_signal(barrier, inc=1, device_id={"mp": peer}, device_id_type=MESH)
    pl.semaphore_wait(barrier, len(peers))


def remote(source, target, sems, slot, peer):
    sends, receives = sems
    return pltpu.make_async_remote_copy(
        src_ref=source,
        dst_ref=target,
        send_sem=sends.at[slot],
        recv_sem=receives.at[slot],
        device_id={"mp": peer},
        device_id_type=MESH,
    )


def semaphores(count):
    return [pltpu.SemaphoreType.DMA((count,)), pltpu.SemaphoreType.DMA((count,))]


def rms(values, gain):
    return values * lax.rsqrt(jnp.mean(values * values, axis=1, keepdims=True) + EPSILON) * gain


def rms_back(grads, values, gain):
    scale = lax.rsqrt(jnp.mean(values * values, axis=1, keepdims=True) + EPSILON)
    gain_grad = jnp.sum(grads * values * scale, axis=0, keepdims=True)
    raised = grads * gain
    mean = jnp.mean(raised * values, axis=1, keepdims=True)
    return scale * raised - values * (scale * scale * scale * mean), gain_grad


def bucket_hits(bucket_ref, buckets):
    span = bucket_ref.shape[1]
    rows = lax.broadcasted_iota(jnp.int32, (buckets, span), 0)
    return rows == jnp.broadcast_to(bucket_ref[...], (buckets, span))


def bias_table_kernel(bucket_ref, bias_ref, table_ref):
    span = bucket_ref.shape[1]
    hits = bucket_hits(bucket_ref, bias_ref.shape[0])
    for head in range(bias_ref.shape[1]):
        line = jnp.sum(jnp.where(hits, bias_ref[:, head : head + 1], 0.0), axis=0, keepdims=True)
        skew = pltpu.roll(
            jnp.broadcast_to(line * LOG2E, (LANES, span)), span - LANES + 1, 1, stride=1, stride_axis=0
        )
        for block in range(span // LANES - 1):
            cut = slice(block * LANES, (block + 1) * LANES)
            table_ref[head, cut, :] = skew[:, cut].T


def bias_grad_kernel(table_ref, bucket_ref, grad_ref):
    span = bucket_ref.shape[1]
    hits = bucket_hits(bucket_ref, grad_ref.shape[0])
    columns = []
    for head in range(table_ref.shape[0]):
        blocks = [
            table_ref[head, block * LANES : (block + 1) * LANES, :].T
            for block in range(span // LANES - 1)
        ]
        skew = jnp.concatenate(blocks + [jnp.zeros((LANES, LANES), F32)], axis=1)
        rows = LANES // 2
        while rows >= 8:
            skew = skew[:rows] + pltpu.roll(skew[rows:], span - rows, 1)
            rows //= 2
        line = jnp.zeros((1, span), F32)
        for row in range(8):
            line = line + pltpu.roll(skew[row : row + 1], LANES - 1 - row, 1)
        columns.append(jnp.sum(jnp.where(hits, line, 0.0), axis=1, keepdims=True))
    grad_ref[...] = jnp.concatenate(columns, axis=1)


def word_numbers(starts):
    rows = starts.shape[0]
    upper = lax.broadcasted_iota(jnp.int32, (LANES, LANES), 0) <= lax.broadcasted_iota(
        jnp.int32, (LANES, LANES), 1
    )
    within = dot(starts.astype(F32).astype(BF16), upper.astype(F32).astype(BF16))
    totals = jnp.broadcast_to(within[:, LANES - 1 :], (rows, LANES)).astype(BF16)
    lower = lax.broadcasted_iota(jnp.int32, (rows, rows), 1) < lax.broadcasted_iota(
        jnp.int32, (rows, rows), 0
    )
    return within + dot(lower.astype(F32).astype(BF16), totals) - 1.0


class Words:
    def __init__(self, starts_ref, ids_ref, me, ranks_count):
        ids = word_numbers(starts_ref[...])
        ids_ref[...] = ids
        per = ids.shape[0] // ranks_count
        self.firsts = [ids[per * rank : per * rank + 1, 0:1] for rank in range(ranks_count)]
        self.lasts = [
            ids[per * (rank + 1) - 1 : per * (rank + 1), LANES - 1 :] for rank in range(ranks_count)
        ]
        pieces = [ids_ref[pl.ds(me * per + piece, 1), :] for piece in range(per)]
        self.row = jnp.concatenate(pieces, axis=1)
        self.first = self.row[:, 0:1]
        self.last = self.row[:, per * LANES - 1 :]
        self.me = me
        self.count = per * LANES

    def table(self):
        shape = (self.count + 16, self.count)
        rows = lax.broadcasted_iota(jnp.int32, shape, 0).astype(F32)
        return (rows == self.row - self.first + HALO).astype(F32).astype(BF16)

    def pick(self, target):
        slots = lax.broadcasted_iota(jnp.int32, (8, 1), 0)
        hits = target(slots, self.first, self.last) == self.row
        return hits.astype(F32).astype(BF16)

    def place(self, target, valid):
        width = 2 * LANES
        lane = lax.broadcasted_iota(jnp.int32, (1, width), 1) % LANES
        slots, rank = lane % 8, lane // 8
        goal = jnp.full((1, width), -9.0, F32)
        for index, (first, last) in enumerate(zip(self.firsts, self.lasts)):
            goal = jnp.where(rank == index, target(slots, first, last), goal)
        known = valid(slots, rank, self.me) & (rank < len(self.firsts))
        goal = jnp.where(known, goal - self.first + HALO, -1.0)
        rows = lax.broadcasted_iota(jnp.int32, (self.count + 16, width), 0).astype(F32)
        return (rows == goal).astype(F32).astype(BF16)


def stacked(summary_ref):
    parts = [summary_ref[rank] for rank in range(summary_ref.shape[0])]
    rest = LANES - sum(part.shape[0] for part in parts)
    parts.append(jnp.zeros((rest, parts[0].shape[1]), F32))
    return jnp.concatenate(split(jnp.concatenate(parts, axis=0)), axis=0)


def ahead_target(slots, first, last):
    later = jnp.where(slots <= 4, last - (slots - 1).astype(F32), -9.0)
    return jnp.where(slots == 0, first, later)


def ahead_valid(slots, rank, me):
    return ((rank < me) & (slots >= 1) & (slots <= 4)) | ((rank > me) & (slots == 0))


def back_target(slots, first, last):
    return jnp.where(slots <= 3, first + slots.astype(F32), jnp.where(slots == 4, last, -9.0))


def back_valid(slots, rank, me):
    return ((rank > me) & (slots <= 3)) | ((rank < me) & (slots == 4))


def join_kernel(
    width,
    states_ref,
    starts_ref,
    taps_ref,
    join_ref,
    gain_ref,
    joint_ref,
    bucket_ref,
    bias_ref,
    residual_ref,
    normed_ref,
    query_ref,
    query_t_ref,
    twice_ref,
    key_t_ref,
    value_ref,
    value_t_ref,
    table_ref,
    divisor_ref,
    pooled_ref,
    mix_ref,
    all_taps_ref,
    all_join_ref,
    ids_ref,
    summary_ref,
    taps_in_ref,
    *sems,
):
    me, near, far, cross = ranks()
    peers = (near, far, cross)
    rows, model = states_ref.shape
    share = join_ref.shape[0]
    words = Words(starts_ref, ids_ref, me, 4)
    states = states_ref[...]
    wide_states = jnp.concatenate([states, jnp.ones((rows, LANES), BF16)], axis=1)
    summary_ref[me] = dot(words.pick(ahead_target), wide_states)
    taps_in_ref[me] = taps_ref[...]
    all_join_ref[pl.ds(pl.multiple_of(me * share, share), share), :] = join_ref[...]
    greet(peers)
    early = []
    for slot, peer in enumerate(peers):
        part = all_join_ref.at[pl.ds(pl.multiple_of(me * share, share), share), :]
        early.append(remote(summary_ref.at[me], summary_ref.at[me], sems, slot, peer))
        early.append(remote(taps_in_ref.at[me], taps_in_ref.at[me], sems, 3 + slot, peer))
        early.append(remote(part, part, sems, 6 + slot, peer))
    for copy in early:
        copy.start()
    table = words.table()
    sums = dot(table, wide_states)
    place = words.place(ahead_target, ahead_valid)
    for copy in early:
        copy.wait()
    sums = sums + dot(place, stacked(summary_ref))
    divisor = jnp.maximum(sums[:, model:], 1.0)
    divisor_ref[...] = divisor
    pooled = sums[:, :model] / jnp.concatenate([divisor] * (model // LANES), axis=1)
    pooled_ref[...] = pooled
    taps = jnp.concatenate([taps_in_ref[rank] for rank in range(4)], axis=1)
    all_taps_ref[...] = taps
    total = pooled * taps[0:1]
    for lag in range(1, 4):
        total = total + pltpu.roll(pooled, lag, 0) * taps[lag : lag + 1]
    mix = dot_tn(table, total.astype(BF16)).astype(BF16)
    mix_ref[...] = mix
    residual = states.astype(F32) + dot(mix, all_join_ref[...])
    residual_ref[...] = residual
    own = pl.ds(pl.multiple_of(me * rows, rows), rows)
    normed_ref[own, :] = rms(residual, gain_ref[...]).astype(BF16)

    def block(rank, part):
        half = rows // 2
        return normed_ref.at[pl.ds(pl.multiple_of(rank * rows + part * half, half), half), :]

    sends = []
    for part in range(2):
        sends.append(remote(block(me, part), block(me, part), sems, 9 + part, far))
    for part in range(2):
        sends.append(remote(block(me, part), block(me, part), sems, 11 + part, near))
    for copy in sends:
        copy.start()

    def project(rank):
        cut = pl.ds(pl.multiple_of(rank * rows, rows), rows)
        made = dot(normed_ref[cut, :], joint_ref[...])
        inner = query_ref.shape[1]
        query, key, value = [
            made[:, index * inner : (index + 1) * inner].astype(BF16) for index in range(3)
        ]
        query_ref[cut, :] = query
        query_t_ref[:, cut] = turned(query)
        key_t_ref[:, cut] = turned(key)
        value_ref[cut, :] = value
        value_t_ref[:, cut] = turned(value)
        for head in range(inner // width):
            part = key[:, head * width : (head + 1) * width]
            twice_ref[head, cut, :] = jnp.concatenate([part, part], axis=1)

    project(me)
    bias_table_kernel(bucket_ref, bias_ref, table_ref)
    sends[2].wait_recv()
    sends[3].wait_recv()
    project(near)
    passed = []
    for part in range(2):
        sends[part].wait_recv()
        passed.append(remote(block(far, part), block(far, part), sems, 13 + part, near))
        passed[part].start()
    project(far)
    for copy in passed:
        copy.wait_recv()
    project(cross)
    for copy in sends + passed:
        copy.wait_send()


def attend_kernel(
    width,
    query_ref,
    twice_ref,
    value_ref,
    table_ref,
    out_weight_ref,
    gate_ref,
    up_ref,
    down_ref,
    grad_ref,
    out_ref,
    total_ref,
    attended_ref,
    all_out_ref,
    near_gate_ref,
    near_up_ref,
    near_down_ref,
    far_grad_ref,
    score_ref,
    stage_ref,
    *sems,
):
    me, near, far, cross = ranks()
    peers = (near, far, cross)
    heads, length = twice_ref.shape[0], twice_ref.shape[1]
    share, model = out_weight_ref.shape
    wide = deep = length // 4
    all_out_ref[pl.ds(pl.multiple_of(me * share, share), share), :] = out_weight_ref[...]
    greet(peers)
    copies = [
        remote(gate_ref, near_gate_ref, sems, 4, near),
        remote(up_ref, near_up_ref, sems, 5, near),
        remote(down_ref, near_down_ref, sems, 6, near),
    ]
    for slot, peer in enumerate(peers):
        part = all_out_ref.at[pl.ds(pl.multiple_of(me * share, share), share), :]
        copies.append(remote(part, part, sems, 7 + slot, peer))
    copies.append(remote(grad_ref, far_grad_ref, sems, 10, far))
    for copy in copies:
        copy.start()

    def owner(order):
        chip = (me // 2 + 1 + order // 2) % 2
        core = (me % 2 + (order + 1) // 2) % 2
        return 2 * chip + core

    def handed(order):
        return remote(stage_ref.at[order], attended_ref.at[me], sems, order, owner(order))

    def step(index, carry):
        order, head = index // heads, index % heads
        begin = pl.multiple_of(owner(order) * wide, wide)
        span = pl.ds(begin, wide)
        rows = pl.ds(pl.multiple_of(head * width, width), width)
        scaled = query_ref[rows, span].astype(F32) * LOG2E
        queries = jnp.concatenate(split(scaled), axis=0)
        peak = jnp.full((8, wide), -1e30, F32)
        for part in range(length // deep):
            cut = slice(part * deep, (part + 1) * deep)
            raw = dot(twice_ref[head, cut, :], queries)
            columns = []
            for lane in range(0, wide, LANES):
                offset = pl.multiple_of(part * deep - begin - lane + length - LANES, LANES)
                columns.append(raw[:, lane : lane + LANES] + table_ref[head, pl.ds(offset, deep), :])
            scores = jnp.concatenate(columns, axis=1)
            score_ref[cut, :] = scores
            peak = jnp.maximum(peak, jnp.max(scores.reshape(deep // 8, 8, wide), axis=0))
        peak = jnp.max(peak, axis=0, keepdims=True)
        sums = jnp.zeros((8, wide), F32)
        made = jnp.zeros((width, wide), F32)
        for part in range(length // deep):
            cut = slice(part * deep, (part + 1) * deep)
            raised = jnp.exp2(score_ref[cut, :] - peak)
            sums = sums + jnp.sum(raised.reshape(deep // 8, 8, wide), axis=0)
            made = made + dot(value_ref[rows, cut], raised.astype(BF16))
        total = jnp.sum(sums, axis=0, keepdims=True)
        made = made / total
        out_ref[rows, span] = made
        total_ref[head, :, span] = peak + jnp.log2(total)
        stage_ref[order, rows, :] = made.astype(BF16)

        @pl.when((head == heads - 1) & (order < 3))
        def _():
            handed(order).start()

        return carry

    lax.fori_loop(0, heads * 4, step, 0)
    attended_ref[me] = stage_ref[3]
    for order in range(3):
        handed(order).wait()
    for copy in copies:
        copy.wait()


def ffn_kernel(
    attended_ref,
    all_out_ref,
    residual_ref,
    gain_ref,
    grad_ref,
    far_grad_ref,
    gate_ref,
    near_gate_ref,
    up_ref,
    near_up_ref,
    down_ref,
    near_down_ref,
    states_out_ref,
    middle_grad_ref,
    gain_grad_ref,
    gate_grad_ref,
    up_grad_ref,
    down_grad_ref,
    out_grad_ref,
    attended_grad_ref,
    middle_ref,
    normed_ref,
    made_ref,
    back_ref,
    sums_ref,
    far_out_ref,
    far_in_ref,
    near_out_ref,
    near_in_ref,
    part_out_ref,
    part_in_ref,
    grad_stage_ref,
    *sems,
):
    me, near, far, cross = ranks()
    peers = (near, far, cross)
    rows, model = residual_ref.shape
    share = attended_ref.shape[1]
    attended = attended_ref[...].reshape(4 * share, rows)
    middle = residual_ref[...] + dot_tn(attended, all_out_ref[...])
    middle_ref[...] = middle
    normed_ref[0] = rms(middle, gain_ref[...]).astype(BF16)
    greet(peers)
    there = remote(normed_ref.at[0], normed_ref.at[1], sems, 0, far)
    there.start()

    def work(side, grads, gate, up, down, slab):
        given = normed_ref[side]
        gate_value = dot(given, gate)
        up_value = dot(given, up)
        hidden_grad = dot_nt(grads, down)
        square = gate_value * gate_value
        curve = jnp.tanh(GELU_SCALE * gate_value * (1.0 + GELU_CUBE * square))
        half = 0.5 + 0.5 * curve
        gelu = gate_value * half
        slope = half + (0.5 * GELU_SCALE) * gate_value * (1.0 - curve * curve) * (
            1.0 + (3.0 * GELU_CUBE) * square
        )
        hidden = (gelu * up_value).astype(BF16)
        gate_back = (hidden_grad * up_value * slope).astype(BF16)
        up_back = (hidden_grad * gelu).astype(BF16)
        sums = [dot_tn(given, gate_back), dot_tn(given, up_back), dot_tn(hidden, grads)]
        for index in range(3):
            if side == 0:
                sums_ref[slab, index] = sums[index]
            else:
                sums_ref[slab, index] += sums[index]
        made = dot(hidden, down)
        back = dot_nt(gate_back, gate) + dot_nt(up_back, up)
        if slab == 0:
            made_ref[side] = made
            back_ref[side] = back
        else:
            made_ref[side] += made
            back_ref[side] += back

    mine = (gate_ref, up_ref, down_ref)
    other = (near_gate_ref, near_up_ref, near_down_ref)
    for slab, weights in enumerate((mine, other)):
        work(0, grad_ref[...], *[ref[...] for ref in weights], slab)
    there.wait_recv()
    for slab, weights in enumerate((mine, other)):
        work(1, far_grad_ref[...], *[ref[...] for ref in weights], slab)
    far_out_ref[0] = back_ref[1].astype(BF16)
    returned = [remote(far_out_ref.at[0], far_in_ref.at[0], sems, 1, far)]
    returned[0].start()
    far_out_ref[1] = made_ref[1].astype(BF16)
    returned.append(remote(far_out_ref.at[1], far_in_ref.at[1], sems, 2, far))
    returned[1].start()
    near_out_ref[...] = sums_ref[1].astype(BF16)
    swap = remote(near_out_ref, near_in_ref, sems, 3, near)
    swap.start()
    returned[0].wait_recv()
    normed_grad = back_ref[0] + far_in_ref[0].astype(F32)
    part, gain_grad = rms_back(normed_grad, middle_ref[...], gain_ref[...])
    gain_grad_ref[...] = jnp.broadcast_to(gain_grad, gain_grad_ref.shape)
    middle_grad = grad_ref[...].astype(F32) + part
    middle_grad_ref[...] = middle_grad
    low = middle_grad.astype(BF16)
    grad_stage_ref[...] = dot_nt(all_out_ref[...], low).astype(BF16).reshape(4, share, rows)
    copies = []
    for slot, peer in enumerate(peers):
        copies.append(remote(grad_stage_ref.at[peer], attended_grad_ref.at[me], sems, 4 + slot, peer))
        copies[-1].start()
    attended_grad_ref[me] = grad_stage_ref[me]
    part_out_ref[...] = dot(attended, low).astype(BF16).reshape(4, share, model)
    for slot, peer in enumerate(peers):
        copies.append(remote(part_out_ref.at[peer], part_in_ref.at[me], sems, 7 + slot, peer))
        copies[-1].start()
    part_in_ref[me] = part_out_ref[me]
    returned[1].wait_recv()
    states_out_ref[...] = middle_ref[...] + (made_ref[0] + far_in_ref[1].astype(F32))
    swap.wait_recv()
    for index, ref in enumerate((gate_grad_ref, up_grad_ref, down_grad_ref)):
        ref[...] = (sums_ref[0, index] + near_in_ref[index].astype(F32)).astype(BF16)
    for copy in copies:
        copy.wait_recv()
    out_total = part_in_ref[0].astype(F32)
    for rank in range(1, 4):
        out_total = out_total + part_in_ref[rank].astype(F32)
    out_grad_ref[...] = out_total.astype(BF16)
    for copy in copies + returned + [there, swap]:
        copy.wait_send()


def attend_back_kernel(
    width,
    query_t_ref,
    query_ref,
    twice_ref,
    key_t_ref,
    value_ref,
    grad_t_ref,
    out_ref,
    total_ref,
    table_ref,
    normed_ref,
    joint_ref,
    bucket_ref,
    joint_in_ref,
    all_joint_ref,
    weight_grad_ref,
    bias_grad_ref,
    joint_grad_ref,
    grad_ref,
    query_grad_ref,
    key_grad_ref,
    value_grad_ref,
    table_grad_ref,
    *sems,
):
    me, near, far, cross = ranks()
    peers = (near, far, cross)
    heads, length = twice_ref.shape[0], twice_ref.shape[1]
    inner = heads * width
    wide, deep = length // 4, length // 8
    greet(peers)
    copies = []
    for slot, peer in enumerate(peers):
        copies.append(remote(joint_ref, all_joint_ref.at[me], sems, slot, peer))
        copies[-1].start()
    all_joint_ref[me] = joint_ref[...]
    key_grad_ref[...] = jnp.zeros_like(key_grad_ref)
    value_grad_ref[...] = jnp.zeros_like(value_grad_ref)
    table_grad_ref[...] = jnp.zeros_like(table_grad_ref)
    for block in range(4):
        grad_ref[block * wide : (block + 1) * wide, :] = turned(grad_t_ref[block])

    def step(index, carry):
        block, head = index // heads, index % heads
        begin = pl.multiple_of(block * wide, wide)
        span = pl.ds(begin, wide)
        rows = pl.ds(pl.multiple_of(head * width, width), width)
        scaled = query_t_ref[rows, span].astype(F32) * LOG2E
        queries = jnp.concatenate(split(scaled), axis=0)
        total = total_ref[head, :, span]
        grads = grad_t_ref[block, rows, :].astype(F32)
        dots = jnp.sum(grads * out_ref[rows, span], axis=0, keepdims=True)
        own_rows = lax.broadcasted_iota(jnp.int32, (inner, wide), 0) // width == head
        own_lanes = lax.broadcasted_iota(jnp.int32, (wide, inner), 1) // width == head
        grad_t_own = jnp.where(own_rows, grad_t_ref[block].astype(F32), 0.0).astype(BF16)
        query_own = jnp.where(own_lanes, query_ref[span, :].astype(F32), 0.0).astype(BF16)
        grad_own = jnp.where(own_lanes, grad_ref[span, :].astype(F32), 0.0).astype(BF16)
        query_grad = jnp.zeros((width, wide), F32)
        for part in range(length // deep):
            cut = slice(part * deep, (part + 1) * deep)
            raw = dot(twice_ref[head, cut, :], queries)
            raw_grad = dot(value_ref[cut, :], grad_t_own)
            probs, score_grads = [], []
            for lane in range(0, wide, LANES):
                piece = slice(lane, lane + LANES)
                offset = pl.multiple_of(part * deep - begin - lane + length - LANES, LANES)
                shift = table_ref[head, pl.ds(offset, deep), :]
                prob = jnp.exp2(raw[:, piece] + shift - total[:, piece])
                low = (prob * (raw_grad[:, piece] - dots[:, piece])).astype(BF16)
                table_grad_ref[head, pl.ds(offset, deep), :] += low.astype(F32)
                probs.append(prob.astype(BF16))
                score_grads.append(low)
            probs = jnp.concatenate(probs, axis=1)
            score_grads = jnp.concatenate(score_grads, axis=1)
            value_grad_ref[cut, :] += dot(probs, grad_own)
            key_grad_ref[cut, :] += dot(score_grads, query_own)
            query_grad = query_grad + dot(key_t_ref[rows, cut], score_grads)
        query_grad_ref[rows, span] = query_grad
        return carry

    lax.fori_loop(0, heads * 4, step, 0)
    joint_grad_ref[:, :inner] = query_grad_ref[...].T.astype(BF16)
    joint_grad_ref[:, inner : 2 * inner] = key_grad_ref[...].astype(BF16)
    joint_grad_ref[:, 2 * inner :] = value_grad_ref[...].astype(BF16)
    for slot, peer in enumerate(peers):
        part = joint_grad_ref.at[pl.ds(pl.multiple_of(peer * wide, wide), wide), :]
        copies.append(remote(part, joint_in_ref.at[me], sems, 3 + slot, peer))
        copies[-1].start()
    joint_in_ref[me] = joint_grad_ref[pl.ds(pl.multiple_of(me * wide, wide), wide), :]
    weight_grad_ref[...] = dot_tn(normed_ref[...], joint_grad_ref[...]).astype(BF16)
    bias_grad_kernel(table_grad_ref, bucket_ref, bias_grad_ref)
    for copy in copies:
        copy.wait()


def join_back_kernel(
    joint_in_ref,
    all_joint_ref,
    residual_ref,
    gain_ref,
    middle_grad_ref,
    starts_ref,
    divisor_ref,
    pooled_ref,
    mix_ref,
    all_taps_ref,
    all_join_ref,
    input_grad_ref,
    join_grad_ref,
    tap_grad_ref,
    gain_grad_ref,
    ids_ref,
    summary_ref,
    part_out_ref,
    part_in_ref,
    *sems,
):
    me, near, far, cross = ranks()
    peers = (near, far, cross)
    rows, model = residual_ref.shape
    share = part_out_ref.shape[1]
    words = Words(starts_ref, ids_ref, me, 4)
    normed_grad = dot_nt(joint_in_ref[0], all_joint_ref[0])
    for rank in range(1, 4):
        normed_grad = normed_grad + dot_nt(joint_in_ref[rank], all_joint_ref[rank])
    part, gain_grad = rms_back(normed_grad, residual_ref[...], gain_ref[...])
    gain_grad_ref[...] = jnp.broadcast_to(gain_grad, gain_grad_ref.shape)
    residual_grad = middle_grad_ref[...] + part
    low = residual_grad.astype(BF16)
    high_mix, low_mix = split(dot_nt(low, all_join_ref[...]))
    picked = words.pick(back_target)
    summary_ref[me] = dot(picked, high_mix) + dot(picked, low_mix)
    greet(peers)
    copies = []
    for slot, peer in enumerate(peers):
        copies.append(remote(summary_ref.at[me], summary_ref.at[me], sems, slot, peer))
        copies[-1].start()
    part_out_ref[...] = dot_tn(mix_ref[...], low).astype(BF16).reshape(4, share, model)
    for slot, peer in enumerate(peers):
        copies.append(remote(part_out_ref.at[peer], part_in_ref.at[me], sems, 3 + slot, peer))
        copies[-1].start()
    part_in_ref[me] = part_out_ref[me]
    table = words.table()
    word_grad = dot(table, high_mix) + dot(table, low_mix)
    pooled = pooled_ref[...]
    tap_rows = [jnp.sum(pooled * word_grad, axis=0, keepdims=True)]
    for lag in range(1, 4):
        tap_rows.append(jnp.sum(pltpu.roll(pooled, lag, 0) * word_grad, axis=0, keepdims=True))
    tap_grad_ref[...] = jnp.concatenate(tap_rows + [jnp.zeros((4, model), F32)], axis=0)
    place = words.place(back_target, back_valid)
    for copy in copies[:3]:
        copy.wait_recv()
    word_grad = word_grad + dot(place, stacked(summary_ref))
    taps = all_taps_ref[...]
    count = word_grad.shape[0]
    pooled_grad = word_grad * taps[0:1]
    for lag in range(1, 4):
        pooled_grad = pooled_grad + pltpu.roll(word_grad, count - lag, 0) * taps[lag : lag + 1]
    divisor = divisor_ref[...]
    pooled_grad = pooled_grad / jnp.concatenate([divisor] * (model // LANES), axis=1)
    high, low = split(pooled_grad)
    input_grad_ref[...] = residual_grad + (dot_tn(table, high) + dot_tn(table, low))
    for copy in copies[3:]:
        copy.wait_recv()
    total = part_in_ref[0].astype(F32)
    for rank in range(1, 4):
        total = total + part_in_ref[rank].astype(F32)
    join_grad_ref[...] = total.astype(BF16)
    for copy in copies:
        copy.wait_send()


def shards(
    byte_states,
    word_start,
    bucket_ids,
    conv_two,
    conv_three,
    conv_four,
    join_weight,
    norm_gain,
    query_weight,
    key_weight,
    value_weight,
    position_bias,
    out_weight,
    ffn_gain,
    gate_weight,
    up_weight,
    down_weight,
    out_grad,
):
    rows, batch, model = byte_states.shape
    length = word_start.shape[0]
    buckets, heads = position_bias.shape
    inner = query_weight.shape[1]
    width = inner // heads
    share = join_weight.shape[0]
    hidden = gate_weight.shape[1]
    count = rows + 16
    states = byte_states.reshape(rows, model)
    grads = out_grad.reshape(rows, model)
    starts = word_start.reshape(length // LANES, LANES)
    bucket_row = jnp.pad(bucket_ids, (0, 1), constant_values=-1)[None]
    span = bucket_row.shape[1] - LANES
    taps = jnp.stack(
        [
            conv_two[0] + conv_three[0] + conv_four[0],
            conv_two[1] + conv_three[1] + conv_four[1],
            conv_three[2] + conv_four[2],
            conv_four[3],
        ]
    )
    taps = jnp.pad(taps, ((0, 4), (0, 0)))
    joint_weight = jnp.concatenate([query_weight, key_weight, value_weight], axis=1)
    (
        residual,
        normed,
        queries,
        queries_t,
        twice_keys,
        keys_t,
        values,
        values_t,
        table,
        divisor,
        pooled,
        mix,
        all_taps,
        all_join,
    ) = pl.pallas_call(
        functools.partial(join_kernel, width),
        out_shape=(
            like((rows, model), F32),
            like((length, model), BF16),
            like((length, inner), BF16),
            like((inner, length), BF16),
            like((heads, length, 2 * width), BF16),
            like((inner, length), BF16),
            like((length, inner), BF16),
            like((inner, length), BF16),
            like((heads, span, LANES), F32),
            like((count, LANES), F32),
            like((count, model), F32),
            like((rows, model), BF16),
            like((8, model), F32),
            like((4 * share, model), BF16),
        ),
        in_specs=whole(8),
        out_specs=whole(14),
        scratch_shapes=[
            pltpu.VMEM((length // LANES, LANES), F32),
            pltpu.VMEM((4, 8, model + LANES), F32),
            pltpu.VMEM((4, 8, share), F32),
            *semaphores(15),
        ],
        compiler_params=params(0),
        name="join",
    )(states, starts, taps, join_weight, norm_gain[None], joint_weight, bucket_row, position_bias)
    (
        outs,
        totals,
        attended,
        all_out,
        near_gate,
        near_up,
        near_down,
        far_grads,
    ) = pl.pallas_call(
        functools.partial(attend_kernel, width),
        out_shape=(
            like((inner, length), F32),
            like((heads, 1, length), F32),
            like((4, inner, rows), BF16),
            like((4 * inner, model), BF16),
            like(gate_weight.shape, BF16),
            like(up_weight.shape, BF16),
            like(down_weight.shape, BF16),
            like((rows, model), BF16),
        ),
        in_specs=whole(5) + anywhere(4),
        out_specs=whole(4) + anywhere(4),
        scratch_shapes=[
            pltpu.VMEM((length, rows), F32),
            pltpu.VMEM((4, inner, rows), BF16),
            *semaphores(11),
        ],
        compiler_params=params(1),
        name="attend",
    )(
        queries_t,
        twice_keys,
        values_t,
        table,
        out_weight,
        gate_weight,
        up_weight,
        down_weight,
        grads,
    )
    (
        out_states,
        middle_grad,
        ffn_gain_grad,
        gate_grad,
        up_grad,
        down_grad,
        out_weight_grad,
        attended_grad,
    ) = pl.pallas_call(
        ffn_kernel,
        out_shape=(
            like((rows, model), F32),
            like((rows, model), F32),
            like((8, model), F32),
            like((model, hidden), BF16),
            like((model, hidden), BF16),
            like((hidden, model), BF16),
            like((inner, model), BF16),
            like((4, inner, rows), BF16),
        ),
        in_specs=whole(12),
        out_specs=whole(8),
        scratch_shapes=[
            pltpu.VMEM((rows, model), F32),
            pltpu.VMEM((2, rows, model), BF16),
            pltpu.VMEM((2, rows, model), F32),
            pltpu.VMEM((2, rows, model), F32),
            pltpu.VMEM((2, 3, model, hidden), F32),
            pltpu.VMEM((2, rows, model), BF16),
            pltpu.VMEM((2, rows, model), BF16),
            pltpu.VMEM((3, model, hidden), BF16),
            pltpu.VMEM((3, model, hidden), BF16),
            pltpu.VMEM((4, inner, model), BF16),
            pltpu.VMEM((4, inner, model), BF16),
            pltpu.VMEM((4, inner, rows), BF16),
            *semaphores(10),
        ],
        compiler_params=params(2),
        name="ffn",
    )(
        attended,
        all_out,
        residual,
        ffn_gain[None],
        grads,
        far_grads,
        gate_weight,
        near_gate,
        up_weight,
        near_up,
        down_weight,
        near_down,
    )
    early = lax.psum((gate_grad, up_grad, down_grad, out_weight_grad), "dp")
    joint_in, all_joint, joint_grad, bias_grad = pl.pallas_call(
        functools.partial(attend_back_kernel, width),
        out_shape=(
            like((4, rows, 3 * inner), BF16),
            like((4, model, 3 * inner), BF16),
            like((model, 3 * inner), BF16),
            like((buckets, heads), F32),
        ),
        in_specs=whole(12),
        out_specs=whole(4),
        scratch_shapes=[
            pltpu.VMEM((length, 3 * inner), BF16),
            pltpu.VMEM((length, inner), BF16),
            pltpu.VMEM((inner, length), F32),
            pltpu.VMEM((length, inner), F32),
            pltpu.VMEM((length, inner), F32),
            pltpu.VMEM((heads, span, LANES), F32),
            *semaphores(6),
        ],
        compiler_params=params(3),
        name="attend_back",
    )(
        queries_t,
        queries,
        twice_keys,
        keys_t,
        values,
        attended_grad,
        outs,
        totals,
        table,
        normed,
        joint_weight,
        bucket_row,
    )
    joint_total = lax.psum(joint_grad, "dp")
    input_grad, join_grad, tap_grad, norm_gain_grad = pl.pallas_call(
        join_back_kernel,
        out_shape=(
            like((rows, model), F32),
            like((share, model), BF16),
            like((8, model), F32),
            like((8, model), F32),
        ),
        in_specs=whole(11),
        out_specs=whole(4),
        scratch_shapes=[
            pltpu.VMEM((length // LANES, LANES), F32),
            pltpu.VMEM((4, 8, model), F32),
            pltpu.VMEM((4, share, model), BF16),
            pltpu.VMEM((4, share, model), BF16),
            *semaphores(6),
        ],
        compiler_params=params(4),
        name="join_back",
    )(
        joint_in,
        all_joint,
        residual,
        norm_gain[None],
        middle_grad,
        starts,
        divisor,
        pooled,
        mix,
        all_taps,
        all_join,
    )
    join_total = lax.psum(join_grad, "dp")
    bias_total = lax.psum(bias_grad, "dp")
    small = lax.psum(
        jnp.concatenate([tap_grad[:4], norm_gain_grad[:1], ffn_gain_grad[:1]], axis=0), ("dp", "mp")
    )
    own_taps = lax.dynamic_slice_in_dim(small[:4], lax.axis_index("mp") * share, share, 1)
    gate_total, up_total, down_total, out_total = [part.astype(F32) for part in early]
    joint_total = joint_total.astype(F32)
    return (
        out_states[:, None, :],
        input_grad[:, None, :],
        own_taps[:2],
        own_taps[:3],
        own_taps,
        join_total.astype(F32),
        small[4],
        joint_total[:, :inner],
        joint_total[:, inner : 2 * inner],
        joint_total[:, 2 * inner :],
        bias_total,
        out_total,
        small[5],
        gate_total,
        up_total,
        down_total,
    )


def solution(mesh):
    return jax.shard_map(
        shards,
        mesh=mesh,
        in_specs=(
            P("mp", "dp", None),
            P(None, "dp"),
            P(),
            P(None, "mp"),
            P(None, "mp"),
            P(None, "mp"),
            P("mp", None),
            P(),
            P(None, "mp"),
            P(None, "mp"),
            P(None, "mp"),
            P(None, "mp"),
            P("mp", None),
            P(),
            P(None, "mp"),
            P(None, "mp"),
            P("mp", None),
            P("mp", "dp", None),
        ),
        out_specs=(
            P("mp", "dp", None),
            P("mp", "dp", None),
            P(None, "mp"),
            P(None, "mp"),
            P(None, "mp"),
            P("mp", None),
            P(),
            P(None, "mp"),
            P(None, "mp"),
            P(None, "mp"),
            P(None, "mp"),
            P("mp", None),
            P(),
            P(None, "mp"),
            P(None, "mp"),
            P("mp", None),
        ),
        check_vma=False,
    )
```

```python
import functools

import jax
import jax.numpy as jnp
from jax import lax
from jax.experimental import pallas as pl
from jax.experimental.pallas import tpu as pltpu
from jax.sharding import PartitionSpec as P

EPSILON = 1e-06
LOG2E = 1.4426950408889634
GELU_SCALE = 0.7978845608028654
GELU_CUBE = 0.044715
F32 = jnp.float32
BF16 = jnp.bfloat16
LANES = 128
HALO = 3
VMEM_LIMIT = 56 << 20
MESH = pl.DeviceIdType.MESH


def whole(count):
    return [pl.BlockSpec(memory_space=pltpu.VMEM)] * count


def anywhere(count):
    return [pl.BlockSpec(memory_space=pl.ANY)] * count


def params(collective=None):
    return pltpu.CompilerParams(
        vmem_limit_bytes=VMEM_LIMIT, collective_id=collective, has_side_effects=collective is not None
    )


def like(shape, dtype):
    return jax.ShapeDtypeStruct(shape, dtype)


def dot(lhs, rhs):
    return jnp.dot(lhs, rhs, preferred_element_type=F32)


def dot_nt(lhs, rhs):
    return lax.dot_general(lhs, rhs, (((1,), (1,)), ((), ())), preferred_element_type=F32)


def dot_tn(lhs, rhs):
    return lax.dot_general(lhs, rhs, (((0,), (0,)), ((), ())), preferred_element_type=F32)


def split(values):
    high = values.astype(BF16)
    return high, (values - high.astype(F32)).astype(BF16)


def turned(values):
    return values.astype(F32).T.astype(BF16)


def ranks():
    me = lax.axis_index("mp")
    near = me + 1 - 2 * (me % 2)
    return me, near, (me + 2) % 4, (near + 2) % 4


def greet(peers, strides=()):
    barrier = pltpu.get_barrier_semaphore()
    for peer in peers:
        pl.semaphore_signal(barrier, inc=1, device_id={"mp": peer}, device_id_type=MESH)
    for stride in strides:
        pl.semaphore_signal(barrier, inc=1, device_id={"dp": partner(stride)}, device_id_type=MESH)
    pl.semaphore_wait(barrier, len(peers) + len(strides))


def side_of(stride):
    return (lax.axis_index("dp") // stride) % 2


def partner(stride):
    return lax.axis_index("dp") + stride - 2 * stride * side_of(stride)


def strides_of(count):
    strides = []
    while 2 ** len(strides) < count:
        strides.append(2 ** len(strides))
    return strides


class remote:
    def __init__(self, *given, axis="mp"):
        self.given, self.axis = given, axis

    def start(self):
        described(*self.given, self.axis).start()

    def wait_recv(self):
        described(*self.given, self.axis).wait_recv()

    def wait_send(self):
        described(*self.given, self.axis).wait_send()

    def wait(self):
        described(*self.given, self.axis).wait()


def described(source, target, sems, slot, peer, axis):
    source, target, peer = [part() if callable(part) else part for part in (source, target, peer)]
    sends, receives = sems
    return pltpu.make_async_remote_copy(
        src_ref=source,
        dst_ref=target,
        send_sem=sends.at[slot],
        recv_sem=receives.at[slot],
        device_id={axis: peer},
        device_id_type=MESH,
    )


def semaphores(count):
    return [pltpu.SemaphoreType.DMA((count,)), pltpu.SemaphoreType.DMA((count,))]


class Chain:
    def __init__(self, source_ref, base, rows, strides, scratch, sems, first_slot):
        self.source, self.base, self.rows, self.strides = source_ref, base, rows, strides
        (
            self.half_in,
            self.half,
            self.quarter_in,
            self.quarter,
            self.whole_quarter,
            self.gathered_quarter,
            self.both,
            self.gathered_half,
        ) = scratch
        self.sems, self.slot, self.at = sems, first_slot, 0
        self.copy, self.copies = None, []
        self.steps = len(strides) + 3

    @staticmethod
    def scratch(rows, width, exchanges):
        half, quarter = (rows // 2, width), (rows // 4, width)
        return [
            pltpu.VMEM(half, BF16),
            pltpu.VMEM(half, BF16),
            pltpu.VMEM((exchanges + 1, *quarter), BF16),
            pltpu.VMEM((exchanges, *quarter), BF16),
            pltpu.VMEM(quarter, BF16),
            pltpu.VMEM(quarter, BF16),
            pltpu.VMEM(half, BF16),
            pltpu.VMEM(half, BF16),
        ]

    @staticmethod
    def slots(strides):
        return len(strides) + 2

    def send(self, source, target, stride):
        copy = remote(
            source, target, self.sems, self.slot + len(self.copies), lambda: partner(stride), axis="dp"
        )
        copy.start()
        self.copies.append(copy)

    def step(self, finish=None):
        first, second, others = self.strides[0], self.strides[1], self.strides[2:]
        half, quarter = self.rows // 2, self.rows // 4
        at = self.at
        self.at += 1
        if at > 0:
            self.copies[-1].wait_recv()
        if at == 0:
            self.send(lambda: self.source.at[pl.ds(pl.multiple_of(self.base + (1 - side_of(first)) * half, 16), half), :], self.half_in, first)
        elif at == 1:
            begin = pl.multiple_of(self.base + side_of(first) * half, 16)
            mine = self.source[pl.ds(begin, half), :].astype(F32)
            self.half[...] = (mine + self.half_in[...].astype(F32)).astype(BF16)
            self.send(lambda: self.half.at[pl.ds(pl.multiple_of((1 - side_of(second)) * quarter, 16), quarter), :], lambda: self.quarter_in.at[0], second)
        elif at <= 1 + len(others):
            if at == 2:
                mine = self.half[pl.ds(pl.multiple_of(side_of(second) * quarter, 16), quarter), :]
            else:
                mine = self.quarter[at - 3]
            total = mine.astype(F32) + self.quarter_in[at - 2].astype(F32)
            self.quarter[at - 2] = total.astype(BF16)
            self.send(
                lambda: self.quarter.at[at - 2], lambda: self.quarter_in.at[at - 1], others[at - 2]
            )
        elif at == 2 + len(others):
            total = self.quarter[at - 3].astype(F32) + self.quarter_in[at - 2].astype(F32)
            self.whole_quarter[...] = total.astype(BF16)
            self.send(self.whole_quarter, self.gathered_quarter, second)
        elif at == 3 + len(others):
            side = side_of(second)
            mine = pl.ds(pl.multiple_of(side * quarter, 16), quarter)
            other = pl.ds(pl.multiple_of((1 - side) * quarter, 16), quarter)
            self.both[mine, :] = self.whole_quarter[...]
            self.both[other, :] = self.gathered_quarter[...]
            self.send(self.both, self.gathered_half, first)
        else:
            side = side_of(first)
            mine = pl.ds(pl.multiple_of(self.base + side * half, 16), half)
            other = pl.ds(pl.multiple_of(self.base + (1 - side) * half, 16), half)
            finish(mine, self.both[...].astype(F32))
            finish(other, self.gathered_half[...].astype(F32))
            for copy in self.copies:
                copy.wait_send()


def rms(values, gain):
    return values * lax.rsqrt(jnp.mean(values * values, axis=1, keepdims=True) + EPSILON) * gain


def rms_back(grads, values, gain):
    scale = lax.rsqrt(jnp.mean(values * values, axis=1, keepdims=True) + EPSILON)
    gain_grad = jnp.sum(grads * values * scale, axis=0, keepdims=True)
    raised = grads * gain
    mean = jnp.mean(raised * values, axis=1, keepdims=True)
    return scale * raised - values * (scale * scale * scale * mean), gain_grad


def bucket_hits(bucket_ref, buckets):
    span = bucket_ref.shape[1]
    rows = lax.broadcasted_iota(jnp.int32, (buckets, span), 0)
    return rows == jnp.broadcast_to(bucket_ref[...], (buckets, span))


def bias_table_kernel(bucket_ref, bias_ref, table_ref):
    span = bucket_ref.shape[1]
    hits = bucket_hits(bucket_ref, bias_ref.shape[0])
    for head in range(bias_ref.shape[1]):
        line = jnp.sum(jnp.where(hits, bias_ref[:, head : head + 1], 0.0), axis=0, keepdims=True)
        skew = pltpu.roll(
            jnp.broadcast_to(line * LOG2E, (LANES, span)), span - LANES + 1, 1, stride=1, stride_axis=0
        )
        for block in range(span // LANES - 1):
            cut = slice(block * LANES, (block + 1) * LANES)
            table_ref[head, cut, :] = skew[:, cut].T


def bias_grad_kernel(table_ref, bucket_ref, grad_ref):
    span = bucket_ref.shape[1]
    buckets, lanes = grad_ref.shape
    hits = bucket_hits(bucket_ref, buckets)
    columns = []
    for head in range(table_ref.shape[0]):
        blocks = [
            table_ref[head, block * LANES : (block + 1) * LANES, :].T
            for block in range(span // LANES - 1)
        ]
        skew = jnp.concatenate(blocks + [jnp.zeros((LANES, LANES), F32)], axis=1)
        rows = LANES // 2
        while rows >= 8:
            skew = skew[:rows] + pltpu.roll(skew[rows:], span - rows, 1)
            rows //= 2
        line = jnp.zeros((1, span), F32)
        for row in range(8):
            line = line + pltpu.roll(skew[row : row + 1], LANES - 1 - row, 1)
        columns.append(jnp.sum(jnp.where(hits, line, 0.0), axis=1, keepdims=True))
    lane = lax.broadcasted_iota(jnp.int32, (buckets, lanes), 1)
    made = jnp.zeros((buckets, lanes), F32)
    for head, column in enumerate(columns):
        made = jnp.where(lane == head, column, made)
    grad_ref[...] = made


def word_numbers(starts):
    rows = starts.shape[0]
    upper = lax.broadcasted_iota(jnp.int32, (LANES, LANES), 0) <= lax.broadcasted_iota(
        jnp.int32, (LANES, LANES), 1
    )
    within = dot(starts.astype(F32).astype(BF16), upper.astype(F32).astype(BF16))
    totals = jnp.broadcast_to(within[:, LANES - 1 :], (rows, LANES)).astype(BF16)
    lower = lax.broadcasted_iota(jnp.int32, (rows, rows), 1) < lax.broadcasted_iota(
        jnp.int32, (rows, rows), 0
    )
    return within + dot(lower.astype(F32).astype(BF16), totals) - 1.0


class Words:
    def __init__(self, starts_ref, ids_ref, me, ranks_count):
        ids = word_numbers(starts_ref[...])
        ids_ref[...] = ids
        per = ids.shape[0] // ranks_count
        self.firsts = [ids[per * rank : per * rank + 1, 0:1] for rank in range(ranks_count)]
        self.lasts = [
            ids[per * (rank + 1) - 1 : per * (rank + 1), LANES - 1 :] for rank in range(ranks_count)
        ]
        pieces = [ids_ref[pl.ds(me * per + piece, 1), :] for piece in range(per)]
        self.row = jnp.concatenate(pieces, axis=1)
        self.first = self.row[:, 0:1]
        self.last = self.row[:, per * LANES - 1 :]
        self.me = me
        self.count = per * LANES

    def table(self):
        shape = (self.count + 16, self.count)
        rows = lax.broadcasted_iota(jnp.int32, shape, 0).astype(F32)
        return (rows == self.row - self.first + HALO).astype(F32).astype(BF16)

    def pick(self, target):
        slots = lax.broadcasted_iota(jnp.int32, (8, 1), 0)
        hits = target(slots, self.first, self.last) == self.row
        return hits.astype(F32).astype(BF16)

    def place(self, target, valid):
        width = 2 * LANES
        lane = lax.broadcasted_iota(jnp.int32, (1, width), 1) % LANES
        slots, rank = lane % 8, lane // 8
        goal = jnp.full((1, width), -9.0, F32)
        for index, (first, last) in enumerate(zip(self.firsts, self.lasts)):
            goal = jnp.where(rank == index, target(slots, first, last), goal)
        known = valid(slots, rank, self.me) & (rank < len(self.firsts))
        goal = jnp.where(known, goal - self.first + HALO, -1.0)
        rows = lax.broadcasted_iota(jnp.int32, (self.count + 16, width), 0).astype(F32)
        return (rows == goal).astype(F32).astype(BF16)


def stacked(summary_ref):
    parts = [summary_ref[rank] for rank in range(summary_ref.shape[0])]
    rest = LANES - sum(part.shape[0] for part in parts)
    parts.append(jnp.zeros((rest, parts[0].shape[1]), F32))
    return jnp.concatenate(split(jnp.concatenate(parts, axis=0)), axis=0)


def ahead_target(slots, first, last):
    later = jnp.where(slots <= 4, last - (slots - 1).astype(F32), -9.0)
    return jnp.where(slots == 0, first, later)


def ahead_valid(slots, rank, me):
    return ((rank < me) & (slots >= 1) & (slots <= 4)) | ((rank > me) & (slots == 0))


def back_target(slots, first, last):
    return jnp.where(slots <= 3, first + slots.astype(F32), jnp.where(slots == 4, last, -9.0))


def back_valid(slots, rank, me):
    return ((rank > me) & (slots <= 3)) | ((rank < me) & (slots == 4))


def join_kernel(
    width,
    states_ref,
    starts_ref,
    taps_ref,
    join_ref,
    gain_ref,
    joint_ref,
    bucket_ref,
    bias_ref,
    residual_ref,
    normed_ref,
    query_ref,
    query_t_ref,
    twice_ref,
    key_t_ref,
    value_ref,
    value_t_ref,
    table_ref,
    divisor_ref,
    pooled_ref,
    mix_ref,
    all_taps_ref,
    all_join_ref,
    ids_ref,
    summary_ref,
    taps_in_ref,
    *sems,
):
    me, near, far, cross = ranks()
    peers = (near, far, cross)
    rows, model = states_ref.shape
    share = join_ref.shape[0]
    words = Words(starts_ref, ids_ref, me, 4)
    states = states_ref[...]
    wide_states = jnp.concatenate([states, jnp.ones((rows, LANES), BF16)], axis=1)
    summary_ref[me] = dot(words.pick(ahead_target), wide_states)
    taps_in_ref[me] = taps_ref[...]
    all_join_ref[pl.ds(pl.multiple_of(me * share, share), share), :] = join_ref[...]
    greet(peers)
    early = []
    for slot, peer in enumerate(peers):
        part = all_join_ref.at[pl.ds(pl.multiple_of(me * share, share), share), :]
        early.append(remote(summary_ref.at[me], summary_ref.at[me], sems, slot, peer))
        early.append(remote(taps_in_ref.at[me], taps_in_ref.at[me], sems, 3 + slot, peer))
        early.append(remote(part, part, sems, 6 + slot, peer))
    for copy in early:
        copy.start()
    table = words.table()
    sums = dot(table, wide_states)
    place = words.place(ahead_target, ahead_valid)
    for copy in early:
        copy.wait()
    sums = sums + dot(place, stacked(summary_ref))
    divisor = jnp.maximum(sums[:, model:], 1.0)
    divisor_ref[...] = divisor
    pooled = sums[:, :model] / jnp.concatenate([divisor] * (model // LANES), axis=1)
    pooled_ref[...] = pooled
    taps = jnp.concatenate([taps_in_ref[rank] for rank in range(4)], axis=1)
    all_taps_ref[...] = taps
    total = pooled * taps[0:1]
    for lag in range(1, 4):
        total = total + pltpu.roll(pooled, lag, 0) * taps[lag : lag + 1]
    mix = dot_tn(table, total.astype(BF16)).astype(BF16)
    mix_ref[...] = mix
    residual = states.astype(F32) + dot(mix, all_join_ref[...])
    residual_ref[...] = residual
    own = pl.ds(pl.multiple_of(me * rows, rows), rows)
    normed_ref[own, :] = rms(residual, gain_ref[...]).astype(BF16)

    def block(rank, part):
        half = rows // 2
        return normed_ref.at[pl.ds(pl.multiple_of(rank * rows + part * half, half), half), :]

    sends = []
    for part in range(2):
        sends.append(remote(block(me, part), block(me, part), sems, 9 + part, far))
    for part in range(2):
        sends.append(remote(block(me, part), block(me, part), sems, 11 + part, near))
    for copy in sends:
        copy.start()

    def project(rank):
        cut = pl.ds(pl.multiple_of(rank * rows, rows), rows)
        made = dot(normed_ref[cut, :], joint_ref[...])
        inner = query_ref.shape[1]
        query, key, value = [
            made[:, index * inner : (index + 1) * inner].astype(BF16) for index in range(3)
        ]
        query_ref[cut, :] = query
        query_t_ref[:, cut] = turned(query)
        key_t_ref[:, cut] = turned(key)
        value_ref[cut, :] = value
        value_t_ref[:, cut] = turned(value)
        for head in range(inner // width):
            part = key[:, head * width : (head + 1) * width]
            twice_ref[head, cut, :] = jnp.concatenate([part, part], axis=1)

    project(me)
    bias_table_kernel(bucket_ref, bias_ref, table_ref)
    sends[2].wait_recv()
    sends[3].wait_recv()
    project(near)
    passed = []
    for part in range(2):
        sends[part].wait_recv()
        passed.append(remote(block(far, part), block(far, part), sems, 13 + part, near))
        passed[part].start()
    project(far)
    for copy in passed:
        copy.wait_recv()
    project(cross)
    for copy in sends + passed:
        copy.wait_send()


def attend_kernel(
    width,
    query_ref,
    twice_ref,
    value_ref,
    table_ref,
    out_weight_ref,
    gate_ref,
    up_ref,
    down_ref,
    grad_ref,
    out_ref,
    total_ref,
    attended_ref,
    all_out_ref,
    near_gate_ref,
    near_up_ref,
    near_down_ref,
    far_grad_ref,
    score_ref,
    stage_ref,
    *sems,
):
    me, near, far, cross = ranks()
    peers = (near, far, cross)
    heads, length = twice_ref.shape[0], twice_ref.shape[1]
    share, model = out_weight_ref.shape
    wide = deep = length // 4
    all_out_ref[pl.ds(pl.multiple_of(me * share, share), share), :] = out_weight_ref[...]
    greet(peers)
    copies = [
        remote(gate_ref, near_gate_ref, sems, 4, near),
        remote(up_ref, near_up_ref, sems, 5, near),
        remote(down_ref, near_down_ref, sems, 6, near),
    ]
    for slot, peer in enumerate(peers):
        part = all_out_ref.at[pl.ds(pl.multiple_of(me * share, share), share), :]
        copies.append(remote(part, part, sems, 7 + slot, peer))
    copies.append(remote(grad_ref, far_grad_ref, sems, 10, far))
    for copy in copies:
        copy.start()

    def owner(order):
        chip = (me // 2 + 1 + order // 2) % 2
        core = (me % 2 + (order + 1) // 2) % 2
        return 2 * chip + core

    def handed(order):
        return remote(stage_ref.at[order], attended_ref.at[me], sems, order, owner(order))

    def step(index, carry):
        order, head = index // heads, index % heads
        begin = pl.multiple_of(owner(order) * wide, wide)
        span = pl.ds(begin, wide)
        rows = pl.ds(pl.multiple_of(head * width, width), width)
        scaled = query_ref[rows, span].astype(F32) * LOG2E
        queries = jnp.concatenate(split(scaled), axis=0)
        peak = jnp.full((8, wide), -1e30, F32)
        for part in range(length // deep):
            cut = slice(part * deep, (part + 1) * deep)
            raw = dot(twice_ref[head, cut, :], queries)
            columns = []
            for lane in range(0, wide, LANES):
                offset = pl.multiple_of(part * deep - begin - lane + length - LANES, LANES)
                columns.append(raw[:, lane : lane + LANES] + table_ref[head, pl.ds(offset, deep), :])
            scores = jnp.concatenate(columns, axis=1)
            score_ref[cut, :] = scores
            peak = jnp.maximum(peak, jnp.max(scores.reshape(deep // 8, 8, wide), axis=0))
        peak = jnp.max(peak, axis=0, keepdims=True)
        sums = jnp.zeros((8, wide), F32)
        made = jnp.zeros((width, wide), F32)
        for part in range(length // deep):
            cut = slice(part * deep, (part + 1) * deep)
            raised = jnp.exp2(score_ref[cut, :] - peak)
            sums = sums + jnp.sum(raised.reshape(deep // 8, 8, wide), axis=0)
            made = made + dot(value_ref[rows, cut], raised.astype(BF16))
        total = jnp.sum(sums, axis=0, keepdims=True)
        made = made / total
        out_ref[rows, span] = made
        total_ref[head, :, span] = peak + jnp.log2(total)
        stage_ref[order, rows, :] = made.astype(BF16)

        @pl.when((head == heads - 1) & (order < 3))
        def _():
            handed(order).start()

        return carry

    lax.fori_loop(0, heads * 4, step, 0)
    attended_ref[me] = stage_ref[3]
    for order in range(3):
        handed(order).wait()
    for copy in copies:
        copy.wait()


def ffn_kernel(
    attended_ref,
    all_out_ref,
    residual_ref,
    gain_ref,
    grad_ref,
    far_grad_ref,
    gate_ref,
    near_gate_ref,
    up_ref,
    near_up_ref,
    down_ref,
    near_down_ref,
    states_part_ref,
    far_made_ref,
    middle_grad_ref,
    gain_grad_ref,
    weight_grad_ref,
    out_part_ref,
    grad_stage_ref,
    middle_ref,
    normed_ref,
    made_ref,
    back_ref,
    sums_ref,
    far_out_ref,
    far_in_ref,
    near_out_ref,
    near_in_ref,
    *sems,
):
    me, near, far, cross = ranks()
    peers = (near, far, cross)
    rows, model = residual_ref.shape
    share = attended_ref.shape[1]
    attended = attended_ref[...].reshape(4 * share, rows)
    middle = residual_ref[...] + dot_tn(attended, all_out_ref[...])
    middle_ref[...] = middle
    normed_ref[0] = rms(middle, gain_ref[...]).astype(BF16)
    greet(peers)
    there = remote(normed_ref.at[0], normed_ref.at[1], sems, 0, far)
    there.start()

    def work(side, grads, gate, up, down, slab):
        given = normed_ref[side]
        gate_value = dot(given, gate)
        up_value = dot(given, up)
        hidden_grad = dot_nt(grads, down)
        square = gate_value * gate_value
        curve = jnp.tanh(GELU_SCALE * gate_value * (1.0 + GELU_CUBE * square))
        half = 0.5 + 0.5 * curve
        gelu = gate_value * half
        slope = half + (0.5 * GELU_SCALE) * gate_value * (1.0 - curve * curve) * (
            1.0 + (3.0 * GELU_CUBE) * square
        )
        hidden = (gelu * up_value).astype(BF16)
        gate_back = (hidden_grad * up_value * slope).astype(BF16)
        up_back = (hidden_grad * gelu).astype(BF16)
        sums = [dot_tn(given, gate_back), dot_tn(given, up_back), dot_tn(hidden, grads)]
        for index in range(3):
            if side == 0:
                sums_ref[slab, index] = sums[index]
            else:
                sums_ref[slab, index] += sums[index]
        made = dot(hidden, down)
        back = dot_nt(gate_back, gate) + dot_nt(up_back, up)
        if slab == 0:
            made_ref[side] = made
            back_ref[side] = back
        else:
            made_ref[side] += made
            back_ref[side] += back

    mine = (gate_ref, up_ref, down_ref)
    other = (near_gate_ref, near_up_ref, near_down_ref)
    for slab, weights in enumerate((mine, other)):
        work(0, grad_ref[...], *[ref[...] for ref in weights], slab)
    there.wait_recv()
    for slab, weights in enumerate((mine, other)):
        work(1, far_grad_ref[...], *[ref[...] for ref in weights], slab)
    far_out_ref[...] = back_ref[1].astype(BF16)
    returned = remote(far_out_ref, far_in_ref, sems, 1, far)
    returned.start()
    near_out_ref[...] = sums_ref[1].astype(BF16)
    swap = remote(near_out_ref, near_in_ref, sems, 2, near)
    swap.start()
    far_made_ref[...] = made_ref[1].astype(BF16)
    states_part_ref[...] = middle_ref[...] + made_ref[0]
    returned.wait_recv()
    normed_grad = back_ref[0] + far_in_ref[...].astype(F32)
    part, gain_grad = rms_back(normed_grad, middle_ref[...], gain_ref[...])
    gain_grad_ref[...] = jnp.broadcast_to(gain_grad, gain_grad_ref.shape)
    middle_grad = grad_ref[...].astype(F32) + part
    middle_grad_ref[...] = middle_grad
    low = middle_grad.astype(BF16)
    grad_stage_ref[...] = dot_nt(all_out_ref[...], low).astype(BF16).reshape(4, share, rows)
    out_part = dot(attended, low)
    for rank in range(4):
        out_part_ref[rank] = out_part[rank * share : (rank + 1) * share, :].T.astype(BF16)
    swap.wait_recv()
    depth = weight_grad_ref.shape[0] // 3
    for index in range(3):
        total = sums_ref[0, index] + near_in_ref[index].astype(F32)
        weight_grad_ref[index * depth : (index + 1) * depth, :] = total.astype(BF16)
    for copy in (returned, there, swap):
        copy.wait_send()


def back_kernel(
    width,
    count,
    query_t_ref,
    query_ref,
    twice_ref,
    key_t_ref,
    value_ref,
    grad_stage_ref,
    out_ref,
    total_ref,
    table_ref,
    normed_ref,
    joint_ref,
    bucket_ref,
    residual_ref,
    gain_ref,
    middle_grad_ref,
    starts_ref,
    divisor_ref,
    pooled_ref,
    mix_ref,
    all_taps_ref,
    all_join_ref,
    weight_grad_ref,
    out_part_ref,
    far_made_ref,
    states_part_ref,
    ffn_gain_grad_ref,
    input_grad_ref,
    states_out_ref,
    weight_total_ref,
    joint_total_ref,
    out_total_ref,
    join_total_ref,
    small_total_ref,
    bias_total_ref,
    grad_t_ref,
    grad_ref,
    query_grad_ref,
    key_grad_ref,
    value_grad_ref,
    table_grad_ref,
    joint_grad_ref,
    joint_in_ref,
    all_joint_ref,
    made_in_ref,
    out_near_ref,
    out_sum_ref,
    out_far_ref,
    late_ref,
    ids_ref,
    summary_ref,
    join_part_ref,
    join_near_ref,
    join_sum_ref,
    join_far_ref,
    join_ref,
    small_near_ref,
    small_ref,
    small_in_ref,
    bias_ref,
    bias_in_ref,
    sends_ref,
    receives_ref,
    chain_sends_ref,
    chain_receives_ref,
    *chain_refs,
):
    me, near, far, cross = ranks()
    peers = (near, far, cross)
    sems = (sends_ref, receives_ref)
    chain_sems = (chain_sends_ref, chain_receives_ref)
    heads, length = twice_ref.shape[0], twice_ref.shape[1]
    rows, model = residual_ref.shape
    share = join_part_ref.shape[1]
    inner = heads * width
    wide, deep = length // 4, length // 8
    strides = strides_of(count)
    turned_strides = [strides[1], strides[0]] + strides[2:]
    chains = []
    plan = [
        (weight_grad_ref, weight_grad_ref.shape[0], strides),
        (weight_grad_ref, weight_grad_ref.shape[0], turned_strides),
        (late_ref, late_ref.shape[0], strides),
        (late_ref, late_ref.shape[0], turned_strides),
        (join_ref, join_ref.shape[0], strides),
        (join_ref, join_ref.shape[0], turned_strides),
    ]
    for index, (ref, height, order) in enumerate(plan):
        half = height // 2
        chains.append(
            Chain(
                ref,
                (index % 2) * half,
                half,
                order,
                chain_refs[8 * index : 8 * index + 8],
                chain_sems,
                index * Chain.slots(strides),
            )
        )
    weight_chains, late_chains, join_chains = chains[0:2], chains[2:4], chains[4:6]

    greet(peers, strides)
    gradient_copies = []
    for slot, peer in enumerate(peers):
        copy = remote(
            lambda peer=peer: grad_stage_ref.at[peer], lambda: grad_t_ref.at[me], sems, slot, peer
        )
        copy.start()
        gradient_copies.append(copy)
    out_copies = [
        remote(lambda: out_part_ref.at[near], lambda: out_near_ref.at[0], sems, 3, near),
        remote(lambda: out_part_ref.at[cross], lambda: out_near_ref.at[1], sems, 4, near),
    ]
    for copy in out_copies:
        copy.start()
    joint_copies = [
        remote(joint_ref, lambda: all_joint_ref.at[me], sems, 5, far),
        remote(joint_ref, lambda: all_joint_ref.at[me], sems, 6, near),
    ]
    for copy in joint_copies:
        copy.start()
    joint_pass = remote(
        lambda: all_joint_ref.at[far], lambda: all_joint_ref.at[far], sems, 7, near
    )
    made_copy = remote(far_made_ref, made_in_ref, sems, 8, far)
    out_copy = remote(out_sum_ref, out_far_ref, sems, 9, far)
    for chain in weight_chains:
        chain.step()
    grad_t_ref[me] = grad_stage_ref[me]
    all_joint_ref[me] = joint_ref[...]
    key_grad_ref[...] = jnp.zeros_like(key_grad_ref)
    value_grad_ref[...] = jnp.zeros_like(value_grad_ref)
    table_grad_ref[...] = jnp.zeros_like(table_grad_ref)

    def step(index, carry):
        order, head = index // heads, index % heads
        block = 2 * ((me // 2 + order // 2) % 2) + (me % 2 + order % 2) % 2
        begin = pl.multiple_of(block * wide, wide)
        span = pl.ds(begin, wide)
        rows = pl.ds(pl.multiple_of(head * width, width), width)
        for slot in range(3):

            @pl.when(index == (slot + 1) * heads)
            def _(slot=slot):
                gradient_copies[slot].wait_recv()

        @pl.when(head == 0)
        def _():
            grad_ref[span, :] = turned(grad_t_ref[block])

        @pl.when(index == 3)
        def _():
            for copy in out_copies:
                copy.wait_recv()
            for slot, rank in enumerate((far, me)):
                ours = out_part_ref[rank].astype(F32) + out_near_ref[1 - slot].astype(F32)
                if slot == 0:
                    out_sum_ref[...] = ours.astype(BF16)
                else:
                    late_ref[:, 3 * inner :] = ours.astype(BF16)
            out_copy.start()
            made_copy.start()

        @pl.when(index == 4)
        def _():
            weight_chains[0].step()
            weight_chains[1].step()

        @pl.when(index == 5)
        def _():
            joint_copies[0].wait_recv()
            joint_pass.start()

        @pl.when(index == 6)
        def _():
            weight_chains[0].step()
            weight_chains[1].step()

        scaled = query_t_ref[rows, span].astype(F32) * LOG2E
        queries = jnp.concatenate(split(scaled), axis=0)
        total = total_ref[head, :, span]
        grads = grad_t_ref[block, rows, :].astype(F32)
        dots = jnp.sum(grads * out_ref[rows, span], axis=0, keepdims=True)
        own_rows = lax.broadcasted_iota(jnp.int32, (inner, wide), 0) // width == head
        own_lanes = lax.broadcasted_iota(jnp.int32, (wide, inner), 1) // width == head
        grad_t_own = jnp.where(own_rows, grad_t_ref[block].astype(F32), 0.0).astype(BF16)
        query_own = jnp.where(own_lanes, query_ref[span, :].astype(F32), 0.0).astype(BF16)
        grad_own = jnp.where(own_lanes, grad_ref[span, :].astype(F32), 0.0).astype(BF16)
        query_grad = jnp.zeros((width, wide), F32)
        for part in range(length // deep):
            cut = slice(part * deep, (part + 1) * deep)
            raw = dot(twice_ref[head, cut, :], queries)
            raw_grad = dot(value_ref[cut, :], grad_t_own)
            probs, score_grads = [], []
            for lane in range(0, wide, LANES):
                piece = slice(lane, lane + LANES)
                offset = pl.multiple_of(part * deep - begin - lane + length - LANES, LANES)
                shift = table_ref[head, pl.ds(offset, deep), :]
                prob = jnp.exp2(raw[:, piece] + shift - total[:, piece])
                low = (prob * (raw_grad[:, piece] - dots[:, piece])).astype(BF16)
                table_grad_ref[head, pl.ds(offset, deep), :] += low.astype(F32)
                probs.append(prob.astype(BF16))
                score_grads.append(low)
            probs = jnp.concatenate(probs, axis=1)
            score_grads = jnp.concatenate(score_grads, axis=1)
            value_grad_ref[cut, :] += dot(probs, grad_own)
            key_grad_ref[cut, :] += dot(score_grads, query_own)
            query_grad = query_grad + dot(key_t_ref[rows, cut], score_grads)
        query_grad_ref[rows, span] = query_grad
        return carry

    lax.fori_loop(0, heads * 4, step, 0)
    joint_grad_ref[:, :inner] = query_grad_ref[...].T.astype(BF16)
    joint_grad_ref[:, inner : 2 * inner] = key_grad_ref[...].astype(BF16)
    joint_grad_ref[:, 2 * inner :] = value_grad_ref[...].astype(BF16)
    handed = []
    for slot, peer in enumerate(peers):
        part = joint_grad_ref.at[pl.ds(pl.multiple_of(peer * wide, wide), wide), :]
        handed.append(remote(part, joint_in_ref.at[me], sems, 10 + slot, peer))
        handed[-1].start()
    joint_in_ref[me] = joint_grad_ref[pl.ds(pl.multiple_of(me * wide, wide), wide), :]
    for chain in weight_chains:
        chain.step()
    late_ref[:, : 3 * inner] = dot_tn(normed_ref[...], joint_grad_ref[...]).astype(BF16)
    out_copy.wait_recv()
    out_sum = late_ref[:, 3 * inner :].astype(F32) + out_far_ref[...].astype(F32)
    late_ref[:, 3 * inner :] = out_sum.astype(BF16)
    for chain in late_chains:
        chain.step()
    bias_grad_kernel(table_grad_ref, bucket_ref, bias_ref.at[0])
    for chain in weight_chains:
        chain.step()
    words = Words(starts_ref, ids_ref, me, 4)
    table = words.table()
    picked = words.pick(back_target)
    place = words.place(back_target, back_valid)
    joint_copies[1].wait_recv()
    joint_pass.wait_recv()
    normed_grad = dot_nt(joint_in_ref[me], all_joint_ref[me])
    for slot, peer in enumerate(peers):
        handed[slot].wait_recv()
        normed_grad = normed_grad + dot_nt(joint_in_ref[peer], all_joint_ref[peer])
    part, gain_grad = rms_back(normed_grad, residual_ref[...], gain_ref[...])
    residual_grad = middle_grad_ref[...] + part
    low = residual_grad.astype(BF16)
    high_mix, low_mix = split(dot_nt(low, all_join_ref[...]))
    summary_ref[me] = dot(picked, high_mix) + dot(picked, low_mix)
    copies = []
    for slot, peer in enumerate(peers):
        copies.append(remote(summary_ref.at[me], summary_ref.at[me], sems, 13 + slot, peer))
        copies[-1].start()
    join_part_ref[...] = dot_tn(mix_ref[...], low).astype(BF16).reshape(4, share, model)
    join_copies = [
        remote(join_part_ref.at[near], join_near_ref.at[0], sems, 16, near),
        remote(join_part_ref.at[cross], join_near_ref.at[1], sems, 17, near),
    ]
    for copy in join_copies:
        copy.start()
    for chain in late_chains:
        chain.step()
    word_grad = dot(table, high_mix) + dot(table, low_mix)
    pooled = pooled_ref[...]
    tap_rows = [jnp.sum(pooled * word_grad, axis=0, keepdims=True)]
    for lag in range(1, 4):
        tap_rows.append(jnp.sum(pltpu.roll(pooled, lag, 0) * word_grad, axis=0, keepdims=True))
    tap_rows += [gain_grad, ffn_gain_grad_ref[0:1], jnp.zeros((2, model), F32)]
    small_near_ref[me] = jnp.concatenate(tap_rows, axis=0)
    for slot, peer in enumerate(peers):
        copies.append(remote(small_near_ref.at[me], small_near_ref.at[me], sems, 18 + slot, peer))
        copies[-1].start()
    for copy in join_copies:
        copy.wait_recv()
    join_sum_ref[...] = (
        join_part_ref[far].astype(F32) + join_near_ref[1].astype(F32)
    ).astype(BF16)
    join_copy = remote(join_sum_ref, join_far_ref, sems, 21, far)
    join_copy.start()
    for copy in copies[:3]:
        copy.wait_recv()
    word_grad = word_grad + dot(place, stacked(summary_ref))
    for chain in late_chains:
        chain.step()
    for copy in copies[3:]:
        copy.wait_recv()
    small = small_near_ref[0]
    for rank in range(1, 4):
        small = small + small_near_ref[rank]
    small_ref[0] = small
    small_copies = []

    def exchange(index):
        stride = strides[index]
        small_copies.append(
            remote(small_ref.at[index], small_in_ref.at[index], sems, 22 + 2 * index, lambda: partner(stride), axis="dp")
        )
        small_copies.append(
            remote(bias_ref.at[index], bias_in_ref.at[index], sems, 23 + 2 * index, lambda: partner(stride), axis="dp")
        )
        small_copies[-2].start()
        small_copies[-1].start()

    exchange(0)
    join_copy.wait_recv()
    join_ref[...] = (
        join_part_ref[me].astype(F32) + join_near_ref[0].astype(F32) + join_far_ref[...].astype(F32)
    ).astype(BF16)
    for chain in join_chains:
        chain.step()
    taps = all_taps_ref[...]
    height = word_grad.shape[0]
    pooled_grad = word_grad * taps[0:1]
    for lag in range(1, 4):
        pooled_grad = pooled_grad + pltpu.roll(word_grad, height - lag, 0) * taps[lag : lag + 1]
    divisor = divisor_ref[...]
    pooled_grad = pooled_grad / jnp.concatenate([divisor] * (model // LANES), axis=1)
    high, low = split(pooled_grad)
    input_grad_ref[...] = residual_grad + (dot_tn(table, high) + dot_tn(table, low))
    made_copy.wait_recv()
    states_out_ref[...] = states_part_ref[...] + made_in_ref[...].astype(F32)

    def write_weights(span, values):
        weight_total_ref[span, :] = values

    def write_late(span, values):
        joint_total_ref[span, :] = values

    def write_join(span, values):
        join_total_ref[span, :] = values

    for turn in range(weight_chains[0].steps):
        for index in (0, 1):
            for group, finish in (
                (join_chains, write_join),
                (late_chains, write_late),
                (weight_chains, write_weights),
            ):
                chain = group[index]
                if chain.at < chain.steps:
                    chain.step(finish)
        if turn < len(strides):
            small_copies[2 * turn].wait_recv()
            small_copies[2 * turn + 1].wait_recv()
            small = small_ref[turn] + small_in_ref[turn]
            bias = bias_ref[turn] + bias_in_ref[turn]
            if turn + 1 < len(strides):
                small_ref[turn + 1] = small
                bias_ref[turn + 1] = bias
                exchange(turn + 1)
            else:
                small_total_ref[...] = small
                bias_total_ref[...] = bias
    out_total_ref[...] = joint_total_ref[:, 3 * inner :].T
    finished = gradient_copies + out_copies + joint_copies + [joint_pass, made_copy, out_copy]
    for copy in finished + handed + copies + join_copies + [join_copy] + small_copies:
        copy.wait_send()


def shards(
    byte_states,
    word_start,
    bucket_ids,
    conv_two,
    conv_three,
    conv_four,
    join_weight,
    norm_gain,
    query_weight,
    key_weight,
    value_weight,
    position_bias,
    out_weight,
    ffn_gain,
    gate_weight,
    up_weight,
    down_weight,
    out_grad,
):
    rows, batch, model = byte_states.shape
    length = word_start.shape[0]
    buckets, heads = position_bias.shape
    inner = query_weight.shape[1]
    width = inner // heads
    share = join_weight.shape[0]
    hidden = gate_weight.shape[1]
    count = rows + 16
    states = byte_states.reshape(rows, model)
    grads = out_grad.reshape(rows, model)
    starts = word_start.reshape(length // LANES, LANES)
    bucket_row = jnp.pad(bucket_ids, (0, 1), constant_values=-1)[None]
    span = bucket_row.shape[1] - LANES
    taps = jnp.stack(
        [
            conv_two[0] + conv_three[0] + conv_four[0],
            conv_two[1] + conv_three[1] + conv_four[1],
            conv_three[2] + conv_four[2],
            conv_four[3],
        ]
    )
    taps = jnp.pad(taps, ((0, 4), (0, 0)))
    joint_weight = jnp.concatenate([query_weight, key_weight, value_weight], axis=1)
    (
        residual,
        normed,
        queries,
        queries_t,
        twice_keys,
        keys_t,
        values,
        values_t,
        table,
        divisor,
        pooled,
        mix,
        all_taps,
        all_join,
    ) = pl.pallas_call(
        functools.partial(join_kernel, width),
        out_shape=(
            like((rows, model), F32),
            like((length, model), BF16),
            like((length, inner), BF16),
            like((inner, length), BF16),
            like((heads, length, 2 * width), BF16),
            like((inner, length), BF16),
            like((length, inner), BF16),
            like((inner, length), BF16),
            like((heads, span, LANES), F32),
            like((count, LANES), F32),
            like((count, model), F32),
            like((rows, model), BF16),
            like((8, model), F32),
            like((4 * share, model), BF16),
        ),
        in_specs=whole(8),
        out_specs=whole(14),
        scratch_shapes=[
            pltpu.VMEM((length // LANES, LANES), F32),
            pltpu.VMEM((4, 8, model + LANES), F32),
            pltpu.VMEM((4, 8, share), F32),
            *semaphores(15),
        ],
        compiler_params=params(0),
        name="join",
    )(states, starts, taps, join_weight, norm_gain[None], joint_weight, bucket_row, position_bias)
    (
        outs,
        totals,
        attended,
        all_out,
        near_gate,
        near_up,
        near_down,
        far_grads,
    ) = pl.pallas_call(
        functools.partial(attend_kernel, width),
        out_shape=(
            like((inner, length), F32),
            like((heads, 1, length), F32),
            like((4, inner, rows), BF16),
            like((4 * inner, model), BF16),
            like(gate_weight.shape, BF16),
            like(up_weight.shape, BF16),
            like(down_weight.shape, BF16),
            like((rows, model), BF16),
        ),
        in_specs=whole(5) + anywhere(4),
        out_specs=whole(4) + anywhere(4),
        scratch_shapes=[
            pltpu.VMEM((length, rows), F32),
            pltpu.VMEM((4, inner, rows), BF16),
            *semaphores(11),
        ],
        compiler_params=params(1),
        name="attend",
    )(
        queries_t,
        twice_keys,
        values_t,
        table,
        out_weight,
        gate_weight,
        up_weight,
        down_weight,
        grads,
    )
    (
        states_part,
        far_made,
        middle_grad,
        ffn_gain_grad,
        weight_grad,
        out_part,
        grad_stage,
    ) = pl.pallas_call(
        ffn_kernel,
        out_shape=(
            like((rows, model), F32),
            like((rows, model), BF16),
            like((rows, model), F32),
            like((8, model), F32),
            like((3 * model, hidden), BF16),
            like((4, model, inner), BF16),
            like((4, inner, rows), BF16),
        ),
        in_specs=whole(12),
        out_specs=whole(7),
        scratch_shapes=[
            pltpu.VMEM((rows, model), F32),
            pltpu.VMEM((2, rows, model), BF16),
            pltpu.VMEM((2, rows, model), F32),
            pltpu.VMEM((2, rows, model), F32),
            pltpu.VMEM((2, 3, model, hidden), F32),
            pltpu.VMEM((rows, model), BF16),
            pltpu.VMEM((rows, model), BF16),
            pltpu.VMEM((3, model, hidden), BF16),
            pltpu.VMEM((3, model, hidden), BF16),
            *semaphores(3),
        ],
        compiler_params=params(2),
        name="ffn",
    )(
        attended,
        all_out,
        residual,
        ffn_gain[None],
        grads,
        far_grads,
        gate_weight,
        near_gate,
        up_weight,
        near_up,
        down_weight,
        near_down,
    )
    replicas = lax.axis_size("dp")
    strides = strides_of(replicas)
    chain_scratch = []
    for height, lanes in ((3 * model, hidden), (model, 4 * inner), (share, model)):
        for _ in range(2):
            chain_scratch += Chain.scratch(height // 2, lanes, len(strides) - 2)
    (
        input_grad,
        out_states,
        weight_total,
        joint_total,
        out_total,
        join_total,
        small,
        bias_total,
    ) = pl.pallas_call(
        functools.partial(back_kernel, width, replicas),
        out_shape=(
            like((rows, model), F32),
            like((rows, model), F32),
            like((3 * model, hidden), F32),
            like((model, 4 * inner), F32),
            like((inner, model), F32),
            like((share, model), F32),
            like((8, model), F32),
            like((buckets, LANES), F32),
        ),
        in_specs=whole(26),
        out_specs=whole(8),
        scratch_shapes=[
            pltpu.VMEM((4, inner, rows), BF16),
            pltpu.VMEM((length, inner), BF16),
            pltpu.VMEM((inner, length), F32),
            pltpu.VMEM((length, inner), F32),
            pltpu.VMEM((length, inner), F32),
            pltpu.VMEM((heads, span, LANES), F32),
            pltpu.VMEM((length, 3 * inner), BF16),
            pltpu.VMEM((4, rows, 3 * inner), BF16),
            pltpu.VMEM((4, model, 3 * inner), BF16),
            pltpu.VMEM((rows, model), BF16),
            pltpu.VMEM((2, model, inner), BF16),
            pltpu.VMEM((model, inner), BF16),
            pltpu.VMEM((model, inner), BF16),
            pltpu.VMEM((model, 4 * inner), BF16),
            pltpu.VMEM((length // LANES, LANES), F32),
            pltpu.VMEM((4, 8, model), F32),
            pltpu.VMEM((4, share, model), BF16),
            pltpu.VMEM((2, share, model), BF16),
            pltpu.VMEM((share, model), BF16),
            pltpu.VMEM((share, model), BF16),
            pltpu.VMEM((share, model), BF16),
            pltpu.VMEM((4, 8, model), F32),
            pltpu.VMEM((len(strides), 8, model), F32),
            pltpu.VMEM((len(strides), 8, model), F32),
            pltpu.VMEM((len(strides), buckets, LANES), F32),
            pltpu.VMEM((len(strides), buckets, LANES), F32),
            *semaphores(22 + 2 * len(strides)),
            *semaphores(6 * Chain.slots(strides)),
            *chain_scratch,
        ],
        compiler_params=params(3),
        name="back",
    )(
        queries_t,
        queries,
        twice_keys,
        keys_t,
        values,
        grad_stage,
        outs,
        totals,
        table,
        normed,
        joint_weight,
        bucket_row,
        residual,
        norm_gain[None],
        middle_grad,
        starts,
        divisor,
        pooled,
        mix,
        all_taps,
        all_join,
        weight_grad,
        out_part,
        far_made,
        states_part,
        ffn_gain_grad,
    )
    own_taps = lax.dynamic_slice_in_dim(small[:4], lax.axis_index("mp") * share, share, 1)
    return (
        out_states[:, None, :],
        input_grad[:, None, :],
        own_taps[:2],
        own_taps[:3],
        own_taps,
        join_total,
        small[4],
        joint_total[:, :inner],
        joint_total[:, inner : 2 * inner],
        joint_total[:, 2 * inner : 3 * inner],
        bias_total[:, :heads],
        out_total,
        small[5],
        weight_total[:model],
        weight_total[model : 2 * model],
        weight_total[2 * model :],
    )


def solution(mesh):
    return jax.shard_map(
        shards,
        mesh=mesh,
        in_specs=(
            P("mp", "dp", None),
            P(None, "dp"),
            P(),
            P(None, "mp"),
            P(None, "mp"),
            P(None, "mp"),
            P("mp", None),
            P(),
            P(None, "mp"),
            P(None, "mp"),
            P(None, "mp"),
            P(None, "mp"),
            P("mp", None),
            P(),
            P(None, "mp"),
            P(None, "mp"),
            P("mp", None),
            P("mp", "dp", None),
        ),
        out_specs=(
            P("mp", "dp", None),
            P("mp", "dp", None),
            P(None, "mp"),
            P(None, "mp"),
            P(None, "mp"),
            P("mp", None),
            P(),
            P(None, "mp"),
            P(None, "mp"),
            P(None, "mp"),
            P(None, "mp"),
            P("mp", None),
            P(),
            P(None, "mp"),
            P(None, "mp"),
            P("mp", None),
        ),
        check_vma=False,
    )
```

```python
import functools

import jax
import jax.numpy as jnp
from jax import lax
from jax.experimental import pallas as pl
from jax.experimental.pallas import tpu as pltpu
from jax.sharding import PartitionSpec as P

EPSILON = 1e-06
LOG2E = 1.4426950408889634
GELU_SCALE = 0.7978845608028654
GELU_CUBE = 0.044715
F32 = jnp.float32
BF16 = jnp.bfloat16
LANES = 128
HALO = 3
VMEM_LIMIT = 56 << 20
MESH = pl.DeviceIdType.MESH


def whole(count):
    return [pl.BlockSpec(memory_space=pltpu.VMEM)] * count


def anywhere(count):
    return [pl.BlockSpec(memory_space=pl.ANY)] * count


def params(collective=None):
    return pltpu.CompilerParams(
        vmem_limit_bytes=VMEM_LIMIT, collective_id=collective, has_side_effects=collective is not None
    )


def like(shape, dtype):
    return jax.ShapeDtypeStruct(shape, dtype)


def dot(lhs, rhs):
    return jnp.dot(lhs, rhs, preferred_element_type=F32)


def dot_nt(lhs, rhs):
    return lax.dot_general(lhs, rhs, (((1,), (1,)), ((), ())), preferred_element_type=F32)


def dot_tn(lhs, rhs):
    return lax.dot_general(lhs, rhs, (((0,), (0,)), ((), ())), preferred_element_type=F32)


def split(values):
    high = values.astype(BF16)
    return high, (values - high.astype(F32)).astype(BF16)


def turned(values):
    return values.astype(F32).T.astype(BF16)


def ranks():
    me = lax.axis_index("mp")
    near = me + 1 - 2 * (me % 2)
    return me, near, (me + 2) % 4, (near + 2) % 4


def greet(peers, strides=()):
    barrier = pltpu.get_barrier_semaphore()
    for peer in peers:
        pl.semaphore_signal(barrier, inc=1, device_id={"mp": peer}, device_id_type=MESH)
    for stride in strides:
        pl.semaphore_signal(barrier, inc=1, device_id={"dp": partner(stride)}, device_id_type=MESH)
    pl.semaphore_wait(barrier, len(peers) + len(strides))


def side_of(stride):
    return (lax.axis_index("dp") // stride) % 2


def partner(stride):
    return lax.axis_index("dp") + stride - 2 * stride * side_of(stride)


def strides_of(count):
    strides = []
    while 2 ** len(strides) < count:
        strides.append(2 ** len(strides))
    return strides


class remote:
    def __init__(self, *given, axis="mp"):
        self.given, self.axis = given, axis

    def start(self):
        described(*self.given, self.axis).start()

    def wait_recv(self):
        described(*self.given, self.axis).wait_recv()

    def wait_send(self):
        described(*self.given, self.axis).wait_send()

    def wait(self):
        described(*self.given, self.axis).wait()


def described(source, target, sems, slot, peer, axis):
    source, target, peer = [part() if callable(part) else part for part in (source, target, peer)]
    sends, receives = sems
    return pltpu.make_async_remote_copy(
        src_ref=source,
        dst_ref=target,
        send_sem=sends.at[slot],
        recv_sem=receives.at[slot],
        device_id={axis: peer},
        device_id_type=MESH,
    )


def semaphores(count):
    return [pltpu.SemaphoreType.DMA((count,)), pltpu.SemaphoreType.DMA((count,))]


class Chain:
    def __init__(self, source_ref, base, rows, strides, scratch, sems, first_slot):
        self.source, self.base, self.rows, self.strides = source_ref, base, rows, strides
        (
            self.half_in,
            self.half,
            self.quarter_in,
            self.quarter,
            self.whole_quarter,
            self.gathered_quarter,
            self.both,
            self.gathered_half,
        ) = scratch
        self.sems, self.slot, self.at = sems, first_slot, 0
        self.copy, self.copies = None, []
        self.steps = len(strides) + 3

    @staticmethod
    def scratch(rows, width, exchanges):
        half, quarter = (rows // 2, width), (rows // 4, width)
        return [
            pltpu.VMEM(half, BF16),
            pltpu.VMEM(half, BF16),
            pltpu.VMEM((exchanges + 1, *quarter), BF16),
            pltpu.VMEM((exchanges, *quarter), BF16),
            pltpu.VMEM(quarter, BF16),
            pltpu.VMEM(quarter, BF16),
            pltpu.VMEM(half, BF16),
            pltpu.VMEM(half, BF16),
        ]

    @staticmethod
    def slots(strides):
        return len(strides) + 2

    def send(self, source, target, stride):
        copy = remote(
            source, target, self.sems, self.slot + len(self.copies), lambda: partner(stride), axis="dp"
        )
        copy.start()
        self.copies.append(copy)

    def step(self, finish=None):
        first, second, others = self.strides[0], self.strides[1], self.strides[2:]
        half, quarter = self.rows // 2, self.rows // 4
        at = self.at
        self.at += 1
        if at > 0:
            self.copies[-1].wait_recv()
        if at == 0:
            self.send(lambda: self.source.at[pl.ds(pl.multiple_of(self.base + (1 - side_of(first)) * half, 16), half), :], self.half_in, first)
        elif at == 1:
            begin = pl.multiple_of(self.base + side_of(first) * half, 16)
            mine = self.source[pl.ds(begin, half), :].astype(F32)
            self.half[...] = (mine + self.half_in[...].astype(F32)).astype(BF16)
            self.send(lambda: self.half.at[pl.ds(pl.multiple_of((1 - side_of(second)) * quarter, 16), quarter), :], lambda: self.quarter_in.at[0], second)
        elif at <= 1 + len(others):
            if at == 2:
                mine = self.half[pl.ds(pl.multiple_of(side_of(second) * quarter, 16), quarter), :]
            else:
                mine = self.quarter[at - 3]
            total = mine.astype(F32) + self.quarter_in[at - 2].astype(F32)
            self.quarter[at - 2] = total.astype(BF16)
            self.send(
                lambda: self.quarter.at[at - 2], lambda: self.quarter_in.at[at - 1], others[at - 2]
            )
        elif at == 2 + len(others):
            total = self.quarter[at - 3].astype(F32) + self.quarter_in[at - 2].astype(F32)
            self.whole_quarter[...] = total.astype(BF16)
            self.send(self.whole_quarter, self.gathered_quarter, second)
        elif at == 3 + len(others):
            side = side_of(second)
            mine = pl.ds(pl.multiple_of(side * quarter, 16), quarter)
            other = pl.ds(pl.multiple_of((1 - side) * quarter, 16), quarter)
            self.both[mine, :] = self.whole_quarter[...]
            self.both[other, :] = self.gathered_quarter[...]
            self.send(self.both, self.gathered_half, first)
        else:
            side = side_of(first)
            mine = pl.ds(pl.multiple_of(self.base + side * half, 16), half)
            other = pl.ds(pl.multiple_of(self.base + (1 - side) * half, 16), half)
            finish(mine, self.both[...].astype(F32))
            finish(other, self.gathered_half[...].astype(F32))
            for copy in self.copies:
                copy.wait_send()


def rms(values, gain):
    return values * lax.rsqrt(jnp.mean(values * values, axis=1, keepdims=True) + EPSILON) * gain


def rms_back(grads, values, gain):
    scale = lax.rsqrt(jnp.mean(values * values, axis=1, keepdims=True) + EPSILON)
    gain_grad = jnp.sum(grads * values * scale, axis=0, keepdims=True)
    raised = grads * gain
    mean = jnp.mean(raised * values, axis=1, keepdims=True)
    return scale * raised - values * (scale * scale * scale * mean), gain_grad


def bucket_hits(bucket_ref, buckets):
    span = bucket_ref.shape[1]
    rows = lax.broadcasted_iota(jnp.int32, (buckets, span), 0)
    return rows == jnp.broadcast_to(bucket_ref[...], (buckets, span))


def fill_bias_table(bucket_ref, bias_ref, table_ref):
    span = bucket_ref.shape[1]
    heads, buckets = bias_ref.shape
    hits = bucket_hits(bucket_ref, buckets).astype(F32).astype(BF16)
    bias = bias_ref[...]
    first = bias.astype(BF16)
    second, third = split(bias - first.astype(F32))
    rows = jnp.concatenate([first, second, third, jnp.zeros((16 - 3 * heads, buckets), BF16)], axis=0)
    lines = dot(rows, hits)
    for head in range(heads):
        line = lines[head : head + 1] + (
            lines[heads + head : heads + head + 1] + lines[2 * heads + head : 2 * heads + head + 1]
        )
        skew = pltpu.roll(
            jnp.broadcast_to(line * LOG2E, (LANES, span)), span - LANES + 1, 1, stride=1, stride_axis=0
        )
        for block in range(span // LANES - 1):
            cut = slice(block * LANES, (block + 1) * LANES)
            table_ref[head, cut, :] = skew[:, cut].T


def bias_grad_kernel(table_ref, bucket_ref, grad_ref):
    span = bucket_ref.shape[1]
    buckets, lanes = grad_ref.shape
    hits = bucket_hits(bucket_ref, buckets)
    columns = []
    for head in range(table_ref.shape[0]):
        blocks = [
            table_ref[head, block * LANES : (block + 1) * LANES, :].T
            for block in range(span // LANES - 1)
        ]
        skew = jnp.concatenate(blocks + [jnp.zeros((LANES, LANES), F32)], axis=1)
        rows = LANES // 2
        while rows >= 8:
            skew = skew[:rows] + pltpu.roll(skew[rows:], span - rows, 1)
            rows //= 2
        line = jnp.zeros((1, span), F32)
        for row in range(8):
            line = line + pltpu.roll(skew[row : row + 1], LANES - 1 - row, 1)
        columns.append(jnp.sum(jnp.where(hits, line, 0.0), axis=1, keepdims=True))
    lane = lax.broadcasted_iota(jnp.int32, (buckets, lanes), 1)
    made = jnp.zeros((buckets, lanes), F32)
    for head, column in enumerate(columns):
        made = jnp.where(lane == head, column, made)
    grad_ref[...] = made


def word_numbers(starts):
    rows = starts.shape[0]
    upper = lax.broadcasted_iota(jnp.int32, (LANES, LANES), 0) <= lax.broadcasted_iota(
        jnp.int32, (LANES, LANES), 1
    )
    within = dot(starts.astype(F32).astype(BF16), upper.astype(F32).astype(BF16))
    totals = jnp.broadcast_to(within[:, LANES - 1 :], (rows, LANES)).astype(BF16)
    lower = lax.broadcasted_iota(jnp.int32, (rows, rows), 1) < lax.broadcasted_iota(
        jnp.int32, (rows, rows), 0
    )
    return within + dot(lower.astype(F32).astype(BF16), totals) - 1.0


class Words:
    def __init__(self, starts_ref, ids_ref, me, ranks_count):
        ids = word_numbers(starts_ref[...])
        ids_ref[...] = ids
        per = ids.shape[0] // ranks_count
        self.firsts = [ids[per * rank : per * rank + 1, 0:1] for rank in range(ranks_count)]
        self.lasts = [
            ids[per * (rank + 1) - 1 : per * (rank + 1), LANES - 1 :] for rank in range(ranks_count)
        ]
        pieces = [ids_ref[pl.ds(me * per + piece, 1), :] for piece in range(per)]
        self.row = jnp.concatenate(pieces, axis=1)
        self.first = self.row[:, 0:1]
        self.last = self.row[:, per * LANES - 1 :]
        self.me = me
        self.count = per * LANES

    def table(self):
        shape = (self.count + 16, self.count)
        rows = lax.broadcasted_iota(jnp.int32, shape, 0).astype(F32)
        return (rows == self.row - self.first + HALO).astype(F32).astype(BF16)

    def pick(self, target):
        slots = lax.broadcasted_iota(jnp.int32, (8, 1), 0)
        hits = target(slots, self.first, self.last) == self.row
        return hits.astype(F32).astype(BF16)

    def place(self, target, valid):
        width = 2 * LANES
        lane = lax.broadcasted_iota(jnp.int32, (1, width), 1) % LANES
        slots, rank = lane % 8, lane // 8
        goal = jnp.full((1, width), -9.0, F32)
        for index, (first, last) in enumerate(zip(self.firsts, self.lasts)):
            goal = jnp.where(rank == index, target(slots, first, last), goal)
        known = valid(slots, rank, self.me) & (rank < len(self.firsts))
        goal = jnp.where(known, goal - self.first + HALO, -1.0)
        rows = lax.broadcasted_iota(jnp.int32, (self.count + 16, width), 0).astype(F32)
        return (rows == goal).astype(F32).astype(BF16)


def stacked(summary_ref):
    parts = [summary_ref[rank] for rank in range(summary_ref.shape[0])]
    rest = LANES - sum(part.shape[0] for part in parts)
    parts.append(jnp.zeros((rest, parts[0].shape[1]), F32))
    return jnp.concatenate(split(jnp.concatenate(parts, axis=0)), axis=0)


def ahead_target(slots, first, last):
    later = jnp.where(slots <= 4, last - (slots - 1).astype(F32), -9.0)
    return jnp.where(slots == 0, first, later)


def ahead_valid(slots, rank, me):
    return ((rank < me) & (slots >= 1) & (slots <= 4)) | ((rank > me) & (slots == 0))


def back_target(slots, first, last):
    return jnp.where(slots <= 3, first + slots.astype(F32), jnp.where(slots == 4, last, -9.0))


def back_valid(slots, rank, me):
    return ((rank > me) & (slots <= 3)) | ((rank < me) & (slots == 4))


def forward_kernel(
    width,
    states_ref,
    starts_ref,
    two_ref,
    three_ref,
    four_ref,
    join_ref,
    gain_ref,
    query_weight_ref,
    key_weight_ref,
    value_weight_ref,
    bucket_ref,
    bias_ref,
    out_weight_ref,
    gate_ref,
    up_ref,
    down_ref,
    grad_ref,
    residual_out,
    normed_out,
    query_out,
    query_t_out,
    twice_out,
    key_t_out,
    value_out,
    table_out,
    divisor_out,
    pooled_out,
    mix_out,
    all_taps_ref,
    all_join_out,
    joint_out,
    padded_out,
    out_ref,
    total_ref,
    attended_ref,
    all_out_ref,
    near_gate_ref,
    near_up_ref,
    near_down_ref,
    far_grad_ref,
    residual_ref,
    normed_ref,
    query_ref,
    query_t_ref,
    twice_ref,
    key_t_ref,
    value_ref,
    table_ref,
    divisor_ref,
    pooled_ref,
    mix_ref,
    all_join_ref,
    joint_ref,
    padded_ref,
    value_t_ref,
    ids_ref,
    summary_ref,
    taps_in_ref,
    score_ref,
    stage_ref,
    ship_ref,
    *sems,
):
    me, near, far, cross = ranks()
    peers = (near, far, cross)
    rows, model = states_ref.shape
    share = join_ref.shape[0]
    inner = query_weight_ref.shape[1]
    heads, length = twice_ref.shape[0], twice_ref.shape[1]
    shipped = []

    def ship(source, target):
        copy = pltpu.make_async_copy(source, target, ship_ref.at[len(shipped)])
        copy.start()
        shipped.append(copy)

    def band(ref, rank):
        return ref.at[pl.ds(pl.multiple_of(rank * share, share), share), :]

    words = Words(starts_ref, ids_ref, me, 4)
    states = states_ref[...]
    wide_states = jnp.concatenate([states, jnp.ones((rows, LANES), BF16)], axis=1)
    summary_ref[me] = dot(words.pick(ahead_target), wide_states)
    two, three, four = two_ref[...], three_ref[...], four_ref[...]
    taps_in_ref[me] = jnp.concatenate(
        [
            two[0:1] + three[0:1] + four[0:1],
            two[1:2] + three[1:2] + four[1:2],
            three[2:3] + four[2:3],
            four[3:4],
            jnp.zeros((4, share), F32),
        ],
        axis=0,
    )
    all_join_ref[pl.ds(pl.multiple_of(me * share, share), share), :] = join_ref[...]
    all_out_ref[pl.ds(pl.multiple_of(me * share, share), share), :] = out_weight_ref[...]
    greet(peers)
    early = []
    for slot, peer in enumerate(peers):
        early.append(remote(summary_ref.at[me], summary_ref.at[me], sems, slot, peer))
        early.append(remote(taps_in_ref.at[me], taps_in_ref.at[me], sems, 3 + slot, peer))
    joins = [
        remote(band(all_join_ref, me), band(all_join_ref, me), sems, 6, far),
        remote(band(all_join_ref, me), band(all_join_ref, me), sems, 7, near),
    ]
    for copy in early + joins:
        copy.start()
    padded_ref[...] = jnp.full(padded_ref.shape, -1, jnp.int32)
    padded_ref[:, : bucket_ref.shape[1]] = bucket_ref[...]
    joint_ref[:, :inner] = query_weight_ref[...]
    joint_ref[:, inner : 2 * inner] = key_weight_ref[...]
    joint_ref[:, 2 * inner :] = value_weight_ref[...]
    ship(joint_ref, joint_out)
    ship(padded_ref, padded_out)
    table = words.table()
    sums = dot(table, wide_states)
    place = words.place(ahead_target, ahead_valid)
    for copy in early:
        copy.wait_recv()
    sums = sums + dot(place, stacked(summary_ref))
    divisor = jnp.maximum(sums[:, model:], 1.0)
    divisor_ref[...] = divisor
    ship(divisor_ref, divisor_out)
    pooled = sums[:, :model] / jnp.concatenate([divisor] * (model // LANES), axis=1)
    pooled_ref[...] = pooled
    ship(pooled_ref, pooled_out)
    taps = jnp.concatenate([taps_in_ref[rank] for rank in range(4)], axis=1)
    all_taps_ref[...] = taps
    joins[0].wait_recv()
    joins.append(remote(band(all_join_ref, far), band(all_join_ref, far), sems, 8, near))
    joins[2].start()
    total = pooled * taps[0:1]
    for lag in range(1, 4):
        total = total + pltpu.roll(pooled, lag, 0) * taps[lag : lag + 1]
    mix = dot_tn(table, total.astype(BF16)).astype(BF16)
    mix_ref[...] = mix
    ship(mix_ref, mix_out)
    joins[1].wait_recv()
    joins[2].wait_recv()
    residual = states.astype(F32) + dot(mix, all_join_ref[...])
    residual_ref[...] = residual
    own = pl.ds(pl.multiple_of(me * rows, rows), rows)
    normed_ref[own, :] = rms(residual, gain_ref[...]).astype(BF16)

    def block(rank, part):
        half = rows // 2
        return normed_ref.at[pl.ds(pl.multiple_of(rank * rows + part * half, half), half), :]

    sends = []
    for part in range(2):
        sends.append(remote(block(me, part), block(me, part), sems, 9 + part, far))
    for part in range(2):
        sends.append(remote(block(me, part), block(me, part), sems, 11 + part, near))
    for copy in sends:
        copy.start()
    copies = [
        remote(grad_ref, far_grad_ref, sems, 15, far),
        remote(band(all_out_ref, me), band(all_out_ref, me), sems, 16, near),
        remote(gate_ref, near_gate_ref, sems, 17, near),
        remote(up_ref, near_up_ref, sems, 18, near),
        remote(down_ref, near_down_ref, sems, 19, near),
    ]
    out_far = remote(
        lambda: band(all_out_ref, me), lambda: band(all_out_ref, me), sems, 20, far
    )
    out_pass = remote(
        lambda: band(all_out_ref, far), lambda: band(all_out_ref, far), sems, 21, near
    )
    out_far.start()
    for copy in copies:
        copy.start()
    ship(residual_ref, residual_out)
    ship(all_join_ref, all_join_out)

    def project(rank):
        cut = pl.ds(pl.multiple_of(rank * rows, rows), rows)
        made = dot(normed_ref[cut, :], joint_ref[...])
        query, key, value = [
            made[:, index * inner : (index + 1) * inner].astype(BF16) for index in range(3)
        ]
        query_ref[cut, :] = query
        query_t_ref[:, cut] = turned(query)
        key_t_ref[:, cut] = turned(key)
        value_ref[cut, :] = value
        value_t_ref[:, cut] = turned(value)
        for head in range(heads):
            part = key[:, head * width : (head + 1) * width]
            twice_ref[head, cut, :] = jnp.concatenate([part, part], axis=1)

    project(me)
    fill_bias_table(padded_ref, bias_ref, table_ref)
    ship(table_ref, table_out)
    sends[2].wait_recv()
    sends[3].wait_recv()
    project(near)
    passed = []
    for part in range(2):
        sends[part].wait_recv()
        passed.append(remote(block(far, part), block(far, part), sems, 13 + part, near))
        passed[part].start()
    project(far)
    for copy in passed:
        copy.wait_recv()
    project(cross)
    for source, target in (
        (normed_ref, normed_out),
        (query_ref, query_out),
        (query_t_ref, query_t_out),
        (twice_ref, twice_out),
        (key_t_ref, key_t_out),
        (value_ref, value_out),
    ):
        ship(source, target)
    wide = deep = length // 4

    def owner(order):
        chip = (me // 2 + 1 + order // 2) % 2
        core = (me % 2 + (order + 1) // 2) % 2
        return 2 * chip + core

    def handed(order):
        return remote(stage_ref.at[order], attended_ref.at[me], sems, 22 + order, owner(order))

    def step(index, carry):
        order, head = index // heads, index % heads
        begin = pl.multiple_of(owner(order) * wide, wide)
        span = pl.ds(begin, wide)
        rows = pl.ds(pl.multiple_of(head * width, width), width)
        scaled = query_t_ref[rows, span].astype(F32) * LOG2E
        queries = jnp.concatenate(split(scaled), axis=0)
        peak = jnp.full((8, wide), -1e30, F32)
        for part in range(length // deep):
            cut = slice(part * deep, (part + 1) * deep)
            raw = dot(twice_ref[head, cut, :], queries)
            columns = []
            for lane in range(0, wide, LANES):
                offset = pl.multiple_of(part * deep - begin - lane + length - LANES, LANES)
                columns.append(raw[:, lane : lane + LANES] + table_ref[head, pl.ds(offset, deep), :])
            scores = jnp.concatenate(columns, axis=1)
            score_ref[cut, :] = scores
            peak = jnp.maximum(peak, jnp.max(scores.reshape(deep // 8, 8, wide), axis=0))
        peak = jnp.max(peak, axis=0, keepdims=True)
        sums = jnp.zeros((8, wide), F32)
        made = jnp.zeros((width, wide), F32)
        for part in range(length // deep):
            cut = slice(part * deep, (part + 1) * deep)
            raised = jnp.exp2(score_ref[cut, :] - peak)
            sums = sums + jnp.sum(raised.reshape(deep // 8, 8, wide), axis=0)
            made = made + dot(value_t_ref[rows, cut], raised.astype(BF16))
        total = jnp.sum(sums, axis=0, keepdims=True)
        made = made / total
        out_ref[rows, span] = made
        total_ref[head, :, span] = peak + jnp.log2(total)
        stage_ref[order, rows, :] = made.astype(BF16)

        @pl.when((head == heads - 1) & (order < 3))
        def _():
            handed(order).start()

        @pl.when(index == heads)
        def _():
            out_far.wait_recv()
            out_pass.start()

        return carry

    lax.fori_loop(0, heads * 4, step, 0)
    attended_ref[me] = stage_ref[3]
    for order in range(3):
        handed(order).wait()
    for copy in copies:
        copy.wait()
    out_pass.wait()
    for copy in early + joins + sends + passed + [out_far]:
        copy.wait_send()
    for copy in shipped:
        copy.wait()


def ffn_kernel(
    attended_ref,
    all_out_ref,
    residual_ref,
    gain_ref,
    grad_ref,
    far_grad_ref,
    gate_ref,
    near_gate_ref,
    up_ref,
    near_up_ref,
    down_ref,
    near_down_ref,
    states_part_ref,
    far_made_ref,
    middle_grad_ref,
    gain_grad_ref,
    weight_grad_ref,
    out_part_ref,
    grad_stage_ref,
    middle_ref,
    normed_ref,
    made_ref,
    back_ref,
    sums_ref,
    far_out_ref,
    far_in_ref,
    near_out_ref,
    near_in_ref,
    *sems,
):
    me, near, far, cross = ranks()
    peers = (near, far, cross)
    rows, model = residual_ref.shape
    share = attended_ref.shape[1]
    attended = attended_ref[...].reshape(4 * share, rows)
    middle = residual_ref[...] + dot_tn(attended, all_out_ref[...])
    middle_ref[...] = middle
    normed_ref[0] = rms(middle, gain_ref[...]).astype(BF16)
    greet(peers)
    there = remote(normed_ref.at[0], normed_ref.at[1], sems, 0, far)
    there.start()

    def work(side, grads, gate, up, down, slab):
        given = normed_ref[side]
        gate_value = dot(given, gate)
        up_value = dot(given, up)
        hidden_grad = dot_nt(grads, down)
        square = gate_value * gate_value
        curve = jnp.tanh(GELU_SCALE * gate_value * (1.0 + GELU_CUBE * square))
        half = 0.5 + 0.5 * curve
        gelu = gate_value * half
        slope = half + (0.5 * GELU_SCALE) * gate_value * (1.0 - curve * curve) * (
            1.0 + (3.0 * GELU_CUBE) * square
        )
        hidden = (gelu * up_value).astype(BF16)
        gate_back = (hidden_grad * up_value * slope).astype(BF16)
        up_back = (hidden_grad * gelu).astype(BF16)
        sums = [dot_tn(given, gate_back), dot_tn(given, up_back), dot_tn(hidden, grads)]
        for index in range(3):
            if side == 0:
                sums_ref[slab, index] = sums[index]
            else:
                sums_ref[slab, index] += sums[index]
        made = dot(hidden, down)
        back = dot_nt(gate_back, gate) + dot_nt(up_back, up)
        if slab == 0:
            made_ref[side] = made
            back_ref[side] = back
        else:
            made_ref[side] += made
            back_ref[side] += back

    mine = (gate_ref, up_ref, down_ref)
    other = (near_gate_ref, near_up_ref, near_down_ref)
    for slab, weights in enumerate((mine, other)):
        work(0, grad_ref[...], *[ref[...] for ref in weights], slab)
    there.wait_recv()
    for slab, weights in enumerate((mine, other)):
        work(1, far_grad_ref[...], *[ref[...] for ref in weights], slab)
    far_out_ref[...] = back_ref[1].astype(BF16)
    returned = remote(far_out_ref, far_in_ref, sems, 1, far)
    returned.start()
    near_out_ref[...] = sums_ref[1].astype(BF16)
    swap = remote(near_out_ref, near_in_ref, sems, 2, near)
    swap.start()
    far_made_ref[...] = made_ref[1].astype(BF16)
    states_part_ref[...] = middle_ref[...] + made_ref[0]
    returned.wait_recv()
    normed_grad = back_ref[0] + far_in_ref[...].astype(F32)
    part, gain_grad = rms_back(normed_grad, middle_ref[...], gain_ref[...])
    gain_grad_ref[...] = jnp.broadcast_to(gain_grad, gain_grad_ref.shape)
    middle_grad = grad_ref[...].astype(F32) + part
    middle_grad_ref[...] = middle_grad
    low = middle_grad.astype(BF16)
    grad_stage_ref[...] = dot_nt(all_out_ref[...], low).astype(BF16).reshape(4, share, rows)
    out_part = dot(attended, low)
    for rank in range(4):
        out_part_ref[rank] = out_part[rank * share : (rank + 1) * share, :].T.astype(BF16)
    swap.wait_recv()
    depth = weight_grad_ref.shape[0] // 3
    for index in range(3):
        total = sums_ref[0, index] + near_in_ref[index].astype(F32)
        weight_grad_ref[index * depth : (index + 1) * depth, :] = total.astype(BF16)
    for copy in (returned, there, swap):
        copy.wait_send()


def back_kernel(
    width,
    count,
    query_t_ref,
    query_ref,
    twice_ref,
    key_t_ref,
    value_ref,
    grad_stage_ref,
    out_ref,
    total_ref,
    table_ref,
    normed_ref,
    joint_ref,
    bucket_ref,
    residual_ref,
    gain_ref,
    middle_grad_ref,
    starts_ref,
    divisor_ref,
    pooled_ref,
    mix_ref,
    all_taps_ref,
    all_join_ref,
    weight_grad_ref,
    out_part_ref,
    far_made_ref,
    states_part_ref,
    ffn_gain_grad_ref,
    input_grad_ref,
    states_out_ref,
    weight_total_ref,
    joint_total_ref,
    out_total_ref,
    join_total_ref,
    small_total_ref,
    bias_total_ref,
    grad_t_ref,
    grad_ref,
    query_grad_ref,
    key_grad_ref,
    value_grad_ref,
    table_grad_ref,
    joint_grad_ref,
    joint_in_ref,
    all_joint_ref,
    made_in_ref,
    out_near_ref,
    out_sum_ref,
    out_far_ref,
    late_ref,
    ids_ref,
    summary_ref,
    join_part_ref,
    join_near_ref,
    join_sum_ref,
    join_far_ref,
    join_ref,
    small_near_ref,
    small_ref,
    small_in_ref,
    bias_ref,
    bias_in_ref,
    sends_ref,
    receives_ref,
    chain_sends_ref,
    chain_receives_ref,
    *chain_refs,
):
    me, near, far, cross = ranks()
    peers = (near, far, cross)
    sems = (sends_ref, receives_ref)
    chain_sems = (chain_sends_ref, chain_receives_ref)
    heads, length = twice_ref.shape[0], twice_ref.shape[1]
    rows, model = residual_ref.shape
    share = join_part_ref.shape[1]
    inner = heads * width
    wide, deep = length // 4, length // 8
    strides = strides_of(count)
    turned_strides = [strides[1], strides[0]] + strides[2:]
    chains = []
    plan = [
        (weight_grad_ref, weight_grad_ref.shape[0], strides),
        (weight_grad_ref, weight_grad_ref.shape[0], turned_strides),
        (late_ref, late_ref.shape[0], strides),
        (late_ref, late_ref.shape[0], turned_strides),
        (join_ref, join_ref.shape[0], strides),
        (join_ref, join_ref.shape[0], turned_strides),
    ]
    for index, (ref, height, order) in enumerate(plan):
        half = height // 2
        chains.append(
            Chain(
                ref,
                (index % 2) * half,
                half,
                order,
                chain_refs[8 * index : 8 * index + 8],
                chain_sems,
                index * Chain.slots(strides),
            )
        )
    weight_chains, late_chains, join_chains = chains[0:2], chains[2:4], chains[4:6]

    greet(peers, strides)
    gradient_copies = []
    for slot, peer in enumerate(peers):
        copy = remote(
            lambda peer=peer: grad_stage_ref.at[peer], lambda: grad_t_ref.at[me], sems, slot, peer
        )
        copy.start()
        gradient_copies.append(copy)
    out_copies = [
        remote(lambda: out_part_ref.at[near], lambda: out_near_ref.at[0], sems, 3, near),
        remote(lambda: out_part_ref.at[cross], lambda: out_near_ref.at[1], sems, 4, near),
    ]
    for copy in out_copies:
        copy.start()
    joint_copies = [
        remote(joint_ref, lambda: all_joint_ref.at[me], sems, 5, far),
        remote(joint_ref, lambda: all_joint_ref.at[me], sems, 6, near),
    ]
    for copy in joint_copies:
        copy.start()
    joint_pass = remote(
        lambda: all_joint_ref.at[far], lambda: all_joint_ref.at[far], sems, 7, near
    )
    made_copy = remote(far_made_ref, made_in_ref, sems, 8, far)
    out_copy = remote(out_sum_ref, out_far_ref, sems, 9, far)
    for chain in weight_chains:
        chain.step()
    grad_t_ref[me] = grad_stage_ref[me]
    all_joint_ref[me] = joint_ref[...]
    key_grad_ref[...] = jnp.zeros_like(key_grad_ref)
    value_grad_ref[...] = jnp.zeros_like(value_grad_ref)
    table_grad_ref[...] = jnp.zeros_like(table_grad_ref)

    def step(index, carry):
        order, head = index // heads, index % heads
        block = 2 * ((me // 2 + order // 2) % 2) + (me % 2 + order % 2) % 2
        begin = pl.multiple_of(block * wide, wide)
        span = pl.ds(begin, wide)
        rows = pl.ds(pl.multiple_of(head * width, width), width)
        for slot in range(3):

            @pl.when(index == (slot + 1) * heads)
            def _(slot=slot):
                gradient_copies[slot].wait_recv()

        @pl.when(head == 0)
        def _():
            grad_ref[span, :] = turned(grad_t_ref[block])

        @pl.when(index == 3)
        def _():
            for copy in out_copies:
                copy.wait_recv()
            for slot, rank in enumerate((far, me)):
                ours = out_part_ref[rank].astype(F32) + out_near_ref[1 - slot].astype(F32)
                if slot == 0:
                    out_sum_ref[...] = ours.astype(BF16)
                else:
                    late_ref[:, 3 * inner :] = ours.astype(BF16)
            out_copy.start()
            made_copy.start()

        @pl.when(index == 4)
        def _():
            weight_chains[0].step()
            weight_chains[1].step()

        @pl.when(index == 5)
        def _():
            joint_copies[0].wait_recv()
            joint_pass.start()

        @pl.when(index == 6)
        def _():
            weight_chains[0].step()
            weight_chains[1].step()

        scaled = query_t_ref[rows, span].astype(F32) * LOG2E
        queries = jnp.concatenate(split(scaled), axis=0)
        total = total_ref[head, :, span]
        grads = grad_t_ref[block, rows, :].astype(F32)
        dots = jnp.sum(grads * out_ref[rows, span], axis=0, keepdims=True)
        own_rows = lax.broadcasted_iota(jnp.int32, (inner, wide), 0) // width == head
        own_lanes = lax.broadcasted_iota(jnp.int32, (wide, inner), 1) // width == head
        grad_t_own = jnp.where(own_rows, grad_t_ref[block].astype(F32), 0.0).astype(BF16)
        query_own = jnp.where(own_lanes, query_ref[span, :].astype(F32), 0.0).astype(BF16)
        grad_own = jnp.where(own_lanes, grad_ref[span, :].astype(F32), 0.0).astype(BF16)
        query_grad = jnp.zeros((width, wide), F32)
        for part in range(length // deep):
            cut = slice(part * deep, (part + 1) * deep)
            raw = dot(twice_ref[head, cut, :], queries)
            raw_grad = dot(value_ref[cut, :], grad_t_own)
            probs, score_grads = [], []
            for lane in range(0, wide, LANES):
                piece = slice(lane, lane + LANES)
                offset = pl.multiple_of(part * deep - begin - lane + length - LANES, LANES)
                shift = table_ref[head, pl.ds(offset, deep), :]
                prob = jnp.exp2(raw[:, piece] + shift - total[:, piece])
                low = (prob * (raw_grad[:, piece] - dots[:, piece])).astype(BF16)
                table_grad_ref[head, pl.ds(offset, deep), :] += low.astype(F32)
                probs.append(prob.astype(BF16))
                score_grads.append(low)
            probs = jnp.concatenate(probs, axis=1)
            score_grads = jnp.concatenate(score_grads, axis=1)
            value_grad_ref[cut, :] += dot(probs, grad_own)
            key_grad_ref[cut, :] += dot(score_grads, query_own)
            query_grad = query_grad + dot(key_t_ref[rows, cut], score_grads)
        query_grad_ref[rows, span] = query_grad
        return carry

    lax.fori_loop(0, heads * 4, step, 0)
    joint_grad_ref[:, :inner] = query_grad_ref[...].T.astype(BF16)
    joint_grad_ref[:, inner : 2 * inner] = key_grad_ref[...].astype(BF16)
    joint_grad_ref[:, 2 * inner :] = value_grad_ref[...].astype(BF16)
    handed = []
    for slot, peer in enumerate(peers):
        part = joint_grad_ref.at[pl.ds(pl.multiple_of(peer * wide, wide), wide), :]
        handed.append(remote(part, joint_in_ref.at[me], sems, 10 + slot, peer))
        handed[-1].start()
    joint_in_ref[me] = joint_grad_ref[pl.ds(pl.multiple_of(me * wide, wide), wide), :]
    for chain in weight_chains:
        chain.step()
    late_ref[:, : 3 * inner] = dot_tn(normed_ref[...], joint_grad_ref[...]).astype(BF16)
    out_copy.wait_recv()
    out_sum = late_ref[:, 3 * inner :].astype(F32) + out_far_ref[...].astype(F32)
    late_ref[:, 3 * inner :] = out_sum.astype(BF16)
    for chain in late_chains:
        chain.step()
    bias_grad_kernel(table_grad_ref, bucket_ref, bias_ref.at[0])
    for chain in weight_chains:
        chain.step()
    words = Words(starts_ref, ids_ref, me, 4)
    table = words.table()
    picked = words.pick(back_target)
    place = words.place(back_target, back_valid)
    joint_copies[1].wait_recv()
    joint_pass.wait_recv()
    normed_grad = dot_nt(joint_in_ref[me], all_joint_ref[me])
    for slot, peer in enumerate(peers):
        handed[slot].wait_recv()
        normed_grad = normed_grad + dot_nt(joint_in_ref[peer], all_joint_ref[peer])
    part, gain_grad = rms_back(normed_grad, residual_ref[...], gain_ref[...])
    residual_grad = middle_grad_ref[...] + part
    low = residual_grad.astype(BF16)
    high_mix, low_mix = split(dot_nt(low, all_join_ref[...]))
    summary_ref[me] = dot(picked, high_mix) + dot(picked, low_mix)
    copies = []
    for slot, peer in enumerate(peers):
        copies.append(remote(summary_ref.at[me], summary_ref.at[me], sems, 13 + slot, peer))
        copies[-1].start()
    join_part_ref[...] = dot_tn(mix_ref[...], low).astype(BF16).reshape(4, share, model)
    join_copies = [
        remote(join_part_ref.at[near], join_near_ref.at[0], sems, 16, near),
        remote(join_part_ref.at[cross], join_near_ref.at[1], sems, 17, near),
    ]
    for copy in join_copies:
        copy.start()
    for chain in late_chains:
        chain.step()
    word_grad = dot(table, high_mix) + dot(table, low_mix)
    pooled = pooled_ref[...]
    tap_rows = [jnp.sum(pooled * word_grad, axis=0, keepdims=True)]
    for lag in range(1, 4):
        tap_rows.append(jnp.sum(pltpu.roll(pooled, lag, 0) * word_grad, axis=0, keepdims=True))
    tap_rows += [gain_grad, ffn_gain_grad_ref[0:1], jnp.zeros((2, model), F32)]
    small_near_ref[me] = jnp.concatenate(tap_rows, axis=0)
    for slot, peer in enumerate(peers):
        copies.append(remote(small_near_ref.at[me], small_near_ref.at[me], sems, 18 + slot, peer))
        copies[-1].start()
    for copy in join_copies:
        copy.wait_recv()
    join_sum_ref[...] = (
        join_part_ref[far].astype(F32) + join_near_ref[1].astype(F32)
    ).astype(BF16)
    join_copy = remote(join_sum_ref, join_far_ref, sems, 21, far)
    join_copy.start()
    for copy in copies[:3]:
        copy.wait_recv()
    word_grad = word_grad + dot(place, stacked(summary_ref))
    for chain in late_chains:
        chain.step()
    for copy in copies[3:]:
        copy.wait_recv()
    small = small_near_ref[0]
    for rank in range(1, 4):
        small = small + small_near_ref[rank]
    small_ref[0] = small
    small_copies = []

    def exchange(index):
        stride = strides[index]
        small_copies.append(
            remote(small_ref.at[index], small_in_ref.at[index], sems, 22 + 2 * index, lambda: partner(stride), axis="dp")
        )
        small_copies.append(
            remote(bias_ref.at[index], bias_in_ref.at[index], sems, 23 + 2 * index, lambda: partner(stride), axis="dp")
        )
        small_copies[-2].start()
        small_copies[-1].start()

    exchange(0)
    join_copy.wait_recv()
    join_ref[...] = (
        join_part_ref[me].astype(F32) + join_near_ref[0].astype(F32) + join_far_ref[...].astype(F32)
    ).astype(BF16)
    for chain in join_chains:
        chain.step()
    taps = all_taps_ref[...]
    height = word_grad.shape[0]
    pooled_grad = word_grad * taps[0:1]
    for lag in range(1, 4):
        pooled_grad = pooled_grad + pltpu.roll(word_grad, height - lag, 0) * taps[lag : lag + 1]
    divisor = divisor_ref[...]
    pooled_grad = pooled_grad / jnp.concatenate([divisor] * (model // LANES), axis=1)
    high, low = split(pooled_grad)
    input_grad_ref[...] = residual_grad + (dot_tn(table, high) + dot_tn(table, low))
    made_copy.wait_recv()
    states_out_ref[...] = states_part_ref[...] + made_in_ref[...].astype(F32)

    def write_weights(span, values):
        weight_total_ref[span, :] = values

    def write_late(span, values):
        joint_total_ref[span, :] = values

    def write_join(span, values):
        join_total_ref[span, :] = values

    for turn in range(weight_chains[0].steps):
        for index in (0, 1):
            for group, finish in (
                (join_chains, write_join),
                (late_chains, write_late),
                (weight_chains, write_weights),
            ):
                chain = group[index]
                if chain.at < chain.steps:
                    chain.step(finish)
        if turn < len(strides):
            small_copies[2 * turn].wait_recv()
            small_copies[2 * turn + 1].wait_recv()
            small = small_ref[turn] + small_in_ref[turn]
            bias = bias_ref[turn] + bias_in_ref[turn]
            if turn + 1 < len(strides):
                small_ref[turn + 1] = small
                bias_ref[turn + 1] = bias
                exchange(turn + 1)
            else:
                small_total_ref[...] = small
                bias_total_ref[...] = bias
    out_total_ref[...] = joint_total_ref[:, 3 * inner :].T
    finished = gradient_copies + out_copies + joint_copies + [joint_pass, made_copy, out_copy]
    for copy in finished + handed + copies + join_copies + [join_copy] + small_copies:
        copy.wait_send()


def shards(
    byte_states,
    word_start,
    bucket_ids,
    conv_two,
    conv_three,
    conv_four,
    join_weight,
    norm_gain,
    query_weight,
    key_weight,
    value_weight,
    position_bias,
    out_weight,
    ffn_gain,
    gate_weight,
    up_weight,
    down_weight,
    out_grad,
):
    rows, batch, model = byte_states.shape
    length = word_start.shape[0]
    buckets, heads = position_bias.shape
    inner = query_weight.shape[1]
    width = inner // heads
    share = join_weight.shape[0]
    hidden = gate_weight.shape[1]
    count = rows + 16
    states = byte_states.reshape(rows, model)
    grads = out_grad.reshape(rows, model)
    starts = word_start.reshape(length // LANES, LANES)
    span = bucket_ids.shape[0] + 1 - LANES
    made = (
        like((rows, model), F32),
        like((length, model), BF16),
        like((length, inner), BF16),
        like((inner, length), BF16),
        like((heads, length, 2 * width), BF16),
        like((inner, length), BF16),
        like((length, inner), BF16),
        like((heads, span, LANES), F32),
        like((count, LANES), F32),
        like((count, model), F32),
        like((rows, model), BF16),
        like((4 * share, model), BF16),
        like((model, 3 * inner), BF16),
        like((1, span + LANES), jnp.int32),
    )
    (
        residual,
        normed,
        queries,
        queries_t,
        twice_keys,
        keys_t,
        values,
        table,
        divisor,
        pooled,
        mix,
        all_taps,
        all_join,
        joint_weight,
        bucket_row,
        outs,
        totals,
        attended,
        all_out,
        near_gate,
        near_up,
        near_down,
        far_grads,
    ) = pl.pallas_call(
        functools.partial(forward_kernel, width),
        out_shape=(
            *made[:11],
            like((8, model), F32),
            *made[11:],
            like((inner, length), F32),
            like((heads, 1, length), F32),
            like((4, inner, rows), BF16),
            like((4 * inner, model), BF16),
            like(gate_weight.shape, BF16),
            like(up_weight.shape, BF16),
            like(down_weight.shape, BF16),
            like((rows, model), BF16),
        ),
        in_specs=whole(13) + anywhere(4),
        out_specs=anywhere(11) + whole(1) + anywhere(3) + whole(4) + anywhere(4),
        scratch_shapes=[
            *[pltpu.VMEM(part.shape, part.dtype) for part in made],
            pltpu.VMEM((inner, length), BF16),
            pltpu.VMEM((length // LANES, LANES), F32),
            pltpu.VMEM((4, 8, model + LANES), F32),
            pltpu.VMEM((4, 8, share), F32),
            pltpu.VMEM((length, rows), F32),
            pltpu.VMEM((4, inner, rows), BF16),
            pltpu.SemaphoreType.DMA((len(made),)),
            *semaphores(25),
        ],
        compiler_params=params(0),
        name="forward",
    )(
        states,
        starts,
        conv_two,
        conv_three,
        conv_four,
        join_weight,
        norm_gain[None],
        query_weight,
        key_weight,
        value_weight,
        bucket_ids[None],
        position_bias.T,
        out_weight,
        gate_weight,
        up_weight,
        down_weight,
        grads,
    )
    (
        states_part,
        far_made,
        middle_grad,
        ffn_gain_grad,
        weight_grad,
        out_part,
        grad_stage,
    ) = pl.pallas_call(
        ffn_kernel,
        out_shape=(
            like((rows, model), F32),
            like((rows, model), BF16),
            like((rows, model), F32),
            like((8, model), F32),
            like((3 * model, hidden), BF16),
            like((4, model, inner), BF16),
            like((4, inner, rows), BF16),
        ),
        in_specs=whole(12),
        out_specs=whole(7),
        scratch_shapes=[
            pltpu.VMEM((rows, model), F32),
            pltpu.VMEM((2, rows, model), BF16),
            pltpu.VMEM((2, rows, model), F32),
            pltpu.VMEM((2, rows, model), F32),
            pltpu.VMEM((2, 3, model, hidden), F32),
            pltpu.VMEM((rows, model), BF16),
            pltpu.VMEM((rows, model), BF16),
            pltpu.VMEM((3, model, hidden), BF16),
            pltpu.VMEM((3, model, hidden), BF16),
            *semaphores(3),
        ],
        compiler_params=params(2),
        name="ffn",
    )(
        attended,
        all_out,
        residual,
        ffn_gain[None],
        grads,
        far_grads,
        gate_weight,
        near_gate,
        up_weight,
        near_up,
        down_weight,
        near_down,
    )
    replicas = lax.axis_size("dp")
    strides = strides_of(replicas)
    chain_scratch = []
    for height, lanes in ((3 * model, hidden), (model, 4 * inner), (share, model)):
        for _ in range(2):
            chain_scratch += Chain.scratch(height // 2, lanes, len(strides) - 2)
    (
        input_grad,
        out_states,
        weight_total,
        joint_total,
        out_total,
        join_total,
        small,
        bias_total,
    ) = pl.pallas_call(
        functools.partial(back_kernel, width, replicas),
        out_shape=(
            like((rows, model), F32),
            like((rows, model), F32),
            like((3 * model, hidden), F32),
            like((model, 4 * inner), F32),
            like((inner, model), F32),
            like((share, model), F32),
            like((8, model), F32),
            like((buckets, LANES), F32),
        ),
        in_specs=whole(26),
        out_specs=whole(8),
        scratch_shapes=[
            pltpu.VMEM((4, inner, rows), BF16),
            pltpu.VMEM((length, inner), BF16),
            pltpu.VMEM((inner, length), F32),
            pltpu.VMEM((length, inner), F32),
            pltpu.VMEM((length, inner), F32),
            pltpu.VMEM((heads, span, LANES), F32),
            pltpu.VMEM((length, 3 * inner), BF16),
            pltpu.VMEM((4, rows, 3 * inner), BF16),
            pltpu.VMEM((4, model, 3 * inner), BF16),
            pltpu.VMEM((rows, model), BF16),
            pltpu.VMEM((2, model, inner), BF16),
            pltpu.VMEM((model, inner), BF16),
            pltpu.VMEM((model, inner), BF16),
            pltpu.VMEM((model, 4 * inner), BF16),
            pltpu.VMEM((length // LANES, LANES), F32),
            pltpu.VMEM((4, 8, model), F32),
            pltpu.VMEM((4, share, model), BF16),
            pltpu.VMEM((2, share, model), BF16),
            pltpu.VMEM((share, model), BF16),
            pltpu.VMEM((share, model), BF16),
            pltpu.VMEM((share, model), BF16),
            pltpu.VMEM((4, 8, model), F32),
            pltpu.VMEM((len(strides), 8, model), F32),
            pltpu.VMEM((len(strides), 8, model), F32),
            pltpu.VMEM((len(strides), buckets, LANES), F32),
            pltpu.VMEM((len(strides), buckets, LANES), F32),
            *semaphores(22 + 2 * len(strides)),
            *semaphores(6 * Chain.slots(strides)),
            *chain_scratch,
        ],
        compiler_params=params(3),
        name="back",
    )(
        queries_t,
        queries,
        twice_keys,
        keys_t,
        values,
        grad_stage,
        outs,
        totals,
        table,
        normed,
        joint_weight,
        bucket_row,
        residual,
        norm_gain[None],
        middle_grad,
        starts,
        divisor,
        pooled,
        mix,
        all_taps,
        all_join,
        weight_grad,
        out_part,
        far_made,
        states_part,
        ffn_gain_grad,
    )
    own_taps = lax.dynamic_slice_in_dim(small[:4], lax.axis_index("mp") * share, share, 1)
    return (
        out_states[:, None, :],
        input_grad[:, None, :],
        own_taps[:2],
        own_taps[:3],
        own_taps,
        join_total,
        small[4],
        joint_total[:, :inner],
        joint_total[:, inner : 2 * inner],
        joint_total[:, 2 * inner : 3 * inner],
        bias_total[:, :heads],
        out_total,
        small[5],
        weight_total[:model],
        weight_total[model : 2 * model],
        weight_total[2 * model :],
    )


def solution(mesh):
    return jax.shard_map(
        shards,
        mesh=mesh,
        in_specs=(
            P("mp", "dp", None),
            P(None, "dp"),
            P(),
            P(None, "mp"),
            P(None, "mp"),
            P(None, "mp"),
            P("mp", None),
            P(),
            P(None, "mp"),
            P(None, "mp"),
            P(None, "mp"),
            P(None, "mp"),
            P("mp", None),
            P(),
            P(None, "mp"),
            P(None, "mp"),
            P("mp", None),
            P("mp", "dp", None),
        ),
        out_specs=(
            P("mp", "dp", None),
            P("mp", "dp", None),
            P(None, "mp"),
            P(None, "mp"),
            P(None, "mp"),
            P("mp", None),
            P(),
            P(None, "mp"),
            P(None, "mp"),
            P(None, "mp"),
            P(None, "mp"),
            P("mp", None),
            P(),
            P(None, "mp"),
            P(None, "mp"),
            P("mp", None),
        ),
        check_vma=False,
    )
```

```python
import functools

import jax
import jax.numpy as jnp
from jax import lax
from jax.experimental import pallas as pl
from jax.experimental.pallas import tpu as pltpu
from jax.sharding import PartitionSpec as P

EPSILON = 1e-06
LOG2E = 1.4426950408889634
GELU_SCALE = 0.7978845608028654
GELU_CUBE = 0.044715
F32 = jnp.float32
BF16 = jnp.bfloat16
LANES = 128
HALO = 3
VMEM_LIMIT = 56 << 20
MESH = pl.DeviceIdType.MESH


def whole(count):
    return [pl.BlockSpec(memory_space=pltpu.VMEM)] * count


def anywhere(count):
    return [pl.BlockSpec(memory_space=pl.ANY)] * count


def params(collective=None):
    return pltpu.CompilerParams(
        vmem_limit_bytes=VMEM_LIMIT, collective_id=collective, has_side_effects=collective is not None
    )


def like(shape, dtype):
    return jax.ShapeDtypeStruct(shape, dtype)


def dot(lhs, rhs):
    return jnp.dot(lhs, rhs, preferred_element_type=F32)


def dot_nt(lhs, rhs):
    return lax.dot_general(lhs, rhs, (((1,), (1,)), ((), ())), preferred_element_type=F32)


def dot_tn(lhs, rhs):
    return lax.dot_general(lhs, rhs, (((0,), (0,)), ((), ())), preferred_element_type=F32)


def split(values):
    high = values.astype(BF16)
    return high, (values - high.astype(F32)).astype(BF16)


def turned(values):
    return values.astype(F32).T.astype(BF16)


def ranks():
    me = lax.axis_index("mp")
    near = me + 1 - 2 * (me % 2)
    return me, near, (me + 2) % 4, (near + 2) % 4


def greet(peers, strides=()):
    barrier = pltpu.get_barrier_semaphore()
    for peer in peers:
        pl.semaphore_signal(barrier, inc=1, device_id={"mp": peer}, device_id_type=MESH)
    for stride in strides:
        pl.semaphore_signal(barrier, inc=1, device_id={"dp": partner(stride)}, device_id_type=MESH)
    pl.semaphore_wait(barrier, len(peers) + len(strides))


def side_of(stride):
    return (lax.axis_index("dp") // stride) % 2


def partner(stride):
    return lax.axis_index("dp") + stride - 2 * stride * side_of(stride)


def strides_of(count):
    strides = []
    while 2 ** len(strides) < count:
        strides.append(2 ** len(strides))
    return strides


class remote:
    def __init__(self, *given, axis="mp"):
        self.given, self.axis = given, axis

    def start(self):
        described(*self.given, self.axis).start()

    def wait_recv(self):
        described(*self.given, self.axis).wait_recv()

    def wait_send(self):
        described(*self.given, self.axis).wait_send()

    def wait(self):
        described(*self.given, self.axis).wait()


def described(source, target, sems, slot, peer, axis):
    source, target, peer = [part() if callable(part) else part for part in (source, target, peer)]
    sends, receives = sems
    return pltpu.make_async_remote_copy(
        src_ref=source,
        dst_ref=target,
        send_sem=sends.at[slot],
        recv_sem=receives.at[slot],
        device_id={axis: peer},
        device_id_type=MESH,
    )


def semaphores(count):
    return [pltpu.SemaphoreType.DMA((count,)), pltpu.SemaphoreType.DMA((count,))]


class Exchange:
    def __init__(self, source_ref, base, rows, strides, scratch, sems, first_slot):
        self.source, self.base, self.rows, self.strides = source_ref, base, rows, strides
        self.ours, self.theirs = scratch
        self.sems, self.slot, self.at = sems, first_slot, 0
        self.copies = []
        self.steps = len(strides) + 1

    @staticmethod
    def scratch(rows, width, strides):
        return [pltpu.VMEM((strides, rows, width), BF16)] * 2

    def step(self, finish=None):
        at = self.at
        self.at += 1
        if at == 0:
            total = self.source[self.base : self.base + self.rows, :].astype(F32)
        else:
            self.copies[-1].wait_recv()
            total = self.ours[at - 1].astype(F32) + self.theirs[at - 1].astype(F32)
        if at < len(self.strides):
            self.ours[at] = total.astype(BF16)
            stride = self.strides[at]
            copy = remote(
                lambda: self.ours.at[at],
                lambda: self.theirs.at[at],
                self.sems,
                self.slot + at,
                lambda: partner(stride),
                axis="dp",
            )
            copy.start()
            self.copies.append(copy)
        else:
            finish(slice(self.base, self.base + self.rows), total)
            for copy in self.copies:
                copy.wait_send()


class Chain:
    def __init__(self, source_ref, base, rows, strides, scratch, sems, first_slot):
        self.source, self.base, self.rows, self.strides = source_ref, base, rows, strides
        (
            self.half_in,
            self.half,
            self.quarter_in,
            self.quarter,
            self.whole_quarter,
            self.gathered_quarter,
            self.both,
            self.gathered_half,
        ) = scratch
        self.sems, self.slot, self.at = sems, first_slot, 0
        self.copies = []
        self.steps = len(strides) + 3
        self.half_base = 0

    def halved(self, half_ref, base):
        self.half, self.half_base, self.at = half_ref, base, 1
        return self

    @staticmethod
    def scratch(rows, width, exchanges, halved=False):
        half, quarter = (rows // 2, width), (rows // 4, width)
        first = (16, LANES) if halved else half
        return [
            pltpu.VMEM(first, BF16),
            pltpu.VMEM(first, BF16),
            pltpu.VMEM((exchanges + 1, *quarter), BF16),
            pltpu.VMEM((exchanges, *quarter), BF16),
            pltpu.VMEM(quarter, BF16),
            pltpu.VMEM(quarter, BF16),
            pltpu.VMEM(half, BF16),
            pltpu.VMEM(half, BF16),
        ]

    @staticmethod
    def slots(strides):
        return len(strides) + 2

    def send(self, source, target, stride):
        copy = remote(
            source, target, self.sems, self.slot + len(self.copies), lambda: partner(stride), axis="dp"
        )
        copy.start()
        self.copies.append(copy)

    def step(self, finish=None):
        first, second, others = self.strides[0], self.strides[1], self.strides[2:]
        half, quarter = self.rows // 2, self.rows // 4
        at = self.at
        self.at += 1
        if self.copies:
            self.copies[-1].wait_recv()
        if at == 0:
            self.send(lambda: self.source.at[pl.ds(pl.multiple_of(self.base + (1 - side_of(first)) * half, 16), half), :], self.half_in, first)
        elif at == 1:
            if self.copies:
                begin = pl.multiple_of(self.base + side_of(first) * half, 16)
                mine = self.source[pl.ds(begin, half), :].astype(F32)
                self.half[...] = (mine + self.half_in[...].astype(F32)).astype(BF16)
            self.send(lambda: self.half.at[
                    pl.ds(
                        pl.multiple_of(self.half_base + (1 - side_of(second)) * quarter, 16), quarter
                    ),
                    :,
                ], lambda: self.quarter_in.at[0], second)
        elif at <= 1 + len(others):
            if at == 2:
                begin = pl.multiple_of(self.half_base + side_of(second) * quarter, 16)
                mine = self.half[pl.ds(begin, quarter), :]
            else:
                mine = self.quarter[at - 3]
            total = mine.astype(F32) + self.quarter_in[at - 2].astype(F32)
            self.quarter[at - 2] = total.astype(BF16)
            self.send(
                lambda: self.quarter.at[at - 2], lambda: self.quarter_in.at[at - 1], others[at - 2]
            )
        elif at == 2 + len(others):
            total = self.quarter[at - 3].astype(F32) + self.quarter_in[at - 2].astype(F32)
            self.whole_quarter[...] = total.astype(BF16)
            self.send(self.whole_quarter, self.gathered_quarter, second)
        elif at == 3 + len(others):
            side = side_of(second)
            mine = pl.ds(pl.multiple_of(side * quarter, 16), quarter)
            other = pl.ds(pl.multiple_of((1 - side) * quarter, 16), quarter)
            self.both[mine, :] = self.whole_quarter[...]
            self.both[other, :] = self.gathered_quarter[...]
            self.send(self.both, self.gathered_half, first)
        else:
            side = side_of(first)
            mine = pl.ds(pl.multiple_of(self.base + side * half, 16), half)
            other = pl.ds(pl.multiple_of(self.base + (1 - side) * half, 16), half)
            finish(mine, self.both[...].astype(F32))
            finish(other, self.gathered_half[...].astype(F32))
            for copy in self.copies:
                copy.wait_send()


def rms(values, gain):
    return values * lax.rsqrt(jnp.mean(values * values, axis=1, keepdims=True) + EPSILON) * gain


def rms_back(grads, values, gain):
    scale = lax.rsqrt(jnp.mean(values * values, axis=1, keepdims=True) + EPSILON)
    gain_grad = jnp.sum(grads * values * scale, axis=0, keepdims=True)
    raised = grads * gain
    mean = jnp.mean(raised * values, axis=1, keepdims=True)
    return scale * raised - values * (scale * scale * scale * mean), gain_grad


def bucket_hits(bucket_ref, buckets):
    span = bucket_ref.shape[1]
    rows = lax.broadcasted_iota(jnp.int32, (buckets, span), 0)
    return rows == jnp.broadcast_to(bucket_ref[...], (buckets, span))


def fill_bias_table(bucket_ref, bias_ref, table_ref):
    span = bucket_ref.shape[1]
    heads, buckets = bias_ref.shape
    hits = bucket_hits(bucket_ref, buckets).astype(F32).astype(BF16)
    bias = bias_ref[...]
    first = bias.astype(BF16)
    second, third = split(bias - first.astype(F32))
    rows = jnp.concatenate([first, second, third, jnp.zeros((16 - 3 * heads, buckets), BF16)], axis=0)
    lines = dot(rows, hits)
    for head in range(heads):
        line = lines[head : head + 1] + (
            lines[heads + head : heads + head + 1] + lines[2 * heads + head : 2 * heads + head + 1]
        )
        skew = pltpu.roll(
            jnp.broadcast_to(line * LOG2E, (LANES, span)), span - LANES + 1, 1, stride=1, stride_axis=0
        )
        for block in range(span // LANES - 1):
            cut = slice(block * LANES, (block + 1) * LANES)
            table_ref[head, cut, :] = skew[:, cut].T


def bias_grad_rows(table_ref, bucket_ref, buckets):
    span = bucket_ref.shape[1]
    heads = table_ref.shape[0]
    hits = bucket_hits(bucket_ref, buckets).astype(F32).astype(BF16)
    lines = []
    for head in range(heads):
        blocks = [
            table_ref[head, block * LANES : (block + 1) * LANES, :].T
            for block in range(span // LANES - 1)
        ]
        skew = jnp.concatenate(blocks + [jnp.zeros((LANES, LANES), F32)], axis=1)
        rows = LANES // 2
        while rows >= 8:
            skew = skew[:rows] + pltpu.roll(skew[rows:], span - rows, 1)
            rows //= 2
        line = jnp.zeros((1, span), F32)
        for row in range(8):
            line = line + pltpu.roll(skew[row : row + 1], LANES - 1 - row, 1)
        lines.append(line)
    lines = jnp.concatenate(lines + [jnp.zeros((8 - heads, span), F32)], axis=0)
    first = lines.astype(BF16)
    second, third = split(lines - first.astype(F32))
    parts = dot_nt(jnp.concatenate([first.astype(F32), second.astype(F32)], axis=0).astype(BF16), hits)
    rest = dot_nt(jnp.concatenate([third.astype(F32), jnp.zeros((8, span), F32)], axis=0).astype(BF16), hits)
    made = parts[:8] + (parts[8:] + rest[:8])
    return jnp.concatenate([made, jnp.zeros((8, LANES - buckets), F32)], axis=1)


def word_numbers(starts):
    rows = starts.shape[0]
    upper = lax.broadcasted_iota(jnp.int32, (LANES, LANES), 0) <= lax.broadcasted_iota(
        jnp.int32, (LANES, LANES), 1
    )
    within = dot(starts.astype(F32).astype(BF16), upper.astype(F32).astype(BF16))
    totals = jnp.broadcast_to(within[:, LANES - 1 :], (rows, LANES)).astype(BF16)
    lower = lax.broadcasted_iota(jnp.int32, (rows, rows), 1) < lax.broadcasted_iota(
        jnp.int32, (rows, rows), 0
    )
    return within + dot(lower.astype(F32).astype(BF16), totals) - 1.0


class Words:
    def __init__(self, starts_ref, ids_ref, me, ranks_count):
        ids = word_numbers(starts_ref[...])
        ids_ref[...] = ids
        per = ids.shape[0] // ranks_count
        self.firsts = [ids[per * rank : per * rank + 1, 0:1] for rank in range(ranks_count)]
        self.lasts = [
            ids[per * (rank + 1) - 1 : per * (rank + 1), LANES - 1 :] for rank in range(ranks_count)
        ]
        pieces = [ids_ref[pl.ds(me * per + piece, 1), :] for piece in range(per)]
        self.row = jnp.concatenate(pieces, axis=1)
        self.first = self.row[:, 0:1]
        self.last = self.row[:, per * LANES - 1 :]
        self.me = me
        self.count = per * LANES

    def table(self):
        shape = (self.count + 16, self.count)
        rows = lax.broadcasted_iota(jnp.int32, shape, 0).astype(F32)
        return (rows == self.row - self.first + HALO).astype(F32).astype(BF16)

    def pick(self, target):
        slots = lax.broadcasted_iota(jnp.int32, (8, 1), 0)
        hits = target(slots, self.first, self.last) == self.row
        return hits.astype(F32).astype(BF16)

    def place(self, target, valid):
        width = 2 * LANES
        lane = lax.broadcasted_iota(jnp.int32, (1, width), 1) % LANES
        slots, rank = lane % 8, lane // 8
        goal = jnp.full((1, width), -9.0, F32)
        for index, (first, last) in enumerate(zip(self.firsts, self.lasts)):
            goal = jnp.where(rank == index, target(slots, first, last), goal)
        known = valid(slots, rank, self.me) & (rank < len(self.firsts))
        goal = jnp.where(known, goal - self.first + HALO, -1.0)
        rows = lax.broadcasted_iota(jnp.int32, (self.count + 16, width), 0).astype(F32)
        return (rows == goal).astype(F32).astype(BF16)


def stacked(summary_ref):
    parts = [summary_ref[rank] for rank in range(summary_ref.shape[0])]
    rest = LANES - sum(part.shape[0] for part in parts)
    parts.append(jnp.zeros((rest, parts[0].shape[1]), F32))
    return jnp.concatenate(split(jnp.concatenate(parts, axis=0)), axis=0)


def ahead_target(slots, first, last):
    later = jnp.where(slots <= 4, last - (slots - 1).astype(F32), -9.0)
    return jnp.where(slots == 0, first, later)


def ahead_valid(slots, rank, me):
    return ((rank < me) & (slots >= 1) & (slots <= 4)) | ((rank > me) & (slots == 0))


def back_target(slots, first, last):
    return jnp.where(slots <= 3, first + slots.astype(F32), jnp.where(slots == 4, last, -9.0))


def back_valid(slots, rank, me):
    return ((rank > me) & (slots <= 3)) | ((rank < me) & (slots == 4))


def forward_kernel(
    width,
    states_ref,
    starts_ref,
    two_ref,
    three_ref,
    four_ref,
    join_ref,
    gain_ref,
    query_weight_ref,
    key_weight_ref,
    value_weight_ref,
    bucket_ref,
    bias_ref,
    out_weight_ref,
    gate_ref,
    up_ref,
    down_ref,
    grad_ref,
    residual_out,
    normed_out,
    query_out,
    query_t_out,
    twice_out,
    key_t_out,
    value_out,
    table_out,
    divisor_out,
    pooled_out,
    mix_out,
    all_taps_ref,
    all_join_out,
    joint_out,
    padded_out,
    out_ref,
    total_ref,
    attended_ref,
    all_out_ref,
    near_gate_ref,
    near_up_ref,
    near_down_ref,
    far_grad_ref,
    residual_ref,
    normed_ref,
    query_ref,
    query_t_ref,
    twice_ref,
    key_t_ref,
    value_ref,
    table_ref,
    divisor_ref,
    pooled_ref,
    mix_ref,
    all_join_ref,
    joint_ref,
    padded_ref,
    value_t_ref,
    ids_ref,
    summary_ref,
    taps_in_ref,
    score_ref,
    stage_ref,
    ship_ref,
    *sems,
):
    me, near, far, cross = ranks()
    peers = (near, far, cross)
    rows, model = states_ref.shape
    share = join_ref.shape[0]
    inner = query_weight_ref.shape[1]
    heads, length = twice_ref.shape[0], twice_ref.shape[1]
    shipped = []

    def ship(source, target):
        copy = pltpu.make_async_copy(source, target, ship_ref.at[len(shipped)])
        copy.start()
        shipped.append(copy)

    def band(ref, rank):
        return ref.at[pl.ds(pl.multiple_of(rank * share, share), share), :]

    words = Words(starts_ref, ids_ref, me, 4)
    states = states_ref[...]
    wide_states = jnp.concatenate([states, jnp.ones((rows, LANES), BF16)], axis=1)
    summary_ref[me] = dot(words.pick(ahead_target), wide_states)
    two, three, four = two_ref[...], three_ref[...], four_ref[...]
    taps_in_ref[me] = jnp.concatenate(
        [
            two[0:1] + three[0:1] + four[0:1],
            two[1:2] + three[1:2] + four[1:2],
            three[2:3] + four[2:3],
            four[3:4],
            jnp.zeros((4, share), F32),
        ],
        axis=0,
    )
    all_join_ref[pl.ds(pl.multiple_of(me * share, share), share), :] = join_ref[...]
    all_out_ref[pl.ds(pl.multiple_of(me * share, share), share), :] = out_weight_ref[...]
    greet(peers)
    early = []
    for slot, peer in enumerate(peers):
        early.append(remote(summary_ref.at[me], summary_ref.at[me], sems, slot, peer))
        early.append(remote(taps_in_ref.at[me], taps_in_ref.at[me], sems, 3 + slot, peer))
    joins = [
        remote(band(all_join_ref, me), band(all_join_ref, me), sems, 6, far),
        remote(band(all_join_ref, me), band(all_join_ref, me), sems, 7, near),
    ]
    for copy in early + joins:
        copy.start()
    padded_ref[...] = jnp.full(padded_ref.shape, -1, jnp.int32)
    padded_ref[:, : bucket_ref.shape[1]] = bucket_ref[...]
    joint_ref[:, :inner] = query_weight_ref[...]
    joint_ref[:, inner : 2 * inner] = key_weight_ref[...]
    joint_ref[:, 2 * inner :] = value_weight_ref[...]
    ship(joint_ref, joint_out)
    ship(padded_ref, padded_out)
    table = words.table()
    sums = dot(table, wide_states)
    place = words.place(ahead_target, ahead_valid)
    for copy in early:
        copy.wait_recv()
    sums = sums + dot(place, stacked(summary_ref))
    divisor = jnp.maximum(sums[:, model:], 1.0)
    divisor_ref[...] = divisor
    ship(divisor_ref, divisor_out)
    pooled = sums[:, :model] / jnp.concatenate([divisor] * (model // LANES), axis=1)
    pooled_ref[...] = pooled
    ship(pooled_ref, pooled_out)
    taps = jnp.concatenate([taps_in_ref[rank] for rank in range(4)], axis=1)
    all_taps_ref[...] = taps
    joins[0].wait_recv()
    joins.append(remote(band(all_join_ref, far), band(all_join_ref, far), sems, 8, near))
    joins[2].start()
    total = pooled * taps[0:1]
    for lag in range(1, 4):
        total = total + pltpu.roll(pooled, lag, 0) * taps[lag : lag + 1]
    mix = dot_tn(table, total.astype(BF16)).astype(BF16)
    mix_ref[...] = mix
    ship(mix_ref, mix_out)
    joins[1].wait_recv()
    joins[2].wait_recv()
    residual = states.astype(F32) + dot(mix, all_join_ref[...])
    residual_ref[...] = residual
    own = pl.ds(pl.multiple_of(me * rows, rows), rows)
    normed_ref[own, :] = rms(residual, gain_ref[...]).astype(BF16)

    def block(rank, part):
        half = rows // 2
        return normed_ref.at[pl.ds(pl.multiple_of(rank * rows + part * half, half), half), :]

    sends = []
    for part in range(2):
        sends.append(remote(block(me, part), block(me, part), sems, 9 + part, far))
    for part in range(2):
        sends.append(remote(block(me, part), block(me, part), sems, 11 + part, near))
    for copy in sends:
        copy.start()
    copies = [
        remote(grad_ref, far_grad_ref, sems, 15, far),
        remote(band(all_out_ref, me), band(all_out_ref, me), sems, 16, near),
        remote(gate_ref, near_gate_ref, sems, 17, near),
        remote(up_ref, near_up_ref, sems, 18, near),
        remote(down_ref, near_down_ref, sems, 19, near),
    ]
    out_far = remote(
        lambda: band(all_out_ref, me), lambda: band(all_out_ref, me), sems, 20, far
    )
    out_pass = remote(
        lambda: band(all_out_ref, far), lambda: band(all_out_ref, far), sems, 21, near
    )
    out_far.start()
    for copy in copies:
        copy.start()
    ship(residual_ref, residual_out)
    ship(all_join_ref, all_join_out)

    def project(rank):
        cut = pl.ds(pl.multiple_of(rank * rows, rows), rows)
        made = dot(normed_ref[cut, :], joint_ref[...])
        query, key, value = [
            made[:, index * inner : (index + 1) * inner].astype(BF16) for index in range(3)
        ]
        query_ref[cut, :] = query
        query_t_ref[:, cut] = turned(query)
        key_t_ref[:, cut] = turned(key)
        value_ref[cut, :] = value
        value_t_ref[:, cut] = turned(value)
        for head in range(heads):
            part = key[:, head * width : (head + 1) * width]
            twice_ref[head, cut, :] = jnp.concatenate([part, part], axis=1)

    project(me)
    fill_bias_table(padded_ref, bias_ref, table_ref)
    ship(table_ref, table_out)
    sends[2].wait_recv()
    sends[3].wait_recv()
    project(near)
    passed = []
    for part in range(2):
        sends[part].wait_recv()
        passed.append(remote(block(far, part), block(far, part), sems, 13 + part, near))
        passed[part].start()
    project(far)
    for copy in passed:
        copy.wait_recv()
    project(cross)
    for source, target in (
        (normed_ref, normed_out),
        (query_ref, query_out),
        (query_t_ref, query_t_out),
        (twice_ref, twice_out),
        (key_t_ref, key_t_out),
        (value_ref, value_out),
    ):
        ship(source, target)
    wide = deep = length // 4

    def owner(order):
        chip = (me // 2 + 1 + order // 2) % 2
        core = (me % 2 + (order + 1) // 2) % 2
        return 2 * chip + core

    def handed(order):
        return remote(stage_ref.at[order], attended_ref.at[me], sems, 22 + order, owner(order))

    def step(index, carry):
        order, head = index // heads, index % heads
        begin = pl.multiple_of(owner(order) * wide, wide)
        span = pl.ds(begin, wide)
        rows = pl.ds(pl.multiple_of(head * width, width), width)
        scaled = query_t_ref[rows, span].astype(F32) * LOG2E
        queries = jnp.concatenate(split(scaled), axis=0)
        peak = jnp.full((8, wide), -1e30, F32)
        for part in range(length // deep):
            cut = slice(part * deep, (part + 1) * deep)
            raw = dot(twice_ref[head, cut, :], queries)
            columns = []
            for lane in range(0, wide, LANES):
                offset = pl.multiple_of(part * deep - begin - lane + length - LANES, LANES)
                columns.append(raw[:, lane : lane + LANES] + table_ref[head, pl.ds(offset, deep), :])
            scores = jnp.concatenate(columns, axis=1)
            score_ref[cut, :] = scores
            peak = jnp.maximum(peak, jnp.max(scores.reshape(deep // 8, 8, wide), axis=0))
        peak = jnp.max(peak, axis=0, keepdims=True)
        sums = jnp.zeros((8, wide), F32)
        made = jnp.zeros((width, wide), F32)
        for part in range(length // deep):
            cut = slice(part * deep, (part + 1) * deep)
            raised = jnp.exp2(score_ref[cut, :] - peak)
            sums = sums + jnp.sum(raised.reshape(deep // 8, 8, wide), axis=0)
            made = made + dot(value_t_ref[rows, cut], raised.astype(BF16))
        total = jnp.sum(sums, axis=0, keepdims=True)
        made = made / total
        out_ref[rows, span] = made
        total_ref[head, :, span] = peak + jnp.log2(total)
        stage_ref[order, rows, :] = made.astype(BF16)

        @pl.when((head == heads - 1) & (order < 3))
        def _():
            handed(order).start()

        @pl.when(index == heads)
        def _():
            out_far.wait_recv()
            out_pass.start()

        return carry

    lax.fori_loop(0, heads * 4, step, 0)
    attended_ref[me] = stage_ref[3]
    for order in range(3):
        handed(order).wait()
    for copy in copies:
        copy.wait()
    out_pass.wait()
    for copy in early + joins + sends + passed + [out_far]:
        copy.wait_send()
    for copy in shipped:
        copy.wait()


def ffn_kernel(
    count,
    attended_ref,
    all_out_ref,
    residual_ref,
    gain_ref,
    grad_ref,
    far_grad_ref,
    gate_ref,
    near_gate_ref,
    up_ref,
    near_up_ref,
    down_ref,
    near_down_ref,
    states_part_ref,
    far_made_ref,
    middle_grad_ref,
    gain_grad_ref,
    weight_half_ref,
    out_part_ref,
    grad_stage_ref,
    middle_ref,
    normed_ref,
    made_ref,
    back_ref,
    sums_ref,
    far_out_ref,
    far_in_ref,
    near_out_ref,
    near_in_ref,
    weight_ref,
    half_in_ref,
    sends_ref,
    receives_ref,
    half_sends_ref,
    half_receives_ref,
):
    me, near, far, cross = ranks()
    sems = (sends_ref, receives_ref)
    strides = strides_of(count)[:2]
    peers = (near, far, cross)
    rows, model = residual_ref.shape
    share = attended_ref.shape[1]
    attended = attended_ref[...].reshape(4 * share, rows)
    middle = residual_ref[...] + dot_tn(attended, all_out_ref[...])
    middle_ref[...] = middle
    normed_ref[0] = rms(middle, gain_ref[...]).astype(BF16)
    half = rows // 2
    greet(peers, strides)
    there, returned = [], []
    for part in range(2):
        cut = pl.ds(part * half, half)
        there.append(remote(normed_ref.at[0, cut], normed_ref.at[1, cut], sems, part, far))
        there[part].start()
        returned.append(remote(far_out_ref.at[cut], far_in_ref.at[cut], sems, 2 + part, far))

    def work(side, cut, grads, gate, up, down, slab, first):
        given = normed_ref[side, cut]
        gate_value = dot(given, gate)
        up_value = dot(given, up)
        hidden_grad = dot_nt(grads, down)
        square = gate_value * gate_value
        curve = jnp.tanh(GELU_SCALE * gate_value * (1.0 + GELU_CUBE * square))
        half = 0.5 + 0.5 * curve
        gelu = gate_value * half
        slope = half + (0.5 * GELU_SCALE) * gate_value * (1.0 - curve * curve) * (
            1.0 + (3.0 * GELU_CUBE) * square
        )
        hidden = (gelu * up_value).astype(BF16)
        gate_back = (hidden_grad * up_value * slope).astype(BF16)
        up_back = (hidden_grad * gelu).astype(BF16)
        sums = [dot_tn(given, gate_back), dot_tn(given, up_back), dot_tn(hidden, grads)]
        for index in range(3):
            if side == 0:
                sums_ref[slab, index] = sums[index]
            else:
                sums_ref[slab, index] += sums[index]
        made = dot(hidden, down)
        back = dot_nt(gate_back, gate) + dot_nt(up_back, up)
        if first:
            made_ref[side, cut] = made
            back_ref[side, cut] = back
        else:
            made_ref[side, cut] += made
            back_ref[side, cut] += back

    slabs = ((1, (near_gate_ref, near_up_ref, near_down_ref)), (0, (gate_ref, up_ref, down_ref)))
    for slab, weights in slabs:
        work(0, slice(0, rows), grad_ref[...], *[ref[...] for ref in weights], slab, slab == 1)
    for part in range(2):
        cut = slice(part * half, (part + 1) * half)
        there[part].wait_recv()
        for slab, weights in slabs:
            work(1, cut, far_grad_ref[cut, :], *[ref[...] for ref in weights], slab, slab == 1)
            if part == 1 and slab == 1:
                near_out_ref[...] = sums_ref[1].astype(BF16)
                swap = remote(near_out_ref, near_in_ref, sems, 4, near)
                swap.start()
        far_out_ref[cut, :] = back_ref[1, cut].astype(BF16)
        returned[part].start()
    far_made_ref[...] = made_ref[1].astype(BF16)
    states_part_ref[...] = middle_ref[...] + made_ref[0]
    swap.wait_recv()
    depth = weight_ref.shape[0] // 3
    for index in range(3):
        total = sums_ref[0, index] + near_in_ref[index].astype(F32)
        weight_ref[index * depth : (index + 1) * depth, :] = total.astype(BF16)
    size = weight_ref.shape[0] // 4
    halves = []
    for index, stride in enumerate(strides):
        begin = pl.multiple_of(2 * size * index + (1 - side_of(stride)) * size, 16)
        halves.append(
            remote(
                weight_ref.at[pl.ds(begin, size), :],
                half_in_ref.at[index],
                (half_sends_ref, half_receives_ref),
                index,
                partner(stride),
                axis="dp",
            )
        )
        halves[-1].start()
    for copy in returned:
        copy.wait_recv()
    normed_grad = back_ref[0] + far_in_ref[...].astype(F32)
    part, gain_grad = rms_back(normed_grad, middle_ref[...], gain_ref[...])
    gain_grad_ref[...] = jnp.broadcast_to(gain_grad, gain_grad_ref.shape)
    middle_grad = grad_ref[...].astype(F32) + part
    middle_grad_ref[...] = middle_grad
    low = middle_grad.astype(BF16)
    grad_stage_ref[...] = dot_nt(all_out_ref[...], low).astype(BF16).reshape(4, share, rows)
    out_part = dot(attended, low)
    for rank in range(4):
        out_part_ref[rank] = out_part[rank * share : (rank + 1) * share, :].T.astype(BF16)
    for index, stride in enumerate(strides):
        halves[index].wait_recv()
        begin = pl.multiple_of(2 * size * index + side_of(stride) * size, 16)
        total = weight_ref[pl.ds(begin, size), :].astype(F32) + half_in_ref[index].astype(F32)
        weight_half_ref[index * size : (index + 1) * size, :] = total.astype(BF16)
    for copy in halves:
        copy.wait_send()
    for copy in returned + there + [swap]:
        copy.wait_send()


def back_kernel(
    width,
    count,
    buckets,
    query_t_ref,
    query_ref,
    twice_ref,
    key_t_ref,
    value_ref,
    grad_stage_ref,
    out_ref,
    total_ref,
    table_ref,
    joint_ref,
    bucket_ref,
    gain_ref,
    starts_ref,
    all_taps_ref,
    weight_half_ref,
    out_part_ref,
    far_made_ref,
    ffn_gain_grad_ref,
    normed_hbm,
    residual_hbm,
    middle_grad_hbm,
    divisor_hbm,
    pooled_hbm,
    mix_hbm,
    all_join_hbm,
    states_part_hbm,
    input_grad_out,
    states_out_out,
    weight_total_out,
    joint_total_out,
    out_total_ref,
    join_total_ref,
    taps_total_ref,
    gains_total_ref,
    bias_total_ref,
    normed_ref,
    residual_ref,
    middle_grad_ref,
    divisor_ref,
    pooled_ref,
    mix_ref,
    all_join_ref,
    states_part_ref,
    load_ref,
    grad_t_ref,
    grad_ref,
    query_grad_ref,
    key_grad_ref,
    value_grad_ref,
    table_grad_ref,
    joint_grad_ref,
    core_out_ref,
    core_in_ref,
    chip_out_ref,
    chip_in_ref,
    made_in_ref,
    out_near_ref,
    out_sum_ref,
    out_far_ref,
    late_ref,
    ids_ref,
    summary_ref,
    join_part_ref,
    join_near_ref,
    join_sum_ref,
    join_far_ref,
    join_ref,
    small_near_ref,
    small_ref,
    small_in_ref,
    bias_ref,
    bias_in_ref,
    input_grad_ref,
    states_out_ref,
    weight_total_ref,
    joint_total_ref,
    ship_ref,
    sends_ref,
    receives_ref,
    chain_sends_ref,
    chain_receives_ref,
    *chain_refs,
):
    me, near, far, cross = ranks()
    peers = (near, far, cross)
    sems = (sends_ref, receives_ref)
    chain_sems = (chain_sends_ref, chain_receives_ref)
    heads, length = twice_ref.shape[0], twice_ref.shape[1]
    rows, model = residual_ref.shape
    share = join_part_ref.shape[1]
    inner = heads * width
    wide, deep = length // 4, length // 8
    strides = strides_of(count)
    turned_strides = [strides[1], strides[0]] + strides[2:]
    chains = []
    plan = [
        (None, 2 * weight_half_ref.shape[0], strides),
        (None, 2 * weight_half_ref.shape[0], turned_strides),
        (late_ref, late_ref.shape[0], strides),
        (late_ref, late_ref.shape[0], turned_strides),
    ]
    for index, (ref, height, order) in enumerate(plan):
        half = height // 2
        chains.append(
            Chain(
                ref,
                (index % 2) * half,
                half,
                order,
                chain_refs[8 * index : 8 * index + 8],
                chain_sems,
                index * Chain.slots(strides),
            )
        )
    weight_chains, late_chains, join_chains = chains[0:2], chains[2:4], []
    for index, chain in enumerate(weight_chains):
        chain.halved(weight_half_ref, index * (weight_half_ref.shape[0] // 2))
    for index, order in enumerate((strides, turned_strides)):
        join_chains.append(
            Exchange(
                join_ref,
                index * (join_ref.shape[0] // 2),
                join_ref.shape[0] // 2,
                order,
                chain_refs[32 + 2 * index : 34 + 2 * index],
                chain_sems,
                4 * Chain.slots(strides) + index * len(strides),
            )
        )
    loads = []
    for source, target in (
        (normed_hbm, normed_ref),
        (residual_hbm, residual_ref),
        (middle_grad_hbm, middle_grad_ref),
        (divisor_hbm, divisor_ref),
        (pooled_hbm, pooled_ref),
        (mix_hbm, mix_ref),
        (all_join_hbm, all_join_ref),
        (states_part_hbm, states_part_ref),
    ):
        loads.append(pltpu.make_async_copy(source, target, load_ref.at[len(loads)]))
        loads[-1].start()
    greet(peers, strides)
    gradient_copies = []
    for slot, peer in enumerate(peers):
        copy = remote(
            lambda peer=peer: grad_stage_ref.at[peer], lambda: grad_t_ref.at[me], sems, slot, peer
        )
        copy.start()
        gradient_copies.append(copy)
    out_copies = [
        remote(lambda: out_part_ref.at[near], lambda: out_near_ref.at[0], sems, 3, near),
        remote(lambda: out_part_ref.at[cross], lambda: out_near_ref.at[1], sems, 4, near),
    ]
    for copy in out_copies:
        copy.start()
    out_copy = remote(out_sum_ref, out_far_ref, sems, 5, far)
    made_copy = remote(far_made_ref, made_in_ref, sems, 6, far)
    core_copies = [
        remote(lambda: core_out_ref.at[0], lambda: core_in_ref.at[0], sems, 7, near),
        remote(lambda: core_out_ref.at[1], lambda: core_in_ref.at[1], sems, 8, near),
    ]
    chip_copy = remote(chip_out_ref, chip_in_ref, sems, 9, far)
    for chain in weight_chains:
        chain.step()
    made_copy.start()
    grad_t_ref[me] = grad_stage_ref[me]
    query_grad_ref[...] = jnp.zeros_like(query_grad_ref)
    key_grad_ref[...] = jnp.zeros_like(key_grad_ref)
    value_grad_ref[...] = jnp.zeros_like(value_grad_ref)
    table_grad_ref[...] = jnp.zeros_like(table_grad_ref)

    def gather_rows(rank):
        cut = pl.ds(pl.multiple_of(rank * wide, wide), wide)
        joint_grad_ref[cut, :inner] = query_grad_ref[:, cut].T.astype(BF16)
        joint_grad_ref[cut, inner : 2 * inner] = key_grad_ref[cut, :].astype(BF16)
        joint_grad_ref[cut, 2 * inner :] = value_grad_ref[cut, :].astype(BF16)
        return dot_nt(joint_grad_ref[cut, :], joint_ref[...])

    def block_of(relation):
        return 2 * ((me // 2 + relation // 2) % 2) + (me % 2 + relation % 2) % 2

    def step(index, carry):
        phase = index // 4
        middle = ((phase + 1) // 2) % 2
        block = block_of(middle * (1 + phase) + (1 - middle) * ((index % 4) // 2))
        other = block_of(middle * (index % 4) + (1 - middle) * (index % 2 + 2 * (1 - phase // 3)))
        begin = pl.multiple_of(block * wide, wide)
        start = pl.multiple_of(other * wide, wide)
        span = pl.ds(begin, wide)
        for slot, at in enumerate((2, 4, 8)):

            @pl.when(index == at)
            def _(slot=slot):
                gradient_copies[slot].wait_recv()

        @pl.when((index == 0) | (index == 2) | (index == 4) | (index == 8))
        def _():
            grad_ref[span, :] = turned(grad_t_ref[block])

        @pl.when(index == 3)
        def _():
            for copy in out_copies:
                copy.wait_recv()
            ours = out_part_ref[far].astype(F32) + out_near_ref[1].astype(F32)
            out_sum_ref[...] = ours.astype(BF16)
            out_copy.start()

        @pl.when(index == 4)
        def _():
            weight_chains[0].step()
            weight_chains[1].step()

        @pl.when(index == 14)
        def _():
            weight_chains[0].step()
            weight_chains[1].step()

        @pl.when(index == 12)
        def _():
            core_out_ref[0] = gather_rows(cross).astype(BF16)
            core_copies[0].start()
            chip_out_ref[...] = gather_rows(far).astype(BF16)

        @pl.when(index == 13)
        def _():
            core_copies[0].wait_recv()
            total = chip_out_ref[...].astype(F32) + core_in_ref[0].astype(F32)
            chip_out_ref[...] = total.astype(BF16)
            chip_copy.start()

        for head in range(heads):
            rows = slice(head * width, (head + 1) * width)
            scaled = query_t_ref[rows, span].astype(F32) * LOG2E
            queries = jnp.concatenate(split(scaled), axis=0)
            total = total_ref[head, :, span]
            grads = grad_t_ref[block, rows, :].astype(F32)
            dots = jnp.sum(grads * out_ref[rows, span], axis=0, keepdims=True)
            own_rows = lax.broadcasted_iota(jnp.int32, (inner, wide), 0) // width == head
            own_lanes = lax.broadcasted_iota(jnp.int32, (wide, inner), 1) // width == head
            grad_t_own = jnp.where(own_rows, grad_t_ref[block].astype(F32), 0.0).astype(BF16)
            query_own = jnp.where(own_lanes, query_ref[span, :].astype(F32), 0.0).astype(BF16)
            grad_own = jnp.where(own_lanes, grad_ref[span, :].astype(F32), 0.0).astype(BF16)
            query_grad = jnp.zeros((width, wide), F32)
            for part in range(wide // deep):
                cut = pl.ds(pl.multiple_of(start + part * deep, deep), deep)
                raw = dot(twice_ref[head, cut, :], queries)
                raw_grad = dot(value_ref[cut, :], grad_t_own)
                probs, score_grads = [], []
                for lane in range(0, wide, LANES):
                    piece = slice(lane, lane + LANES)
                    offset = start + part * deep - begin - lane + length - LANES
                    offset = pl.multiple_of(offset, LANES)
                    shift = table_ref[head, pl.ds(offset, deep), :]
                    prob = jnp.exp2(raw[:, piece] + shift - total[:, piece])
                    low = (prob * (raw_grad[:, piece] - dots[:, piece])).astype(BF16)
                    table_grad_ref[head, pl.ds(offset, deep), :] += low.astype(F32)
                    probs.append(prob.astype(BF16))
                    score_grads.append(low)
                probs = jnp.concatenate(probs, axis=1)
                score_grads = jnp.concatenate(score_grads, axis=1)
                value_grad_ref[cut, :] += dot(probs, grad_own)
                key_grad_ref[cut, :] += dot(score_grads, query_own)
                query_grad = query_grad + dot(key_t_ref[rows, cut], score_grads)
            query_grad_ref[rows, span] += query_grad
        return carry

    lax.fori_loop(0, 16, step, 0)
    core_out_ref[1] = gather_rows(near).astype(BF16)
    core_copies[1].start()
    normed_grad = gather_rows(me)
    for copy in loads:
        copy.wait()
    late_ref[:, : 3 * inner] = dot_tn(normed_ref[...], joint_grad_ref[...]).astype(BF16)
    out_copy.wait_recv()
    out_sum = (
        out_part_ref[me].astype(F32) + out_near_ref[0].astype(F32) + out_far_ref[...].astype(F32)
    )
    late_ref[:, 3 * inner :] = out_sum.astype(BF16)
    for chain in late_chains:
        chain.step()
    words = Words(starts_ref, ids_ref, me, 4)
    table = words.table()
    picked = words.pick(back_target)
    place = words.place(back_target, back_valid)
    core_copies[1].wait_recv()
    normed_grad = normed_grad + core_in_ref[1].astype(F32)
    chip_copy.wait_recv()
    normed_grad = normed_grad + chip_in_ref[...].astype(F32)
    part, gain_grad = rms_back(normed_grad, residual_ref[...], gain_ref[...])
    residual_grad = middle_grad_ref[...] + part
    low = residual_grad.astype(BF16)
    join_part_ref[...] = dot_tn(mix_ref[...], low).astype(BF16).reshape(4, share, model)
    join_copies = [
        remote(join_part_ref.at[near], join_near_ref.at[0], sems, 16, near),
        remote(join_part_ref.at[cross], join_near_ref.at[1], sems, 17, near),
    ]
    for copy in join_copies:
        copy.start()
    high_mix, low_mix = split(dot_nt(low, all_join_ref[...]))
    summary_ref[me] = dot(picked, high_mix) + dot(picked, low_mix)
    copies = []
    for slot, peer in enumerate(peers):
        copies.append(remote(summary_ref.at[me], summary_ref.at[me], sems, 13 + slot, peer))
        copies[-1].start()
    for chain in weight_chains:
        chain.step()
    for copy in join_copies:
        copy.wait_recv()
    join_sum_ref[...] = (
        join_part_ref[far].astype(F32) + join_near_ref[1].astype(F32)
    ).astype(BF16)
    join_copy = remote(join_sum_ref, join_far_ref, sems, 21, far)
    join_copy.start()
    word_grad = dot(table, high_mix) + dot(table, low_mix)
    pooled = pooled_ref[...]
    tap_rows = [jnp.sum(pooled * word_grad, axis=0, keepdims=True)]
    for lag in range(1, 4):
        tap_rows.append(jnp.sum(pltpu.roll(pooled, lag, 0) * word_grad, axis=0, keepdims=True))
    tap_rows += [gain_grad, ffn_gain_grad_ref[0:1], jnp.zeros((2, model), F32)]
    small_near_ref[me] = jnp.concatenate(tap_rows, axis=0)
    for slot, peer in enumerate(peers):
        copies.append(remote(small_near_ref.at[me], small_near_ref.at[me], sems, 18 + slot, peer))
        copies[-1].start()
    for chain in late_chains:
        chain.step()
    bias_ref[0] = bias_grad_rows(table_grad_ref, bucket_ref, buckets)
    join_copy.wait_recv()
    join_ref[...] = (
        join_part_ref[me].astype(F32) + join_near_ref[0].astype(F32) + join_far_ref[...].astype(F32)
    ).astype(BF16)
    for chain in join_chains:
        chain.step()
    for copy in copies:
        copy.wait_recv()
    small = small_near_ref[0]
    for rank in range(1, 4):
        small = small + small_near_ref[rank]
    small_ref[0] = small
    small_copies = []

    def exchange(index):
        stride = strides[index]
        small_copies.append(
            remote(
                small_ref.at[index],
                small_in_ref.at[index],
                sems,
                22 + 2 * index,
                lambda: partner(stride),
                axis="dp",
            )
        )
        small_copies.append(
            remote(
                bias_ref.at[index],
                bias_in_ref.at[index],
                sems,
                23 + 2 * index,
                lambda: partner(stride),
                axis="dp",
            )
        )
        small_copies[-2].start()
        small_copies[-1].start()

    exchange(0)
    for chain in late_chains:
        chain.step()
    word_grad = word_grad + dot(place, stacked(summary_ref))
    taps = all_taps_ref[...]
    height = word_grad.shape[0]
    pooled_grad = word_grad * taps[0:1]
    for lag in range(1, 4):
        pooled_grad = pooled_grad + pltpu.roll(word_grad, height - lag, 0) * taps[lag : lag + 1]
    divisor = divisor_ref[...]
    pooled_grad = pooled_grad / jnp.concatenate([divisor] * (model // LANES), axis=1)
    high, low = split(pooled_grad)
    input_grad = residual_grad + (dot_tn(table, high) + dot_tn(table, low))
    for chain in join_chains:
        chain.step()
    input_grad_ref[...] = input_grad[:, None, :]
    shipped = [pltpu.make_async_copy(input_grad_ref, input_grad_out, ship_ref.at[0])]
    shipped[0].start()
    made_copy.wait_recv()
    states_out_ref[...] = (states_part_ref[...] + made_in_ref[...].astype(F32))[:, None, :]
    shipped.append(pltpu.make_async_copy(states_out_ref, states_out_out, ship_ref.at[1]))
    shipped[1].start()

    def write_weights(span, values):
        weight_total_ref[span, :] = values

    def write_late(span, values):
        joint_total_ref[span, :] = values

    def write_join(span, values):
        join_total_ref[span, :] = values

    for turn in range(weight_chains[0].steps):
        for group, finish in (
            (join_chains, write_join),
            (weight_chains, write_weights),
            (late_chains, write_late),
        ):
            for chain in group:
                if chain.at < chain.steps:
                    chain.step(finish)
                    if chain is weight_chains[1] and chain.at == chain.steps:
                        shipped.append(
                            pltpu.make_async_copy(weight_total_ref, weight_total_out, ship_ref.at[2])
                        )
                        shipped[-1].start()
        if turn < len(strides):
            small_copies[2 * turn].wait_recv()
            small_copies[2 * turn + 1].wait_recv()
            small = small_ref[turn] + small_in_ref[turn]
            bias = bias_ref[turn] + bias_in_ref[turn]
            if turn + 1 < len(strides):
                small_ref[turn + 1] = small
                bias_ref[turn + 1] = bias
                exchange(turn + 1)
            else:
                own = jnp.zeros((8, share), F32)
                for rank in range(4):
                    own = jnp.where(me == rank, small[:, rank * share : (rank + 1) * share], own)
                taps_total_ref[...] = own
                gains_total_ref[...] = small
                bias_total_ref[...] = bias
    shipped.append(pltpu.make_async_copy(joint_total_ref, joint_total_out, ship_ref.at[3]))
    shipped[-1].start()
    out_total_ref[...] = joint_total_ref[:, 3 * inner :].T
    for copy in shipped:
        copy.wait()
    finished = gradient_copies + out_copies + core_copies + [chip_copy, made_copy, out_copy]
    for copy in finished + copies + join_copies + [join_copy] + small_copies:
        copy.wait_send()


def place_kernel(
    joint_hbm,
    weight_hbm,
    states_hbm,
    input_hbm,
    out_hbm,
    join_hbm,
    taps_ref,
    gains_ref,
    bias_ref,
    states_out,
    input_out,
    two_out,
    three_out,
    four_out,
    join_out,
    norm_out,
    query_out,
    key_out,
    value_out,
    bias_out,
    out_out,
    ffn_out,
    gate_out,
    up_out,
    down_out,
    joint_ref,
    weight_ref,
    states_ref,
    input_ref,
    out_ref,
    join_ref,
    sems,
):
    loads = []
    for source, target in (
        (weight_hbm, weight_ref),
        (states_hbm, states_ref),
        (input_hbm, input_ref),
        (joint_hbm, joint_ref),
        (out_hbm, out_ref),
        (join_hbm, join_ref),
    ):
        loads.append(pltpu.make_async_copy(source, target, sems.at[10 + len(loads)]))
        loads[-1].start()
    inner, model = query_out.shape[1], gate_out.shape[0]
    pairs = [
        (weight_ref.at[pl.ds(index * model, model), :], target, 0)
        for index, target in enumerate((gate_out, up_out, down_out))
    ]
    pairs += [(states_ref, states_out, 1), (input_ref, input_out, 2)]
    pairs += [
        (joint_ref.at[:, pl.ds(index * inner, inner)], target, 3)
        for index, target in enumerate((query_out, key_out, value_out))
    ]
    pairs += [(out_ref, out_out, 4), (join_ref, join_out, 5)]
    copies, arrived = [], -1
    for index, (source, target, load) in enumerate(pairs):
        if load > arrived:
            loads[load].wait()
            arrived = load
        copies.append(pltpu.make_async_copy(source, target, sems.at[index]))
        copies[-1].start()
    two_out[...] = taps_ref[:2]
    three_out[...] = taps_ref[:3]
    four_out[...] = taps_ref[:4]
    norm_out[...] = gains_ref[4:5]
    ffn_out[...] = gains_ref[5:6]
    heads, buckets = bias_out.shape
    bias_out[...] = bias_ref[:heads, :buckets]
    for copy in copies:
        copy.wait()


def shards(
    byte_states,
    word_start,
    bucket_ids,
    conv_two,
    conv_three,
    conv_four,
    join_weight,
    norm_gain,
    query_weight,
    key_weight,
    value_weight,
    position_bias,
    out_weight,
    ffn_gain,
    gate_weight,
    up_weight,
    down_weight,
    out_grad,
):
    rows, batch, model = byte_states.shape
    length = word_start.shape[0]
    buckets, heads = position_bias.shape
    inner = query_weight.shape[1]
    width = inner // heads
    share = join_weight.shape[0]
    hidden = gate_weight.shape[1]
    count = rows + 16
    replicas = lax.axis_size("dp")
    strides = strides_of(replicas)
    states = byte_states.reshape(rows, model)
    grads = out_grad.reshape(rows, model)
    starts = word_start.reshape(length // LANES, LANES)
    span = bucket_ids.shape[0] + 1 - LANES
    made = (
        like((rows, model), F32),
        like((length, model), BF16),
        like((length, inner), BF16),
        like((inner, length), BF16),
        like((heads, length, 2 * width), BF16),
        like((inner, length), BF16),
        like((length, inner), BF16),
        like((heads, span, LANES), F32),
        like((count, LANES), F32),
        like((count, model), F32),
        like((rows, model), BF16),
        like((4 * share, model), BF16),
        like((model, 3 * inner), BF16),
        like((1, span + LANES), jnp.int32),
    )
    (
        residual,
        normed,
        queries,
        queries_t,
        twice_keys,
        keys_t,
        values,
        table,
        divisor,
        pooled,
        mix,
        all_taps,
        all_join,
        joint_weight,
        bucket_row,
        outs,
        totals,
        attended,
        all_out,
        near_gate,
        near_up,
        near_down,
        far_grads,
    ) = pl.pallas_call(
        functools.partial(forward_kernel, width),
        out_shape=(
            *made[:11],
            like((8, model), F32),
            *made[11:],
            like((inner, length), F32),
            like((heads, 1, length), F32),
            like((4, inner, rows), BF16),
            like((4 * inner, model), BF16),
            like(gate_weight.shape, BF16),
            like(up_weight.shape, BF16),
            like(down_weight.shape, BF16),
            like((rows, model), BF16),
        ),
        in_specs=whole(13) + anywhere(4),
        out_specs=anywhere(11) + whole(1) + anywhere(3) + whole(4) + anywhere(4),
        scratch_shapes=[
            *[pltpu.VMEM(part.shape, part.dtype) for part in made],
            pltpu.VMEM((inner, length), BF16),
            pltpu.VMEM((length // LANES, LANES), F32),
            pltpu.VMEM((4, 8, model + LANES), F32),
            pltpu.VMEM((4, 8, share), F32),
            pltpu.VMEM((length, rows), F32),
            pltpu.VMEM((4, inner, rows), BF16),
            pltpu.SemaphoreType.DMA((len(made),)),
            *semaphores(25),
        ],
        compiler_params=params(0),
        name="forward",
    )(
        states,
        starts,
        conv_two,
        conv_three,
        conv_four,
        join_weight,
        norm_gain[None],
        query_weight,
        key_weight,
        value_weight,
        bucket_ids[None],
        position_bias.T,
        out_weight,
        gate_weight,
        up_weight,
        down_weight,
        grads,
    )
    (
        states_part,
        far_made,
        middle_grad,
        ffn_gain_grad,
        weight_grad,
        out_part,
        grad_stage,
    ) = pl.pallas_call(
        functools.partial(ffn_kernel, replicas),
        out_shape=(
            like((rows, model), F32),
            like((rows, model), BF16),
            like((rows, model), F32),
            like((8, model), F32),
            like((3 * model // 2, hidden), BF16),
            like((4, model, inner), BF16),
            like((4, inner, rows), BF16),
        ),
        in_specs=whole(12),
        out_specs=whole(7),
        scratch_shapes=[
            pltpu.VMEM((rows, model), F32),
            pltpu.VMEM((2, rows, model), BF16),
            pltpu.VMEM((2, rows, model), F32),
            pltpu.VMEM((2, rows, model), F32),
            pltpu.VMEM((2, 3, model, hidden), F32),
            pltpu.VMEM((rows, model), BF16),
            pltpu.VMEM((rows, model), BF16),
            pltpu.VMEM((3, model, hidden), BF16),
            pltpu.VMEM((3, model, hidden), BF16),
            pltpu.VMEM((3 * model, hidden), BF16),
            pltpu.VMEM((2, 3 * model // 4, hidden), BF16),
            *semaphores(5),
            *semaphores(2),
        ],
        compiler_params=params(2),
        name="ffn",
    )(
        attended,
        all_out,
        residual,
        ffn_gain[None],
        grads,
        far_grads,
        gate_weight,
        near_gate,
        up_weight,
        near_up,
        down_weight,
        near_down,
    )
    chain_scratch = []
    for height, lanes in ((3 * model, hidden), (model, 4 * inner)):
        for _ in range(2):
            chain_scratch += Chain.scratch(
                height // 2, lanes, len(strides) - 2, height == 3 * model
            )
    for _ in range(2):
        chain_scratch += Exchange.scratch(share // 2, model, len(strides))
    late_inputs = (normed, residual, middle_grad, divisor, pooled, mix, all_join, states_part)
    (
        input_grad,
        out_states,
        weight_total,
        joint_total,
        out_total,
        join_total,
        taps_total,
        gains_total,
        bias_total,
    ) = pl.pallas_call(
        functools.partial(back_kernel, width, replicas, buckets),
        out_shape=(
            like((rows, 1, model), F32),
            like((rows, 1, model), F32),
            like((3 * model, hidden), F32),
            like((model, 4 * inner), F32),
            like((inner, model), F32),
            like((share, model), F32),
            like((8, share), F32),
            like((8, model), F32),
            like((8, LANES), F32),
        ),
        in_specs=whole(18) + anywhere(8),
        out_specs=anywhere(4) + whole(5),
        scratch_shapes=[
            *[pltpu.VMEM(part.shape, part.dtype) for part in late_inputs],
            pltpu.SemaphoreType.DMA((len(late_inputs),)),
            pltpu.VMEM((4, inner, rows), BF16),
            pltpu.VMEM((length, inner), BF16),
            pltpu.VMEM((inner, length), F32),
            pltpu.VMEM((length, inner), F32),
            pltpu.VMEM((length, inner), F32),
            pltpu.VMEM((heads, span, LANES), F32),
            pltpu.VMEM((length, 3 * inner), BF16),
            pltpu.VMEM((2, rows, model), BF16),
            pltpu.VMEM((2, rows, model), BF16),
            pltpu.VMEM((rows, model), BF16),
            pltpu.VMEM((rows, model), BF16),
            pltpu.VMEM((rows, model), BF16),
            pltpu.VMEM((2, model, inner), BF16),
            pltpu.VMEM((model, inner), BF16),
            pltpu.VMEM((model, inner), BF16),
            pltpu.VMEM((model, 4 * inner), BF16),
            pltpu.VMEM((length // LANES, LANES), F32),
            pltpu.VMEM((4, 8, model), F32),
            pltpu.VMEM((4, share, model), BF16),
            pltpu.VMEM((2, share, model), BF16),
            pltpu.VMEM((share, model), BF16),
            pltpu.VMEM((share, model), BF16),
            pltpu.VMEM((share, model), BF16),
            pltpu.VMEM((4, 8, model), F32),
            pltpu.VMEM((len(strides), 8, model), F32),
            pltpu.VMEM((len(strides), 8, model), F32),
            pltpu.VMEM((len(strides), 8, LANES), F32),
            pltpu.VMEM((len(strides), 8, LANES), F32),
            pltpu.VMEM((rows, 1, model), F32),
            pltpu.VMEM((rows, 1, model), F32),
            pltpu.VMEM((3 * model, hidden), F32),
            pltpu.VMEM((model, 4 * inner), F32),
            pltpu.SemaphoreType.DMA((4,)),
            *semaphores(22 + 2 * len(strides)),
            *semaphores(4 * Chain.slots(strides) + 2 * len(strides)),
            *chain_scratch,
        ],
        compiler_params=params(3),
        name="back",
    )(
        queries_t,
        queries,
        twice_keys,
        keys_t,
        values,
        grad_stage,
        outs,
        totals,
        table,
        joint_weight,
        bucket_row,
        norm_gain[None],
        starts,
        all_taps,
        weight_grad,
        out_part,
        far_made,
        ffn_gain_grad,
        *late_inputs,
    )
    placed = pl.pallas_call(
        place_kernel,
        out_shape=(
            like((rows, 1, model), F32),
            like((rows, 1, model), F32),
            like(conv_two.shape, F32),
            like(conv_three.shape, F32),
            like(conv_four.shape, F32),
            like((share, model), F32),
            like((1, model), F32),
            like((model, inner), F32),
            like((model, inner), F32),
            like((model, inner), F32),
            like((heads, buckets), F32),
            like((inner, model), F32),
            like((1, model), F32),
            like((model, hidden), F32),
            like((model, hidden), F32),
            like((hidden, model), F32),
        ),
        in_specs=anywhere(6) + whole(3),
        out_specs=anywhere(2)
        + whole(3)
        + anywhere(1)
        + whole(1)
        + anywhere(3)
        + whole(1)
        + anywhere(1)
        + whole(1)
        + anywhere(3),
        scratch_shapes=[
            *[
                pltpu.VMEM(part.shape, F32)
                for part in (joint_total, weight_total, out_states, input_grad, out_total, join_total)
            ],
            pltpu.SemaphoreType.DMA((16,)),
        ],
        compiler_params=params(),
        name="place",
    )(
        joint_total,
        weight_total,
        out_states,
        input_grad,
        out_total,
        join_total,
        taps_total,
        gains_total,
        bias_total,
    )
    placed = list(placed)
    placed[6], placed[10], placed[12] = placed[6][0], placed[10].T, placed[12][0]
    return tuple(placed)


def solution(mesh):
    return jax.shard_map(
        shards,
        mesh=mesh,
        in_specs=(
            P("mp", "dp", None),
            P(None, "dp"),
            P(),
            P(None, "mp"),
            P(None, "mp"),
            P(None, "mp"),
            P("mp", None),
            P(),
            P(None, "mp"),
            P(None, "mp"),
            P(None, "mp"),
            P(None, "mp"),
            P("mp", None),
            P(),
            P(None, "mp"),
            P(None, "mp"),
            P("mp", None),
            P("mp", "dp", None),
        ),
        out_specs=(
            P("mp", "dp", None),
            P("mp", "dp", None),
            P(None, "mp"),
            P(None, "mp"),
            P(None, "mp"),
            P("mp", None),
            P(),
            P(None, "mp"),
            P(None, "mp"),
            P(None, "mp"),
            P(None, "mp"),
            P("mp", None),
            P(),
            P(None, "mp"),
            P(None, "mp"),
            P("mp", None),
        ),
        check_vma=False,
    )
```

```python
import functools

import jax
import jax.numpy as jnp
from jax import lax
from jax.experimental import pallas as pl
from jax.experimental.pallas import tpu as pltpu
from jax.sharding import PartitionSpec as P

EPSILON = 1e-06
LOG2E = 1.4426950408889634
GELU_SCALE = 0.7978845608028654
GELU_CUBE = 0.044715
F32 = jnp.float32
BF16 = jnp.bfloat16
LANES = 128
HALO = 3
VMEM_LIMIT = 56 << 20
MESH = pl.DeviceIdType.MESH


def whole(count):
    return [pl.BlockSpec(memory_space=pltpu.VMEM)] * count


def anywhere(count):
    return [pl.BlockSpec(memory_space=pl.ANY)] * count


def params(collective=None):
    return pltpu.CompilerParams(
        vmem_limit_bytes=VMEM_LIMIT, collective_id=collective, has_side_effects=collective is not None
    )


def like(shape, dtype):
    return jax.ShapeDtypeStruct(shape, dtype)


def dot(lhs, rhs):
    return jnp.dot(lhs, rhs, preferred_element_type=F32)


def dot_nt(lhs, rhs):
    return lax.dot_general(lhs, rhs, (((1,), (1,)), ((), ())), preferred_element_type=F32)


def dot_tn(lhs, rhs):
    return lax.dot_general(lhs, rhs, (((0,), (0,)), ((), ())), preferred_element_type=F32)


def split(values):
    high = values.astype(BF16)
    return high, (values - high.astype(F32)).astype(BF16)


def turned(values):
    return values.astype(F32).T.astype(BF16)


def ranks():
    me = lax.axis_index("mp")
    near = me + 1 - 2 * (me % 2)
    return me, near, (me + 2) % 4, (near + 2) % 4


def greet(peers, strides=()):
    barrier = pltpu.get_barrier_semaphore()
    for peer in peers:
        pl.semaphore_signal(barrier, inc=1, device_id={"mp": peer}, device_id_type=MESH)
    for stride in strides:
        pl.semaphore_signal(barrier, inc=1, device_id={"dp": partner(stride)}, device_id_type=MESH)


def greeted(peers, strides=()):
    pl.semaphore_wait(pltpu.get_barrier_semaphore(), len(peers) + len(strides))


def load_all(pairs, sems):
    copies = []
    for source, target in pairs:
        copies.append(pltpu.make_async_copy(source, target, sems.at[len(copies)]))
        copies[-1].start()
    return copies


def side_of(stride):
    return (lax.axis_index("dp") // stride) % 2


def partner(stride):
    return lax.axis_index("dp") + stride - 2 * stride * side_of(stride)


def strides_of(count):
    strides = []
    while 2 ** len(strides) < count:
        strides.append(2 ** len(strides))
    return strides


class remote:
    def __init__(self, *given, axis="mp"):
        self.given, self.axis = given, axis

    def start(self):
        described(*self.given, self.axis).start()

    def wait_recv(self):
        described(*self.given, self.axis).wait_recv()

    def wait_send(self):
        described(*self.given, self.axis).wait_send()

    def wait(self):
        described(*self.given, self.axis).wait()


def described(source, target, sems, slot, peer, axis):
    source, target, peer = [part() if callable(part) else part for part in (source, target, peer)]
    sends, receives = sems
    return pltpu.make_async_remote_copy(
        src_ref=source,
        dst_ref=target,
        send_sem=sends.at[slot],
        recv_sem=receives.at[slot],
        device_id={axis: peer},
        device_id_type=MESH,
    )


def semaphores(count):
    return [pltpu.SemaphoreType.DMA((count,)), pltpu.SemaphoreType.DMA((count,))]


class Quad:
    def __init__(self, source_ref, base, rows, strides, scratch, sems, first_slot):
        self.source, self.base, self.rows, self.strides = source_ref, base, rows, strides
        self.half_in, self.half, self.pieces_in, self.pieces, self.others_in, self.gathered, self.far_half = scratch
        self.sems, self.slot, self.at = sems, first_slot, 0
        self.copies, self.count = [], 0
        self.steps = len(strides) + 2

    @staticmethod
    def scratch(rows, width, exchanges):
        half, piece = rows // 2, rows // 8
        return [
            pltpu.VMEM((half, width), BF16),
            pltpu.VMEM((half, width), BF16),
            pltpu.VMEM((3, piece, width), BF16),
            pltpu.VMEM((exchanges + 1, piece, width), BF16),
            pltpu.VMEM((exchanges + 1, piece, width), BF16),
            pltpu.VMEM((3, piece, width), BF16),
            pltpu.VMEM((half, width), BF16),
        ]

    @staticmethod
    def slots(strides):
        return len(strides) + 6

    def send(self, source, target, peer):
        copy = remote(source, target, self.sems, self.slot + self.count, peer, axis="dp")
        copy.start()
        self.copies.append(copy)
        self.count += 1

    def away(self, turn):
        first, second = self.strides[1:3]
        flips = (turn % 2, turn // 2)
        device, place = lax.axis_index("dp"), 0
        for flip, stride, weight in zip(flips, (first, second), (1, 2)):
            side = side_of(stride)
            device = device + flip * (stride - 2 * stride * side)
            place = place + weight * (side + flip * (1 - 2 * side))
        return device, place

    def piece(self, turn):
        height = self.rows // 8
        return pl.ds(pl.multiple_of(self.away(turn)[1] * height, 16), height)

    def step(self, finish=None):
        at, half = self.at, self.rows // 2
        first, others = self.strides[0], self.strides[3:]
        self.at += 1
        for copy in self.copies:
            copy.wait_recv()
        done, self.copies = self.copies, []
        if at == 0:
            begin = pl.multiple_of(self.base + (1 - side_of(first)) * half, 16)
            self.send(self.source.at[pl.ds(begin, half), :], self.half_in, partner(first))
        elif at == 1:
            begin = pl.multiple_of(self.base + side_of(first) * half, 16)
            mine = self.source[pl.ds(begin, half), :].astype(F32)
            self.half[...] = (mine + self.half_in[...].astype(F32)).astype(BF16)
            for turn in range(1, 4):
                part = self.half.at[self.piece(turn), :]
                self.send(part, self.pieces_in.at[turn - 1], self.away(turn)[0])
        elif at <= 2 + len(others):
            if at == 2:
                total = self.half[self.piece(0), :].astype(F32)
                for turn in range(1, 4):
                    total = total + self.pieces_in[turn - 1].astype(F32)
            else:
                total = self.pieces[at - 3].astype(F32) + self.others_in[at - 3].astype(F32)
            self.pieces[at - 2] = total.astype(BF16)
            if at < 2 + len(others):
                stride = others[at - 2]
                self.send(self.pieces.at[at - 2], self.others_in.at[at - 2], partner(stride))
            else:
                for turn in range(1, 4):
                    self.send(self.pieces.at[at - 2], self.gathered.at[turn - 1], self.away(turn)[0])
        elif at == 3 + len(others):
            self.half[self.piece(0), :] = self.pieces[len(others)]
            for turn in range(1, 4):
                self.half[self.piece(turn), :] = self.gathered[turn - 1]
            self.send(self.half, self.far_half, partner(first))
        else:
            side = side_of(first)
            mine = pl.ds(pl.multiple_of(self.base + side * half, 16), half)
            other = pl.ds(pl.multiple_of(self.base + (1 - side) * half, 16), half)
            finish(mine, self.half[...].astype(F32))
            finish(other, self.far_half[...].astype(F32))
        for copy in done:
            copy.wait_send()


class Exchange:
    def __init__(self, source_ref, base, rows, strides, scratch, sems, first_slot):
        self.source, self.base, self.rows, self.strides = source_ref, base, rows, strides
        self.ours, self.theirs = scratch
        self.sems, self.slot, self.at = sems, first_slot, 0
        self.copies = []
        self.steps = len(strides) + 1

    @staticmethod
    def scratch(rows, width, strides):
        return [pltpu.VMEM((strides, rows, width), BF16)] * 2

    def step(self, finish=None):
        at = self.at
        self.at += 1
        if at == 0:
            total = self.source[self.base : self.base + self.rows, :].astype(F32)
        else:
            self.copies[-1].wait_recv()
            total = self.ours[at - 1].astype(F32) + self.theirs[at - 1].astype(F32)
        if at < len(self.strides):
            self.ours[at] = total.astype(BF16)
            stride = self.strides[at]
            copy = remote(
                lambda: self.ours.at[at],
                lambda: self.theirs.at[at],
                self.sems,
                self.slot + at,
                lambda: partner(stride),
                axis="dp",
            )
            copy.start()
            self.copies.append(copy)
        else:
            finish(slice(self.base, self.base + self.rows), total)
            for copy in self.copies:
                copy.wait_send()


class Chain:
    def __init__(self, source_ref, base, rows, strides, scratch, sems, first_slot):
        self.source, self.base, self.rows, self.strides = source_ref, base, rows, strides
        (
            self.half_in,
            self.half,
            self.quarter_in,
            self.quarter,
            self.whole_quarter,
            self.gathered_quarter,
            self.both,
            self.gathered_half,
        ) = scratch
        self.sems, self.slot, self.at = sems, first_slot, 0
        self.copies = []
        self.steps = len(strides) + 3
        self.half_base = 0

    def halved(self, half_ref, base):
        self.half, self.half_base, self.at = half_ref, base, 1
        return self

    @staticmethod
    def scratch(rows, width, exchanges, halved=False):
        half, quarter = (rows // 2, width), (rows // 4, width)
        first = (16, LANES) if halved else half
        return [
            pltpu.VMEM(first, BF16),
            pltpu.VMEM(first, BF16),
            pltpu.VMEM((exchanges + 1, *quarter), BF16),
            pltpu.VMEM((exchanges, *quarter), BF16),
            pltpu.VMEM(quarter, BF16),
            pltpu.VMEM(quarter, BF16),
            pltpu.VMEM(half, BF16),
            pltpu.VMEM(half, BF16),
        ]

    @staticmethod
    def slots(strides):
        return len(strides) + 2

    def send(self, source, target, stride):
        copy = remote(
            source, target, self.sems, self.slot + len(self.copies), lambda: partner(stride), axis="dp"
        )
        copy.start()
        self.copies.append(copy)

    def step(self, finish=None):
        first, second, others = self.strides[0], self.strides[1], self.strides[2:]
        half, quarter = self.rows // 2, self.rows // 4
        at = self.at
        self.at += 1
        if self.copies:
            self.copies[-1].wait_recv()
        if at == 0:
            self.send(lambda: self.source.at[pl.ds(pl.multiple_of(self.base + (1 - side_of(first)) * half, 16), half), :], self.half_in, first)
        elif at == 1:
            if self.copies:
                begin = pl.multiple_of(self.base + side_of(first) * half, 16)
                mine = self.source[pl.ds(begin, half), :].astype(F32)
                self.half[...] = (mine + self.half_in[...].astype(F32)).astype(BF16)
            self.send(lambda: self.half.at[
                    pl.ds(
                        pl.multiple_of(self.half_base + (1 - side_of(second)) * quarter, 16), quarter
                    ),
                    :,
                ], lambda: self.quarter_in.at[0], second)
        elif at <= 1 + len(others):
            if at == 2:
                begin = pl.multiple_of(self.half_base + side_of(second) * quarter, 16)
                mine = self.half[pl.ds(begin, quarter), :]
            else:
                mine = self.quarter[at - 3]
            total = mine.astype(F32) + self.quarter_in[at - 2].astype(F32)
            self.quarter[at - 2] = total.astype(BF16)
            self.send(
                lambda: self.quarter.at[at - 2], lambda: self.quarter_in.at[at - 1], others[at - 2]
            )
        elif at == 2 + len(others):
            total = self.quarter[at - 3].astype(F32) + self.quarter_in[at - 2].astype(F32)
            self.whole_quarter[...] = total.astype(BF16)
            self.send(self.whole_quarter, self.gathered_quarter, second)
        elif at == 3 + len(others):
            side = side_of(second)
            mine = pl.ds(pl.multiple_of(side * quarter, 16), quarter)
            other = pl.ds(pl.multiple_of((1 - side) * quarter, 16), quarter)
            self.both[mine, :] = self.whole_quarter[...]
            self.both[other, :] = self.gathered_quarter[...]
            self.send(self.both, self.gathered_half, first)
        else:
            side = side_of(first)
            mine = pl.ds(pl.multiple_of(self.base + side * half, 16), half)
            other = pl.ds(pl.multiple_of(self.base + (1 - side) * half, 16), half)
            finish(mine, self.both[...].astype(F32))
            finish(other, self.gathered_half[...].astype(F32))
            for copy in self.copies:
                copy.wait_send()


def rms(values, gain):
    return values * lax.rsqrt(jnp.mean(values * values, axis=1, keepdims=True) + EPSILON) * gain


def rms_back(grads, values, gain):
    scale = lax.rsqrt(jnp.mean(values * values, axis=1, keepdims=True) + EPSILON)
    gain_grad = jnp.sum(grads * values * scale, axis=0, keepdims=True)
    raised = grads * gain
    mean = jnp.mean(raised * values, axis=1, keepdims=True)
    return scale * raised - values * (scale * scale * scale * mean), gain_grad


def bucket_hits(bucket_ref, buckets):
    span = bucket_ref.shape[1]
    rows = lax.broadcasted_iota(jnp.int32, (buckets, span), 0)
    return rows == jnp.broadcast_to(bucket_ref[...], (buckets, span))


def fill_bias_table(bucket_ref, bias_ref, table_ref):
    span = bucket_ref.shape[1]
    heads, buckets = bias_ref.shape
    hits = bucket_hits(bucket_ref, buckets).astype(F32).astype(BF16)
    bias = bias_ref[...]
    first = bias.astype(BF16)
    second, third = split(bias - first.astype(F32))
    rows = jnp.concatenate([first, second, third, jnp.zeros((16 - 3 * heads, buckets), BF16)], axis=0)
    lines = dot(rows, hits)
    for head in range(heads):
        line = lines[head : head + 1] + (
            lines[heads + head : heads + head + 1] + lines[2 * heads + head : 2 * heads + head + 1]
        )
        skew = pltpu.roll(
            jnp.broadcast_to(line * LOG2E, (LANES, span)), span - LANES + 1, 1, stride=1, stride_axis=0
        )
        for block in range(span // LANES - 1):
            cut = slice(block * LANES, (block + 1) * LANES)
            table_ref[head, cut, :] = skew[:, cut].T


def bias_grad_rows(table_ref, bucket_ref, buckets):
    span = bucket_ref.shape[1]
    heads = table_ref.shape[0]
    hits = bucket_hits(bucket_ref, buckets).astype(F32).astype(BF16)
    lines = []
    for head in range(heads):
        blocks = [
            table_ref[head, block * LANES : (block + 1) * LANES, :].T
            for block in range(span // LANES - 1)
        ]
        skew = jnp.concatenate(blocks + [jnp.zeros((LANES, LANES), F32)], axis=1)
        rows = LANES // 2
        while rows >= 8:
            skew = skew[:rows] + pltpu.roll(skew[rows:], span - rows, 1)
            rows //= 2
        line = jnp.zeros((1, span), F32)
        for row in range(8):
            line = line + pltpu.roll(skew[row : row + 1], LANES - 1 - row, 1)
        lines.append(line)
    lines = jnp.concatenate(lines + [jnp.zeros((8 - heads, span), F32)], axis=0)
    first = lines.astype(BF16)
    second, third = split(lines - first.astype(F32))
    parts = dot_nt(jnp.concatenate([first.astype(F32), second.astype(F32)], axis=0).astype(BF16), hits)
    rest = dot_nt(jnp.concatenate([third.astype(F32), jnp.zeros((8, span), F32)], axis=0).astype(BF16), hits)
    made = parts[:8] + (parts[8:] + rest[:8])
    return jnp.concatenate([made, jnp.zeros((8, LANES - buckets), F32)], axis=1)


def word_numbers(starts):
    rows = starts.shape[0]
    upper = lax.broadcasted_iota(jnp.int32, (LANES, LANES), 0) <= lax.broadcasted_iota(
        jnp.int32, (LANES, LANES), 1
    )
    within = dot(starts.astype(F32).astype(BF16), upper.astype(F32).astype(BF16))
    totals = jnp.broadcast_to(within[:, LANES - 1 :], (rows, LANES)).astype(BF16)
    lower = lax.broadcasted_iota(jnp.int32, (rows, rows), 1) < lax.broadcasted_iota(
        jnp.int32, (rows, rows), 0
    )
    return within + dot(lower.astype(F32).astype(BF16), totals) - 1.0


class Words:
    def __init__(self, starts_ref, ids_ref, me, ranks_count):
        ids = word_numbers(starts_ref[...])
        ids_ref[...] = ids
        per = ids.shape[0] // ranks_count
        self.firsts = [ids[per * rank : per * rank + 1, 0:1] for rank in range(ranks_count)]
        self.lasts = [
            ids[per * (rank + 1) - 1 : per * (rank + 1), LANES - 1 :] for rank in range(ranks_count)
        ]
        pieces = [ids_ref[pl.ds(me * per + piece, 1), :] for piece in range(per)]
        self.row = jnp.concatenate(pieces, axis=1)
        self.first = self.row[:, 0:1]
        self.last = self.row[:, per * LANES - 1 :]
        self.me = me
        self.count = per * LANES

    def table(self):
        shape = (self.count + 16, self.count)
        rows = lax.broadcasted_iota(jnp.int32, shape, 0).astype(F32)
        return (rows == self.row - self.first + HALO).astype(F32).astype(BF16)

    def pick(self, target):
        slots = lax.broadcasted_iota(jnp.int32, (8, 1), 0)
        hits = target(slots, self.first, self.last) == self.row
        return hits.astype(F32).astype(BF16)

    def place(self, target, valid):
        width = 2 * LANES
        lane = lax.broadcasted_iota(jnp.int32, (1, width), 1) % LANES
        slots, rank = lane % 8, lane // 8
        goal = jnp.full((1, width), -9.0, F32)
        for index, (first, last) in enumerate(zip(self.firsts, self.lasts)):
            goal = jnp.where(rank == index, target(slots, first, last), goal)
        known = valid(slots, rank, self.me) & (rank < len(self.firsts))
        goal = jnp.where(known, goal - self.first + HALO, -1.0)
        rows = lax.broadcasted_iota(jnp.int32, (self.count + 16, width), 0).astype(F32)
        return (rows == goal).astype(F32).astype(BF16)


def stacked(summary_ref):
    parts = [summary_ref[rank] for rank in range(summary_ref.shape[0])]
    rest = LANES - sum(part.shape[0] for part in parts)
    parts.append(jnp.zeros((rest, parts[0].shape[1]), F32))
    return jnp.concatenate(split(jnp.concatenate(parts, axis=0)), axis=0)


def ahead_target(slots, first, last):
    later = jnp.where(slots <= 4, last - (slots - 1).astype(F32), -9.0)
    return jnp.where(slots == 0, first, later)


def ahead_valid(slots, rank, me):
    return ((rank < me) & (slots >= 1) & (slots <= 4)) | ((rank > me) & (slots == 0))


def back_target(slots, first, last):
    return jnp.where(slots <= 3, first + slots.astype(F32), jnp.where(slots == 4, last, -9.0))


def back_valid(slots, rank, me):
    return ((rank > me) & (slots <= 3)) | ((rank < me) & (slots == 4))


def forward_kernel(
    width,
    states_ref,
    starts_ref,
    two_ref,
    three_ref,
    four_ref,
    join_ref,
    gain_ref,
    query_weight_ref,
    key_weight_ref,
    value_weight_ref,
    bucket_ref,
    bias_ref,
    out_weight_ref,
    gate_ref,
    up_ref,
    down_ref,
    grad_ref,
    residual_out,
    normed_out,
    query_out,
    query_t_out,
    twice_out,
    key_t_out,
    value_out,
    table_out,
    divisor_out,
    pooled_out,
    mix_out,
    all_taps_ref,
    all_join_out,
    joint_out,
    padded_out,
    out_ref,
    total_ref,
    attended_ref,
    all_out_ref,
    near_gate_ref,
    near_up_ref,
    near_down_ref,
    far_grad_ref,
    residual_ref,
    normed_ref,
    query_ref,
    query_t_ref,
    twice_ref,
    key_t_ref,
    value_ref,
    table_ref,
    divisor_ref,
    pooled_ref,
    mix_ref,
    all_join_ref,
    joint_ref,
    padded_ref,
    value_t_ref,
    ids_ref,
    summary_ref,
    taps_in_ref,
    score_ref,
    stage_ref,
    ship_ref,
    *sems,
):
    me, near, far, cross = ranks()
    peers = (near, far, cross)
    rows, model = states_ref.shape
    share = join_ref.shape[0]
    inner = query_weight_ref.shape[1]
    heads, length = twice_ref.shape[0], twice_ref.shape[1]
    shipped = []

    def ship(source, target):
        copy = pltpu.make_async_copy(source, target, ship_ref.at[len(shipped)])
        copy.start()
        shipped.append(copy)

    def band(ref, rank):
        return ref.at[pl.ds(pl.multiple_of(rank * share, share), share), :]

    greet(peers)
    words = Words(starts_ref, ids_ref, me, 4)
    states = states_ref[...]
    wide_states = jnp.concatenate([states, jnp.ones((rows, LANES), BF16)], axis=1)
    summary_ref[me] = dot(words.pick(ahead_target), wide_states)
    two, three, four = two_ref[...], three_ref[...], four_ref[...]
    taps_in_ref[me] = jnp.concatenate(
        [
            two[0:1] + three[0:1] + four[0:1],
            two[1:2] + three[1:2] + four[1:2],
            three[2:3] + four[2:3],
            four[3:4],
            jnp.zeros((4, share), F32),
        ],
        axis=0,
    )
    all_join_ref[pl.ds(pl.multiple_of(me * share, share), share), :] = join_ref[...]
    all_out_ref[pl.ds(pl.multiple_of(me * share, share), share), :] = out_weight_ref[...]
    greeted(peers)
    early = []
    for slot, peer in enumerate(peers):
        early.append(remote(summary_ref.at[me], summary_ref.at[me], sems, slot, peer))
        early.append(remote(taps_in_ref.at[me], taps_in_ref.at[me], sems, 3 + slot, peer))
    joins = [
        remote(band(all_join_ref, me), band(all_join_ref, me), sems, 6, far),
        remote(band(all_join_ref, me), band(all_join_ref, me), sems, 7, near),
    ]
    for copy in early + joins:
        copy.start()
    padded_ref[...] = jnp.full(padded_ref.shape, -1, jnp.int32)
    padded_ref[:, : bucket_ref.shape[1]] = bucket_ref[...]
    joint_ref[:, :inner] = query_weight_ref[...]
    joint_ref[:, inner : 2 * inner] = key_weight_ref[...]
    joint_ref[:, 2 * inner :] = value_weight_ref[...]
    ship(joint_ref, joint_out)
    ship(padded_ref, padded_out)
    table = words.table()
    sums = dot(table, wide_states)
    place = words.place(ahead_target, ahead_valid)
    for copy in early:
        copy.wait_recv()
    sums = sums + dot(place, stacked(summary_ref))
    divisor = jnp.maximum(sums[:, model:], 1.0)
    divisor_ref[...] = divisor
    ship(divisor_ref, divisor_out)
    pooled = sums[:, :model] / jnp.concatenate([divisor] * (model // LANES), axis=1)
    pooled_ref[...] = pooled
    ship(pooled_ref, pooled_out)
    taps = jnp.concatenate([taps_in_ref[rank] for rank in range(4)], axis=1)
    all_taps_ref[...] = taps
    joins[0].wait_recv()
    joins.append(remote(band(all_join_ref, far), band(all_join_ref, far), sems, 8, near))
    joins[2].start()
    total = pooled * taps[0:1]
    for lag in range(1, 4):
        total = total + pltpu.roll(pooled, lag, 0) * taps[lag : lag + 1]
    mix = dot_tn(table, total.astype(BF16)).astype(BF16)
    mix_ref[...] = mix
    ship(mix_ref, mix_out)
    joins[1].wait_recv()
    joins[2].wait_recv()
    residual = states.astype(F32) + dot(mix, all_join_ref[...])
    residual_ref[...] = residual
    own = pl.ds(pl.multiple_of(me * rows, rows), rows)
    normed_ref[own, :] = rms(residual, gain_ref[...]).astype(BF16)

    def block(rank, part):
        half = rows // 2
        return normed_ref.at[pl.ds(pl.multiple_of(rank * rows + part * half, half), half), :]

    sends = []
    for part in range(2):
        sends.append(remote(block(me, part), block(me, part), sems, 9 + part, far))
    for part in range(2):
        sends.append(remote(block(me, part), block(me, part), sems, 11 + part, near))
    for copy in sends:
        copy.start()
    copies = [
        remote(grad_ref, far_grad_ref, sems, 15, far),
        remote(band(all_out_ref, me), band(all_out_ref, me), sems, 16, near),
        remote(gate_ref, near_gate_ref, sems, 17, near),
        remote(up_ref, near_up_ref, sems, 18, near),
        remote(down_ref, near_down_ref, sems, 19, near),
    ]
    out_far = remote(
        lambda: band(all_out_ref, me), lambda: band(all_out_ref, me), sems, 20, far
    )
    out_pass = remote(
        lambda: band(all_out_ref, far), lambda: band(all_out_ref, far), sems, 21, near
    )
    out_far.start()
    for copy in copies:
        copy.start()
    ship(residual_ref, residual_out)
    ship(all_join_ref, all_join_out)

    def project(rank):
        cut = pl.ds(pl.multiple_of(rank * rows, rows), rows)
        made = dot(normed_ref[cut, :], joint_ref[...])
        query, key, value = [
            made[:, index * inner : (index + 1) * inner].astype(BF16) for index in range(3)
        ]
        query_ref[cut, :] = query
        query_t_ref[:, cut] = turned(query)
        key_t_ref[:, cut] = turned(key)
        value_ref[cut, :] = value
        value_t_ref[:, cut] = turned(value)
        for head in range(heads):
            part = key[:, head * width : (head + 1) * width]
            twice_ref[head, cut, :] = jnp.concatenate([part, part], axis=1)

    project(me)
    fill_bias_table(padded_ref, bias_ref, table_ref)
    ship(table_ref, table_out)
    sends[2].wait_recv()
    sends[3].wait_recv()
    project(near)
    passed = []
    for part in range(2):
        sends[part].wait_recv()
        passed.append(remote(block(far, part), block(far, part), sems, 13 + part, near))
        passed[part].start()
    project(far)
    for copy in passed:
        copy.wait_recv()
    project(cross)
    for source, target in (
        (normed_ref, normed_out),
        (query_ref, query_out),
        (query_t_ref, query_t_out),
        (twice_ref, twice_out),
        (key_t_ref, key_t_out),
        (value_ref, value_out),
    ):
        ship(source, target)
    wide = deep = length // 4

    def owner(order):
        chip = (me // 2 + 1 + order // 2) % 2
        core = (me % 2 + (order + 1) // 2) % 2
        return 2 * chip + core

    def handed(order):
        return remote(stage_ref.at[order], attended_ref.at[me], sems, 22 + order, owner(order))

    def step(index, carry):
        order, head = index // heads, index % heads
        begin = pl.multiple_of(owner(order) * wide, wide)
        span = pl.ds(begin, wide)
        rows = pl.ds(pl.multiple_of(head * width, width), width)
        scaled = query_t_ref[rows, span].astype(F32) * LOG2E
        queries = jnp.concatenate(split(scaled), axis=0)
        peak = jnp.full((8, wide), -1e30, F32)
        for part in range(length // deep):
            cut = slice(part * deep, (part + 1) * deep)
            raw = dot(twice_ref[head, cut, :], queries)
            columns = []
            for lane in range(0, wide, LANES):
                offset = pl.multiple_of(part * deep - begin - lane + length - LANES, LANES)
                columns.append(raw[:, lane : lane + LANES] + table_ref[head, pl.ds(offset, deep), :])
            scores = jnp.concatenate(columns, axis=1)
            score_ref[cut, :] = scores
            peak = jnp.maximum(peak, jnp.max(scores.reshape(deep // 8, 8, wide), axis=0))
        peak = jnp.max(peak, axis=0, keepdims=True)
        sums = jnp.zeros((8, wide), F32)
        made = jnp.zeros((width, wide), F32)
        for part in range(length // deep):
            cut = slice(part * deep, (part + 1) * deep)
            raised = jnp.exp2(score_ref[cut, :] - peak)
            sums = sums + jnp.sum(raised.reshape(deep // 8, 8, wide), axis=0)
            made = made + dot(value_t_ref[rows, cut], raised.astype(BF16))
        total = jnp.sum(sums, axis=0, keepdims=True)
        made = made / total
        out_ref[rows, span] = made
        total_ref[head, :, span] = peak + jnp.log2(total)
        stage_ref[order, rows, :] = made.astype(BF16)

        @pl.when((head == heads - 1) & (order < 3))
        def _():
            handed(order).start()

        @pl.when(index == heads)
        def _():
            out_far.wait_recv()
            out_pass.start()

        return carry

    lax.fori_loop(0, heads * 4, step, 0)
    attended_ref[me] = stage_ref[3]
    for order in range(3):
        handed(order).wait()
    for copy in copies:
        copy.wait()
    out_pass.wait()
    for copy in early + joins + sends + passed + [out_far]:
        copy.wait_send()
    for copy in shipped:
        copy.wait()


def ffn_kernel(
    count,
    attended_ref,
    all_out_ref,
    residual_ref,
    gain_ref,
    grad_hbm,
    far_grad_hbm,
    gate_hbm,
    near_gate_hbm,
    up_hbm,
    near_up_hbm,
    down_hbm,
    near_down_hbm,
    states_part_ref,
    far_made_ref,
    middle_grad_ref,
    gain_grad_ref,
    weight_half_ref,
    out_part_ref,
    grad_stage_ref,
    middle_ref,
    normed_ref,
    made_ref,
    back_ref,
    sums_ref,
    far_out_ref,
    far_in_ref,
    near_out_ref,
    near_in_ref,
    weight_ref,
    half_in_ref,
    grad_ref,
    far_grad_ref,
    gate_ref,
    near_gate_ref,
    up_ref,
    near_up_ref,
    down_ref,
    near_down_ref,
    load_ref,
    sends_ref,
    receives_ref,
    half_sends_ref,
    half_receives_ref,
):
    me, near, far, cross = ranks()
    sems = (sends_ref, receives_ref)
    strides = strides_of(count)[:2]
    peers = (near, far, cross)
    rows, model = residual_ref.shape
    share = attended_ref.shape[1]
    greet(peers, strides)
    loads = load_all(
        (
            (grad_hbm, grad_ref),
            (far_grad_hbm, far_grad_ref),
            (gate_hbm, gate_ref),
            (near_gate_hbm, near_gate_ref),
            (up_hbm, up_ref),
            (near_up_hbm, near_up_ref),
            (down_hbm, down_ref),
            (near_down_hbm, near_down_ref),
        ),
        load_ref,
    )
    attended = attended_ref[...].reshape(4 * share, rows)
    middle = residual_ref[...] + dot_tn(attended, all_out_ref[...])
    middle_ref[...] = middle
    normed_ref[0] = rms(middle, gain_ref[...]).astype(BF16)
    half = rows // 2
    greeted(peers, strides)
    there, returned = [], []
    for part in range(2):
        cut = pl.ds(part * half, half)
        there.append(remote(normed_ref.at[0, cut], normed_ref.at[1, cut], sems, part, far))
        there[part].start()
        returned.append(remote(far_out_ref.at[cut], far_in_ref.at[cut], sems, 2 + part, far))

    def work(side, cut, grads, gate, up, down, slab, first):
        given = normed_ref[side, cut]
        gate_value = dot(given, gate)
        up_value = dot(given, up)
        hidden_grad = dot_nt(grads, down)
        square = gate_value * gate_value
        curve = jnp.tanh(GELU_SCALE * gate_value * (1.0 + GELU_CUBE * square))
        half = 0.5 + 0.5 * curve
        gelu = gate_value * half
        slope = half + (0.5 * GELU_SCALE) * gate_value * (1.0 - curve * curve) * (
            1.0 + (3.0 * GELU_CUBE) * square
        )
        hidden = (gelu * up_value).astype(BF16)
        gate_back = (hidden_grad * up_value * slope).astype(BF16)
        up_back = (hidden_grad * gelu).astype(BF16)
        sums = [dot_tn(given, gate_back), dot_tn(given, up_back), dot_tn(hidden, grads)]
        for index in range(3):
            if side == 0:
                sums_ref[slab, index] = sums[index]
            else:
                sums_ref[slab, index] += sums[index]
        made = dot(hidden, down)
        back = dot_nt(gate_back, gate) + dot_nt(up_back, up)
        if first:
            made_ref[side, cut] = made
            back_ref[side, cut] = back
        else:
            made_ref[side, cut] += made
            back_ref[side, cut] += back

    for copy in loads:
        copy.wait()
    slabs = ((1, (near_gate_ref, near_up_ref, near_down_ref)), (0, (gate_ref, up_ref, down_ref)))
    for slab, weights in slabs:
        work(0, slice(0, rows), grad_ref[...], *[ref[...] for ref in weights], slab, slab == 1)
    for part in range(2):
        cut = slice(part * half, (part + 1) * half)
        there[part].wait_recv()
        for slab, weights in slabs:
            work(1, cut, far_grad_ref[cut, :], *[ref[...] for ref in weights], slab, slab == 1)
            if part == 1 and slab == 1:
                near_out_ref[...] = sums_ref[1].astype(BF16)
                swap = remote(near_out_ref, near_in_ref, sems, 4, near)
                swap.start()
        far_out_ref[cut, :] = back_ref[1, cut].astype(BF16)
        returned[part].start()
    far_made_ref[...] = made_ref[1].astype(BF16)
    states_part_ref[...] = middle_ref[...] + made_ref[0]
    swap.wait_recv()
    depth = weight_ref.shape[0] // 3
    for index in range(3):
        total = sums_ref[0, index] + near_in_ref[index].astype(F32)
        weight_ref[index * depth : (index + 1) * depth, :] = total.astype(BF16)
    size = weight_ref.shape[0] // 4
    halves = []
    for index, stride in enumerate(strides):
        begin = pl.multiple_of(2 * size * index + (1 - side_of(stride)) * size, 16)
        halves.append(
            remote(
                weight_ref.at[pl.ds(begin, size), :],
                half_in_ref.at[index],
                (half_sends_ref, half_receives_ref),
                index,
                partner(stride),
                axis="dp",
            )
        )
        halves[-1].start()
    for copy in returned:
        copy.wait_recv()
    normed_grad = back_ref[0] + far_in_ref[...].astype(F32)
    part, gain_grad = rms_back(normed_grad, middle_ref[...], gain_ref[...])
    gain_grad_ref[...] = jnp.broadcast_to(gain_grad, gain_grad_ref.shape)
    middle_grad = grad_ref[...].astype(F32) + part
    middle_grad_ref[...] = middle_grad
    low = middle_grad.astype(BF16)
    grad_stage_ref[...] = dot_nt(all_out_ref[...], low).astype(BF16).reshape(4, share, rows)
    out_part = dot(attended, low)
    for rank in range(4):
        out_part_ref[rank] = out_part[rank * share : (rank + 1) * share, :].T.astype(BF16)
    for index, stride in enumerate(strides):
        halves[index].wait_recv()
        begin = pl.multiple_of(2 * size * index + side_of(stride) * size, 16)
        total = weight_ref[pl.ds(begin, size), :].astype(F32) + half_in_ref[index].astype(F32)
        weight_half_ref[index * size : (index + 1) * size, :] = total.astype(BF16)
    for copy in halves:
        copy.wait_send()
    for copy in returned + there + [swap]:
        copy.wait_send()


def back_kernel(
    width,
    count,
    buckets,
    grad_stage_ref,
    total_ref,
    joint_ref,
    bucket_ref,
    gain_ref,
    starts_ref,
    all_taps_ref,
    weight_half_ref,
    out_part_ref,
    far_made_ref,
    ffn_gain_grad_ref,
    query_t_hbm,
    query_hbm,
    twice_hbm,
    key_t_hbm,
    value_hbm,
    out_hbm,
    table_hbm,
    normed_hbm,
    residual_hbm,
    middle_grad_hbm,
    divisor_hbm,
    pooled_hbm,
    mix_hbm,
    all_join_hbm,
    states_part_hbm,
    input_grad_out,
    states_out_out,
    weight_total_out,
    joint_total_out,
    out_total_ref,
    join_total_ref,
    taps_total_ref,
    gains_total_ref,
    bias_total_ref,
    query_t_ref,
    query_ref,
    twice_ref,
    key_t_ref,
    value_ref,
    out_ref,
    table_ref,
    normed_ref,
    residual_ref,
    middle_grad_ref,
    divisor_ref,
    pooled_ref,
    mix_ref,
    all_join_ref,
    states_part_ref,
    load_ref,
    grad_t_ref,
    grad_ref,
    query_grad_ref,
    key_grad_ref,
    value_grad_ref,
    table_grad_ref,
    joint_grad_ref,
    core_out_ref,
    core_in_ref,
    chip_out_ref,
    chip_in_ref,
    made_in_ref,
    out_near_ref,
    out_sum_ref,
    out_far_ref,
    late_ref,
    ids_ref,
    summary_ref,
    join_part_ref,
    join_near_ref,
    join_sum_ref,
    join_far_ref,
    join_ref,
    small_near_ref,
    small_ref,
    small_in_ref,
    bias_ref,
    bias_in_ref,
    input_grad_ref,
    states_out_ref,
    weight_total_ref,
    joint_total_ref,
    ship_ref,
    sends_ref,
    receives_ref,
    chain_sends_ref,
    chain_receives_ref,
    *chain_refs,
):
    me, near, far, cross = ranks()
    peers = (near, far, cross)
    sems = (sends_ref, receives_ref)
    chain_sems = (chain_sends_ref, chain_receives_ref)
    heads, length = twice_ref.shape[0], twice_ref.shape[1]
    rows, model = residual_ref.shape
    share = join_part_ref.shape[1]
    inner = heads * width
    wide, deep = length // 4, length // 8
    strides = strides_of(count)
    turned_strides = [strides[1], strides[0]] + strides[2:]
    chains = []
    plan = [
        (None, 2 * weight_half_ref.shape[0], strides),
        (None, 2 * weight_half_ref.shape[0], turned_strides),
    ]
    for index, (ref, height, order) in enumerate(plan):
        half = height // 2
        chains.append(
            Chain(
                ref,
                (index % 2) * half,
                half,
                order,
                chain_refs[8 * index : 8 * index + 8],
                chain_sems,
                index * Chain.slots(strides),
            )
        )
    weight_chains, late_chains, join_chains = chains, [], []
    for index, chain in enumerate(weight_chains):
        chain.halved(weight_half_ref, index * (weight_half_ref.shape[0] // 2))
    for index, order in enumerate((strides, turned_strides)):
        join_chains.append(
            Exchange(
                join_ref,
                index * (join_ref.shape[0] // 2),
                join_ref.shape[0] // 2,
                order,
                chain_refs[30 + 2 * index : 32 + 2 * index],
                chain_sems,
                2 * Chain.slots(strides) + 2 * Quad.slots(strides) + index * len(strides),
            )
        )
        late_chains.append(
            Quad(
                late_ref,
                index * (late_ref.shape[0] // 2),
                late_ref.shape[0] // 2,
                order,
                chain_refs[16 + 7 * index : 23 + 7 * index],
                chain_sems,
                2 * Chain.slots(strides) + index * Quad.slots(strides),
            )
        )
    greet(peers, strides)
    loads = load_all(
        (
            (query_t_hbm, query_t_ref),
            (query_hbm, query_ref),
            (twice_hbm, twice_ref),
            (key_t_hbm, key_t_ref),
            (value_hbm, value_ref),
            (out_hbm, out_ref),
            (table_hbm, table_ref),
            (normed_hbm, normed_ref),
            (residual_hbm, residual_ref),
            (middle_grad_hbm, middle_grad_ref),
            (divisor_hbm, divisor_ref),
            (pooled_hbm, pooled_ref),
            (mix_hbm, mix_ref),
            (all_join_hbm, all_join_ref),
            (states_part_hbm, states_part_ref),
        ),
        load_ref,
    )
    greeted(peers, strides)
    gradient_copies = []
    for slot, peer in enumerate(peers):
        copy = remote(
            lambda peer=peer: grad_stage_ref.at[peer], lambda: grad_t_ref.at[me], sems, slot, peer
        )
        copy.start()
        gradient_copies.append(copy)
    out_copies = [
        remote(lambda: out_part_ref.at[near], lambda: out_near_ref.at[0], sems, 3, near),
        remote(lambda: out_part_ref.at[cross], lambda: out_near_ref.at[1], sems, 4, near),
    ]
    for copy in out_copies:
        copy.start()
    out_copy = remote(out_sum_ref, out_far_ref, sems, 5, far)
    made_copy = remote(far_made_ref, made_in_ref, sems, 6, far)
    core_copies = [
        remote(lambda: core_out_ref.at[0], lambda: core_in_ref.at[0], sems, 7, near),
        remote(lambda: core_out_ref.at[1], lambda: core_in_ref.at[1], sems, 8, near),
    ]
    chip_copy = remote(chip_out_ref, chip_in_ref, sems, 9, far)
    for chain in weight_chains:
        chain.step()
    made_copy.start()
    grad_t_ref[me] = grad_stage_ref[me]
    query_grad_ref[...] = jnp.zeros_like(query_grad_ref)
    key_grad_ref[...] = jnp.zeros_like(key_grad_ref)
    value_grad_ref[...] = jnp.zeros_like(value_grad_ref)
    table_grad_ref[...] = jnp.zeros_like(table_grad_ref)

    def gather_rows(rank):
        cut = pl.ds(pl.multiple_of(rank * wide, wide), wide)
        joint_grad_ref[cut, :inner] = query_grad_ref[:, cut].T.astype(BF16)
        joint_grad_ref[cut, inner : 2 * inner] = key_grad_ref[cut, :].astype(BF16)
        joint_grad_ref[cut, 2 * inner :] = value_grad_ref[cut, :].astype(BF16)
        return dot_nt(joint_grad_ref[cut, :], joint_ref[...])

    def block_of(relation):
        return 2 * ((me // 2 + relation // 2) % 2) + (me % 2 + relation % 2) % 2

    core = me % 2

    def step(index, carry):
        phase = index // 4
        middle = ((phase + 1) // 2) % 2
        away = middle * (2 + (core + phase - 1) % 2)
        block = block_of(away + (1 - middle) * ((index % 4) // 2))
        turn = (index + (2 + core) * (phase // 2)) % 4
        other = block_of(middle * turn + (1 - middle) * (index % 2 + 2 * (1 - phase // 3)))
        begin = pl.multiple_of(block * wide, wide)
        start = pl.multiple_of(other * wide, wide)
        span = pl.ds(begin, wide)
        @pl.when(index == 2)
        def _():
            gradient_copies[0].wait_recv()

        for first in range(2):

            @pl.when((index == 4 + 4 * first) & (core == first))
            def _():
                gradient_copies[1].wait_recv()

            @pl.when((index == 4 + 4 * first) & (core == 1 - first))
            def _():
                gradient_copies[2].wait_recv()

        @pl.when((index == 0) | (index == 2) | (index == 4) | (index == 8))
        def _():
            grad_ref[span, :] = turned(grad_t_ref[block])

        @pl.when(index == 3)
        def _():
            for copy in out_copies:
                copy.wait_recv()
            ours = out_part_ref[far].astype(F32) + out_near_ref[1].astype(F32)
            out_sum_ref[...] = ours.astype(BF16)
            out_copy.start()

        @pl.when(index == 4)
        def _():
            weight_chains[0].step()
            weight_chains[1].step()

        for first in range(2):

            @pl.when((index == 9 + 3 * first) & (core == first))
            def _():
                chip_out_ref[...] = gather_rows(far).astype(BF16)

            @pl.when((index == 9 + 3 * first) & (core == 1 - first))
            def _():
                core_out_ref[0] = gather_rows(cross).astype(BF16)
                core_copies[0].start()

            @pl.when((index == 10 + 3 * first) & (core == first))
            def _():
                core_copies[0].wait_recv()
                total = chip_out_ref[...].astype(F32) + core_in_ref[0].astype(F32)
                chip_out_ref[...] = total.astype(BF16)
                chip_copy.start()

        for head in range(heads):
            rows = slice(head * width, (head + 1) * width)
            scaled = query_t_ref[rows, span].astype(F32) * LOG2E
            queries = jnp.concatenate(split(scaled), axis=0)
            total = total_ref[head, :, span]
            grads = grad_t_ref[block, rows, :].astype(F32)
            dots = jnp.sum(grads * out_ref[rows, span], axis=0, keepdims=True)
            own_rows = lax.broadcasted_iota(jnp.int32, (inner, wide), 0) // width == head
            own_lanes = lax.broadcasted_iota(jnp.int32, (wide, inner), 1) // width == head
            grad_t_own = jnp.where(own_rows, grad_t_ref[block].astype(F32), 0.0).astype(BF16)
            query_own = jnp.where(own_lanes, query_ref[span, :].astype(F32), 0.0).astype(BF16)
            grad_own = jnp.where(own_lanes, grad_ref[span, :].astype(F32), 0.0).astype(BF16)
            query_grad = jnp.zeros((width, wide), F32)
            for part in range(wide // deep):
                cut = pl.ds(pl.multiple_of(start + part * deep, deep), deep)
                raw = dot(twice_ref[head, cut, :], queries)
                raw_grad = dot(value_ref[cut, :], grad_t_own)
                probs, score_grads = [], []
                for lane in range(0, wide, LANES):
                    piece = slice(lane, lane + LANES)
                    offset = start + part * deep - begin - lane + length - LANES
                    offset = pl.multiple_of(offset, LANES)
                    shift = table_ref[head, pl.ds(offset, deep), :]
                    prob = jnp.exp2(raw[:, piece] + shift - total[:, piece])
                    low = (prob * (raw_grad[:, piece] - dots[:, piece])).astype(BF16)
                    table_grad_ref[head, pl.ds(offset, deep), :] += low.astype(F32)
                    probs.append(prob.astype(BF16))
                    score_grads.append(low)
                probs = jnp.concatenate(probs, axis=1)
                score_grads = jnp.concatenate(score_grads, axis=1)
                value_grad_ref[cut, :] += dot(probs, grad_own)
                key_grad_ref[cut, :] += dot(score_grads, query_own)
                query_grad = query_grad + dot(key_t_ref[rows, cut], score_grads)
            query_grad_ref[rows, span] += query_grad
        return carry

    for copy in loads[:7]:
        copy.wait()
    lax.fori_loop(0, 16, step, 0)
    core_out_ref[1] = gather_rows(near).astype(BF16)
    core_copies[1].start()
    for chain in weight_chains:
        chain.step()
    normed_grad = gather_rows(me)
    for copy in loads[7:]:
        copy.wait()
    late_ref[:, : 3 * inner] = dot_tn(normed_ref[...], joint_grad_ref[...]).astype(BF16)
    out_copy.wait_recv()
    out_sum = (
        out_part_ref[me].astype(F32) + out_near_ref[0].astype(F32) + out_far_ref[...].astype(F32)
    )
    late_ref[:, 3 * inner :] = out_sum.astype(BF16)
    for chain in late_chains:
        chain.step()
    core_copies[1].wait_recv()
    normed_grad = normed_grad + core_in_ref[1].astype(F32)
    chip_copy.wait_recv()
    normed_grad = normed_grad + chip_in_ref[...].astype(F32)
    part, gain_grad = rms_back(normed_grad, residual_ref[...], gain_ref[...])
    residual_grad = middle_grad_ref[...] + part
    low = residual_grad.astype(BF16)
    join_part_ref[...] = dot_tn(mix_ref[...], low).astype(BF16).reshape(4, share, model)
    join_copies = [
        remote(join_part_ref.at[near], join_near_ref.at[0], sems, 16, near),
        remote(join_part_ref.at[cross], join_near_ref.at[1], sems, 17, near),
    ]
    for copy in join_copies:
        copy.start()
    words = Words(starts_ref, ids_ref, me, 4)
    picked = words.pick(back_target)
    high_mix, low_mix = split(dot_nt(low, all_join_ref[...]))
    summary_ref[me] = dot(picked, high_mix) + dot(picked, low_mix)
    copies = []
    for slot, peer in enumerate(peers):
        copies.append(remote(summary_ref.at[me], summary_ref.at[me], sems, 13 + slot, peer))
        copies[-1].start()
    for copy in join_copies:
        copy.wait_recv()
    join_sum_ref[...] = (
        join_part_ref[far].astype(F32) + join_near_ref[1].astype(F32)
    ).astype(BF16)
    join_copy = remote(join_sum_ref, join_far_ref, sems, 21, far)
    join_copy.start()
    for chain in weight_chains:
        chain.step()
    for chain in late_chains:
        chain.step()
    table = words.table()
    word_grad = dot(table, high_mix) + dot(table, low_mix)
    pooled = pooled_ref[...]
    tap_rows = [jnp.sum(pooled * word_grad, axis=0, keepdims=True)]
    for lag in range(1, 4):
        tap_rows.append(jnp.sum(pltpu.roll(pooled, lag, 0) * word_grad, axis=0, keepdims=True))
    tap_rows += [gain_grad, ffn_gain_grad_ref[0:1], jnp.zeros((2, model), F32)]
    small_near_ref[me] = jnp.concatenate(tap_rows, axis=0)
    for slot, peer in enumerate(peers):
        copies.append(remote(small_near_ref.at[me], small_near_ref.at[me], sems, 18 + slot, peer))
        copies[-1].start()
    shipped = []

    def ship(source, target):
        copy = pltpu.make_async_copy(source, target, ship_ref.at[len(shipped)])
        copy.start()
        shipped.append(copy)

    def write_weights(span, values):
        weight_total_ref[span, :] = values

    def write_late(span, values):
        joint_total_ref[span, :] = values

    def write_join(span, values):
        join_total_ref[span, :] = values

    bias_copies, small_copies = [], []

    def exchange(index, copies, ours, theirs, slot):
        stride = strides[index]
        copies.append(
            remote(
                ours.at[index],
                theirs.at[index],
                sems,
                slot + 2 * index,
                lambda: partner(stride),
                axis="dp",
            )
        )
        copies[-1].start()

    def pass_on(index, copies, ours, theirs, slot):
        copies[index].wait_recv()
        total = ours[index] + theirs[index]
        if index + 1 < len(strides):
            ours[index + 1] = total
            exchange(index + 1, copies, ours, theirs, slot)
        return total

    bias_parts = (bias_copies, bias_ref, bias_in_ref, 23)
    small_parts = (small_copies, small_ref, small_in_ref, 22)
    bias_ref[0] = bias_grad_rows(table_grad_ref, bucket_ref, buckets)
    exchange(0, *bias_parts)
    join_copy.wait_recv()
    join_ref[...] = (
        join_part_ref[me].astype(F32) + join_near_ref[0].astype(F32) + join_far_ref[...].astype(F32)
    ).astype(BF16)
    for chain in join_chains:
        chain.step(write_join)
    for copy in copies:
        copy.wait_recv()
    small = small_near_ref[0]
    for rank in range(1, 4):
        small = small + small_near_ref[rank]
    small_ref[0] = small
    exchange(0, *small_parts)
    for chain in late_chains:
        chain.step()
    word_grad = word_grad + dot(words.place(back_target, back_valid), stacked(summary_ref))
    taps = all_taps_ref[...]
    height = word_grad.shape[0]
    pooled_grad = word_grad * taps[0:1]
    for lag in range(1, 4):
        pooled_grad = pooled_grad + pltpu.roll(word_grad, height - lag, 0) * taps[lag : lag + 1]
    divisor = divisor_ref[...]
    pooled_grad = pooled_grad / jnp.concatenate([divisor] * (model // LANES), axis=1)
    high, low = split(pooled_grad)
    input_grad = residual_grad + (dot_tn(table, high) + dot_tn(table, low))
    input_grad_ref[...] = input_grad[:, None, :]
    ship(input_grad_ref, input_grad_out)
    bias = pass_on(0, *bias_parts)
    small = pass_on(0, *small_parts)
    for chain in join_chains:
        chain.step(write_join)
    made_copy.wait_recv()
    states_out_ref[...] = (states_part_ref[...] + made_in_ref[...].astype(F32))[:, None, :]
    ship(states_out_ref, states_out_out)
    for chain in weight_chains:
        while chain.at < chain.steps:
            chain.step(write_weights)
    ship(weight_total_ref, weight_total_out)
    for chain in late_chains:
        chain.step()
    bias = pass_on(1, *bias_parts)
    small = pass_on(1, *small_parts)
    for chain in join_chains:
        chain.step(write_join)
    for turn in range(1, len(strides) + 1):
        for group, finish in ((join_chains, write_join), (late_chains, write_late)):
            for chain in group:
                if chain.at < chain.steps:
                    chain.step(finish)
        if 1 < turn < len(strides):
            bias = pass_on(turn, *bias_parts)
            small = pass_on(turn, *small_parts)
    for chain in join_chains:
        while chain.at < chain.steps:
            chain.step(write_join)
    for chain in late_chains:
        while chain.at < chain.steps:
            chain.step(write_late)
    ship(joint_total_ref, joint_total_out)
    own = jnp.zeros((8, share), F32)
    for rank in range(4):
        own = jnp.where(me == rank, small[:, rank * share : (rank + 1) * share], own)
    taps_total_ref[...] = own
    gains_total_ref[...] = small
    bias_total_ref[...] = bias
    out_total_ref[...] = joint_total_ref[:, 3 * inner :].T
    for copy in shipped:
        copy.wait()
    finished = gradient_copies + out_copies + core_copies + [chip_copy, made_copy, out_copy]
    for copy in finished + copies + join_copies + [join_copy] + small_copies + bias_copies:
        copy.wait_send()


def place_kernel(
    joint_hbm,
    weight_hbm,
    states_hbm,
    input_hbm,
    out_hbm,
    join_hbm,
    taps_ref,
    gains_ref,
    bias_ref,
    states_out,
    input_out,
    two_out,
    three_out,
    four_out,
    join_out,
    norm_out,
    query_out,
    key_out,
    value_out,
    bias_out,
    out_out,
    ffn_out,
    gate_out,
    up_out,
    down_out,
    joint_ref,
    weight_ref,
    states_ref,
    input_ref,
    out_ref,
    join_ref,
    sems,
):
    loads = []
    for source, target in (
        (weight_hbm, weight_ref),
        (states_hbm, states_ref),
        (input_hbm, input_ref),
        (joint_hbm, joint_ref),
        (out_hbm, out_ref),
        (join_hbm, join_ref),
    ):
        loads.append(pltpu.make_async_copy(source, target, sems.at[10 + len(loads)]))
        loads[-1].start()
    inner, model = query_out.shape[1], gate_out.shape[0]
    pairs = [
        (weight_ref.at[pl.ds(index * model, model), :], target, 0)
        for index, target in enumerate((gate_out, up_out, down_out))
    ]
    pairs += [(states_ref, states_out, 1), (input_ref, input_out, 2)]
    pairs += [
        (joint_ref.at[:, pl.ds(index * inner, inner)], target, 3)
        for index, target in enumerate((query_out, key_out, value_out))
    ]
    pairs += [(out_ref, out_out, 4), (join_ref, join_out, 5)]
    copies, arrived = [], -1
    for index, (source, target, load) in enumerate(pairs):
        if load > arrived:
            loads[load].wait()
            arrived = load
        copies.append(pltpu.make_async_copy(source, target, sems.at[index]))
        copies[-1].start()
    two_out[...] = taps_ref[:2]
    three_out[...] = taps_ref[:3]
    four_out[...] = taps_ref[:4]
    norm_out[...] = gains_ref[4:5]
    ffn_out[...] = gains_ref[5:6]
    heads, buckets = bias_out.shape
    bias_out[...] = bias_ref[:heads, :buckets]
    for copy in copies:
        copy.wait()


def shards(
    byte_states,
    word_start,
    bucket_ids,
    conv_two,
    conv_three,
    conv_four,
    join_weight,
    norm_gain,
    query_weight,
    key_weight,
    value_weight,
    position_bias,
    out_weight,
    ffn_gain,
    gate_weight,
    up_weight,
    down_weight,
    out_grad,
):
    rows, batch, model = byte_states.shape
    length = word_start.shape[0]
    buckets, heads = position_bias.shape
    inner = query_weight.shape[1]
    width = inner // heads
    share = join_weight.shape[0]
    hidden = gate_weight.shape[1]
    count = rows + 16
    replicas = lax.axis_size("dp")
    strides = strides_of(replicas)
    states = byte_states.reshape(rows, model)
    grads = out_grad.reshape(rows, model)
    starts = word_start.reshape(length // LANES, LANES)
    span = bucket_ids.shape[0] + 1 - LANES
    made = (
        like((rows, model), F32),
        like((length, model), BF16),
        like((length, inner), BF16),
        like((inner, length), BF16),
        like((heads, length, 2 * width), BF16),
        like((inner, length), BF16),
        like((length, inner), BF16),
        like((heads, span, LANES), F32),
        like((count, LANES), F32),
        like((count, model), F32),
        like((rows, model), BF16),
        like((4 * share, model), BF16),
        like((model, 3 * inner), BF16),
        like((1, span + LANES), jnp.int32),
    )
    (
        residual,
        normed,
        queries,
        queries_t,
        twice_keys,
        keys_t,
        values,
        table,
        divisor,
        pooled,
        mix,
        all_taps,
        all_join,
        joint_weight,
        bucket_row,
        outs,
        totals,
        attended,
        all_out,
        near_gate,
        near_up,
        near_down,
        far_grads,
    ) = pl.pallas_call(
        functools.partial(forward_kernel, width),
        out_shape=(
            *made[:11],
            like((8, model), F32),
            *made[11:],
            like((inner, length), F32),
            like((heads, 1, length), F32),
            like((4, inner, rows), BF16),
            like((4 * inner, model), BF16),
            like(gate_weight.shape, BF16),
            like(up_weight.shape, BF16),
            like(down_weight.shape, BF16),
            like((rows, model), BF16),
        ),
        in_specs=whole(13) + anywhere(4),
        out_specs=anywhere(11) + whole(1) + anywhere(3) + whole(4) + anywhere(4),
        scratch_shapes=[
            *[pltpu.VMEM(part.shape, part.dtype) for part in made],
            pltpu.VMEM((inner, length), BF16),
            pltpu.VMEM((length // LANES, LANES), F32),
            pltpu.VMEM((4, 8, model + LANES), F32),
            pltpu.VMEM((4, 8, share), F32),
            pltpu.VMEM((length, rows), F32),
            pltpu.VMEM((4, inner, rows), BF16),
            pltpu.SemaphoreType.DMA((len(made),)),
            *semaphores(25),
        ],
        compiler_params=params(0),
        name="forward",
    )(
        states,
        starts,
        conv_two,
        conv_three,
        conv_four,
        join_weight,
        norm_gain[None],
        query_weight,
        key_weight,
        value_weight,
        bucket_ids[None],
        position_bias.T,
        out_weight,
        gate_weight,
        up_weight,
        down_weight,
        grads,
    )
    ffn_inputs = (
        grads,
        far_grads,
        gate_weight,
        near_gate,
        up_weight,
        near_up,
        down_weight,
        near_down,
    )
    (
        states_part,
        far_made,
        middle_grad,
        ffn_gain_grad,
        weight_grad,
        out_part,
        grad_stage,
    ) = pl.pallas_call(
        functools.partial(ffn_kernel, replicas),
        out_shape=(
            like((rows, model), F32),
            like((rows, model), BF16),
            like((rows, model), F32),
            like((8, model), F32),
            like((3 * model // 2, hidden), BF16),
            like((4, model, inner), BF16),
            like((4, inner, rows), BF16),
        ),
        in_specs=whole(4) + anywhere(8),
        out_specs=whole(7),
        scratch_shapes=[
            pltpu.VMEM((rows, model), F32),
            pltpu.VMEM((2, rows, model), BF16),
            pltpu.VMEM((2, rows, model), F32),
            pltpu.VMEM((2, rows, model), F32),
            pltpu.VMEM((2, 3, model, hidden), F32),
            pltpu.VMEM((rows, model), BF16),
            pltpu.VMEM((rows, model), BF16),
            pltpu.VMEM((3, model, hidden), BF16),
            pltpu.VMEM((3, model, hidden), BF16),
            pltpu.VMEM((3 * model, hidden), BF16),
            pltpu.VMEM((2, 3 * model // 4, hidden), BF16),
            *[pltpu.VMEM(part.shape, BF16) for part in ffn_inputs],
            pltpu.SemaphoreType.DMA((len(ffn_inputs),)),
            *semaphores(5),
            *semaphores(2),
        ],
        compiler_params=params(2),
        name="ffn",
    )(
        attended,
        all_out,
        residual,
        ffn_gain[None],
        *ffn_inputs,
    )
    chain_scratch = []
    for _ in range(2):
        chain_scratch += Chain.scratch(3 * model // 2, hidden, len(strides) - 2, True)
    for _ in range(2):
        chain_scratch += Quad.scratch(model // 2, 4 * inner, len(strides) - 3)
    for _ in range(2):
        chain_scratch += Exchange.scratch(share // 2, model, len(strides))
    loaded = (queries_t, queries, twice_keys, keys_t, values, outs, table)
    loaded += (normed, residual, middle_grad, divisor, pooled, mix, all_join, states_part)
    (
        input_grad,
        out_states,
        weight_total,
        joint_total,
        out_total,
        join_total,
        taps_total,
        gains_total,
        bias_total,
    ) = pl.pallas_call(
        functools.partial(back_kernel, width, replicas, buckets),
        out_shape=(
            like((rows, 1, model), F32),
            like((rows, 1, model), F32),
            like((3 * model, hidden), F32),
            like((model, 4 * inner), F32),
            like((inner, model), F32),
            like((share, model), F32),
            like((8, share), F32),
            like((8, model), F32),
            like((8, LANES), F32),
        ),
        in_specs=whole(11) + anywhere(len(loaded)),
        out_specs=anywhere(4) + whole(5),
        scratch_shapes=[
            *[pltpu.VMEM(part.shape, part.dtype) for part in loaded],
            pltpu.SemaphoreType.DMA((len(loaded),)),
            pltpu.VMEM((4, inner, rows), BF16),
            pltpu.VMEM((length, inner), BF16),
            pltpu.VMEM((inner, length), F32),
            pltpu.VMEM((length, inner), F32),
            pltpu.VMEM((length, inner), F32),
            pltpu.VMEM((heads, span, LANES), F32),
            pltpu.VMEM((length, 3 * inner), BF16),
            pltpu.VMEM((2, rows, model), BF16),
            pltpu.VMEM((2, rows, model), BF16),
            pltpu.VMEM((rows, model), BF16),
            pltpu.VMEM((rows, model), BF16),
            pltpu.VMEM((rows, model), BF16),
            pltpu.VMEM((2, model, inner), BF16),
            pltpu.VMEM((model, inner), BF16),
            pltpu.VMEM((model, inner), BF16),
            pltpu.VMEM((model, 4 * inner), BF16),
            pltpu.VMEM((length // LANES, LANES), F32),
            pltpu.VMEM((4, 8, model), F32),
            pltpu.VMEM((4, share, model), BF16),
            pltpu.VMEM((2, share, model), BF16),
            pltpu.VMEM((share, model), BF16),
            pltpu.VMEM((share, model), BF16),
            pltpu.VMEM((share, model), BF16),
            pltpu.VMEM((4, 8, model), F32),
            pltpu.VMEM((len(strides), 8, model), F32),
            pltpu.VMEM((len(strides), 8, model), F32),
            pltpu.VMEM((len(strides), 8, LANES), F32),
            pltpu.VMEM((len(strides), 8, LANES), F32),
            pltpu.VMEM((rows, 1, model), F32),
            pltpu.VMEM((rows, 1, model), F32),
            pltpu.VMEM((3 * model, hidden), F32),
            pltpu.VMEM((model, 4 * inner), F32),
            pltpu.SemaphoreType.DMA((4,)),
            *semaphores(22 + 2 * len(strides)),
            *semaphores(2 * Chain.slots(strides) + 2 * Quad.slots(strides) + 2 * len(strides)),
            *chain_scratch,
        ],
        compiler_params=params(3),
        name="back",
    )(
        grad_stage,
        totals,
        joint_weight,
        bucket_row,
        norm_gain[None],
        starts,
        all_taps,
        weight_grad,
        out_part,
        far_made,
        ffn_gain_grad,
        *loaded,
    )
    placed = pl.pallas_call(
        place_kernel,
        out_shape=(
            like((rows, 1, model), F32),
            like((rows, 1, model), F32),
            like(conv_two.shape, F32),
            like(conv_three.shape, F32),
            like(conv_four.shape, F32),
            like((share, model), F32),
            like((1, model), F32),
            like((model, inner), F32),
            like((model, inner), F32),
            like((model, inner), F32),
            like((heads, buckets), F32),
            like((inner, model), F32),
            like((1, model), F32),
            like((model, hidden), F32),
            like((model, hidden), F32),
            like((hidden, model), F32),
        ),
        in_specs=anywhere(6) + whole(3),
        out_specs=anywhere(2)
        + whole(3)
        + anywhere(1)
        + whole(1)
        + anywhere(3)
        + whole(1)
        + anywhere(1)
        + whole(1)
        + anywhere(3),
        scratch_shapes=[
            *[
                pltpu.VMEM(part.shape, F32)
                for part in (joint_total, weight_total, out_states, input_grad, out_total, join_total)
            ],
            pltpu.SemaphoreType.DMA((16,)),
        ],
        compiler_params=params(),
        name="place",
    )(
        joint_total,
        weight_total,
        out_states,
        input_grad,
        out_total,
        join_total,
        taps_total,
        gains_total,
        bias_total,
    )
    placed = list(placed)
    placed[6], placed[10], placed[12] = placed[6][0], placed[10].T, placed[12][0]
    return tuple(placed)


def solution(mesh):
    return jax.shard_map(
        shards,
        mesh=mesh,
        in_specs=(
            P("mp", "dp", None),
            P(None, "dp"),
            P(),
            P(None, "mp"),
            P(None, "mp"),
            P(None, "mp"),
            P("mp", None),
            P(),
            P(None, "mp"),
            P(None, "mp"),
            P(None, "mp"),
            P(None, "mp"),
            P("mp", None),
            P(),
            P(None, "mp"),
            P(None, "mp"),
            P("mp", None),
            P("mp", "dp", None),
        ),
        out_specs=(
            P("mp", "dp", None),
            P("mp", "dp", None),
            P(None, "mp"),
            P(None, "mp"),
            P(None, "mp"),
            P("mp", None),
            P(),
            P(None, "mp"),
            P(None, "mp"),
            P(None, "mp"),
            P(None, "mp"),
            P("mp", None),
            P(),
            P(None, "mp"),
            P(None, "mp"),
            P("mp", None),
        ),
        check_vma=False,
    )
```

```python
import functools

import jax
import jax.numpy as jnp
from jax import lax
from jax.experimental import pallas as pl
from jax.experimental.pallas import tpu as pltpu
from jax.sharding import PartitionSpec as P

EPSILON = 1e-06
LOG2E = 1.4426950408889634
GELU_SCALE = 0.7978845608028654
GELU_CUBE = 0.044715
F32 = jnp.float32
BF16 = jnp.bfloat16
LANES = 128
HALO = 3
VMEM_LIMIT = 56 << 20
MESH = pl.DeviceIdType.MESH


def whole(count):
    return [pl.BlockSpec(memory_space=pltpu.VMEM)] * count


def anywhere(count):
    return [pl.BlockSpec(memory_space=pl.ANY)] * count


def params(collective=None):
    return pltpu.CompilerParams(
        vmem_limit_bytes=VMEM_LIMIT, collective_id=collective, has_side_effects=collective is not None
    )


def like(shape, dtype):
    return jax.ShapeDtypeStruct(shape, dtype)


def dot(lhs, rhs):
    return jnp.dot(lhs, rhs, preferred_element_type=F32)


def dot_nt(lhs, rhs):
    return lax.dot_general(lhs, rhs, (((1,), (1,)), ((), ())), preferred_element_type=F32)


def dot_tn(lhs, rhs):
    return lax.dot_general(lhs, rhs, (((0,), (0,)), ((), ())), preferred_element_type=F32)


def split(values):
    high = values.astype(BF16)
    return high, (values - high.astype(F32)).astype(BF16)


def turned(values):
    return values.astype(F32).T.astype(BF16)


def ranks():
    me = lax.axis_index("mp")
    near = me + 1 - 2 * (me % 2)
    return me, near, (me + 2) % 4, (near + 2) % 4


def greet(peers, strides=()):
    barrier = pltpu.get_barrier_semaphore()
    for peer in peers:
        pl.semaphore_signal(barrier, inc=1, device_id={"mp": peer}, device_id_type=MESH)
    for stride in strides:
        pl.semaphore_signal(barrier, inc=1, device_id={"dp": partner(stride)}, device_id_type=MESH)


def greeted(peers, strides=()):
    pl.semaphore_wait(pltpu.get_barrier_semaphore(), len(peers) + len(strides))


def load_all(pairs, sems):
    copies = []
    for source, target in pairs:
        copies.append(pltpu.make_async_copy(source, target, sems.at[len(copies)]))
        copies[-1].start()
    return copies


def side_of(stride):
    return (lax.axis_index("dp") // stride) % 2


def partner(stride):
    return lax.axis_index("dp") + stride - 2 * stride * side_of(stride)


def strides_of(count):
    strides = []
    while 2 ** len(strides) < count:
        strides.append(2 ** len(strides))
    return strides


class remote:
    def __init__(self, *given, axis="mp"):
        self.given, self.axis = given, axis

    def start(self):
        described(*self.given, self.axis).start()

    def wait_recv(self):
        described(*self.given, self.axis).wait_recv()

    def wait_send(self):
        described(*self.given, self.axis).wait_send()

    def wait(self):
        described(*self.given, self.axis).wait()


def described(source, target, sems, slot, peer, axis):
    source, target, peer = [part() if callable(part) else part for part in (source, target, peer)]
    sends, receives = sems
    return pltpu.make_async_remote_copy(
        src_ref=source,
        dst_ref=target,
        send_sem=sends.at[slot],
        recv_sem=receives.at[slot],
        device_id={axis: peer},
        device_id_type=MESH,
    )


def semaphores(count):
    return [pltpu.SemaphoreType.DMA((count,)), pltpu.SemaphoreType.DMA((count,))]


class Quad:
    def __init__(self, source_ref, base, rows, strides, scratch, sems, first_slot):
        self.source, self.base, self.rows, self.strides = source_ref, base, rows, strides
        self.half_in, self.half, self.pieces_in, self.pieces, self.others_in, self.gathered, self.far_half = scratch
        self.sems, self.slot, self.at = sems, first_slot, 0
        self.copies, self.count = [], 0
        self.steps = len(strides) + 2

    @staticmethod
    def scratch(rows, width, exchanges):
        half, piece = rows // 2, rows // 8
        return [
            pltpu.VMEM((half, width), BF16),
            pltpu.VMEM((half, width), BF16),
            pltpu.VMEM((3, piece, width), BF16),
            pltpu.VMEM((exchanges + 1, piece, width), BF16),
            pltpu.VMEM((exchanges + 1, piece, width), BF16),
            pltpu.VMEM((3, piece, width), BF16),
            pltpu.VMEM((half, width), BF16),
        ]

    @staticmethod
    def slots(strides):
        return len(strides) + 6

    def send(self, source, target, peer):
        copy = remote(source, target, self.sems, self.slot + self.count, peer, axis="dp")
        copy.start()
        self.copies.append(copy)
        self.count += 1

    def away(self, turn):
        first, second = self.strides[1:3]
        flips = (turn % 2, turn // 2)
        device, place = lax.axis_index("dp"), 0
        for flip, stride, weight in zip(flips, (first, second), (1, 2)):
            side = side_of(stride)
            device = device + flip * (stride - 2 * stride * side)
            place = place + weight * (side + flip * (1 - 2 * side))
        return device, place

    def piece(self, turn):
        height = self.rows // 8
        return pl.ds(pl.multiple_of(self.away(turn)[1] * height, 16), height)

    def step(self, finish=None):
        at, half = self.at, self.rows // 2
        first, others = self.strides[0], self.strides[3:]
        self.at += 1
        for copy in self.copies:
            copy.wait_recv()
        done, self.copies = self.copies, []
        if at == 0:
            begin = pl.multiple_of(self.base + (1 - side_of(first)) * half, 16)
            self.send(self.source.at[pl.ds(begin, half), :], self.half_in, partner(first))
        elif at == 1:
            begin = pl.multiple_of(self.base + side_of(first) * half, 16)
            mine = self.source[pl.ds(begin, half), :].astype(F32)
            self.half[...] = (mine + self.half_in[...].astype(F32)).astype(BF16)
            for turn in range(1, 4):
                part = self.half.at[self.piece(turn), :]
                self.send(part, self.pieces_in.at[turn - 1], self.away(turn)[0])
        elif at <= 2 + len(others):
            if at == 2:
                total = self.half[self.piece(0), :].astype(F32)
                for turn in range(1, 4):
                    total = total + self.pieces_in[turn - 1].astype(F32)
            else:
                total = self.pieces[at - 3].astype(F32) + self.others_in[at - 3].astype(F32)
            self.pieces[at - 2] = total.astype(BF16)
            if at < 2 + len(others):
                stride = others[at - 2]
                self.send(self.pieces.at[at - 2], self.others_in.at[at - 2], partner(stride))
            else:
                for turn in range(1, 4):
                    self.send(self.pieces.at[at - 2], self.gathered.at[turn - 1], self.away(turn)[0])
        elif at == 3 + len(others):
            self.half[self.piece(0), :] = self.pieces[len(others)]
            for turn in range(1, 4):
                self.half[self.piece(turn), :] = self.gathered[turn - 1]
            self.send(self.half, self.far_half, partner(first))
        else:
            side = side_of(first)
            mine = pl.ds(pl.multiple_of(self.base + side * half, 16), half)
            other = pl.ds(pl.multiple_of(self.base + (1 - side) * half, 16), half)
            finish(mine, self.half[...].astype(F32))
            finish(other, self.far_half[...].astype(F32))
        for copy in done:
            copy.wait_send()


class Exchange:
    def __init__(self, source_ref, base, rows, strides, scratch, sems, first_slot):
        self.source, self.base, self.rows, self.strides = source_ref, base, rows, strides
        self.ours, self.theirs = scratch
        self.sems, self.slot, self.at = sems, first_slot, 0
        self.copies = []
        self.steps = len(strides) + 1

    @staticmethod
    def scratch(rows, width, strides):
        return [pltpu.VMEM((strides, rows, width), BF16)] * 2

    def step(self, finish=None):
        at = self.at
        self.at += 1
        if at == 0:
            total = self.source[self.base : self.base + self.rows, :].astype(F32)
        else:
            self.copies[-1].wait_recv()
            total = self.ours[at - 1].astype(F32) + self.theirs[at - 1].astype(F32)
        if at < len(self.strides):
            self.ours[at] = total.astype(BF16)
            stride = self.strides[at]
            copy = remote(
                lambda: self.ours.at[at],
                lambda: self.theirs.at[at],
                self.sems,
                self.slot + at,
                lambda: partner(stride),
                axis="dp",
            )
            copy.start()
            self.copies.append(copy)
        else:
            finish(slice(self.base, self.base + self.rows), total)
            for copy in self.copies:
                copy.wait_send()


class Chain:
    def __init__(self, source_ref, base, rows, strides, scratch, sems, first_slot):
        self.source, self.base, self.rows, self.strides = source_ref, base, rows, strides
        (
            self.half_in,
            self.half,
            self.quarter_in,
            self.quarter,
            self.whole_quarter,
            self.gathered_quarter,
            self.both,
            self.gathered_half,
        ) = scratch
        self.sems, self.slot, self.at = sems, first_slot, 0
        self.copies = []
        self.steps = len(strides) + 3
        self.half_base = 0

    def halved(self, half_ref, base):
        self.half, self.half_base, self.at = half_ref, base, 1
        return self

    @staticmethod
    def scratch(rows, width, exchanges, halved=False):
        half, quarter = (rows // 2, width), (rows // 4, width)
        first = (16, LANES) if halved else half
        return [
            pltpu.VMEM(first, BF16),
            pltpu.VMEM(first, BF16),
            pltpu.VMEM((exchanges + 1, *quarter), BF16),
            pltpu.VMEM((exchanges, *quarter), BF16),
            pltpu.VMEM(quarter, BF16),
            pltpu.VMEM(quarter, BF16),
            pltpu.VMEM(half, BF16),
            pltpu.VMEM(half, BF16),
        ]

    @staticmethod
    def slots(strides):
        return len(strides) + 2

    def send(self, source, target, stride):
        copy = remote(
            source, target, self.sems, self.slot + len(self.copies), lambda: partner(stride), axis="dp"
        )
        copy.start()
        self.copies.append(copy)

    def step(self, finish=None):
        first, second, others = self.strides[0], self.strides[1], self.strides[2:]
        half, quarter = self.rows // 2, self.rows // 4
        at = self.at
        self.at += 1
        if self.copies:
            self.copies[-1].wait_recv()
        if at == 0:
            self.send(lambda: self.source.at[pl.ds(pl.multiple_of(self.base + (1 - side_of(first)) * half, 16), half), :], self.half_in, first)
        elif at == 1:
            if self.copies:
                begin = pl.multiple_of(self.base + side_of(first) * half, 16)
                mine = self.source[pl.ds(begin, half), :].astype(F32)
                self.half[...] = (mine + self.half_in[...].astype(F32)).astype(BF16)
            self.send(lambda: self.half.at[
                    pl.ds(
                        pl.multiple_of(self.half_base + (1 - side_of(second)) * quarter, 16), quarter
                    ),
                    :,
                ], lambda: self.quarter_in.at[0], second)
        elif at <= 1 + len(others):
            if at == 2:
                begin = pl.multiple_of(self.half_base + side_of(second) * quarter, 16)
                mine = self.half[pl.ds(begin, quarter), :]
            else:
                mine = self.quarter[at - 3]
            total = mine.astype(F32) + self.quarter_in[at - 2].astype(F32)
            self.quarter[at - 2] = total.astype(BF16)
            self.send(
                lambda: self.quarter.at[at - 2], lambda: self.quarter_in.at[at - 1], others[at - 2]
            )
        elif at == 2 + len(others):
            total = self.quarter[at - 3].astype(F32) + self.quarter_in[at - 2].astype(F32)
            self.whole_quarter[...] = total.astype(BF16)
            self.send(self.whole_quarter, self.gathered_quarter, second)
        elif at == 3 + len(others):
            side = side_of(second)
            mine = pl.ds(pl.multiple_of(side * quarter, 16), quarter)
            other = pl.ds(pl.multiple_of((1 - side) * quarter, 16), quarter)
            self.both[mine, :] = self.whole_quarter[...]
            self.both[other, :] = self.gathered_quarter[...]
            self.send(self.both, self.gathered_half, first)
        else:
            side = side_of(first)
            mine = pl.ds(pl.multiple_of(self.base + side * half, 16), half)
            other = pl.ds(pl.multiple_of(self.base + (1 - side) * half, 16), half)
            finish(mine, self.both[...].astype(F32))
            finish(other, self.gathered_half[...].astype(F32))
            for copy in self.copies:
                copy.wait_send()


def rms(values, gain):
    return values * lax.rsqrt(jnp.mean(values * values, axis=1, keepdims=True) + EPSILON) * gain


def rms_back(grads, values, gain):
    scale = lax.rsqrt(jnp.mean(values * values, axis=1, keepdims=True) + EPSILON)
    gain_grad = jnp.sum(grads * values * scale, axis=0, keepdims=True)
    raised = grads * gain
    mean = jnp.mean(raised * values, axis=1, keepdims=True)
    return scale * raised - values * (scale * scale * scale * mean), gain_grad


def bucket_hits(bucket_ref, buckets):
    span = bucket_ref.shape[1]
    rows = lax.broadcasted_iota(jnp.int32, (buckets, span), 0)
    return rows == jnp.broadcast_to(bucket_ref[...], (buckets, span))


def fill_bias_table(bucket_ref, bias_ref, table_ref):
    span = bucket_ref.shape[1]
    heads, buckets = bias_ref.shape
    hits = bucket_hits(bucket_ref, buckets).astype(F32).astype(BF16)
    bias = bias_ref[...]
    first = bias.astype(BF16)
    second, third = split(bias - first.astype(F32))
    rows = jnp.concatenate([first, second, third, jnp.zeros((16 - 3 * heads, buckets), BF16)], axis=0)
    lines = dot(rows, hits)
    for head in range(heads):
        line = lines[head : head + 1] + (
            lines[heads + head : heads + head + 1] + lines[2 * heads + head : 2 * heads + head + 1]
        )
        skew = pltpu.roll(
            jnp.broadcast_to(line * LOG2E, (LANES, span)), span - LANES + 1, 1, stride=1, stride_axis=0
        )
        for block in range(span // LANES - 1):
            cut = slice(block * LANES, (block + 1) * LANES)
            table_ref[head, cut, :] = skew[:, cut].T


def bias_grad_rows(table_ref, bucket_ref, buckets):
    span = bucket_ref.shape[1]
    heads = table_ref.shape[0]
    hits = bucket_hits(bucket_ref, buckets).astype(F32).astype(BF16)
    lines = []
    for head in range(heads):
        blocks = [
            table_ref[head, block * LANES : (block + 1) * LANES, :].T
            for block in range(span // LANES - 1)
        ]
        skew = jnp.concatenate(blocks + [jnp.zeros((LANES, LANES), F32)], axis=1)
        rows = LANES // 2
        while rows >= 8:
            skew = skew[:rows] + pltpu.roll(skew[rows:], span - rows, 1)
            rows //= 2
        line = jnp.zeros((1, span), F32)
        for row in range(8):
            line = line + pltpu.roll(skew[row : row + 1], LANES - 1 - row, 1)
        lines.append(line)
    lines = jnp.concatenate(lines + [jnp.zeros((8 - heads, span), F32)], axis=0)
    first = lines.astype(BF16)
    second, third = split(lines - first.astype(F32))
    parts = dot_nt(jnp.concatenate([first.astype(F32), second.astype(F32)], axis=0).astype(BF16), hits)
    rest = dot_nt(jnp.concatenate([third.astype(F32), jnp.zeros((8, span), F32)], axis=0).astype(BF16), hits)
    made = parts[:8] + (parts[8:] + rest[:8])
    return jnp.concatenate([made, jnp.zeros((8, LANES - buckets), F32)], axis=1)


def word_numbers(starts):
    rows = starts.shape[0]
    upper = lax.broadcasted_iota(jnp.int32, (LANES, LANES), 0) <= lax.broadcasted_iota(
        jnp.int32, (LANES, LANES), 1
    )
    within = dot(starts.astype(F32).astype(BF16), upper.astype(F32).astype(BF16))
    totals = jnp.broadcast_to(within[:, LANES - 1 :], (rows, LANES)).astype(BF16)
    lower = lax.broadcasted_iota(jnp.int32, (rows, rows), 1) < lax.broadcasted_iota(
        jnp.int32, (rows, rows), 0
    )
    return within + dot(lower.astype(F32).astype(BF16), totals) - 1.0


class Words:
    def __init__(self, starts_ref, ids_ref, me, ranks_count):
        ids = word_numbers(starts_ref[...])
        ids_ref[...] = ids
        per = ids.shape[0] // ranks_count
        self.firsts = [ids[per * rank : per * rank + 1, 0:1] for rank in range(ranks_count)]
        self.lasts = [
            ids[per * (rank + 1) - 1 : per * (rank + 1), LANES - 1 :] for rank in range(ranks_count)
        ]
        pieces = [ids_ref[pl.ds(me * per + piece, 1), :] for piece in range(per)]
        self.row = jnp.concatenate(pieces, axis=1)
        self.first = self.row[:, 0:1]
        self.last = self.row[:, per * LANES - 1 :]
        self.me = me
        self.count = per * LANES

    def table(self):
        shape = (self.count + 16, self.count)
        rows = lax.broadcasted_iota(jnp.int32, shape, 0).astype(F32)
        return (rows == self.row - self.first + HALO).astype(F32).astype(BF16)

    def pick(self, target):
        slots = lax.broadcasted_iota(jnp.int32, (8, 1), 0)
        hits = target(slots, self.first, self.last) == self.row
        return hits.astype(F32).astype(BF16)

    def place(self, target, valid):
        width = 2 * LANES
        lane = lax.broadcasted_iota(jnp.int32, (1, width), 1) % LANES
        slots, rank = lane % 8, lane // 8
        goal = jnp.full((1, width), -9.0, F32)
        for index, (first, last) in enumerate(zip(self.firsts, self.lasts)):
            goal = jnp.where(rank == index, target(slots, first, last), goal)
        known = valid(slots, rank, self.me) & (rank < len(self.firsts))
        goal = jnp.where(known, goal - self.first + HALO, -1.0)
        rows = lax.broadcasted_iota(jnp.int32, (self.count + 16, width), 0).astype(F32)
        return (rows == goal).astype(F32).astype(BF16)


def stacked(summary_ref):
    parts = [summary_ref[rank] for rank in range(summary_ref.shape[0])]
    rest = LANES - sum(part.shape[0] for part in parts)
    parts.append(jnp.zeros((rest, parts[0].shape[1]), F32))
    return jnp.concatenate(split(jnp.concatenate(parts, axis=0)), axis=0)


def ahead_target(slots, first, last):
    later = jnp.where(slots <= 4, last - (slots - 1).astype(F32), -9.0)
    return jnp.where(slots == 0, first, later)


def ahead_valid(slots, rank, me):
    return ((rank < me) & (slots >= 1) & (slots <= 4)) | ((rank > me) & (slots == 0))


def back_target(slots, first, last):
    return jnp.where(slots <= 3, first + slots.astype(F32), jnp.where(slots == 4, last, -9.0))


def back_valid(slots, rank, me):
    return ((rank > me) & (slots <= 3)) | ((rank < me) & (slots == 4))


def forward_kernel(
    width,
    states_ref,
    starts_ref,
    two_ref,
    three_ref,
    four_ref,
    join_ref,
    gain_ref,
    query_weight_ref,
    key_weight_ref,
    value_weight_ref,
    bucket_ref,
    bias_ref,
    out_weight_ref,
    gate_ref,
    up_ref,
    down_ref,
    grad_ref,
    residual_out,
    normed_out,
    query_out,
    query_t_out,
    twice_out,
    key_t_out,
    value_out,
    table_out,
    divisor_out,
    pooled_out,
    mix_out,
    all_taps_ref,
    all_join_out,
    joint_out,
    padded_out,
    out_ref,
    total_ref,
    attended_ref,
    all_out_ref,
    near_gate_ref,
    near_up_ref,
    near_down_ref,
    far_grad_ref,
    residual_ref,
    normed_ref,
    query_ref,
    query_t_ref,
    twice_ref,
    key_t_ref,
    value_ref,
    table_ref,
    divisor_ref,
    pooled_ref,
    mix_ref,
    all_join_ref,
    joint_ref,
    padded_ref,
    value_t_ref,
    ids_ref,
    summary_ref,
    taps_in_ref,
    score_ref,
    sum_ref,
    stage_ref,
    ship_ref,
    *sems,
):
    me, near, far, cross = ranks()
    peers = (near, far, cross)
    rows, model = states_ref.shape
    share = join_ref.shape[0]
    inner = query_weight_ref.shape[1]
    heads, length = twice_ref.shape[0], twice_ref.shape[1]
    shipped = []

    def ship(source, target):
        copy = pltpu.make_async_copy(source, target, ship_ref.at[len(shipped)])
        copy.start()
        shipped.append(copy)

    def band(ref, rank):
        return ref.at[pl.ds(pl.multiple_of(rank * share, share), share), :]

    greet(peers)
    words = Words(starts_ref, ids_ref, me, 4)
    states = states_ref[...]
    wide_states = jnp.concatenate([states, jnp.ones((rows, LANES), BF16)], axis=1)
    summary_ref[me] = dot(words.pick(ahead_target), wide_states)
    two, three, four = two_ref[...], three_ref[...], four_ref[...]
    taps_in_ref[me] = jnp.concatenate(
        [
            two[0:1] + three[0:1] + four[0:1],
            two[1:2] + three[1:2] + four[1:2],
            three[2:3] + four[2:3],
            four[3:4],
            jnp.zeros((4, share), F32),
        ],
        axis=0,
    )
    all_join_ref[pl.ds(pl.multiple_of(me * share, share), share), :] = join_ref[...]
    all_out_ref[pl.ds(pl.multiple_of(me * share, share), share), :] = out_weight_ref[...]
    greeted(peers)
    early = []
    for slot, peer in enumerate(peers):
        early.append(remote(summary_ref.at[me], summary_ref.at[me], sems, slot, peer))
        early.append(remote(taps_in_ref.at[me], taps_in_ref.at[me], sems, 3 + slot, peer))
    joins = [
        remote(band(all_join_ref, me), band(all_join_ref, me), sems, 6, far),
        remote(band(all_join_ref, me), band(all_join_ref, me), sems, 7, near),
    ]
    middle = rows // 2
    first_grads = remote(
        grad_ref.at[pl.ds(0, middle)], far_grad_ref.at[pl.ds(0, middle)], sems, 25, far
    )
    for copy in early + joins + [first_grads]:
        copy.start()
    padded_ref[...] = jnp.full(padded_ref.shape, -1, jnp.int32)
    padded_ref[:, : bucket_ref.shape[1]] = bucket_ref[...]
    joint_ref[:, :inner] = query_weight_ref[...]
    joint_ref[:, inner : 2 * inner] = key_weight_ref[...]
    joint_ref[:, 2 * inner :] = value_weight_ref[...]
    ship(joint_ref, joint_out)
    ship(padded_ref, padded_out)
    table = words.table()
    sums = dot(table, wide_states)
    place = words.place(ahead_target, ahead_valid)
    for copy in early:
        copy.wait_recv()
    sums = sums + dot(place, stacked(summary_ref))
    divisor = jnp.maximum(sums[:, model:], 1.0)
    divisor_ref[...] = divisor
    ship(divisor_ref, divisor_out)
    pooled = sums[:, :model] / jnp.concatenate([divisor] * (model // LANES), axis=1)
    pooled_ref[...] = pooled
    ship(pooled_ref, pooled_out)
    taps = jnp.concatenate([taps_in_ref[rank] for rank in range(4)], axis=1)
    all_taps_ref[...] = taps
    joins[0].wait_recv()
    joins.append(remote(band(all_join_ref, far), band(all_join_ref, far), sems, 8, near))
    joins[2].start()
    total = pooled * taps[0:1]
    for lag in range(1, 4):
        total = total + pltpu.roll(pooled, lag, 0) * taps[lag : lag + 1]
    mix = dot_tn(table, total.astype(BF16)).astype(BF16)
    mix_ref[...] = mix
    ship(mix_ref, mix_out)
    joins[1].wait_recv()
    joins[2].wait_recv()
    residual = states.astype(F32) + dot(mix, all_join_ref[...])
    residual_ref[...] = residual
    own = pl.ds(pl.multiple_of(me * rows, rows), rows)
    normed_ref[own, :] = rms(residual, gain_ref[...]).astype(BF16)

    def block(rank, part):
        half = rows // 2
        return normed_ref.at[pl.ds(pl.multiple_of(rank * rows + part * half, half), half), :]

    sends = []
    for part in range(2):
        sends.append(remote(block(me, part), block(me, part), sems, 9 + part, far))
    for part in range(2):
        sends.append(remote(block(me, part), block(me, part), sems, 11 + part, near))
    for copy in sends:
        copy.start()
    copies = [
        remote(
            grad_ref.at[pl.ds(middle, middle)], far_grad_ref.at[pl.ds(middle, middle)], sems, 15, far
        ),
        remote(band(all_out_ref, me), band(all_out_ref, me), sems, 16, near),
        remote(gate_ref, near_gate_ref, sems, 17, near),
        remote(up_ref, near_up_ref, sems, 18, near),
        remote(down_ref, near_down_ref, sems, 19, near),
    ]
    out_far = remote(
        lambda: band(all_out_ref, me), lambda: band(all_out_ref, me), sems, 20, far
    )
    out_pass = remote(
        lambda: band(all_out_ref, far), lambda: band(all_out_ref, far), sems, 21, near
    )
    out_far.start()
    for copy in copies:
        copy.start()
    ship(residual_ref, residual_out)
    ship(all_join_ref, all_join_out)

    def project(rank):
        cut = pl.ds(pl.multiple_of(rank * rows, rows), rows)
        made = dot(normed_ref[cut, :], joint_ref[...])
        query, key, value = [
            made[:, index * inner : (index + 1) * inner].astype(BF16) for index in range(3)
        ]
        query_ref[cut, :] = query
        query_t_ref[:, cut] = turned(query)
        key_t_ref[:, cut] = turned(key)
        value_ref[cut, :] = value
        value_t_ref[:, cut] = turned(value)
        for head in range(heads):
            part = key[:, head * width : (head + 1) * width]
            twice_ref[head, cut, :] = jnp.concatenate([part, part], axis=1)

    project(me)
    fill_bias_table(padded_ref, bias_ref, table_ref)
    ship(table_ref, table_out)
    sends[2].wait_recv()
    sends[3].wait_recv()
    project(near)
    wide = deep = length // 4

    def owner(order):
        chip = (me // 2 + 1 + order // 2) % 2
        core = (me % 2 + (order + 1) // 2) % 2
        return 2 * chip + core

    def handed(order):
        return remote(stage_ref.at[order], attended_ref.at[me], sems, 22 + order, owner(order))

    def half_scores(block, head, chip):
        begin = pl.multiple_of(block * wide, wide)
        start = pl.multiple_of(chip * (length // 2), wide)
        rows = pl.ds(pl.multiple_of(head * width, width), width)
        scaled = query_t_ref[rows, pl.ds(begin, wide)].astype(F32) * LOG2E
        queries = jnp.concatenate(split(scaled), axis=0)
        peak = jnp.full((8, wide), -1e30, F32)
        for part in range(length // 2 // deep):
            keys = pl.ds(pl.multiple_of(start + part * deep, deep), deep)
            raw = dot(twice_ref[head, keys, :], queries)
            columns = []
            for lane in range(0, wide, LANES):
                offset = start + part * deep - begin - lane + length - LANES
                offset = pl.multiple_of(offset, LANES)
                columns.append(raw[:, lane : lane + LANES] + table_ref[head, pl.ds(offset, deep), :])
            scores = jnp.concatenate(columns, axis=1)
            score_ref[part * deep : (part + 1) * deep, :] = scores
            peak = jnp.maximum(peak, jnp.max(scores.reshape(deep // 8, 8, wide), axis=0))
        peak = jnp.max(peak, axis=0, keepdims=True)
        sums = jnp.zeros((8, wide), F32)
        made = jnp.zeros((width, wide), F32)
        for part in range(length // 2 // deep):
            keys = pl.ds(pl.multiple_of(start + part * deep, deep), deep)
            raised = jnp.exp2(score_ref[part * deep : (part + 1) * deep, :] - peak)
            sums = sums + jnp.sum(raised.reshape(deep // 8, 8, wide), axis=0)
            made = made + dot(value_t_ref[rows, keys], raised.astype(BF16))
        return peak, jnp.sum(sums, axis=0, keepdims=True), made

    def early_step(index, carry):
        head = index % heads
        block = 2 * (me // 2) + index // heads
        peak, total, made = half_scores(block, head, me // 2)
        span = pl.ds(pl.multiple_of(block * wide, wide), wide)
        total_ref[head, :, span] = peak
        sum_ref[head, :, span] = total
        out_ref[pl.ds(pl.multiple_of(head * width, width), width), span] = made
        return carry

    lax.fori_loop(0, 2 * heads, early_step, 0)
    passed = []
    for part in range(2):
        sends[part].wait_recv()
        passed.append(remote(block(far, part), block(far, part), sems, 13 + part, near))
        passed[part].start()
    project(far)
    for copy in passed:
        copy.wait_recv()
    project(cross)
    for source, target in (
        (normed_ref, normed_out),
        (query_ref, query_out),
        (query_t_ref, query_t_out),
        (twice_ref, twice_out),
        (key_t_ref, key_t_out),
        (value_ref, value_out),
    ):
        ship(source, target)

    def step(index, carry):
        late = index // (4 * heads)
        rest = index % (4 * heads)
        order = (1 - late) * (rest // (2 * heads)) + late * (2 + rest // heads)
        head = (1 - late) * (rest // 2 % heads) + late * (rest % heads)
        half = (1 - late) * (rest % 2) + late
        block = owner(order)
        peak, total, made = half_scores(block, head, (me // 2 + half) % 2)
        span = pl.ds(pl.multiple_of(block * wide, wide), wide)
        rows = pl.ds(pl.multiple_of(head * width, width), width)

        @pl.when(half == 0)
        def _():
            total_ref[head, :, span] = peak
            sum_ref[head, :, span] = total
            out_ref[rows, span] = made

        @pl.when(half == 1)
        def _():
            before = total_ref[head, :, span]
            top = jnp.maximum(before, peak)
            old, new = jnp.exp2(before - top), jnp.exp2(peak - top)
            all_sum = sum_ref[head, :, span] * old + total * new
            result = (out_ref[rows, span] * old + made * new) / all_sum
            out_ref[rows, span] = result
            total_ref[head, :, span] = top + jnp.log2(all_sum)
            stage_ref[order, rows, :] = result.astype(BF16)

        @pl.when((half == 1) & (head == heads - 1) & (order < 3))
        def _():
            handed(order).start()

        @pl.when(index == 2 * heads)
        def _():
            out_far.wait_recv()
            out_pass.start()

        return carry

    lax.fori_loop(0, 6 * heads, step, 0)
    attended_ref[me] = stage_ref[3]
    for order in range(3):
        handed(order).wait()
    for copy in copies + [first_grads]:
        copy.wait()
    out_pass.wait()
    for copy in early + joins + sends + passed + [out_far]:
        copy.wait_send()
    for copy in shipped:
        copy.wait()


def ffn_kernel(
    count,
    attended_ref,
    all_out_ref,
    residual_ref,
    gain_ref,
    grad_hbm,
    far_grad_hbm,
    gate_hbm,
    near_gate_hbm,
    up_hbm,
    near_up_hbm,
    down_hbm,
    near_down_hbm,
    states_part_ref,
    far_made_ref,
    middle_grad_ref,
    gain_grad_ref,
    weight_half_ref,
    out_part_ref,
    grad_stage_ref,
    middle_ref,
    normed_ref,
    made_ref,
    back_ref,
    sums_ref,
    far_out_ref,
    far_in_ref,
    near_out_ref,
    near_in_ref,
    weight_ref,
    half_in_ref,
    grad_ref,
    far_grad_ref,
    gate_ref,
    near_gate_ref,
    up_ref,
    near_up_ref,
    down_ref,
    near_down_ref,
    load_ref,
    sends_ref,
    receives_ref,
    half_sends_ref,
    half_receives_ref,
):
    me, near, far, cross = ranks()
    sems = (sends_ref, receives_ref)
    strides = strides_of(count)[:2]
    peers = (near, far, cross)
    rows, model = residual_ref.shape
    share = attended_ref.shape[1]
    greet(peers, strides)
    loads = load_all(
        (
            (grad_hbm, grad_ref),
            (far_grad_hbm, far_grad_ref),
            (gate_hbm, gate_ref),
            (near_gate_hbm, near_gate_ref),
            (up_hbm, up_ref),
            (near_up_hbm, near_up_ref),
            (down_hbm, down_ref),
            (near_down_hbm, near_down_ref),
        ),
        load_ref,
    )
    attended = attended_ref[...].reshape(4 * share, rows)
    middle = residual_ref[...] + dot_tn(attended, all_out_ref[...])
    middle_ref[...] = middle
    normed_ref[0] = rms(middle, gain_ref[...]).astype(BF16)
    half = rows // 2
    greeted(peers, strides)
    there, returned = [], []
    for part in range(2):
        cut = pl.ds(part * half, half)
        there.append(remote(normed_ref.at[0, cut], normed_ref.at[1, cut], sems, part, far))
        there[part].start()
        returned.append(remote(far_out_ref.at[cut], far_in_ref.at[cut], sems, 2 + part, far))

    def work(side, cut, grads, gate, up, down, slab, first):
        given = normed_ref[side, cut]
        gate_value = dot(given, gate)
        up_value = dot(given, up)
        hidden_grad = dot_nt(grads, down)
        square = gate_value * gate_value
        curve = jnp.tanh(GELU_SCALE * gate_value * (1.0 + GELU_CUBE * square))
        half = 0.5 + 0.5 * curve
        gelu = gate_value * half
        slope = half + (0.5 * GELU_SCALE) * gate_value * (1.0 - curve * curve) * (
            1.0 + (3.0 * GELU_CUBE) * square
        )
        hidden = (gelu * up_value).astype(BF16)
        gate_back = (hidden_grad * up_value * slope).astype(BF16)
        up_back = (hidden_grad * gelu).astype(BF16)
        sums = [dot_tn(given, gate_back), dot_tn(given, up_back), dot_tn(hidden, grads)]
        for index in range(3):
            if side == 0:
                sums_ref[slab, index] = sums[index]
            else:
                sums_ref[slab, index] += sums[index]
        made = dot(hidden, down)
        back = dot_nt(gate_back, gate) + dot_nt(up_back, up)
        if first:
            made_ref[side, cut] = made
            back_ref[side, cut] = back
        else:
            made_ref[side, cut] += made
            back_ref[side, cut] += back

    for copy in loads:
        copy.wait()
    slabs = ((1, (near_gate_ref, near_up_ref, near_down_ref)), (0, (gate_ref, up_ref, down_ref)))
    for slab, weights in slabs:
        work(0, slice(0, rows), grad_ref[...], *[ref[...] for ref in weights], slab, slab == 1)
    for part in range(2):
        cut = slice(part * half, (part + 1) * half)
        there[part].wait_recv()
        for slab, weights in slabs:
            work(1, cut, far_grad_ref[cut, :], *[ref[...] for ref in weights], slab, slab == 1)
            if part == 1 and slab == 1:
                near_out_ref[...] = sums_ref[1].astype(BF16)
                swap = remote(near_out_ref, near_in_ref, sems, 4, near)
                swap.start()
        far_out_ref[cut, :] = back_ref[1, cut].astype(BF16)
        returned[part].start()
    far_made_ref[...] = made_ref[1].astype(BF16)
    states_part_ref[...] = middle_ref[...] + made_ref[0]
    swap.wait_recv()
    depth = weight_ref.shape[0] // 3
    for index in range(3):
        total = sums_ref[0, index] + near_in_ref[index].astype(F32)
        weight_ref[index * depth : (index + 1) * depth, :] = total.astype(BF16)
    size = weight_ref.shape[0] // 4
    halves = []
    for index, stride in enumerate(strides):
        begin = pl.multiple_of(2 * size * index + (1 - side_of(stride)) * size, 16)
        halves.append(
            remote(
                weight_ref.at[pl.ds(begin, size), :],
                half_in_ref.at[index],
                (half_sends_ref, half_receives_ref),
                index,
                partner(stride),
                axis="dp",
            )
        )
        halves[-1].start()
    for copy in returned:
        copy.wait_recv()
    normed_grad = back_ref[0] + far_in_ref[...].astype(F32)
    part, gain_grad = rms_back(normed_grad, middle_ref[...], gain_ref[...])
    gain_grad_ref[...] = jnp.broadcast_to(gain_grad, gain_grad_ref.shape)
    middle_grad = grad_ref[...].astype(F32) + part
    middle_grad_ref[...] = middle_grad
    low = middle_grad.astype(BF16)
    grad_stage_ref[...] = dot_nt(all_out_ref[...], low).astype(BF16).reshape(4, share, rows)
    out_part = dot(attended, low)
    for rank in range(4):
        out_part_ref[rank] = out_part[rank * share : (rank + 1) * share, :].T.astype(BF16)
    for index, stride in enumerate(strides):
        halves[index].wait_recv()
        begin = pl.multiple_of(2 * size * index + side_of(stride) * size, 16)
        total = weight_ref[pl.ds(begin, size), :].astype(F32) + half_in_ref[index].astype(F32)
        weight_half_ref[index * size : (index + 1) * size, :] = total.astype(BF16)
    for copy in halves:
        copy.wait_send()
    for copy in returned + there + [swap]:
        copy.wait_send()


def back_kernel(
    width,
    count,
    buckets,
    grad_stage_ref,
    total_ref,
    joint_ref,
    bucket_ref,
    gain_ref,
    starts_ref,
    all_taps_ref,
    weight_half_ref,
    out_part_ref,
    far_made_ref,
    ffn_gain_grad_ref,
    query_t_hbm,
    query_hbm,
    twice_hbm,
    key_t_hbm,
    value_hbm,
    out_hbm,
    table_hbm,
    normed_hbm,
    residual_hbm,
    middle_grad_hbm,
    divisor_hbm,
    pooled_hbm,
    mix_hbm,
    all_join_hbm,
    states_part_hbm,
    input_grad_out,
    states_out_out,
    weight_total_out,
    joint_total_out,
    out_total_ref,
    join_total_ref,
    taps_total_ref,
    gains_total_ref,
    bias_total_ref,
    query_t_ref,
    query_ref,
    twice_ref,
    key_t_ref,
    value_ref,
    out_ref,
    table_ref,
    normed_ref,
    residual_ref,
    middle_grad_ref,
    divisor_ref,
    pooled_ref,
    mix_ref,
    all_join_ref,
    states_part_ref,
    load_ref,
    grad_t_ref,
    grad_ref,
    query_grad_ref,
    key_grad_ref,
    value_grad_ref,
    table_grad_ref,
    joint_grad_ref,
    core_out_ref,
    core_in_ref,
    chip_out_ref,
    chip_in_ref,
    made_in_ref,
    out_near_ref,
    out_sum_ref,
    out_far_ref,
    late_ref,
    ids_ref,
    summary_ref,
    join_part_ref,
    join_near_ref,
    join_sum_ref,
    join_far_ref,
    join_ref,
    small_near_ref,
    small_ref,
    small_in_ref,
    bias_ref,
    bias_in_ref,
    input_grad_ref,
    states_out_ref,
    weight_total_ref,
    joint_total_ref,
    ship_ref,
    sends_ref,
    receives_ref,
    chain_sends_ref,
    chain_receives_ref,
    *chain_refs,
):
    me, near, far, cross = ranks()
    peers = (near, far, cross)
    sems = (sends_ref, receives_ref)
    chain_sems = (chain_sends_ref, chain_receives_ref)
    heads, length = twice_ref.shape[0], twice_ref.shape[1]
    rows, model = residual_ref.shape
    share = join_part_ref.shape[1]
    inner = heads * width
    wide, deep = length // 4, length // 8
    strides = strides_of(count)
    turned_strides = [strides[1], strides[0]] + strides[2:]
    chains = []
    plan = [
        (None, 2 * weight_half_ref.shape[0], strides),
        (None, 2 * weight_half_ref.shape[0], turned_strides),
    ]
    for index, (ref, height, order) in enumerate(plan):
        half = height // 2
        chains.append(
            Chain(
                ref,
                (index % 2) * half,
                half,
                order,
                chain_refs[8 * index : 8 * index + 8],
                chain_sems,
                index * Chain.slots(strides),
            )
        )
    weight_chains, late_chains, join_chains = chains, [], []
    for index, chain in enumerate(weight_chains):
        chain.halved(weight_half_ref, index * (weight_half_ref.shape[0] // 2))
    for index, order in enumerate((strides, turned_strides)):
        join_chains.append(
            Exchange(
                join_ref,
                index * (join_ref.shape[0] // 2),
                join_ref.shape[0] // 2,
                order,
                chain_refs[30 + 2 * index : 32 + 2 * index],
                chain_sems,
                2 * Chain.slots(strides) + 2 * Quad.slots(strides) + index * len(strides),
            )
        )
        late_chains.append(
            Quad(
                late_ref,
                index * (late_ref.shape[0] // 2),
                late_ref.shape[0] // 2,
                order,
                chain_refs[16 + 7 * index : 23 + 7 * index],
                chain_sems,
                2 * Chain.slots(strides) + index * Quad.slots(strides),
            )
        )
    greet(peers, strides)
    loads = load_all(
        (
            (query_t_hbm, query_t_ref),
            (query_hbm, query_ref),
            (twice_hbm, twice_ref),
            (key_t_hbm, key_t_ref),
            (value_hbm, value_ref),
            (out_hbm, out_ref),
            (table_hbm, table_ref),
            (normed_hbm, normed_ref),
            (residual_hbm, residual_ref),
            (middle_grad_hbm, middle_grad_ref),
            (divisor_hbm, divisor_ref),
            (pooled_hbm, pooled_ref),
            (mix_hbm, mix_ref),
            (all_join_hbm, all_join_ref),
            (states_part_hbm, states_part_ref),
        ),
        load_ref,
    )
    greeted(peers, strides)
    gradient_copies = []
    for slot, peer in enumerate(peers):
        copy = remote(
            lambda peer=peer: grad_stage_ref.at[peer], lambda: grad_t_ref.at[me], sems, slot, peer
        )
        copy.start()
        gradient_copies.append(copy)
    out_copies = [
        remote(lambda: out_part_ref.at[near], lambda: out_near_ref.at[0], sems, 3, near),
        remote(lambda: out_part_ref.at[cross], lambda: out_near_ref.at[1], sems, 4, near),
    ]
    for copy in out_copies:
        copy.start()
    out_copy = remote(out_sum_ref, out_far_ref, sems, 5, far)
    made_copy = remote(far_made_ref, made_in_ref, sems, 6, far)
    core_copies = [
        remote(lambda: core_out_ref.at[0], lambda: core_in_ref.at[0], sems, 7, near),
        remote(lambda: core_out_ref.at[1], lambda: core_in_ref.at[1], sems, 8, near),
    ]
    chip_copy = remote(chip_out_ref, chip_in_ref, sems, 9, far)
    for chain in weight_chains:
        chain.step()
    made_copy.start()
    grad_t_ref[me] = grad_stage_ref[me]
    query_grad_ref[...] = jnp.zeros_like(query_grad_ref)
    key_grad_ref[...] = jnp.zeros_like(key_grad_ref)
    value_grad_ref[...] = jnp.zeros_like(value_grad_ref)
    table_grad_ref[...] = jnp.zeros_like(table_grad_ref)

    def gather_rows(rank):
        cut = pl.ds(pl.multiple_of(rank * wide, wide), wide)
        joint_grad_ref[cut, :inner] = query_grad_ref[:, cut].T.astype(BF16)
        joint_grad_ref[cut, inner : 2 * inner] = key_grad_ref[cut, :].astype(BF16)
        joint_grad_ref[cut, 2 * inner :] = value_grad_ref[cut, :].astype(BF16)
        return dot_nt(joint_grad_ref[cut, :], joint_ref[...])

    def block_of(relation):
        return 2 * ((me // 2 + relation // 2) % 2) + (me % 2 + relation % 2) % 2

    core = me % 2

    def step(index, carry):
        phase = index // 4
        middle = ((phase + 1) // 2) % 2
        away = middle * (2 + (core + phase - 1) % 2)
        block = block_of(away + (1 - middle) * ((index % 4) // 2))
        turn = (index + (2 + core) * (phase // 2)) % 4
        other = block_of(middle * turn + (1 - middle) * (index % 2 + 2 * (1 - phase // 3)))
        begin = pl.multiple_of(block * wide, wide)
        start = pl.multiple_of(other * wide, wide)
        span = pl.ds(begin, wide)
        @pl.when(index == 2)
        def _():
            gradient_copies[0].wait_recv()

        for first in range(2):

            @pl.when((index == 4 + 4 * first) & (core == first))
            def _():
                gradient_copies[1].wait_recv()

            @pl.when((index == 4 + 4 * first) & (core == 1 - first))
            def _():
                gradient_copies[2].wait_recv()

        @pl.when((index == 0) | (index == 2) | (index == 4) | (index == 8))
        def _():
            grad_ref[span, :] = turned(grad_t_ref[block])

        @pl.when(index == 3)
        def _():
            for copy in out_copies:
                copy.wait_recv()
            ours = out_part_ref[far].astype(F32) + out_near_ref[1].astype(F32)
            out_sum_ref[...] = ours.astype(BF16)
            out_copy.start()

        @pl.when(index == 4)
        def _():
            weight_chains[0].step()
            weight_chains[1].step()

        for first in range(2):

            @pl.when((index == 9 + 3 * first) & (core == first))
            def _():
                chip_out_ref[...] = gather_rows(far).astype(BF16)

            @pl.when((index == 9 + 3 * first) & (core == 1 - first))
            def _():
                core_out_ref[0] = gather_rows(cross).astype(BF16)
                core_copies[0].start()

            @pl.when((index == 10 + 3 * first) & (core == first))
            def _():
                core_copies[0].wait_recv()
                total = chip_out_ref[...].astype(F32) + core_in_ref[0].astype(F32)
                chip_out_ref[...] = total.astype(BF16)
                chip_copy.start()

        for head in range(heads):
            rows = slice(head * width, (head + 1) * width)
            scaled = query_t_ref[rows, span].astype(F32) * LOG2E
            queries = jnp.concatenate(split(scaled), axis=0)
            total = total_ref[head, :, span]
            grads = grad_t_ref[block, rows, :].astype(F32)
            dots = jnp.sum(grads * out_ref[rows, span], axis=0, keepdims=True)
            own_rows = lax.broadcasted_iota(jnp.int32, (inner, wide), 0) // width == head
            own_lanes = lax.broadcasted_iota(jnp.int32, (wide, inner), 1) // width == head
            grad_t_own = jnp.where(own_rows, grad_t_ref[block].astype(F32), 0.0).astype(BF16)
            query_own = jnp.where(own_lanes, query_ref[span, :].astype(F32), 0.0).astype(BF16)
            grad_own = jnp.where(own_lanes, grad_ref[span, :].astype(F32), 0.0).astype(BF16)
            query_grad = jnp.zeros((width, wide), F32)
            for part in range(wide // deep):
                cut = pl.ds(pl.multiple_of(start + part * deep, deep), deep)
                raw = dot(twice_ref[head, cut, :], queries)
                raw_grad = dot(value_ref[cut, :], grad_t_own)
                probs, score_grads = [], []
                for lane in range(0, wide, LANES):
                    piece = slice(lane, lane + LANES)
                    offset = start + part * deep - begin - lane + length - LANES
                    offset = pl.multiple_of(offset, LANES)
                    shift = table_ref[head, pl.ds(offset, deep), :]
                    prob = jnp.exp2(raw[:, piece] + shift - total[:, piece])
                    low = (prob * (raw_grad[:, piece] - dots[:, piece])).astype(BF16)
                    table_grad_ref[head, pl.ds(offset, deep), :] += low.astype(F32)
                    probs.append(prob.astype(BF16))
                    score_grads.append(low)
                probs = jnp.concatenate(probs, axis=1)
                score_grads = jnp.concatenate(score_grads, axis=1)
                value_grad_ref[cut, :] += dot(probs, grad_own)
                key_grad_ref[cut, :] += dot(score_grads, query_own)
                query_grad = query_grad + dot(key_t_ref[rows, cut], score_grads)
            query_grad_ref[rows, span] += query_grad
        return carry

    for copy in loads[:7]:
        copy.wait()
    lax.fori_loop(0, 16, step, 0)
    core_out_ref[1] = gather_rows(near).astype(BF16)
    core_copies[1].start()
    for chain in weight_chains:
        chain.step()
    normed_grad = gather_rows(me)
    for copy in loads[7:]:
        copy.wait()
    late_ref[:, : 3 * inner] = dot_tn(normed_ref[...], joint_grad_ref[...]).astype(BF16)
    out_copy.wait_recv()
    out_sum = (
        out_part_ref[me].astype(F32) + out_near_ref[0].astype(F32) + out_far_ref[...].astype(F32)
    )
    late_ref[:, 3 * inner :] = out_sum.astype(BF16)
    for chain in late_chains:
        chain.step()
    core_copies[1].wait_recv()
    normed_grad = normed_grad + core_in_ref[1].astype(F32)
    chip_copy.wait_recv()
    normed_grad = normed_grad + chip_in_ref[...].astype(F32)
    part, gain_grad = rms_back(normed_grad, residual_ref[...], gain_ref[...])
    residual_grad = middle_grad_ref[...] + part
    low = residual_grad.astype(BF16)
    join_part_ref[...] = dot_tn(mix_ref[...], low).astype(BF16).reshape(4, share, model)
    join_copies = [
        remote(join_part_ref.at[near], join_near_ref.at[0], sems, 16, near),
        remote(join_part_ref.at[cross], join_near_ref.at[1], sems, 17, near),
    ]
    for copy in join_copies:
        copy.start()
    words = Words(starts_ref, ids_ref, me, 4)
    picked = words.pick(back_target)
    high_mix, low_mix = split(dot_nt(low, all_join_ref[...]))
    summary_ref[me] = dot(picked, high_mix) + dot(picked, low_mix)
    copies = []
    for slot, peer in enumerate(peers):
        copies.append(remote(summary_ref.at[me], summary_ref.at[me], sems, 13 + slot, peer))
        copies[-1].start()
    for copy in join_copies:
        copy.wait_recv()
    join_sum_ref[...] = (
        join_part_ref[far].astype(F32) + join_near_ref[1].astype(F32)
    ).astype(BF16)
    join_copy = remote(join_sum_ref, join_far_ref, sems, 21, far)
    join_copy.start()
    for chain in weight_chains:
        chain.step()
    for chain in late_chains:
        chain.step()
    table = words.table()
    word_grad = dot(table, high_mix) + dot(table, low_mix)
    pooled = pooled_ref[...]
    tap_rows = [jnp.sum(pooled * word_grad, axis=0, keepdims=True)]
    for lag in range(1, 4):
        tap_rows.append(jnp.sum(pltpu.roll(pooled, lag, 0) * word_grad, axis=0, keepdims=True))
    tap_rows += [gain_grad, ffn_gain_grad_ref[0:1], jnp.zeros((2, model), F32)]
    small_near_ref[me] = jnp.concatenate(tap_rows, axis=0)
    for slot, peer in enumerate(peers):
        copies.append(remote(small_near_ref.at[me], small_near_ref.at[me], sems, 18 + slot, peer))
        copies[-1].start()
    shipped = []

    def ship(source, target):
        copy = pltpu.make_async_copy(source, target, ship_ref.at[len(shipped)])
        copy.start()
        shipped.append(copy)

    def write_weights(span, values):
        weight_total_ref[span, :] = values

    def write_late(span, values):
        joint_total_ref[span, :] = values

    def write_join(span, values):
        join_total_ref[span, :] = values

    bias_copies, small_copies = [], []

    def exchange(index, copies, ours, theirs, slot):
        stride = strides[index]
        copies.append(
            remote(
                ours.at[index],
                theirs.at[index],
                sems,
                slot + 2 * index,
                lambda: partner(stride),
                axis="dp",
            )
        )
        copies[-1].start()

    def pass_on(index, copies, ours, theirs, slot):
        copies[index].wait_recv()
        total = ours[index] + theirs[index]
        if index + 1 < len(strides):
            ours[index + 1] = total
            exchange(index + 1, copies, ours, theirs, slot)
        return total

    bias_parts = (bias_copies, bias_ref, bias_in_ref, 23)
    small_parts = (small_copies, small_ref, small_in_ref, 22)
    bias_ref[0] = bias_grad_rows(table_grad_ref, bucket_ref, buckets)
    exchange(0, *bias_parts)
    join_copy.wait_recv()
    join_ref[...] = (
        join_part_ref[me].astype(F32) + join_near_ref[0].astype(F32) + join_far_ref[...].astype(F32)
    ).astype(BF16)
    for chain in join_chains:
        chain.step(write_join)
    for copy in copies:
        copy.wait_recv()
    small = small_near_ref[0]
    for rank in range(1, 4):
        small = small + small_near_ref[rank]
    small_ref[0] = small
    exchange(0, *small_parts)
    for chain in late_chains:
        chain.step()
    word_grad = word_grad + dot(words.place(back_target, back_valid), stacked(summary_ref))
    taps = all_taps_ref[...]
    height = word_grad.shape[0]
    pooled_grad = word_grad * taps[0:1]
    for lag in range(1, 4):
        pooled_grad = pooled_grad + pltpu.roll(word_grad, height - lag, 0) * taps[lag : lag + 1]
    divisor = divisor_ref[...]
    pooled_grad = pooled_grad / jnp.concatenate([divisor] * (model // LANES), axis=1)
    high, low = split(pooled_grad)
    input_grad = residual_grad + (dot_tn(table, high) + dot_tn(table, low))
    input_grad_ref[...] = input_grad[:, None, :]
    ship(input_grad_ref, input_grad_out)
    bias = pass_on(0, *bias_parts)
    small = pass_on(0, *small_parts)
    for chain in join_chains:
        chain.step(write_join)
    made_copy.wait_recv()
    states_out_ref[...] = (states_part_ref[...] + made_in_ref[...].astype(F32))[:, None, :]
    ship(states_out_ref, states_out_out)
    for chain in weight_chains:
        while chain.at < chain.steps:
            chain.step(write_weights)
    ship(weight_total_ref, weight_total_out)
    for chain in late_chains:
        chain.step()
    bias = pass_on(1, *bias_parts)
    small = pass_on(1, *small_parts)
    for chain in join_chains:
        chain.step(write_join)
    for turn in range(1, len(strides) + 1):
        for group, finish in ((join_chains, write_join), (late_chains, write_late)):
            for chain in group:
                if chain.at < chain.steps:
                    chain.step(finish)
        if 1 < turn < len(strides):
            bias = pass_on(turn, *bias_parts)
            small = pass_on(turn, *small_parts)
    for chain in join_chains:
        while chain.at < chain.steps:
            chain.step(write_join)
    for chain in late_chains:
        while chain.at < chain.steps:
            chain.step(write_late)
    ship(joint_total_ref, joint_total_out)
    own = jnp.zeros((8, share), F32)
    for rank in range(4):
        own = jnp.where(me == rank, small[:, rank * share : (rank + 1) * share], own)
    taps_total_ref[...] = own
    gains_total_ref[...] = small
    bias_total_ref[...] = bias
    out_total_ref[...] = joint_total_ref[:, 3 * inner :].T
    for copy in shipped:
        copy.wait()
    finished = gradient_copies + out_copies + core_copies + [chip_copy, made_copy, out_copy]
    for copy in finished + copies + join_copies + [join_copy] + small_copies + bias_copies:
        copy.wait_send()


def place_kernel(
    joint_hbm,
    weight_hbm,
    states_hbm,
    input_hbm,
    out_hbm,
    join_hbm,
    taps_ref,
    gains_ref,
    bias_ref,
    states_out,
    input_out,
    two_out,
    three_out,
    four_out,
    join_out,
    norm_out,
    query_out,
    key_out,
    value_out,
    bias_out,
    out_out,
    ffn_out,
    gate_out,
    up_out,
    down_out,
    joint_ref,
    weight_ref,
    states_ref,
    input_ref,
    out_ref,
    join_ref,
    sems,
):
    loads = []
    for source, target in (
        (weight_hbm, weight_ref),
        (states_hbm, states_ref),
        (input_hbm, input_ref),
        (joint_hbm, joint_ref),
        (out_hbm, out_ref),
        (join_hbm, join_ref),
    ):
        loads.append(pltpu.make_async_copy(source, target, sems.at[10 + len(loads)]))
        loads[-1].start()
    inner, model = query_out.shape[1], gate_out.shape[0]
    pairs = [
        (weight_ref.at[pl.ds(index * model, model), :], target, 0)
        for index, target in enumerate((gate_out, up_out, down_out))
    ]
    pairs += [(states_ref, states_out, 1), (input_ref, input_out, 2)]
    pairs += [
        (joint_ref.at[:, pl.ds(index * inner, inner)], target, 3)
        for index, target in enumerate((query_out, key_out, value_out))
    ]
    pairs += [(out_ref, out_out, 4), (join_ref, join_out, 5)]
    copies, arrived = [], -1
    for index, (source, target, load) in enumerate(pairs):
        if load > arrived:
            loads[load].wait()
            arrived = load
        copies.append(pltpu.make_async_copy(source, target, sems.at[index]))
        copies[-1].start()
    two_out[...] = taps_ref[:2]
    three_out[...] = taps_ref[:3]
    four_out[...] = taps_ref[:4]
    norm_out[...] = gains_ref[4:5]
    ffn_out[...] = gains_ref[5:6]
    heads, buckets = bias_out.shape
    bias_out[...] = bias_ref[:heads, :buckets]
    for copy in copies:
        copy.wait()


def shards(
    byte_states,
    word_start,
    bucket_ids,
    conv_two,
    conv_three,
    conv_four,
    join_weight,
    norm_gain,
    query_weight,
    key_weight,
    value_weight,
    position_bias,
    out_weight,
    ffn_gain,
    gate_weight,
    up_weight,
    down_weight,
    out_grad,
):
    rows, batch, model = byte_states.shape
    length = word_start.shape[0]
    buckets, heads = position_bias.shape
    inner = query_weight.shape[1]
    width = inner // heads
    share = join_weight.shape[0]
    hidden = gate_weight.shape[1]
    count = rows + 16
    replicas = lax.axis_size("dp")
    strides = strides_of(replicas)
    states = byte_states.reshape(rows, model)
    grads = out_grad.reshape(rows, model)
    starts = word_start.reshape(length // LANES, LANES)
    span = bucket_ids.shape[0] + 1 - LANES
    made = (
        like((rows, model), F32),
        like((length, model), BF16),
        like((length, inner), BF16),
        like((inner, length), BF16),
        like((heads, length, 2 * width), BF16),
        like((inner, length), BF16),
        like((length, inner), BF16),
        like((heads, span, LANES), F32),
        like((count, LANES), F32),
        like((count, model), F32),
        like((rows, model), BF16),
        like((4 * share, model), BF16),
        like((model, 3 * inner), BF16),
        like((1, span + LANES), jnp.int32),
    )
    (
        residual,
        normed,
        queries,
        queries_t,
        twice_keys,
        keys_t,
        values,
        table,
        divisor,
        pooled,
        mix,
        all_taps,
        all_join,
        joint_weight,
        bucket_row,
        outs,
        totals,
        attended,
        all_out,
        near_gate,
        near_up,
        near_down,
        far_grads,
    ) = pl.pallas_call(
        functools.partial(forward_kernel, width),
        out_shape=(
            *made[:11],
            like((8, model), F32),
            *made[11:],
            like((inner, length), F32),
            like((heads, 1, length), F32),
            like((4, inner, rows), BF16),
            like((4 * inner, model), BF16),
            like(gate_weight.shape, BF16),
            like(up_weight.shape, BF16),
            like(down_weight.shape, BF16),
            like((rows, model), BF16),
        ),
        in_specs=whole(13) + anywhere(4),
        out_specs=anywhere(11) + whole(1) + anywhere(3) + whole(4) + anywhere(4),
        scratch_shapes=[
            *[pltpu.VMEM(part.shape, part.dtype) for part in made],
            pltpu.VMEM((inner, length), BF16),
            pltpu.VMEM((length // LANES, LANES), F32),
            pltpu.VMEM((4, 8, model + LANES), F32),
            pltpu.VMEM((4, 8, share), F32),
            pltpu.VMEM((length // 2, rows), F32),
            pltpu.VMEM((heads, 1, length), F32),
            pltpu.VMEM((4, inner, rows), BF16),
            pltpu.SemaphoreType.DMA((len(made),)),
            *semaphores(26),
        ],
        compiler_params=params(0),
        name="forward",
    )(
        states,
        starts,
        conv_two,
        conv_three,
        conv_four,
        join_weight,
        norm_gain[None],
        query_weight,
        key_weight,
        value_weight,
        bucket_ids[None],
        position_bias.T,
        out_weight,
        gate_weight,
        up_weight,
        down_weight,
        grads,
    )
    ffn_inputs = (
        grads,
        far_grads,
        gate_weight,
        near_gate,
        up_weight,
        near_up,
        down_weight,
        near_down,
    )
    (
        states_part,
        far_made,
        middle_grad,
        ffn_gain_grad,
        weight_grad,
        out_part,
        grad_stage,
    ) = pl.pallas_call(
        functools.partial(ffn_kernel, replicas),
        out_shape=(
            like((rows, model), F32),
            like((rows, model), BF16),
            like((rows, model), F32),
            like((8, model), F32),
            like((3 * model // 2, hidden), BF16),
            like((4, model, inner), BF16),
            like((4, inner, rows), BF16),
        ),
        in_specs=whole(4) + anywhere(8),
        out_specs=whole(7),
        scratch_shapes=[
            pltpu.VMEM((rows, model), F32),
            pltpu.VMEM((2, rows, model), BF16),
            pltpu.VMEM((2, rows, model), F32),
            pltpu.VMEM((2, rows, model), F32),
            pltpu.VMEM((2, 3, model, hidden), F32),
            pltpu.VMEM((rows, model), BF16),
            pltpu.VMEM((rows, model), BF16),
            pltpu.VMEM((3, model, hidden), BF16),
            pltpu.VMEM((3, model, hidden), BF16),
            pltpu.VMEM((3 * model, hidden), BF16),
            pltpu.VMEM((2, 3 * model // 4, hidden), BF16),
            *[pltpu.VMEM(part.shape, BF16) for part in ffn_inputs],
            pltpu.SemaphoreType.DMA((len(ffn_inputs),)),
            *semaphores(5),
            *semaphores(2),
        ],
        compiler_params=params(2),
        name="ffn",
    )(
        attended,
        all_out,
        residual,
        ffn_gain[None],
        *ffn_inputs,
    )
    chain_scratch = []
    for _ in range(2):
        chain_scratch += Chain.scratch(3 * model // 2, hidden, len(strides) - 2, True)
    for _ in range(2):
        chain_scratch += Quad.scratch(model // 2, 4 * inner, len(strides) - 3)
    for _ in range(2):
        chain_scratch += Exchange.scratch(share // 2, model, len(strides))
    loaded = (queries_t, queries, twice_keys, keys_t, values, outs, table)
    loaded += (normed, residual, middle_grad, divisor, pooled, mix, all_join, states_part)
    (
        input_grad,
        out_states,
        weight_total,
        joint_total,
        out_total,
        join_total,
        taps_total,
        gains_total,
        bias_total,
    ) = pl.pallas_call(
        functools.partial(back_kernel, width, replicas, buckets),
        out_shape=(
            like((rows, 1, model), F32),
            like((rows, 1, model), F32),
            like((3 * model, hidden), F32),
            like((model, 4 * inner), F32),
            like((inner, model), F32),
            like((share, model), F32),
            like((8, share), F32),
            like((8, model), F32),
            like((8, LANES), F32),
        ),
        in_specs=whole(11) + anywhere(len(loaded)),
        out_specs=anywhere(4) + whole(5),
        scratch_shapes=[
            *[pltpu.VMEM(part.shape, part.dtype) for part in loaded],
            pltpu.SemaphoreType.DMA((len(loaded),)),
            pltpu.VMEM((4, inner, rows), BF16),
            pltpu.VMEM((length, inner), BF16),
            pltpu.VMEM((inner, length), F32),
            pltpu.VMEM((length, inner), F32),
            pltpu.VMEM((length, inner), F32),
            pltpu.VMEM((heads, span, LANES), F32),
            pltpu.VMEM((length, 3 * inner), BF16),
            pltpu.VMEM((2, rows, model), BF16),
            pltpu.VMEM((2, rows, model), BF16),
            pltpu.VMEM((rows, model), BF16),
            pltpu.VMEM((rows, model), BF16),
            pltpu.VMEM((rows, model), BF16),
            pltpu.VMEM((2, model, inner), BF16),
            pltpu.VMEM((model, inner), BF16),
            pltpu.VMEM((model, inner), BF16),
            pltpu.VMEM((model, 4 * inner), BF16),
            pltpu.VMEM((length // LANES, LANES), F32),
            pltpu.VMEM((4, 8, model), F32),
            pltpu.VMEM((4, share, model), BF16),
            pltpu.VMEM((2, share, model), BF16),
            pltpu.VMEM((share, model), BF16),
            pltpu.VMEM((share, model), BF16),
            pltpu.VMEM((share, model), BF16),
            pltpu.VMEM((4, 8, model), F32),
            pltpu.VMEM((len(strides), 8, model), F32),
            pltpu.VMEM((len(strides), 8, model), F32),
            pltpu.VMEM((len(strides), 8, LANES), F32),
            pltpu.VMEM((len(strides), 8, LANES), F32),
            pltpu.VMEM((rows, 1, model), F32),
            pltpu.VMEM((rows, 1, model), F32),
            pltpu.VMEM((3 * model, hidden), F32),
            pltpu.VMEM((model, 4 * inner), F32),
            pltpu.SemaphoreType.DMA((4,)),
            *semaphores(22 + 2 * len(strides)),
            *semaphores(2 * Chain.slots(strides) + 2 * Quad.slots(strides) + 2 * len(strides)),
            *chain_scratch,
        ],
        compiler_params=params(3),
        name="back",
    )(
        grad_stage,
        totals,
        joint_weight,
        bucket_row,
        norm_gain[None],
        starts,
        all_taps,
        weight_grad,
        out_part,
        far_made,
        ffn_gain_grad,
        *loaded,
    )
    placed = pl.pallas_call(
        place_kernel,
        out_shape=(
            like((rows, 1, model), F32),
            like((rows, 1, model), F32),
            like(conv_two.shape, F32),
            like(conv_three.shape, F32),
            like(conv_four.shape, F32),
            like((share, model), F32),
            like((1, model), F32),
            like((model, inner), F32),
            like((model, inner), F32),
            like((model, inner), F32),
            like((heads, buckets), F32),
            like((inner, model), F32),
            like((1, model), F32),
            like((model, hidden), F32),
            like((model, hidden), F32),
            like((hidden, model), F32),
        ),
        in_specs=anywhere(6) + whole(3),
        out_specs=anywhere(2)
        + whole(3)
        + anywhere(1)
        + whole(1)
        + anywhere(3)
        + whole(1)
        + anywhere(1)
        + whole(1)
        + anywhere(3),
        scratch_shapes=[
            *[
                pltpu.VMEM(part.shape, F32)
                for part in (joint_total, weight_total, out_states, input_grad, out_total, join_total)
            ],
            pltpu.SemaphoreType.DMA((16,)),
        ],
        compiler_params=params(),
        name="place",
    )(
        joint_total,
        weight_total,
        out_states,
        input_grad,
        out_total,
        join_total,
        taps_total,
        gains_total,
        bias_total,
    )
    placed = list(placed)
    placed[6], placed[10], placed[12] = placed[6][0], placed[10].T, placed[12][0]
    return tuple(placed)


def solution(mesh):
    return jax.shard_map(
        shards,
        mesh=mesh,
        in_specs=(
            P("mp", "dp", None),
            P(None, "dp"),
            P(),
            P(None, "mp"),
            P(None, "mp"),
            P(None, "mp"),
            P("mp", None),
            P(),
            P(None, "mp"),
            P(None, "mp"),
            P(None, "mp"),
            P(None, "mp"),
            P("mp", None),
            P(),
            P(None, "mp"),
            P(None, "mp"),
            P("mp", None),
            P("mp", "dp", None),
        ),
        out_specs=(
            P("mp", "dp", None),
            P("mp", "dp", None),
            P(None, "mp"),
            P(None, "mp"),
            P(None, "mp"),
            P("mp", None),
            P(),
            P(None, "mp"),
            P(None, "mp"),
            P(None, "mp"),
            P(None, "mp"),
            P("mp", None),
            P(),
            P(None, "mp"),
            P(None, "mp"),
            P("mp", None),
        ),
        check_vma=False,
    )
```

```python
import functools

import jax
import jax.numpy as jnp
from jax import lax
from jax.experimental import pallas as pl
from jax.experimental.pallas import tpu as pltpu
from jax.sharding import PartitionSpec as P

EPSILON = 1e-06
LOG2E = 1.4426950408889634
GELU_SCALE = 0.7978845608028654
GELU_CUBE = 0.044715
F32 = jnp.float32
BF16 = jnp.bfloat16
LANES = 128
HALO = 3
VMEM_LIMIT = 56 << 20
MESH = pl.DeviceIdType.MESH


def whole(count):
    return [pl.BlockSpec(memory_space=pltpu.VMEM)] * count


def anywhere(count):
    return [pl.BlockSpec(memory_space=pl.ANY)] * count


def params(collective=None):
    return pltpu.CompilerParams(
        vmem_limit_bytes=VMEM_LIMIT, collective_id=collective, has_side_effects=collective is not None
    )


def like(shape, dtype):
    return jax.ShapeDtypeStruct(shape, dtype)


def dot(lhs, rhs):
    return jnp.dot(lhs, rhs, preferred_element_type=F32)


def dot_nt(lhs, rhs):
    return lax.dot_general(lhs, rhs, (((1,), (1,)), ((), ())), preferred_element_type=F32)


def dot_tn(lhs, rhs):
    return lax.dot_general(lhs, rhs, (((0,), (0,)), ((), ())), preferred_element_type=F32)


def split(values):
    high = values.astype(BF16)
    return high, (values - high.astype(F32)).astype(BF16)


def turned(values):
    return values.astype(F32).T.astype(BF16)


def ranks():
    me = lax.axis_index("mp")
    near = me + 1 - 2 * (me % 2)
    return me, near, (me + 2) % 4, (near + 2) % 4


def greet(peers, strides=()):
    barrier = pltpu.get_barrier_semaphore()
    for peer in peers:
        pl.semaphore_signal(barrier, inc=1, device_id={"mp": peer}, device_id_type=MESH)
    for stride in strides:
        pl.semaphore_signal(barrier, inc=1, device_id={"dp": partner(stride)}, device_id_type=MESH)


def greeted(peers, strides=()):
    pl.semaphore_wait(pltpu.get_barrier_semaphore(), len(peers) + len(strides))


def load_all(pairs, sems):
    copies = []
    for source, target in pairs:
        copies.append(pltpu.make_async_copy(source, target, sems.at[len(copies)]))
        copies[-1].start()
    return copies


def side_of(stride):
    return (lax.axis_index("dp") // stride) % 2


def partner(stride):
    return lax.axis_index("dp") + stride - 2 * stride * side_of(stride)


def strides_of(count):
    strides = []
    while 2 ** len(strides) < count:
        strides.append(2 ** len(strides))
    return strides


class remote:
    def __init__(self, *given, axis="mp"):
        self.given, self.axis = given, axis

    def start(self):
        described(*self.given, self.axis).start()

    def wait_recv(self):
        described(*self.given, self.axis).wait_recv()

    def wait_send(self):
        described(*self.given, self.axis).wait_send()

    def wait(self):
        described(*self.given, self.axis).wait()


def described(source, target, sems, slot, peer, axis):
    source, target, peer = [part() if callable(part) else part for part in (source, target, peer)]
    sends, receives = sems
    return pltpu.make_async_remote_copy(
        src_ref=source,
        dst_ref=target,
        send_sem=sends.at[slot],
        recv_sem=receives.at[slot],
        device_id={axis: peer},
        device_id_type=MESH,
    )


def semaphores(count):
    return [pltpu.SemaphoreType.DMA((count,)), pltpu.SemaphoreType.DMA((count,))]


class Quad:
    def __init__(self, source_ref, base, rows, strides, scratch, sems, first_slot):
        self.source, self.base, self.rows, self.strides = source_ref, base, rows, strides
        self.half_in, self.half, self.pieces_in, self.pieces, self.others_in, self.gathered, self.far_half = scratch
        self.sems, self.slot, self.at = sems, first_slot, 0
        self.copies, self.count = [], 0
        self.steps = len(strides) + 2

    @staticmethod
    def scratch(rows, width, exchanges):
        half, piece = rows // 2, rows // 8
        return [
            pltpu.VMEM((half, width), BF16),
            pltpu.VMEM((half, width), BF16),
            pltpu.VMEM((3, piece, width), BF16),
            pltpu.VMEM((exchanges + 1, piece, width), BF16),
            pltpu.VMEM((exchanges + 1, piece, width), BF16),
            pltpu.VMEM((3, piece, width), BF16),
            pltpu.VMEM((half, width), BF16),
        ]

    @staticmethod
    def slots(strides):
        return len(strides) + 6

    def send(self, source, target, peer):
        copy = remote(source, target, self.sems, self.slot + self.count, peer, axis="dp")
        copy.start()
        self.copies.append(copy)
        self.count += 1

    def away(self, turn):
        first, second = self.strides[1:3]
        flips = (turn % 2, turn // 2)
        device, place = lax.axis_index("dp"), 0
        for flip, stride, weight in zip(flips, (first, second), (1, 2)):
            side = side_of(stride)
            device = device + flip * (stride - 2 * stride * side)
            place = place + weight * (side + flip * (1 - 2 * side))
        return device, place

    def piece(self, turn):
        height = self.rows // 8
        return pl.ds(pl.multiple_of(self.away(turn)[1] * height, 16), height)

    def step(self, finish=None):
        at, half = self.at, self.rows // 2
        first, others = self.strides[0], self.strides[3:]
        self.at += 1
        for copy in self.copies:
            copy.wait_recv()
        done, self.copies = self.copies, []
        if at == 0:
            begin = pl.multiple_of(self.base + (1 - side_of(first)) * half, 16)
            self.send(self.source.at[pl.ds(begin, half), :], self.half_in, partner(first))
        elif at == 1:
            begin = pl.multiple_of(self.base + side_of(first) * half, 16)
            mine = self.source[pl.ds(begin, half), :].astype(F32)
            self.half[...] = (mine + self.half_in[...].astype(F32)).astype(BF16)
            for turn in range(1, 4):
                part = self.half.at[self.piece(turn), :]
                self.send(part, self.pieces_in.at[turn - 1], self.away(turn)[0])
        elif at <= 2 + len(others):
            if at == 2:
                total = self.half[self.piece(0), :].astype(F32)
                for turn in range(1, 4):
                    total = total + self.pieces_in[turn - 1].astype(F32)
            else:
                total = self.pieces[at - 3].astype(F32) + self.others_in[at - 3].astype(F32)
            self.pieces[at - 2] = total.astype(BF16)
            if at < 2 + len(others):
                stride = others[at - 2]
                self.send(self.pieces.at[at - 2], self.others_in.at[at - 2], partner(stride))
            else:
                for turn in range(1, 4):
                    self.send(self.pieces.at[at - 2], self.gathered.at[turn - 1], self.away(turn)[0])
        elif at == 3 + len(others):
            self.half[self.piece(0), :] = self.pieces[len(others)]
            for turn in range(1, 4):
                self.half[self.piece(turn), :] = self.gathered[turn - 1]
            self.send(self.half, self.far_half, partner(first))
        else:
            side = side_of(first)
            mine = pl.ds(pl.multiple_of(self.base + side * half, 16), half)
            other = pl.ds(pl.multiple_of(self.base + (1 - side) * half, 16), half)
            finish(mine, self.half[...].astype(F32))
            finish(other, self.far_half[...].astype(F32))
        for copy in done:
            copy.wait_send()


class Exchange:
    def __init__(self, source_ref, base, rows, strides, scratch, sems, first_slot):
        self.source, self.base, self.rows, self.strides = source_ref, base, rows, strides
        self.ours, self.theirs = scratch
        self.sems, self.slot, self.at = sems, first_slot, 0
        self.copies = []
        self.steps = len(strides) + 1

    @staticmethod
    def scratch(rows, width, strides):
        return [pltpu.VMEM((strides, rows, width), BF16)] * 2

    def step(self, finish=None):
        at = self.at
        self.at += 1
        if at == 0:
            total = self.source[self.base : self.base + self.rows, :].astype(F32)
        else:
            self.copies[-1].wait_recv()
            total = self.ours[at - 1].astype(F32) + self.theirs[at - 1].astype(F32)
        if at < len(self.strides):
            self.ours[at] = total.astype(BF16)
            stride = self.strides[at]
            copy = remote(
                lambda: self.ours.at[at],
                lambda: self.theirs.at[at],
                self.sems,
                self.slot + at,
                lambda: partner(stride),
                axis="dp",
            )
            copy.start()
            self.copies.append(copy)
        else:
            finish(slice(self.base, self.base + self.rows), total)
            for copy in self.copies:
                copy.wait_send()


class Chain:
    def __init__(self, source_ref, base, rows, strides, scratch, sems, first_slot):
        self.source, self.base, self.rows, self.strides = source_ref, base, rows, strides
        (
            self.half_in,
            self.half,
            self.quarter_in,
            self.quarter,
            self.whole_quarter,
            self.gathered_quarter,
            self.both,
            self.gathered_half,
        ) = scratch
        self.sems, self.slot, self.at = sems, first_slot, 0
        self.copies = []
        self.steps = len(strides) + 3
        self.half_base = 0

    def halved(self, half_ref, base):
        self.half, self.half_base, self.at = half_ref, base, 1
        return self

    @staticmethod
    def scratch(rows, width, exchanges, halved=False):
        half, quarter = (rows // 2, width), (rows // 4, width)
        first = (16, LANES) if halved else half
        return [
            pltpu.VMEM(first, BF16),
            pltpu.VMEM(first, BF16),
            pltpu.VMEM((exchanges + 1, *quarter), BF16),
            pltpu.VMEM((exchanges, *quarter), BF16),
            pltpu.VMEM(quarter, BF16),
            pltpu.VMEM(quarter, BF16),
            pltpu.VMEM(half, BF16),
            pltpu.VMEM(half, BF16),
        ]

    @staticmethod
    def slots(strides):
        return len(strides) + 2

    def send(self, source, target, stride):
        copy = remote(
            source, target, self.sems, self.slot + len(self.copies), lambda: partner(stride), axis="dp"
        )
        copy.start()
        self.copies.append(copy)

    def step(self, finish=None):
        first, second, others = self.strides[0], self.strides[1], self.strides[2:]
        half, quarter = self.rows // 2, self.rows // 4
        at = self.at
        self.at += 1
        if self.copies:
            self.copies[-1].wait_recv()
        if at == 0:
            self.send(lambda: self.source.at[pl.ds(pl.multiple_of(self.base + (1 - side_of(first)) * half, 16), half), :], self.half_in, first)
        elif at == 1:
            if self.copies:
                begin = pl.multiple_of(self.base + side_of(first) * half, 16)
                mine = self.source[pl.ds(begin, half), :].astype(F32)
                self.half[...] = (mine + self.half_in[...].astype(F32)).astype(BF16)
            self.send(lambda: self.half.at[
                    pl.ds(
                        pl.multiple_of(self.half_base + (1 - side_of(second)) * quarter, 16), quarter
                    ),
                    :,
                ], lambda: self.quarter_in.at[0], second)
        elif at <= 1 + len(others):
            if at == 2:
                begin = pl.multiple_of(self.half_base + side_of(second) * quarter, 16)
                mine = self.half[pl.ds(begin, quarter), :]
            else:
                mine = self.quarter[at - 3]
            total = mine.astype(F32) + self.quarter_in[at - 2].astype(F32)
            self.quarter[at - 2] = total.astype(BF16)
            self.send(
                lambda: self.quarter.at[at - 2], lambda: self.quarter_in.at[at - 1], others[at - 2]
            )
        elif at == 2 + len(others):
            total = self.quarter[at - 3].astype(F32) + self.quarter_in[at - 2].astype(F32)
            self.whole_quarter[...] = total.astype(BF16)
            self.send(self.whole_quarter, self.gathered_quarter, second)
        elif at == 3 + len(others):
            side = side_of(second)
            mine = pl.ds(pl.multiple_of(side * quarter, 16), quarter)
            other = pl.ds(pl.multiple_of((1 - side) * quarter, 16), quarter)
            self.both[mine, :] = self.whole_quarter[...]
            self.both[other, :] = self.gathered_quarter[...]
            self.send(self.both, self.gathered_half, first)
        else:
            side = side_of(first)
            mine = pl.ds(pl.multiple_of(self.base + side * half, 16), half)
            other = pl.ds(pl.multiple_of(self.base + (1 - side) * half, 16), half)
            finish(mine, self.both[...].astype(F32))
            finish(other, self.gathered_half[...].astype(F32))
            for copy in self.copies:
                copy.wait_send()


def rms(values, gain):
    return values * lax.rsqrt(jnp.mean(values * values, axis=1, keepdims=True) + EPSILON) * gain


def rms_back(grads, values, gain):
    scale = lax.rsqrt(jnp.mean(values * values, axis=1, keepdims=True) + EPSILON)
    gain_grad = jnp.sum(grads * values * scale, axis=0, keepdims=True)
    raised = grads * gain
    mean = jnp.mean(raised * values, axis=1, keepdims=True)
    return scale * raised - values * (scale * scale * scale * mean), gain_grad


def bucket_hits(bucket_ref, buckets):
    span = bucket_ref.shape[1]
    rows = lax.broadcasted_iota(jnp.int32, (buckets, span), 0)
    return rows == jnp.broadcast_to(bucket_ref[...], (buckets, span))


def fill_bias_table(bucket_ref, bias_ref, table_ref):
    span = bucket_ref.shape[1]
    heads, buckets = bias_ref.shape
    hits = bucket_hits(bucket_ref, buckets).astype(F32).astype(BF16)
    bias = bias_ref[...]
    first = bias.astype(BF16)
    second, third = split(bias - first.astype(F32))
    rows = jnp.concatenate([first, second, third, jnp.zeros((16 - 3 * heads, buckets), BF16)], axis=0)
    lines = dot(rows, hits)
    for head in range(heads):
        line = lines[head : head + 1] + (
            lines[heads + head : heads + head + 1] + lines[2 * heads + head : 2 * heads + head + 1]
        )
        skew = pltpu.roll(
            jnp.broadcast_to(line * LOG2E, (LANES, span)), span - LANES + 1, 1, stride=1, stride_axis=0
        )
        for block in range(span // LANES - 1):
            cut = slice(block * LANES, (block + 1) * LANES)
            table_ref[head, cut, :] = skew[:, cut].T


def bias_grad_rows(table_ref, bucket_ref, buckets):
    span = bucket_ref.shape[1]
    heads = table_ref.shape[0]
    hits = bucket_hits(bucket_ref, buckets).astype(F32).astype(BF16)
    lines = []
    for head in range(heads):
        blocks = [
            table_ref[head, block * LANES : (block + 1) * LANES, :].T
            for block in range(span // LANES - 1)
        ]
        skew = jnp.concatenate(blocks + [jnp.zeros((LANES, LANES), F32)], axis=1)
        rows = LANES // 2
        while rows >= 8:
            skew = skew[:rows] + pltpu.roll(skew[rows:], span - rows, 1)
            rows //= 2
        line = jnp.zeros((1, span), F32)
        for row in range(8):
            line = line + pltpu.roll(skew[row : row + 1], LANES - 1 - row, 1)
        lines.append(line)
    lines = jnp.concatenate(lines + [jnp.zeros((8 - heads, span), F32)], axis=0)
    first = lines.astype(BF16)
    second, third = split(lines - first.astype(F32))
    parts = dot_nt(jnp.concatenate([first.astype(F32), second.astype(F32)], axis=0).astype(BF16), hits)
    rest = dot_nt(jnp.concatenate([third.astype(F32), jnp.zeros((8, span), F32)], axis=0).astype(BF16), hits)
    made = parts[:8] + (parts[8:] + rest[:8])
    return jnp.concatenate([made, jnp.zeros((8, LANES - buckets), F32)], axis=1)


def word_numbers(starts):
    rows = starts.shape[0]
    upper = lax.broadcasted_iota(jnp.int32, (LANES, LANES), 0) <= lax.broadcasted_iota(
        jnp.int32, (LANES, LANES), 1
    )
    within = dot(starts.astype(F32).astype(BF16), upper.astype(F32).astype(BF16))
    totals = jnp.broadcast_to(within[:, LANES - 1 :], (rows, LANES)).astype(BF16)
    lower = lax.broadcasted_iota(jnp.int32, (rows, rows), 1) < lax.broadcasted_iota(
        jnp.int32, (rows, rows), 0
    )
    return within + dot(lower.astype(F32).astype(BF16), totals) - 1.0


class Words:
    def __init__(self, starts_ref, ids_ref, me, ranks_count):
        ids = word_numbers(starts_ref[...])
        ids_ref[...] = ids
        per = ids.shape[0] // ranks_count
        self.firsts = [ids[per * rank : per * rank + 1, 0:1] for rank in range(ranks_count)]
        self.lasts = [
            ids[per * (rank + 1) - 1 : per * (rank + 1), LANES - 1 :] for rank in range(ranks_count)
        ]
        pieces = [ids_ref[pl.ds(me * per + piece, 1), :] for piece in range(per)]
        self.row = jnp.concatenate(pieces, axis=1)
        self.first = self.row[:, 0:1]
        self.last = self.row[:, per * LANES - 1 :]
        self.me = me
        self.count = per * LANES

    def table(self):
        shape = (self.count + 16, self.count)
        rows = lax.broadcasted_iota(jnp.int32, shape, 0).astype(F32)
        return (rows == self.row - self.first + HALO).astype(F32).astype(BF16)

    def pick(self, target):
        slots = lax.broadcasted_iota(jnp.int32, (8, 1), 0)
        hits = target(slots, self.first, self.last) == self.row
        return hits.astype(F32).astype(BF16)

    def place(self, target, valid):
        width = 2 * LANES
        lane = lax.broadcasted_iota(jnp.int32, (1, width), 1) % LANES
        slots, rank = lane % 8, lane // 8
        goal = jnp.full((1, width), -9.0, F32)
        for index, (first, last) in enumerate(zip(self.firsts, self.lasts)):
            goal = jnp.where(rank == index, target(slots, first, last), goal)
        known = valid(slots, rank, self.me) & (rank < len(self.firsts))
        goal = jnp.where(known, goal - self.first + HALO, -1.0)
        rows = lax.broadcasted_iota(jnp.int32, (self.count + 16, width), 0).astype(F32)
        return (rows == goal).astype(F32).astype(BF16)


def stacked(summary_ref):
    parts = [summary_ref[rank] for rank in range(summary_ref.shape[0])]
    rest = LANES - sum(part.shape[0] for part in parts)
    parts.append(jnp.zeros((rest, parts[0].shape[1]), F32))
    return jnp.concatenate(split(jnp.concatenate(parts, axis=0)), axis=0)


def ahead_target(slots, first, last):
    later = jnp.where(slots <= 4, last - (slots - 1).astype(F32), -9.0)
    return jnp.where(slots == 0, first, later)


def ahead_valid(slots, rank, me):
    return ((rank < me) & (slots >= 1) & (slots <= 4)) | ((rank > me) & (slots == 0))


def back_target(slots, first, last):
    return jnp.where(slots <= 3, first + slots.astype(F32), jnp.where(slots == 4, last, -9.0))


def back_valid(slots, rank, me):
    return ((rank > me) & (slots <= 3)) | ((rank < me) & (slots == 4))


def forward_kernel(
    width,
    count,
    states_ref,
    starts_ref,
    two_ref,
    three_ref,
    four_ref,
    join_ref,
    gain_ref,
    query_weight_ref,
    key_weight_ref,
    value_weight_ref,
    bucket_ref,
    bias_ref,
    out_weight_ref,
    gate_ref,
    up_ref,
    down_ref,
    grad_ref,
    residual_out,
    normed_out,
    query_out,
    query_t_out,
    twice_out,
    key_t_out,
    value_out,
    table_out,
    divisor_out,
    pooled_out,
    mix_out,
    all_taps_ref,
    all_join_out,
    joint_out,
    padded_out,
    out_ref,
    total_ref,
    attended_ref,
    all_out_ref,
    near_gate_ref,
    near_up_ref,
    near_down_ref,
    far_grad_ref,
    residual_ref,
    normed_ref,
    query_ref,
    query_t_ref,
    twice_ref,
    key_t_ref,
    value_ref,
    table_ref,
    divisor_ref,
    pooled_ref,
    mix_ref,
    all_join_ref,
    joint_ref,
    padded_ref,
    value_t_ref,
    ids_ref,
    summary_ref,
    taps_in_ref,
    score_ref,
    sum_ref,
    stage_ref,
    ship_ref,
    *sems,
):
    me, near, far, cross = ranks()
    peers = (near, far, cross)
    rows, model = states_ref.shape
    share = join_ref.shape[0]
    inner = query_weight_ref.shape[1]
    heads, length = twice_ref.shape[0], twice_ref.shape[1]
    shipped = []

    def ship(source, target):
        copy = pltpu.make_async_copy(source, target, ship_ref.at[len(shipped)])
        copy.start()
        shipped.append(copy)

    def band(ref, rank):
        return ref.at[pl.ds(pl.multiple_of(rank * share, share), share), :]

    strides = strides_of(count)[:2]
    greet(peers, strides)
    words = Words(starts_ref, ids_ref, me, 4)
    states = states_ref[...]
    wide_states = jnp.concatenate([states, jnp.ones((rows, LANES), BF16)], axis=1)
    summary_ref[me] = dot(words.pick(ahead_target), wide_states)
    two, three, four = two_ref[...], three_ref[...], four_ref[...]
    taps_in_ref[me] = jnp.concatenate(
        [
            two[0:1] + three[0:1] + four[0:1],
            two[1:2] + three[1:2] + four[1:2],
            three[2:3] + four[2:3],
            four[3:4],
            jnp.zeros((4, share), F32),
        ],
        axis=0,
    )
    all_join_ref[pl.ds(pl.multiple_of(me * share, share), share), :] = join_ref[...]
    all_out_ref[pl.ds(pl.multiple_of(me * share, share), share), :] = out_weight_ref[...]
    greeted(peers, strides)
    early = []
    for slot, peer in enumerate(peers):
        early.append(remote(summary_ref.at[me], summary_ref.at[me], sems, slot, peer))
        early.append(remote(taps_in_ref.at[me], taps_in_ref.at[me], sems, 3 + slot, peer))
    joins = [
        remote(band(all_join_ref, me), band(all_join_ref, me), sems, 6, far),
        remote(band(all_join_ref, me), band(all_join_ref, me), sems, 7, near),
    ]
    middle = rows // 2
    first_grads = remote(
        grad_ref.at[pl.ds(0, middle)], far_grad_ref.at[pl.ds(0, middle)], sems, 25, far
    )
    for copy in early + joins + [first_grads]:
        copy.start()
    padded_ref[...] = jnp.full(padded_ref.shape, -1, jnp.int32)
    padded_ref[:, : bucket_ref.shape[1]] = bucket_ref[...]
    joint_ref[:, :inner] = query_weight_ref[...]
    joint_ref[:, inner : 2 * inner] = key_weight_ref[...]
    joint_ref[:, 2 * inner :] = value_weight_ref[...]
    ship(joint_ref, joint_out)
    ship(padded_ref, padded_out)
    table = words.table()
    sums = dot(table, wide_states)
    place = words.place(ahead_target, ahead_valid)
    for copy in early:
        copy.wait_recv()
    sums = sums + dot(place, stacked(summary_ref))
    divisor = jnp.maximum(sums[:, model:], 1.0)
    divisor_ref[...] = divisor
    ship(divisor_ref, divisor_out)
    pooled = sums[:, :model] / jnp.concatenate([divisor] * (model // LANES), axis=1)
    pooled_ref[...] = pooled
    ship(pooled_ref, pooled_out)
    taps = jnp.concatenate([taps_in_ref[rank] for rank in range(4)], axis=1)
    all_taps_ref[...] = taps
    joins[0].wait_recv()
    joins.append(remote(band(all_join_ref, far), band(all_join_ref, far), sems, 8, near))
    joins[2].start()
    total = pooled * taps[0:1]
    for lag in range(1, 4):
        total = total + pltpu.roll(pooled, lag, 0) * taps[lag : lag + 1]
    mix = dot_tn(table, total.astype(BF16)).astype(BF16)
    mix_ref[...] = mix
    ship(mix_ref, mix_out)
    joins[1].wait_recv()
    joins[2].wait_recv()
    residual = states.astype(F32) + dot(mix, all_join_ref[...])
    residual_ref[...] = residual
    own = pl.ds(pl.multiple_of(me * rows, rows), rows)
    normed_ref[own, :] = rms(residual, gain_ref[...]).astype(BF16)

    def block(rank, part):
        half = rows // 2
        return normed_ref.at[pl.ds(pl.multiple_of(rank * rows + part * half, half), half), :]

    sends = []
    for part in range(2):
        sends.append(remote(block(me, part), block(me, part), sems, 9 + part, far))
    for part in range(2):
        sends.append(remote(block(me, part), block(me, part), sems, 11 + part, near))
    for copy in sends:
        copy.start()
    copies = [
        remote(
            grad_ref.at[pl.ds(middle, middle)], far_grad_ref.at[pl.ds(middle, middle)], sems, 15, far
        ),
        remote(band(all_out_ref, me), band(all_out_ref, me), sems, 16, near),
        remote(gate_ref, near_gate_ref, sems, 17, near),
        remote(up_ref, near_up_ref, sems, 18, near),
        remote(down_ref, near_down_ref, sems, 19, near),
    ]
    out_far = remote(
        lambda: band(all_out_ref, me), lambda: band(all_out_ref, me), sems, 20, far
    )
    out_pass = remote(
        lambda: band(all_out_ref, far), lambda: band(all_out_ref, far), sems, 21, near
    )
    out_far.start()
    for copy in copies:
        copy.start()
    ship(residual_ref, residual_out)
    ship(all_join_ref, all_join_out)

    def project(rank):
        cut = pl.ds(pl.multiple_of(rank * rows, rows), rows)
        made = dot(normed_ref[cut, :], joint_ref[...])
        query, key, value = [
            made[:, index * inner : (index + 1) * inner].astype(BF16) for index in range(3)
        ]
        query_ref[cut, :] = query
        query_t_ref[:, cut] = turned(query)
        key_t_ref[:, cut] = turned(key)
        value_ref[cut, :] = value
        value_t_ref[:, cut] = turned(value)
        for head in range(heads):
            part = key[:, head * width : (head + 1) * width]
            twice_ref[head, cut, :] = jnp.concatenate([part, part], axis=1)

    project(me)
    fill_bias_table(padded_ref, bias_ref, table_ref)
    ship(table_ref, table_out)
    sends[2].wait_recv()
    sends[3].wait_recv()
    project(near)
    wide = deep = length // 4

    def owner(order):
        chip = (me // 2 + 1 + order // 2) % 2
        core = (me % 2 + (order + 1) // 2) % 2
        return 2 * chip + core

    def handed(order):
        return remote(stage_ref.at[order], attended_ref.at[me], sems, 22 + order, owner(order))

    def half_scores(block, head, chip):
        begin = pl.multiple_of(block * wide, wide)
        start = pl.multiple_of(chip * (length // 2), wide)
        rows = pl.ds(pl.multiple_of(head * width, width), width)
        scaled = query_t_ref[rows, pl.ds(begin, wide)].astype(F32) * LOG2E
        queries = jnp.concatenate(split(scaled), axis=0)
        peak = jnp.full((8, wide), -1e30, F32)
        for part in range(length // 2 // deep):
            keys = pl.ds(pl.multiple_of(start + part * deep, deep), deep)
            raw = dot(twice_ref[head, keys, :], queries)
            columns = []
            for lane in range(0, wide, LANES):
                offset = start + part * deep - begin - lane + length - LANES
                offset = pl.multiple_of(offset, LANES)
                columns.append(raw[:, lane : lane + LANES] + table_ref[head, pl.ds(offset, deep), :])
            scores = jnp.concatenate(columns, axis=1)
            score_ref[part * deep : (part + 1) * deep, :] = scores
            peak = jnp.maximum(peak, jnp.max(scores.reshape(deep // 8, 8, wide), axis=0))
        peak = jnp.max(peak, axis=0, keepdims=True)
        sums = jnp.zeros((8, wide), F32)
        made = jnp.zeros((width, wide), F32)
        for part in range(length // 2 // deep):
            keys = pl.ds(pl.multiple_of(start + part * deep, deep), deep)
            raised = jnp.exp2(score_ref[part * deep : (part + 1) * deep, :] - peak)
            sums = sums + jnp.sum(raised.reshape(deep // 8, 8, wide), axis=0)
            made = made + dot(value_t_ref[rows, keys], raised.astype(BF16))
        return peak, jnp.sum(sums, axis=0, keepdims=True), made

    def early_step(index, carry):
        head = index % heads
        block = 2 * (me // 2) + index // heads
        peak, total, made = half_scores(block, head, me // 2)
        span = pl.ds(pl.multiple_of(block * wide, wide), wide)
        total_ref[head, :, span] = peak
        sum_ref[head, :, span] = total
        out_ref[pl.ds(pl.multiple_of(head * width, width), width), span] = made
        return carry

    lax.fori_loop(0, 2 * heads, early_step, 0)
    passed = []
    for part in range(2):
        sends[part].wait_recv()
        passed.append(remote(block(far, part), block(far, part), sems, 13 + part, near))
        passed[part].start()
    project(far)
    for copy in passed:
        copy.wait_recv()
    project(cross)
    for source, target in (
        (normed_ref, normed_out),
        (query_ref, query_out),
        (query_t_ref, query_t_out),
        (twice_ref, twice_out),
        (key_t_ref, key_t_out),
        (value_ref, value_out),
    ):
        ship(source, target)

    def step(index, carry):
        late = index // (4 * heads)
        rest = index % (4 * heads)
        order = (1 - late) * (rest // (2 * heads)) + late * (2 + rest // heads)
        head = (1 - late) * (rest // 2 % heads) + late * (rest % heads)
        half = (1 - late) * (rest % 2) + late
        block = owner(order)
        peak, total, made = half_scores(block, head, (me // 2 + half) % 2)
        span = pl.ds(pl.multiple_of(block * wide, wide), wide)
        rows = pl.ds(pl.multiple_of(head * width, width), width)

        @pl.when(half == 0)
        def _():
            total_ref[head, :, span] = peak
            sum_ref[head, :, span] = total
            out_ref[rows, span] = made

        @pl.when(half == 1)
        def _():
            before = total_ref[head, :, span]
            top = jnp.maximum(before, peak)
            old, new = jnp.exp2(before - top), jnp.exp2(peak - top)
            all_sum = sum_ref[head, :, span] * old + total * new
            result = (out_ref[rows, span] * old + made * new) / all_sum
            out_ref[rows, span] = result
            total_ref[head, :, span] = top + jnp.log2(all_sum)
            stage_ref[order, rows, :] = result.astype(BF16)

        @pl.when((half == 1) & (head == heads - 1) & (order < 3))
        def _():
            handed(order).start()

        @pl.when(index == 2 * heads)
        def _():
            out_far.wait_recv()
            out_pass.start()

        return carry

    lax.fori_loop(0, 6 * heads, step, 0)
    attended_ref[me] = stage_ref[3]
    for order in range(3):
        handed(order).wait()
    for copy in copies + [first_grads]:
        copy.wait()
    out_pass.wait()
    for copy in early + joins + sends + passed + [out_far]:
        copy.wait_send()
    for copy in shipped:
        copy.wait()


def ffn_kernel(
    count,
    attended_ref,
    all_out_ref,
    residual_ref,
    gain_ref,
    grad_ref,
    far_grad_ref,
    gate_ref,
    near_gate_ref,
    up_ref,
    near_up_ref,
    down_ref,
    near_down_ref,
    states_part_ref,
    far_made_ref,
    middle_grad_ref,
    gain_grad_ref,
    weight_half_ref,
    out_part_ref,
    grad_stage_ref,
    middle_ref,
    normed_ref,
    made_ref,
    back_ref,
    sums_ref,
    far_out_ref,
    far_in_ref,
    near_out_ref,
    near_in_ref,
    weight_ref,
    half_in_ref,
    sends_ref,
    receives_ref,
    half_sends_ref,
    half_receives_ref,
):
    me, near, far, cross = ranks()
    sems = (sends_ref, receives_ref)
    strides = strides_of(count)[:2]
    peers = (near, far, cross)
    rows, model = residual_ref.shape
    share = attended_ref.shape[1]
    attended = attended_ref[...].reshape(4 * share, rows)
    middle = residual_ref[...] + dot_tn(attended, all_out_ref[...])
    middle_ref[...] = middle
    normed_ref[0] = rms(middle, gain_ref[...]).astype(BF16)
    half = rows // 2
    there, returned = [], []
    for part in range(2):
        cut = pl.ds(part * half, half)
        there.append(remote(normed_ref.at[0, cut], normed_ref.at[1, cut], sems, part, far))
        there[part].start()
        returned.append(remote(far_out_ref.at[cut], far_in_ref.at[cut], sems, 2 + part, far))

    def work(side, cut, grads, gate, up, down, slab, first):
        given = normed_ref[side, cut]
        gate_value = dot(given, gate)
        up_value = dot(given, up)
        hidden_grad = dot_nt(grads, down)
        square = gate_value * gate_value
        curve = jnp.tanh(GELU_SCALE * gate_value * (1.0 + GELU_CUBE * square))
        half = 0.5 + 0.5 * curve
        gelu = gate_value * half
        slope = half + (0.5 * GELU_SCALE) * gate_value * (1.0 - curve * curve) * (
            1.0 + (3.0 * GELU_CUBE) * square
        )
        hidden = (gelu * up_value).astype(BF16)
        gate_back = (hidden_grad * up_value * slope).astype(BF16)
        up_back = (hidden_grad * gelu).astype(BF16)
        sums = [dot_tn(given, gate_back), dot_tn(given, up_back), dot_tn(hidden, grads)]
        for index in range(3):
            if side == 0:
                sums_ref[slab, index] = sums[index]
            else:
                sums_ref[slab, index] += sums[index]
        made = dot(hidden, down)
        back = dot_nt(gate_back, gate) + dot_nt(up_back, up)
        if first:
            made_ref[side, cut] = made
            back_ref[side, cut] = back
        else:
            made_ref[side, cut] += made
            back_ref[side, cut] += back

    slabs = ((1, (near_gate_ref, near_up_ref, near_down_ref)), (0, (gate_ref, up_ref, down_ref)))
    for slab, weights in slabs:
        work(0, slice(0, rows), grad_ref[...], *[ref[...] for ref in weights], slab, slab == 1)
    for part in range(2):
        cut = slice(part * half, (part + 1) * half)
        there[part].wait_recv()
        for slab, weights in slabs:
            work(1, cut, far_grad_ref[cut, :], *[ref[...] for ref in weights], slab, slab == 1)
            if part == 1 and slab == 1:
                near_out_ref[...] = sums_ref[1].astype(BF16)
                swap = remote(near_out_ref, near_in_ref, sems, 4, near)
                swap.start()
        far_out_ref[cut, :] = back_ref[1, cut].astype(BF16)
        returned[part].start()
    far_made_ref[...] = made_ref[1].astype(BF16)
    states_part_ref[...] = middle_ref[...] + made_ref[0]
    swap.wait_recv()
    depth = weight_ref.shape[0] // 3
    for index in range(3):
        total = sums_ref[0, index] + near_in_ref[index].astype(F32)
        weight_ref[index * depth : (index + 1) * depth, :] = total.astype(BF16)
    size = weight_ref.shape[0] // 4
    halves = []
    for index, stride in enumerate(strides):
        begin = pl.multiple_of(2 * size * index + (1 - side_of(stride)) * size, 16)
        halves.append(
            remote(
                weight_ref.at[pl.ds(begin, size), :],
                half_in_ref.at[index],
                (half_sends_ref, half_receives_ref),
                index,
                partner(stride),
                axis="dp",
            )
        )
        halves[-1].start()
    for copy in returned:
        copy.wait_recv()
    normed_grad = back_ref[0] + far_in_ref[...].astype(F32)
    part, gain_grad = rms_back(normed_grad, middle_ref[...], gain_ref[...])
    gain_grad_ref[...] = jnp.broadcast_to(gain_grad, gain_grad_ref.shape)
    middle_grad = grad_ref[...].astype(F32) + part
    middle_grad_ref[...] = middle_grad
    low = middle_grad.astype(BF16)
    grad_stage_ref[...] = dot_nt(all_out_ref[...], low).astype(BF16).reshape(4, share, rows)
    out_part = dot(attended, low)
    for rank in range(4):
        out_part_ref[rank] = out_part[rank * share : (rank + 1) * share, :].T.astype(BF16)
    for index, stride in enumerate(strides):
        halves[index].wait_recv()
        begin = pl.multiple_of(2 * size * index + side_of(stride) * size, 16)
        total = weight_ref[pl.ds(begin, size), :].astype(F32) + half_in_ref[index].astype(F32)
        weight_half_ref[index * size : (index + 1) * size, :] = total.astype(BF16)
    for copy in halves:
        copy.wait_send()
    for copy in returned + there + [swap]:
        copy.wait_send()


def front_kernel(width, count, *refs):
    given, outs, landing, rest = refs[:18], refs[18:42], refs[42:48], refs[48:]
    attended_ref, all_out_ref, near_gate_ref, near_up_ref, near_down_ref, far_grad_ref = landing
    forward_kernel(width, count, *given[:17], *outs[:17], *landing, *rest[:24])
    gate_ref, up_ref, down_ref, grad_ref, gain_ref = given[13:]
    ffn_kernel(
        count,
        attended_ref,
        all_out_ref,
        rest[0],
        gain_ref,
        grad_ref,
        far_grad_ref,
        gate_ref,
        near_gate_ref,
        up_ref,
        near_up_ref,
        down_ref,
        near_down_ref,
        *outs[17:],
        *rest[24:],
    )


def back_kernel(
    width,
    count,
    buckets,
    grad_stage_ref,
    total_ref,
    joint_ref,
    bucket_ref,
    gain_ref,
    starts_ref,
    all_taps_ref,
    weight_half_ref,
    out_part_ref,
    far_made_ref,
    ffn_gain_grad_ref,
    query_t_hbm,
    query_hbm,
    twice_hbm,
    key_t_hbm,
    value_hbm,
    out_hbm,
    table_hbm,
    normed_hbm,
    residual_hbm,
    middle_grad_hbm,
    divisor_hbm,
    pooled_hbm,
    mix_hbm,
    all_join_hbm,
    states_part_hbm,
    input_grad_out,
    states_out_out,
    weight_total_out,
    joint_total_out,
    out_total_ref,
    join_total_ref,
    taps_total_ref,
    gains_total_ref,
    bias_total_ref,
    query_t_ref,
    query_ref,
    twice_ref,
    key_t_ref,
    value_ref,
    out_ref,
    table_ref,
    normed_ref,
    residual_ref,
    middle_grad_ref,
    divisor_ref,
    pooled_ref,
    mix_ref,
    all_join_ref,
    states_part_ref,
    load_ref,
    grad_t_ref,
    grad_ref,
    query_grad_ref,
    key_grad_ref,
    value_grad_ref,
    table_grad_ref,
    joint_grad_ref,
    core_out_ref,
    core_in_ref,
    chip_out_ref,
    chip_in_ref,
    made_in_ref,
    out_near_ref,
    out_sum_ref,
    out_far_ref,
    late_ref,
    ids_ref,
    summary_ref,
    join_part_ref,
    join_near_ref,
    join_sum_ref,
    join_far_ref,
    join_ref,
    small_near_ref,
    small_ref,
    small_in_ref,
    bias_ref,
    bias_in_ref,
    input_grad_ref,
    states_out_ref,
    weight_total_ref,
    joint_total_ref,
    ship_ref,
    sends_ref,
    receives_ref,
    chain_sends_ref,
    chain_receives_ref,
    *chain_refs,
):
    me, near, far, cross = ranks()
    peers = (near, far, cross)
    sems = (sends_ref, receives_ref)
    chain_sems = (chain_sends_ref, chain_receives_ref)
    heads, length = twice_ref.shape[0], twice_ref.shape[1]
    rows, model = residual_ref.shape
    share = join_part_ref.shape[1]
    inner = heads * width
    wide, deep = length // 4, length // 8
    strides = strides_of(count)
    turned_strides = [strides[1], strides[0]] + strides[2:]
    chains = []
    plan = [
        (None, 2 * weight_half_ref.shape[0], strides),
        (None, 2 * weight_half_ref.shape[0], turned_strides),
    ]
    for index, (ref, height, order) in enumerate(plan):
        half = height // 2
        chains.append(
            Chain(
                ref,
                (index % 2) * half,
                half,
                order,
                chain_refs[8 * index : 8 * index + 8],
                chain_sems,
                index * Chain.slots(strides),
            )
        )
    weight_chains, late_chains, join_chains = chains, [], []
    for index, chain in enumerate(weight_chains):
        chain.halved(weight_half_ref, index * (weight_half_ref.shape[0] // 2))
    for index, order in enumerate((strides, turned_strides)):
        join_chains.append(
            Exchange(
                join_ref,
                index * (join_ref.shape[0] // 2),
                join_ref.shape[0] // 2,
                order,
                chain_refs[30 + 2 * index : 32 + 2 * index],
                chain_sems,
                2 * Chain.slots(strides) + 2 * Quad.slots(strides) + index * len(strides),
            )
        )
        late_chains.append(
            Quad(
                late_ref,
                index * (late_ref.shape[0] // 2),
                late_ref.shape[0] // 2,
                order,
                chain_refs[16 + 7 * index : 23 + 7 * index],
                chain_sems,
                2 * Chain.slots(strides) + index * Quad.slots(strides),
            )
        )
    greet(peers, strides)
    loads = load_all(
        (
            (query_t_hbm, query_t_ref),
            (query_hbm, query_ref),
            (twice_hbm, twice_ref),
            (key_t_hbm, key_t_ref),
            (value_hbm, value_ref),
            (out_hbm, out_ref),
            (table_hbm, table_ref),
            (normed_hbm, normed_ref),
            (residual_hbm, residual_ref),
            (middle_grad_hbm, middle_grad_ref),
            (divisor_hbm, divisor_ref),
            (pooled_hbm, pooled_ref),
            (mix_hbm, mix_ref),
            (all_join_hbm, all_join_ref),
            (states_part_hbm, states_part_ref),
        ),
        load_ref,
    )
    greeted(peers, strides)
    gradient_copies = []
    for slot, peer in enumerate(peers):
        copy = remote(
            lambda peer=peer: grad_stage_ref.at[peer], lambda: grad_t_ref.at[me], sems, slot, peer
        )
        copy.start()
        gradient_copies.append(copy)
    out_copies = [
        remote(lambda: out_part_ref.at[near], lambda: out_near_ref.at[0], sems, 3, near),
        remote(lambda: out_part_ref.at[cross], lambda: out_near_ref.at[1], sems, 4, near),
    ]
    for copy in out_copies:
        copy.start()
    out_copy = remote(out_sum_ref, out_far_ref, sems, 5, far)
    made_copy = remote(far_made_ref, made_in_ref, sems, 6, far)
    core_copies = [
        remote(lambda: core_out_ref.at[0], lambda: core_in_ref.at[0], sems, 7, near),
        remote(lambda: core_out_ref.at[1], lambda: core_in_ref.at[1], sems, 8, near),
    ]
    chip_copy = remote(chip_out_ref, chip_in_ref, sems, 9, far)
    for chain in weight_chains:
        chain.step()
    made_copy.start()
    grad_t_ref[me] = grad_stage_ref[me]
    query_grad_ref[...] = jnp.zeros_like(query_grad_ref)
    key_grad_ref[...] = jnp.zeros_like(key_grad_ref)
    value_grad_ref[...] = jnp.zeros_like(value_grad_ref)
    table_grad_ref[...] = jnp.zeros_like(table_grad_ref)

    def gather_rows(rank):
        cut = pl.ds(pl.multiple_of(rank * wide, wide), wide)
        joint_grad_ref[cut, :inner] = query_grad_ref[:, cut].T.astype(BF16)
        joint_grad_ref[cut, inner : 2 * inner] = key_grad_ref[cut, :].astype(BF16)
        joint_grad_ref[cut, 2 * inner :] = value_grad_ref[cut, :].astype(BF16)
        return dot_nt(joint_grad_ref[cut, :], joint_ref[...])

    def block_of(relation):
        return 2 * ((me // 2 + relation // 2) % 2) + (me % 2 + relation % 2) % 2

    core = me % 2

    def step(index, carry):
        phase = index // 4
        middle = ((phase + 1) // 2) % 2
        away = middle * (2 + (core + phase - 1) % 2)
        block = block_of(away + (1 - middle) * ((index % 4) // 2))
        turn = (index + (2 + core) * (phase // 2)) % 4
        other = block_of(middle * turn + (1 - middle) * (index % 2 + 2 * (1 - phase // 3)))
        begin = pl.multiple_of(block * wide, wide)
        start = pl.multiple_of(other * wide, wide)
        span = pl.ds(begin, wide)
        @pl.when(index == 2)
        def _():
            gradient_copies[0].wait_recv()

        for first in range(2):

            @pl.when((index == 4 + 4 * first) & (core == first))
            def _():
                gradient_copies[1].wait_recv()

            @pl.when((index == 4 + 4 * first) & (core == 1 - first))
            def _():
                gradient_copies[2].wait_recv()

        @pl.when((index == 0) | (index == 2) | (index == 4) | (index == 8))
        def _():
            grad_ref[span, :] = turned(grad_t_ref[block])

        @pl.when(index == 3)
        def _():
            for copy in out_copies:
                copy.wait_recv()
            ours = out_part_ref[far].astype(F32) + out_near_ref[1].astype(F32)
            out_sum_ref[...] = ours.astype(BF16)
            out_copy.start()

        @pl.when(index == 4)
        def _():
            weight_chains[0].step()
            weight_chains[1].step()

        for first in range(2):

            @pl.when((index == 9 + 3 * first) & (core == first))
            def _():
                chip_out_ref[...] = gather_rows(far).astype(BF16)

            @pl.when((index == 9 + 3 * first) & (core == 1 - first))
            def _():
                core_out_ref[0] = gather_rows(cross).astype(BF16)
                core_copies[0].start()

            @pl.when((index == 10 + 3 * first) & (core == first))
            def _():
                core_copies[0].wait_recv()
                total = chip_out_ref[...].astype(F32) + core_in_ref[0].astype(F32)
                chip_out_ref[...] = total.astype(BF16)
                chip_copy.start()

        for head in range(heads):
            rows = slice(head * width, (head + 1) * width)
            scaled = query_t_ref[rows, span].astype(F32) * LOG2E
            queries = jnp.concatenate(split(scaled), axis=0)
            total = total_ref[head, :, span]
            grads = grad_t_ref[block, rows, :].astype(F32)
            dots = jnp.sum(grads * out_ref[rows, span], axis=0, keepdims=True)
            own_rows = lax.broadcasted_iota(jnp.int32, (inner, wide), 0) // width == head
            own_lanes = lax.broadcasted_iota(jnp.int32, (wide, inner), 1) // width == head
            grad_t_own = jnp.where(own_rows, grad_t_ref[block].astype(F32), 0.0).astype(BF16)
            query_own = jnp.where(own_lanes, query_ref[span, :].astype(F32), 0.0).astype(BF16)
            grad_own = jnp.where(own_lanes, grad_ref[span, :].astype(F32), 0.0).astype(BF16)
            query_grad = jnp.zeros((width, wide), F32)
            for part in range(wide // deep):
                cut = pl.ds(pl.multiple_of(start + part * deep, deep), deep)
                raw = dot(twice_ref[head, cut, :], queries)
                raw_grad = dot(value_ref[cut, :], grad_t_own)
                probs, score_grads = [], []
                for lane in range(0, wide, LANES):
                    piece = slice(lane, lane + LANES)
                    offset = start + part * deep - begin - lane + length - LANES
                    offset = pl.multiple_of(offset, LANES)
                    shift = table_ref[head, pl.ds(offset, deep), :]
                    prob = jnp.exp2(raw[:, piece] + shift - total[:, piece])
                    low = (prob * (raw_grad[:, piece] - dots[:, piece])).astype(BF16)
                    table_grad_ref[head, pl.ds(offset, deep), :] += low.astype(F32)
                    probs.append(prob.astype(BF16))
                    score_grads.append(low)
                probs = jnp.concatenate(probs, axis=1)
                score_grads = jnp.concatenate(score_grads, axis=1)
                value_grad_ref[cut, :] += dot(probs, grad_own)
                key_grad_ref[cut, :] += dot(score_grads, query_own)
                query_grad = query_grad + dot(key_t_ref[rows, cut], score_grads)
            query_grad_ref[rows, span] += query_grad
        return carry

    for copy in loads[:7]:
        copy.wait()
    lax.fori_loop(0, 16, step, 0)
    core_out_ref[1] = gather_rows(near).astype(BF16)
    core_copies[1].start()
    for chain in weight_chains:
        chain.step()
    normed_grad = gather_rows(me)
    for copy in loads[7:]:
        copy.wait()
    late_ref[:, : 3 * inner] = dot_tn(normed_ref[...], joint_grad_ref[...]).astype(BF16)
    out_copy.wait_recv()
    out_sum = (
        out_part_ref[me].astype(F32) + out_near_ref[0].astype(F32) + out_far_ref[...].astype(F32)
    )
    late_ref[:, 3 * inner :] = out_sum.astype(BF16)
    for chain in late_chains:
        chain.step()
    core_copies[1].wait_recv()
    normed_grad = normed_grad + core_in_ref[1].astype(F32)
    chip_copy.wait_recv()
    normed_grad = normed_grad + chip_in_ref[...].astype(F32)
    part, gain_grad = rms_back(normed_grad, residual_ref[...], gain_ref[...])
    residual_grad = middle_grad_ref[...] + part
    low = residual_grad.astype(BF16)
    join_part_ref[...] = dot_tn(mix_ref[...], low).astype(BF16).reshape(4, share, model)
    join_copies = [
        remote(join_part_ref.at[near], join_near_ref.at[0], sems, 16, near),
        remote(join_part_ref.at[cross], join_near_ref.at[1], sems, 17, near),
    ]
    for copy in join_copies:
        copy.start()
    words = Words(starts_ref, ids_ref, me, 4)
    picked = words.pick(back_target)
    high_mix, low_mix = split(dot_nt(low, all_join_ref[...]))
    summary_ref[me] = dot(picked, high_mix) + dot(picked, low_mix)
    copies = []
    for slot, peer in enumerate(peers):
        copies.append(remote(summary_ref.at[me], summary_ref.at[me], sems, 13 + slot, peer))
        copies[-1].start()
    for copy in join_copies:
        copy.wait_recv()
    join_sum_ref[...] = (
        join_part_ref[far].astype(F32) + join_near_ref[1].astype(F32)
    ).astype(BF16)
    join_copy = remote(join_sum_ref, join_far_ref, sems, 21, far)
    join_copy.start()
    for chain in weight_chains:
        chain.step()
    for chain in late_chains:
        chain.step()
    table = words.table()
    word_grad = dot(table, high_mix) + dot(table, low_mix)
    pooled = pooled_ref[...]
    tap_rows = [jnp.sum(pooled * word_grad, axis=0, keepdims=True)]
    for lag in range(1, 4):
        tap_rows.append(jnp.sum(pltpu.roll(pooled, lag, 0) * word_grad, axis=0, keepdims=True))
    tap_rows += [gain_grad, ffn_gain_grad_ref[0:1], jnp.zeros((2, model), F32)]
    small_near_ref[me] = jnp.concatenate(tap_rows, axis=0)
    for slot, peer in enumerate(peers):
        copies.append(remote(small_near_ref.at[me], small_near_ref.at[me], sems, 18 + slot, peer))
        copies[-1].start()
    shipped = []

    def ship(source, target):
        copy = pltpu.make_async_copy(source, target, ship_ref.at[len(shipped)])
        copy.start()
        shipped.append(copy)

    def write_weights(span, values):
        weight_total_ref[span, :] = values

    def write_late(span, values):
        joint_total_ref[span, :] = values

    def write_join(span, values):
        join_total_ref[span, :] = values

    bias_copies, small_copies = [], []

    def exchange(index, copies, ours, theirs, slot):
        stride = strides[index]
        copies.append(
            remote(
                ours.at[index],
                theirs.at[index],
                sems,
                slot + 2 * index,
                lambda: partner(stride),
                axis="dp",
            )
        )
        copies[-1].start()

    def pass_on(index, copies, ours, theirs, slot):
        copies[index].wait_recv()
        total = ours[index] + theirs[index]
        if index + 1 < len(strides):
            ours[index + 1] = total
            exchange(index + 1, copies, ours, theirs, slot)
        return total

    bias_parts = (bias_copies, bias_ref, bias_in_ref, 23)
    small_parts = (small_copies, small_ref, small_in_ref, 22)
    bias_ref[0] = bias_grad_rows(table_grad_ref, bucket_ref, buckets)
    exchange(0, *bias_parts)
    join_copy.wait_recv()
    join_ref[...] = (
        join_part_ref[me].astype(F32) + join_near_ref[0].astype(F32) + join_far_ref[...].astype(F32)
    ).astype(BF16)
    for chain in join_chains:
        chain.step(write_join)
    for copy in copies:
        copy.wait_recv()
    small = small_near_ref[0]
    for rank in range(1, 4):
        small = small + small_near_ref[rank]
    small_ref[0] = small
    exchange(0, *small_parts)
    for chain in late_chains:
        chain.step()
    word_grad = word_grad + dot(words.place(back_target, back_valid), stacked(summary_ref))
    taps = all_taps_ref[...]
    height = word_grad.shape[0]
    pooled_grad = word_grad * taps[0:1]
    for lag in range(1, 4):
        pooled_grad = pooled_grad + pltpu.roll(word_grad, height - lag, 0) * taps[lag : lag + 1]
    divisor = divisor_ref[...]
    pooled_grad = pooled_grad / jnp.concatenate([divisor] * (model // LANES), axis=1)
    high, low = split(pooled_grad)
    input_grad = residual_grad + (dot_tn(table, high) + dot_tn(table, low))
    input_grad_ref[...] = input_grad[:, None, :]
    ship(input_grad_ref, input_grad_out)
    bias = pass_on(0, *bias_parts)
    small = pass_on(0, *small_parts)
    for chain in join_chains:
        chain.step(write_join)
    made_copy.wait_recv()
    states_out_ref[...] = (states_part_ref[...] + made_in_ref[...].astype(F32))[:, None, :]
    ship(states_out_ref, states_out_out)
    for chain in weight_chains:
        while chain.at < chain.steps:
            chain.step(write_weights)
    ship(weight_total_ref, weight_total_out)
    for chain in late_chains:
        chain.step()
    bias = pass_on(1, *bias_parts)
    small = pass_on(1, *small_parts)
    for chain in join_chains:
        chain.step(write_join)
    for turn in range(1, len(strides) + 1):
        for group, finish in ((join_chains, write_join), (late_chains, write_late)):
            for chain in group:
                if chain.at < chain.steps:
                    chain.step(finish)
        if 1 < turn < len(strides):
            bias = pass_on(turn, *bias_parts)
            small = pass_on(turn, *small_parts)
    for chain in join_chains:
        while chain.at < chain.steps:
            chain.step(write_join)
    for chain in late_chains:
        while chain.at < chain.steps:
            chain.step(write_late)
    ship(joint_total_ref, joint_total_out)
    own = jnp.zeros((8, share), F32)
    for rank in range(4):
        own = jnp.where(me == rank, small[:, rank * share : (rank + 1) * share], own)
    taps_total_ref[...] = own
    gains_total_ref[...] = small
    bias_total_ref[...] = bias
    out_total_ref[...] = joint_total_ref[:, 3 * inner :].T
    for copy in shipped:
        copy.wait()
    finished = gradient_copies + out_copies + core_copies + [chip_copy, made_copy, out_copy]
    for copy in finished + copies + join_copies + [join_copy] + small_copies + bias_copies:
        copy.wait_send()


def place_kernel(
    joint_hbm,
    weight_hbm,
    states_hbm,
    input_hbm,
    out_hbm,
    join_hbm,
    taps_ref,
    gains_ref,
    bias_ref,
    states_out,
    input_out,
    two_out,
    three_out,
    four_out,
    join_out,
    norm_out,
    query_out,
    key_out,
    value_out,
    bias_out,
    out_out,
    ffn_out,
    gate_out,
    up_out,
    down_out,
    joint_ref,
    weight_ref,
    states_ref,
    input_ref,
    out_ref,
    join_ref,
    sems,
):
    loads = []
    for source, target in (
        (weight_hbm, weight_ref),
        (states_hbm, states_ref),
        (input_hbm, input_ref),
        (joint_hbm, joint_ref),
        (out_hbm, out_ref),
        (join_hbm, join_ref),
    ):
        loads.append(pltpu.make_async_copy(source, target, sems.at[10 + len(loads)]))
        loads[-1].start()
    inner, model = query_out.shape[1], gate_out.shape[0]
    pairs = [
        (weight_ref.at[pl.ds(index * model, model), :], target, 0)
        for index, target in enumerate((gate_out, up_out, down_out))
    ]
    pairs += [(states_ref, states_out, 1), (input_ref, input_out, 2)]
    pairs += [
        (joint_ref.at[:, pl.ds(index * inner, inner)], target, 3)
        for index, target in enumerate((query_out, key_out, value_out))
    ]
    pairs += [(out_ref, out_out, 4), (join_ref, join_out, 5)]
    copies, arrived = [], -1
    for index, (source, target, load) in enumerate(pairs):
        if load > arrived:
            loads[load].wait()
            arrived = load
        copies.append(pltpu.make_async_copy(source, target, sems.at[index]))
        copies[-1].start()
    two_out[...] = taps_ref[:2]
    three_out[...] = taps_ref[:3]
    four_out[...] = taps_ref[:4]
    norm_out[...] = gains_ref[4:5]
    ffn_out[...] = gains_ref[5:6]
    heads, buckets = bias_out.shape
    bias_out[...] = bias_ref[:heads, :buckets]
    for copy in copies:
        copy.wait()


def shards(
    byte_states,
    word_start,
    bucket_ids,
    conv_two,
    conv_three,
    conv_four,
    join_weight,
    norm_gain,
    query_weight,
    key_weight,
    value_weight,
    position_bias,
    out_weight,
    ffn_gain,
    gate_weight,
    up_weight,
    down_weight,
    out_grad,
):
    rows, batch, model = byte_states.shape
    length = word_start.shape[0]
    buckets, heads = position_bias.shape
    inner = query_weight.shape[1]
    width = inner // heads
    share = join_weight.shape[0]
    hidden = gate_weight.shape[1]
    count = rows + 16
    replicas = lax.axis_size("dp")
    strides = strides_of(replicas)
    states = byte_states.reshape(rows, model)
    grads = out_grad.reshape(rows, model)
    starts = word_start.reshape(length // LANES, LANES)
    span = bucket_ids.shape[0] + 1 - LANES
    made = (
        like((rows, model), F32),
        like((length, model), BF16),
        like((length, inner), BF16),
        like((inner, length), BF16),
        like((heads, length, 2 * width), BF16),
        like((inner, length), BF16),
        like((length, inner), BF16),
        like((heads, span, LANES), F32),
        like((count, LANES), F32),
        like((count, model), F32),
        like((rows, model), BF16),
        like((4 * share, model), BF16),
        like((model, 3 * inner), BF16),
        like((1, span + LANES), jnp.int32),
    )
    (
        residual,
        normed,
        queries,
        queries_t,
        twice_keys,
        keys_t,
        values,
        table,
        divisor,
        pooled,
        mix,
        all_taps,
        all_join,
        joint_weight,
        bucket_row,
        outs,
        totals,
        states_part,
        far_made,
        middle_grad,
        ffn_gain_grad,
        weight_half,
        out_part,
        grad_stage,
    ) = pl.pallas_call(
        functools.partial(front_kernel, width, replicas),
        out_shape=(
            *made[:11],
            like((8, model), F32),
            *made[11:],
            like((inner, length), F32),
            like((heads, 1, length), F32),
            like((rows, model), F32),
            like((rows, model), BF16),
            like((rows, model), F32),
            like((8, model), F32),
            like((3 * model // 2, hidden), BF16),
            like((4, model, inner), BF16),
            like((4, inner, rows), BF16),
        ),
        in_specs=whole(18),
        out_specs=anywhere(11) + whole(1) + anywhere(3) + whole(9),
        scratch_shapes=[
            pltpu.VMEM((4, inner, rows), BF16),
            pltpu.VMEM((4 * inner, model), BF16),
            pltpu.VMEM(gate_weight.shape, BF16),
            pltpu.VMEM(up_weight.shape, BF16),
            pltpu.VMEM(down_weight.shape, BF16),
            pltpu.VMEM((rows, model), BF16),
            *[pltpu.VMEM(part.shape, part.dtype) for part in made],
            pltpu.VMEM((inner, length), BF16),
            pltpu.VMEM((length // LANES, LANES), F32),
            pltpu.VMEM((4, 8, model + LANES), F32),
            pltpu.VMEM((4, 8, share), F32),
            pltpu.VMEM((length // 2, rows), F32),
            pltpu.VMEM((heads, 1, length), F32),
            pltpu.VMEM((4, inner, rows), BF16),
            pltpu.SemaphoreType.DMA((len(made),)),
            *semaphores(26),
            pltpu.VMEM((rows, model), F32),
            pltpu.VMEM((2, rows, model), BF16),
            pltpu.VMEM((2, rows, model), F32),
            pltpu.VMEM((2, rows, model), F32),
            pltpu.VMEM((2, 3, model, hidden), F32),
            pltpu.VMEM((rows, model), BF16),
            pltpu.VMEM((rows, model), BF16),
            pltpu.VMEM((3, model, hidden), BF16),
            pltpu.VMEM((3, model, hidden), BF16),
            pltpu.VMEM((3 * model, hidden), BF16),
            pltpu.VMEM((2, 3 * model // 4, hidden), BF16),
            *semaphores(5),
            *semaphores(2),
        ],
        compiler_params=params(0),
        name="front",
    )(
        states,
        starts,
        conv_two,
        conv_three,
        conv_four,
        join_weight,
        norm_gain[None],
        query_weight,
        key_weight,
        value_weight,
        bucket_ids[None],
        position_bias.T,
        out_weight,
        gate_weight,
        up_weight,
        down_weight,
        grads,
        ffn_gain[None],
    )
    chain_scratch = []
    for _ in range(2):
        chain_scratch += Chain.scratch(3 * model // 2, hidden, len(strides) - 2, True)
    for _ in range(2):
        chain_scratch += Quad.scratch(model // 2, 4 * inner, len(strides) - 3)
    for _ in range(2):
        chain_scratch += Exchange.scratch(share // 2, model, len(strides))
    loaded = (queries_t, queries, twice_keys, keys_t, values, outs, table)
    loaded += (normed, residual, middle_grad, divisor, pooled, mix, all_join, states_part)
    (
        input_grad,
        out_states,
        weight_total,
        joint_total,
        out_total,
        join_total,
        taps_total,
        gains_total,
        bias_total,
    ) = pl.pallas_call(
        functools.partial(back_kernel, width, replicas, buckets),
        out_shape=(
            like((rows, 1, model), F32),
            like((rows, 1, model), F32),
            like((3 * model, hidden), F32),
            like((model, 4 * inner), F32),
            like((inner, model), F32),
            like((share, model), F32),
            like((8, share), F32),
            like((8, model), F32),
            like((8, LANES), F32),
        ),
        in_specs=whole(11) + anywhere(len(loaded)),
        out_specs=anywhere(4) + whole(5),
        scratch_shapes=[
            *[pltpu.VMEM(part.shape, part.dtype) for part in loaded],
            pltpu.SemaphoreType.DMA((len(loaded),)),
            pltpu.VMEM((4, inner, rows), BF16),
            pltpu.VMEM((length, inner), BF16),
            pltpu.VMEM((inner, length), F32),
            pltpu.VMEM((length, inner), F32),
            pltpu.VMEM((length, inner), F32),
            pltpu.VMEM((heads, span, LANES), F32),
            pltpu.VMEM((length, 3 * inner), BF16),
            pltpu.VMEM((2, rows, model), BF16),
            pltpu.VMEM((2, rows, model), BF16),
            pltpu.VMEM((rows, model), BF16),
            pltpu.VMEM((rows, model), BF16),
            pltpu.VMEM((rows, model), BF16),
            pltpu.VMEM((2, model, inner), BF16),
            pltpu.VMEM((model, inner), BF16),
            pltpu.VMEM((model, inner), BF16),
            pltpu.VMEM((model, 4 * inner), BF16),
            pltpu.VMEM((length // LANES, LANES), F32),
            pltpu.VMEM((4, 8, model), F32),
            pltpu.VMEM((4, share, model), BF16),
            pltpu.VMEM((2, share, model), BF16),
            pltpu.VMEM((share, model), BF16),
            pltpu.VMEM((share, model), BF16),
            pltpu.VMEM((share, model), BF16),
            pltpu.VMEM((4, 8, model), F32),
            pltpu.VMEM((len(strides), 8, model), F32),
            pltpu.VMEM((len(strides), 8, model), F32),
            pltpu.VMEM((len(strides), 8, LANES), F32),
            pltpu.VMEM((len(strides), 8, LANES), F32),
            pltpu.VMEM((rows, 1, model), F32),
            pltpu.VMEM((rows, 1, model), F32),
            pltpu.VMEM((3 * model, hidden), F32),
            pltpu.VMEM((model, 4 * inner), F32),
            pltpu.SemaphoreType.DMA((4,)),
            *semaphores(22 + 2 * len(strides)),
            *semaphores(2 * Chain.slots(strides) + 2 * Quad.slots(strides) + 2 * len(strides)),
            *chain_scratch,
        ],
        compiler_params=params(3),
        name="back",
    )(
        grad_stage,
        totals,
        joint_weight,
        bucket_row,
        norm_gain[None],
        starts,
        all_taps,
        weight_half,
        out_part,
        far_made,
        ffn_gain_grad,
        *loaded,
    )
    placed = pl.pallas_call(
        place_kernel,
        out_shape=(
            like((rows, 1, model), F32),
            like((rows, 1, model), F32),
            like(conv_two.shape, F32),
            like(conv_three.shape, F32),
            like(conv_four.shape, F32),
            like((share, model), F32),
            like((1, model), F32),
            like((model, inner), F32),
            like((model, inner), F32),
            like((model, inner), F32),
            like((heads, buckets), F32),
            like((inner, model), F32),
            like((1, model), F32),
            like((model, hidden), F32),
            like((model, hidden), F32),
            like((hidden, model), F32),
        ),
        in_specs=anywhere(6) + whole(3),
        out_specs=anywhere(2)
        + whole(3)
        + anywhere(1)
        + whole(1)
        + anywhere(3)
        + whole(1)
        + anywhere(1)
        + whole(1)
        + anywhere(3),
        scratch_shapes=[
            *[
                pltpu.VMEM(part.shape, F32)
                for part in (joint_total, weight_total, out_states, input_grad, out_total, join_total)
            ],
            pltpu.SemaphoreType.DMA((16,)),
        ],
        compiler_params=params(),
        name="place",
    )(
        joint_total,
        weight_total,
        out_states,
        input_grad,
        out_total,
        join_total,
        taps_total,
        gains_total,
        bias_total,
    )
    placed = list(placed)
    placed[6], placed[10], placed[12] = placed[6][0], placed[10].T, placed[12][0]
    return tuple(placed)


def solution(mesh):
    return jax.shard_map(
        shards,
        mesh=mesh,
        in_specs=(
            P("mp", "dp", None),
            P(None, "dp"),
            P(),
            P(None, "mp"),
            P(None, "mp"),
            P(None, "mp"),
            P("mp", None),
            P(),
            P(None, "mp"),
            P(None, "mp"),
            P(None, "mp"),
            P(None, "mp"),
            P("mp", None),
            P(),
            P(None, "mp"),
            P(None, "mp"),
            P("mp", None),
            P("mp", "dp", None),
        ),
        out_specs=(
            P("mp", "dp", None),
            P("mp", "dp", None),
            P(None, "mp"),
            P(None, "mp"),
            P(None, "mp"),
            P("mp", None),
            P(),
            P(None, "mp"),
            P(None, "mp"),
            P(None, "mp"),
            P(None, "mp"),
            P("mp", None),
            P(),
            P(None, "mp"),
            P(None, "mp"),
            P("mp", None),
        ),
        check_vma=False,
    )
```

```python
import functools

import jax
import jax.numpy as jnp
from jax import lax
from jax.experimental import pallas as pl
from jax.experimental.pallas import tpu as pltpu
from jax.sharding import PartitionSpec as P

EPSILON = 1e-06
LOG2E = 1.4426950408889634
GELU_SCALE = 0.7978845608028654
GELU_CUBE = 0.044715
F32 = jnp.float32
BF16 = jnp.bfloat16
LANES = 128
HALO = 3
VMEM_LIMIT = 56 << 20
MESH = pl.DeviceIdType.MESH


def whole(count):
    return [pl.BlockSpec(memory_space=pltpu.VMEM)] * count


def anywhere(count):
    return [pl.BlockSpec(memory_space=pl.ANY)] * count


def params(collective=None):
    return pltpu.CompilerParams(
        vmem_limit_bytes=VMEM_LIMIT, collective_id=collective, has_side_effects=collective is not None
    )


def like(shape, dtype):
    return jax.ShapeDtypeStruct(shape, dtype)


def dot(lhs, rhs):
    return jnp.dot(lhs, rhs, preferred_element_type=F32)


def dot_nt(lhs, rhs):
    return lax.dot_general(lhs, rhs, (((1,), (1,)), ((), ())), preferred_element_type=F32)


def dot_tn(lhs, rhs):
    return lax.dot_general(lhs, rhs, (((0,), (0,)), ((), ())), preferred_element_type=F32)


def split(values):
    high = values.astype(BF16)
    return high, (values - high.astype(F32)).astype(BF16)


def turned(values):
    return values.astype(F32).T.astype(BF16)


def ranks():
    me = lax.axis_index("mp")
    near = me + 1 - 2 * (me % 2)
    return me, near, (me + 2) % 4, (near + 2) % 4


def greet(peers, strides=()):
    barrier = pltpu.get_barrier_semaphore()
    for peer in peers:
        pl.semaphore_signal(barrier, inc=1, device_id={"mp": peer}, device_id_type=MESH)
    for stride in strides:
        pl.semaphore_signal(barrier, inc=1, device_id={"dp": partner(stride)}, device_id_type=MESH)


def greeted(peers, strides=()):
    pl.semaphore_wait(pltpu.get_barrier_semaphore(), len(peers) + len(strides))


def load_all(pairs, sems):
    copies = []
    for source, target in pairs:
        copies.append(pltpu.make_async_copy(source, target, sems.at[len(copies)]))
        copies[-1].start()
    return copies


def side_of(stride):
    return (lax.axis_index("dp") // stride) % 2


def partner(stride):
    return lax.axis_index("dp") + stride - 2 * stride * side_of(stride)


def strides_of(count):
    strides = []
    while 2 ** len(strides) < count:
        strides.append(2 ** len(strides))
    return strides


class remote:
    def __init__(self, *given, axis="mp"):
        self.given, self.axis = given, axis

    def start(self):
        described(*self.given, self.axis).start()

    def wait_recv(self):
        described(*self.given, self.axis).wait_recv()

    def wait_send(self):
        described(*self.given, self.axis).wait_send()

    def wait(self):
        described(*self.given, self.axis).wait()


def described(source, target, sems, slot, peer, axis):
    source, target, peer = [part() if callable(part) else part for part in (source, target, peer)]
    sends, receives = sems
    return pltpu.make_async_remote_copy(
        src_ref=source,
        dst_ref=target,
        send_sem=sends.at[slot],
        recv_sem=receives.at[slot],
        device_id={axis: peer},
        device_id_type=MESH,
    )


def semaphores(count):
    return [pltpu.SemaphoreType.DMA((count,)), pltpu.SemaphoreType.DMA((count,))]


class Quad:
    def __init__(self, source_ref, base, rows, strides, scratch, sems, first_slot):
        self.source, self.base, self.rows, self.strides = source_ref, base, rows, strides
        self.half_in, self.half, self.pieces_in, self.pieces, self.others_in, self.gathered, self.far_half = scratch
        self.sems, self.slot, self.at = sems, first_slot, 0
        self.copies, self.count = [], 0
        self.steps = len(strides) + 2

    @staticmethod
    def scratch(rows, width, exchanges):
        half, piece = rows // 2, rows // 8
        return [
            pltpu.VMEM((half, width), BF16),
            pltpu.VMEM((half, width), BF16),
            pltpu.VMEM((3, piece, width), BF16),
            pltpu.VMEM((exchanges + 1, piece, width), BF16),
            pltpu.VMEM((exchanges + 1, piece, width), BF16),
            pltpu.VMEM((3, piece, width), BF16),
            pltpu.VMEM((half, width), BF16),
        ]

    @staticmethod
    def slots(strides):
        return len(strides) + 6

    def send(self, source, target, peer):
        copy = remote(source, target, self.sems, self.slot + self.count, peer, axis="dp")
        copy.start()
        self.copies.append(copy)
        self.count += 1

    def away(self, turn):
        first, second = self.strides[1:3]
        flips = (turn % 2, turn // 2)
        device, place = lax.axis_index("dp"), 0
        for flip, stride, weight in zip(flips, (first, second), (1, 2)):
            side = side_of(stride)
            device = device + flip * (stride - 2 * stride * side)
            place = place + weight * (side + flip * (1 - 2 * side))
        return device, place

    def piece(self, turn):
        height = self.rows // 8
        return pl.ds(pl.multiple_of(self.away(turn)[1] * height, 16), height)

    def step(self, finish=None):
        at, half = self.at, self.rows // 2
        first, others = self.strides[0], self.strides[3:]
        self.at += 1
        for copy in self.copies:
            copy.wait_recv()
        done, self.copies = self.copies, []
        if at == 0:
            begin = pl.multiple_of(self.base + (1 - side_of(first)) * half, 16)
            self.send(self.source.at[pl.ds(begin, half), :], self.half_in, partner(first))
        elif at == 1:
            begin = pl.multiple_of(self.base + side_of(first) * half, 16)
            mine = self.source[pl.ds(begin, half), :].astype(F32)
            self.half[...] = (mine + self.half_in[...].astype(F32)).astype(BF16)
            for turn in range(1, 4):
                part = self.half.at[self.piece(turn), :]
                self.send(part, self.pieces_in.at[turn - 1], self.away(turn)[0])
        elif at <= 2 + len(others):
            if at == 2:
                total = self.half[self.piece(0), :].astype(F32)
                for turn in range(1, 4):
                    total = total + self.pieces_in[turn - 1].astype(F32)
            else:
                total = self.pieces[at - 3].astype(F32) + self.others_in[at - 3].astype(F32)
            self.pieces[at - 2] = total.astype(BF16)
            if at < 2 + len(others):
                stride = others[at - 2]
                self.send(self.pieces.at[at - 2], self.others_in.at[at - 2], partner(stride))
            else:
                for turn in range(1, 4):
                    self.send(self.pieces.at[at - 2], self.gathered.at[turn - 1], self.away(turn)[0])
        elif at == 3 + len(others):
            self.half[self.piece(0), :] = self.pieces[len(others)]
            for turn in range(1, 4):
                self.half[self.piece(turn), :] = self.gathered[turn - 1]
            self.send(self.half, self.far_half, partner(first))
        else:
            side = side_of(first)
            mine = pl.ds(pl.multiple_of(self.base + side * half, 16), half)
            other = pl.ds(pl.multiple_of(self.base + (1 - side) * half, 16), half)
            finish(mine, self.half[...].astype(F32))
            finish(other, self.far_half[...].astype(F32))
        for copy in done:
            copy.wait_send()


class Exchange:
    def __init__(self, source_ref, base, rows, strides, scratch, sems, first_slot):
        self.source, self.base, self.rows, self.strides = source_ref, base, rows, strides
        self.ours, self.theirs = scratch
        self.sems, self.slot, self.at = sems, first_slot, 0
        self.copies = []
        self.steps = len(strides) + 1

    @staticmethod
    def scratch(rows, width, strides):
        return [pltpu.VMEM((strides, rows, width), BF16)] * 2

    def step(self, finish=None):
        at = self.at
        self.at += 1
        if at == 0:
            total = self.source[self.base : self.base + self.rows, :].astype(F32)
        else:
            self.copies[-1].wait_recv()
            total = self.ours[at - 1].astype(F32) + self.theirs[at - 1].astype(F32)
        if at < len(self.strides):
            self.ours[at] = total.astype(BF16)
            stride = self.strides[at]
            copy = remote(
                lambda: self.ours.at[at],
                lambda: self.theirs.at[at],
                self.sems,
                self.slot + at,
                lambda: partner(stride),
                axis="dp",
            )
            copy.start()
            self.copies.append(copy)
        else:
            finish(slice(self.base, self.base + self.rows), total)
            for copy in self.copies:
                copy.wait_send()


class Chain:
    def __init__(self, source_ref, base, rows, strides, scratch, sems, first_slot):
        self.source, self.base, self.rows, self.strides = source_ref, base, rows, strides
        (
            self.half_in,
            self.half,
            self.quarter_in,
            self.quarter,
            self.whole_quarter,
            self.gathered_quarter,
            self.both,
            self.gathered_half,
        ) = scratch
        self.sems, self.slot, self.at = sems, first_slot, 0
        self.copies = []
        self.steps = len(strides) + 3
        self.half_base = 0

    def halved(self, half_ref, base):
        self.half, self.half_base, self.at = half_ref, base, 1
        return self

    @staticmethod
    def scratch(rows, width, exchanges, halved=False):
        half, quarter = (rows // 2, width), (rows // 4, width)
        first = (16, LANES) if halved else half
        return [
            pltpu.VMEM(first, BF16),
            pltpu.VMEM(first, BF16),
            pltpu.VMEM((exchanges + 1, *quarter), BF16),
            pltpu.VMEM((exchanges, *quarter), BF16),
            pltpu.VMEM(quarter, BF16),
            pltpu.VMEM(quarter, BF16),
            pltpu.VMEM(half, BF16),
            pltpu.VMEM(half, BF16),
        ]

    @staticmethod
    def slots(strides):
        return len(strides) + 2

    def send(self, source, target, stride):
        copy = remote(
            source, target, self.sems, self.slot + len(self.copies), lambda: partner(stride), axis="dp"
        )
        copy.start()
        self.copies.append(copy)

    def step(self, finish=None):
        first, second, others = self.strides[0], self.strides[1], self.strides[2:]
        half, quarter = self.rows // 2, self.rows // 4
        at = self.at
        self.at += 1
        if self.copies:
            self.copies[-1].wait_recv()
        if at == 0:
            self.send(lambda: self.source.at[pl.ds(pl.multiple_of(self.base + (1 - side_of(first)) * half, 16), half), :], self.half_in, first)
        elif at == 1:
            if self.copies:
                begin = pl.multiple_of(self.base + side_of(first) * half, 16)
                mine = self.source[pl.ds(begin, half), :].astype(F32)
                self.half[...] = (mine + self.half_in[...].astype(F32)).astype(BF16)
            self.send(lambda: self.half.at[
                    pl.ds(
                        pl.multiple_of(self.half_base + (1 - side_of(second)) * quarter, 16), quarter
                    ),
                    :,
                ], lambda: self.quarter_in.at[0], second)
        elif at <= 1 + len(others):
            if at == 2:
                begin = pl.multiple_of(self.half_base + side_of(second) * quarter, 16)
                mine = self.half[pl.ds(begin, quarter), :]
            else:
                mine = self.quarter[at - 3]
            total = mine.astype(F32) + self.quarter_in[at - 2].astype(F32)
            self.quarter[at - 2] = total.astype(BF16)
            self.send(
                lambda: self.quarter.at[at - 2], lambda: self.quarter_in.at[at - 1], others[at - 2]
            )
        elif at == 2 + len(others):
            total = self.quarter[at - 3].astype(F32) + self.quarter_in[at - 2].astype(F32)
            self.whole_quarter[...] = total.astype(BF16)
            self.send(self.whole_quarter, self.gathered_quarter, second)
        elif at == 3 + len(others):
            side = side_of(second)
            mine = pl.ds(pl.multiple_of(side * quarter, 16), quarter)
            other = pl.ds(pl.multiple_of((1 - side) * quarter, 16), quarter)
            self.both[mine, :] = self.whole_quarter[...]
            self.both[other, :] = self.gathered_quarter[...]
            self.send(self.both, self.gathered_half, first)
        else:
            side = side_of(first)
            mine = pl.ds(pl.multiple_of(self.base + side * half, 16), half)
            other = pl.ds(pl.multiple_of(self.base + (1 - side) * half, 16), half)
            finish(mine, self.both[...].astype(F32))
            finish(other, self.gathered_half[...].astype(F32))
            for copy in self.copies:
                copy.wait_send()


def rms(values, gain):
    return values * lax.rsqrt(jnp.mean(values * values, axis=1, keepdims=True) + EPSILON) * gain


def rms_back(grads, values, gain):
    scale = lax.rsqrt(jnp.mean(values * values, axis=1, keepdims=True) + EPSILON)
    gain_grad = jnp.sum(grads * values * scale, axis=0, keepdims=True)
    raised = grads * gain
    mean = jnp.mean(raised * values, axis=1, keepdims=True)
    return scale * raised - values * (scale * scale * scale * mean), gain_grad


def bucket_hits(bucket_ref, buckets):
    span = bucket_ref.shape[1]
    rows = lax.broadcasted_iota(jnp.int32, (buckets, span), 0)
    return rows == jnp.broadcast_to(bucket_ref[...], (buckets, span))


def fill_bias_table(bucket_ref, bias_ref, table_ref):
    span = bucket_ref.shape[1]
    heads, buckets = bias_ref.shape
    hits = bucket_hits(bucket_ref, buckets).astype(F32).astype(BF16)
    bias = bias_ref[...]
    first = bias.astype(BF16)
    second, third = split(bias - first.astype(F32))
    rows = jnp.concatenate([first, second, third, jnp.zeros((16 - 3 * heads, buckets), BF16)], axis=0)
    lines = dot(rows, hits)
    for head in range(heads):
        line = lines[head : head + 1] + (
            lines[heads + head : heads + head + 1] + lines[2 * heads + head : 2 * heads + head + 1]
        )
        skew = pltpu.roll(
            jnp.broadcast_to(line * LOG2E, (LANES, span)), span - LANES + 1, 1, stride=1, stride_axis=0
        )
        for block in range(span // LANES - 1):
            cut = slice(block * LANES, (block + 1) * LANES)
            table_ref[head, cut, :] = skew[:, cut].T


def bias_grad_rows(table_ref, bucket_ref, buckets):
    span = bucket_ref.shape[1]
    heads = table_ref.shape[0]
    hits = bucket_hits(bucket_ref, buckets).astype(F32).astype(BF16)
    lines = []
    for head in range(heads):
        blocks = [
            table_ref[head, block * LANES : (block + 1) * LANES, :].T
            for block in range(span // LANES - 1)
        ]
        skew = jnp.concatenate(blocks + [jnp.zeros((LANES, LANES), F32)], axis=1)
        rows = LANES // 2
        while rows >= 8:
            skew = skew[:rows] + pltpu.roll(skew[rows:], span - rows, 1)
            rows //= 2
        line = jnp.zeros((1, span), F32)
        for row in range(8):
            line = line + pltpu.roll(skew[row : row + 1], LANES - 1 - row, 1)
        lines.append(line)
    lines = jnp.concatenate(lines + [jnp.zeros((8 - heads, span), F32)], axis=0)
    first = lines.astype(BF16)
    second, third = split(lines - first.astype(F32))
    parts = dot_nt(jnp.concatenate([first.astype(F32), second.astype(F32)], axis=0).astype(BF16), hits)
    rest = dot_nt(jnp.concatenate([third.astype(F32), jnp.zeros((8, span), F32)], axis=0).astype(BF16), hits)
    made = parts[:8] + (parts[8:] + rest[:8])
    return jnp.concatenate([made, jnp.zeros((8, LANES - buckets), F32)], axis=1)


def word_numbers(starts):
    rows = starts.shape[0]
    upper = lax.broadcasted_iota(jnp.int32, (LANES, LANES), 0) <= lax.broadcasted_iota(
        jnp.int32, (LANES, LANES), 1
    )
    within = dot(starts.astype(F32).astype(BF16), upper.astype(F32).astype(BF16))
    totals = jnp.broadcast_to(within[:, LANES - 1 :], (rows, LANES)).astype(BF16)
    lower = lax.broadcasted_iota(jnp.int32, (rows, rows), 1) < lax.broadcasted_iota(
        jnp.int32, (rows, rows), 0
    )
    return within + dot(lower.astype(F32).astype(BF16), totals) - 1.0


class Words:
    def __init__(self, starts_ref, ids_ref, me, ranks_count):
        ids = word_numbers(starts_ref[...])
        ids_ref[...] = ids
        per = ids.shape[0] // ranks_count
        self.firsts = [ids[per * rank : per * rank + 1, 0:1] for rank in range(ranks_count)]
        self.lasts = [
            ids[per * (rank + 1) - 1 : per * (rank + 1), LANES - 1 :] for rank in range(ranks_count)
        ]
        pieces = [ids_ref[pl.ds(me * per + piece, 1), :] for piece in range(per)]
        self.row = jnp.concatenate(pieces, axis=1)
        self.first = self.row[:, 0:1]
        self.last = self.row[:, per * LANES - 1 :]
        self.me = me
        self.count = per * LANES

    def table(self):
        shape = (self.count + 16, self.count)
        rows = lax.broadcasted_iota(jnp.int32, shape, 0).astype(F32)
        return (rows == self.row - self.first + HALO).astype(F32).astype(BF16)

    def pick(self, target):
        slots = lax.broadcasted_iota(jnp.int32, (8, 1), 0)
        hits = target(slots, self.first, self.last) == self.row
        return hits.astype(F32).astype(BF16)

    def place(self, target, valid):
        width = 2 * LANES
        lane = lax.broadcasted_iota(jnp.int32, (1, width), 1) % LANES
        slots, rank = lane % 8, lane // 8
        goal = jnp.full((1, width), -9.0, F32)
        for index, (first, last) in enumerate(zip(self.firsts, self.lasts)):
            goal = jnp.where(rank == index, target(slots, first, last), goal)
        known = valid(slots, rank, self.me) & (rank < len(self.firsts))
        goal = jnp.where(known, goal - self.first + HALO, -1.0)
        rows = lax.broadcasted_iota(jnp.int32, (self.count + 16, width), 0).astype(F32)
        return (rows == goal).astype(F32).astype(BF16)


def stacked(summary_ref):
    parts = [summary_ref[rank] for rank in range(summary_ref.shape[0])]
    rest = LANES - sum(part.shape[0] for part in parts)
    parts.append(jnp.zeros((rest, parts[0].shape[1]), F32))
    return jnp.concatenate(split(jnp.concatenate(parts, axis=0)), axis=0)


def ahead_target(slots, first, last):
    later = jnp.where(slots <= 4, last - (slots - 1).astype(F32), -9.0)
    return jnp.where(slots == 0, first, later)


def ahead_valid(slots, rank, me):
    return ((rank < me) & (slots >= 1) & (slots <= 4)) | ((rank > me) & (slots == 0))


def back_target(slots, first, last):
    return jnp.where(slots <= 3, first + slots.astype(F32), jnp.where(slots == 4, last, -9.0))


def back_valid(slots, rank, me):
    return ((rank > me) & (slots <= 3)) | ((rank < me) & (slots == 4))


def forward_kernel(
    width,
    count,
    states_ref,
    starts_ref,
    two_ref,
    three_ref,
    four_ref,
    join_ref,
    gain_ref,
    query_weight_ref,
    key_weight_ref,
    value_weight_ref,
    bucket_ref,
    bias_ref,
    out_weight_ref,
    gate_ref,
    up_ref,
    down_ref,
    grad_ref,
    residual_out,
    normed_out,
    query_out,
    query_t_out,
    twice_out,
    key_t_out,
    value_out,
    table_out,
    divisor_out,
    pooled_out,
    mix_out,
    all_taps_ref,
    all_join_out,
    joint_out,
    padded_out,
    out_ref,
    total_ref,
    attended_ref,
    all_out_ref,
    near_gate_ref,
    near_up_ref,
    near_down_ref,
    far_grad_ref,
    residual_ref,
    normed_ref,
    query_ref,
    query_t_ref,
    twice_ref,
    key_t_ref,
    value_ref,
    table_ref,
    divisor_ref,
    pooled_ref,
    mix_ref,
    all_join_ref,
    joint_ref,
    padded_ref,
    value_t_ref,
    ids_ref,
    summary_ref,
    taps_in_ref,
    score_ref,
    sum_ref,
    stage_ref,
    ship_ref,
    *sems,
):
    me, near, far, cross = ranks()
    peers = (near, far, cross)
    rows, model = states_ref.shape
    share = join_ref.shape[0]
    inner = query_weight_ref.shape[1]
    heads, length = twice_ref.shape[0], twice_ref.shape[1]
    shipped = []

    def ship(source, target):
        copy = pltpu.make_async_copy(source, target, ship_ref.at[len(shipped)])
        copy.start()
        shipped.append(copy)

    def band(ref, rank):
        return ref.at[pl.ds(pl.multiple_of(rank * share, share), share), :]

    strides = strides_of(count)[:2]
    greet(peers, strides)
    words = Words(starts_ref, ids_ref, me, 4)
    states = states_ref[...]
    wide_states = jnp.concatenate([states, jnp.ones((rows, LANES), BF16)], axis=1)
    summary_ref[me] = dot(words.pick(ahead_target), wide_states)
    two, three, four = two_ref[...], three_ref[...], four_ref[...]
    taps_in_ref[me] = jnp.concatenate(
        [
            two[0:1] + three[0:1] + four[0:1],
            two[1:2] + three[1:2] + four[1:2],
            three[2:3] + four[2:3],
            four[3:4],
            jnp.zeros((4, share), F32),
        ],
        axis=0,
    )
    all_join_ref[pl.ds(pl.multiple_of(me * share, share), share), :] = join_ref[...]
    all_out_ref[pl.ds(pl.multiple_of(me * share, share), share), :] = out_weight_ref[...]
    greeted(peers, strides)
    early = []
    for slot, peer in enumerate(peers):
        early.append(remote(summary_ref.at[me], summary_ref.at[me], sems, slot, peer))
        early.append(remote(taps_in_ref.at[me], taps_in_ref.at[me], sems, 3 + slot, peer))
    joins = [
        remote(band(all_join_ref, me), band(all_join_ref, me), sems, 6, far),
        remote(band(all_join_ref, me), band(all_join_ref, me), sems, 7, near),
    ]
    middle = rows // 2
    first_grads = remote(
        grad_ref.at[pl.ds(0, middle)], far_grad_ref.at[pl.ds(0, middle)], sems, 25, far
    )
    for copy in early + joins + [first_grads]:
        copy.start()
    padded_ref[...] = jnp.full(padded_ref.shape, -1, jnp.int32)
    padded_ref[:, : bucket_ref.shape[1]] = bucket_ref[...]
    joint_ref[:, :inner] = query_weight_ref[...]
    joint_ref[:, inner : 2 * inner] = key_weight_ref[...]
    joint_ref[:, 2 * inner :] = value_weight_ref[...]
    ship(joint_ref, joint_out)
    ship(padded_ref, padded_out)
    table = words.table()
    sums = dot(table, wide_states)
    place = words.place(ahead_target, ahead_valid)
    for copy in early:
        copy.wait_recv()
    sums = sums + dot(place, stacked(summary_ref))
    divisor = jnp.maximum(sums[:, model:], 1.0)
    divisor_ref[...] = divisor
    ship(divisor_ref, divisor_out)
    pooled = sums[:, :model] / jnp.concatenate([divisor] * (model // LANES), axis=1)
    pooled_ref[...] = pooled
    ship(pooled_ref, pooled_out)
    taps = jnp.concatenate([taps_in_ref[rank] for rank in range(4)], axis=1)
    all_taps_ref[...] = taps
    joins[0].wait_recv()
    joins.append(remote(band(all_join_ref, far), band(all_join_ref, far), sems, 8, near))
    joins[2].start()
    total = pooled * taps[0:1]
    for lag in range(1, 4):
        total = total + pltpu.roll(pooled, lag, 0) * taps[lag : lag + 1]
    mix = dot_tn(table, total.astype(BF16)).astype(BF16)
    mix_ref[...] = mix
    ship(mix_ref, mix_out)
    joins[1].wait_recv()
    joins[2].wait_recv()
    residual = states.astype(F32) + dot(mix, all_join_ref[...])
    residual_ref[...] = residual
    own = pl.ds(pl.multiple_of(me * rows, rows), rows)
    normed_ref[own, :] = rms(residual, gain_ref[...]).astype(BF16)

    def block(rank, part):
        half = rows // 2
        return normed_ref.at[pl.ds(pl.multiple_of(rank * rows + part * half, half), half), :]

    sends = []
    for part in range(2):
        sends.append(remote(block(me, part), block(me, part), sems, 9 + part, far))
    for part in range(2):
        sends.append(remote(block(me, part), block(me, part), sems, 11 + part, near))
    for copy in sends:
        copy.start()
    copies = [
        remote(
            grad_ref.at[pl.ds(middle, middle)], far_grad_ref.at[pl.ds(middle, middle)], sems, 15, far
        ),
        remote(band(all_out_ref, me), band(all_out_ref, me), sems, 16, near),
        remote(gate_ref, near_gate_ref, sems, 17, near),
        remote(up_ref, near_up_ref, sems, 18, near),
        remote(down_ref, near_down_ref, sems, 19, near),
    ]
    out_far = remote(
        lambda: band(all_out_ref, me), lambda: band(all_out_ref, me), sems, 20, far
    )
    out_pass = remote(
        lambda: band(all_out_ref, far), lambda: band(all_out_ref, far), sems, 21, near
    )
    out_far.start()
    for copy in copies:
        copy.start()
    ship(residual_ref, residual_out)
    ship(all_join_ref, all_join_out)

    def project(rank):
        cut = pl.ds(pl.multiple_of(rank * rows, rows), rows)
        made = dot(normed_ref[cut, :], joint_ref[...])
        query, key, value = [
            made[:, index * inner : (index + 1) * inner].astype(BF16) for index in range(3)
        ]
        query_ref[cut, :] = query
        query_t_ref[:, cut] = turned(query)
        key_t_ref[:, cut] = turned(key)
        value_ref[cut, :] = value
        value_t_ref[:, cut] = turned(value)
        for head in range(heads):
            part = key[:, head * width : (head + 1) * width]
            twice_ref[head, cut, :] = jnp.concatenate([part, part], axis=1)

    project(me)
    fill_bias_table(padded_ref, bias_ref, table_ref)
    ship(table_ref, table_out)
    sends[2].wait_recv()
    sends[3].wait_recv()
    project(near)
    wide = deep = length // 4

    def owner(order):
        chip = (me // 2 + 1 + order // 2) % 2
        core = (me % 2 + (order + 1) // 2) % 2
        return 2 * chip + core

    def handed(order):
        return remote(stage_ref.at[order], attended_ref.at[me], sems, 22 + order, owner(order))

    def half_scores(block, head, chip):
        begin = pl.multiple_of(block * wide, wide)
        start = pl.multiple_of(chip * (length // 2), wide)
        rows = pl.ds(pl.multiple_of(head * width, width), width)
        scaled = query_t_ref[rows, pl.ds(begin, wide)].astype(F32) * LOG2E
        queries = jnp.concatenate(split(scaled), axis=0)
        peak = jnp.full((8, wide), -1e30, F32)
        for part in range(length // 2 // deep):
            keys = pl.ds(pl.multiple_of(start + part * deep, deep), deep)
            raw = dot(twice_ref[head, keys, :], queries)
            columns = []
            for lane in range(0, wide, LANES):
                offset = start + part * deep - begin - lane + length - LANES
                offset = pl.multiple_of(offset, LANES)
                columns.append(raw[:, lane : lane + LANES] + table_ref[head, pl.ds(offset, deep), :])
            scores = jnp.concatenate(columns, axis=1)
            score_ref[part * deep : (part + 1) * deep, :] = scores
            peak = jnp.maximum(peak, jnp.max(scores.reshape(deep // 8, 8, wide), axis=0))
        peak = jnp.max(peak, axis=0, keepdims=True)
        sums = jnp.zeros((8, wide), F32)
        made = jnp.zeros((width, wide), F32)
        for part in range(length // 2 // deep):
            keys = pl.ds(pl.multiple_of(start + part * deep, deep), deep)
            raised = jnp.exp2(score_ref[part * deep : (part + 1) * deep, :] - peak)
            sums = sums + jnp.sum(raised.reshape(deep // 8, 8, wide), axis=0)
            made = made + dot(value_t_ref[rows, keys], raised.astype(BF16))
        return peak, jnp.sum(sums, axis=0, keepdims=True), made

    def early_step(index, carry):
        head = index % heads
        block = 2 * (me // 2) + index // heads
        peak, total, made = half_scores(block, head, me // 2)
        span = pl.ds(pl.multiple_of(block * wide, wide), wide)
        total_ref[head, :, span] = peak
        sum_ref[head, :, span] = total
        out_ref[pl.ds(pl.multiple_of(head * width, width), width), span] = made
        return carry

    lax.fori_loop(0, 2 * heads, early_step, 0)
    passed = []
    for part in range(2):
        sends[part].wait_recv()
        passed.append(remote(block(far, part), block(far, part), sems, 13 + part, near))
        passed[part].start()
    project(far)
    for copy in passed:
        copy.wait_recv()
    project(cross)
    for source, target in (
        (normed_ref, normed_out),
        (query_ref, query_out),
        (query_t_ref, query_t_out),
        (twice_ref, twice_out),
        (key_t_ref, key_t_out),
        (value_ref, value_out),
    ):
        ship(source, target)

    def step(index, carry):
        late = index // (4 * heads)
        rest = index % (4 * heads)
        order = (1 - late) * (rest // (2 * heads)) + late * (2 + rest // heads)
        head = (1 - late) * (rest // 2 % heads) + late * (rest % heads)
        half = (1 - late) * (rest % 2) + late
        block = owner(order)
        peak, total, made = half_scores(block, head, (me // 2 + half) % 2)
        span = pl.ds(pl.multiple_of(block * wide, wide), wide)
        rows = pl.ds(pl.multiple_of(head * width, width), width)

        @pl.when(half == 0)
        def _():
            total_ref[head, :, span] = peak
            sum_ref[head, :, span] = total
            out_ref[rows, span] = made

        @pl.when(half == 1)
        def _():
            before = total_ref[head, :, span]
            top = jnp.maximum(before, peak)
            old, new = jnp.exp2(before - top), jnp.exp2(peak - top)
            all_sum = sum_ref[head, :, span] * old + total * new
            result = (out_ref[rows, span] * old + made * new) / all_sum
            out_ref[rows, span] = result
            total_ref[head, :, span] = top + jnp.log2(all_sum)
            stage_ref[order, rows, :] = result.astype(BF16)

        @pl.when((half == 1) & (head == heads - 1) & (order < 3))
        def _():
            handed(order).start()

        @pl.when(index == 2 * heads)
        def _():
            out_far.wait_recv()
            out_pass.start()

        return carry

    lax.fori_loop(0, 6 * heads, step, 0)
    attended_ref[me] = stage_ref[3]
    for order in range(3):
        handed(order).wait()
    for copy in copies + [first_grads]:
        copy.wait()
    out_pass.wait()
    for copy in early + joins + sends + passed + [out_far]:
        copy.wait_send()
    for copy in shipped:
        copy.wait()


def ffn_kernel(
    count,
    hand_on,
    attended_ref,
    all_out_ref,
    residual_ref,
    gain_ref,
    grad_ref,
    far_grad_ref,
    gate_ref,
    near_gate_ref,
    up_ref,
    near_up_ref,
    down_ref,
    near_down_ref,
    states_part_ref,
    far_made_ref,
    middle_grad_ref,
    gain_grad_ref,
    weight_half_ref,
    out_part_ref,
    grad_stage_ref,
    middle_ref,
    normed_ref,
    made_ref,
    back_ref,
    sums_ref,
    far_out_ref,
    far_in_ref,
    near_out_ref,
    near_in_ref,
    weight_ref,
    half_in_ref,
    sends_ref,
    receives_ref,
    half_sends_ref,
    half_receives_ref,
):
    me, near, far, cross = ranks()
    sems = (sends_ref, receives_ref)
    strides = strides_of(count)[:2]
    peers = (near, far, cross)
    rows, model = residual_ref.shape
    share = attended_ref.shape[1]
    attended = attended_ref[...].reshape(4 * share, rows)
    middle = residual_ref[...] + dot_tn(attended, all_out_ref[...])
    middle_ref[...] = middle
    normed_ref[0] = rms(middle, gain_ref[...]).astype(BF16)
    half = rows // 2
    there, returned = [], []
    for part in range(2):
        cut = pl.ds(part * half, half)
        there.append(remote(normed_ref.at[0, cut], normed_ref.at[1, cut], sems, part, far))
        there[part].start()
        returned.append(remote(far_out_ref.at[cut], far_in_ref.at[cut], sems, 2 + part, far))

    def work(side, cut, grads, gate, up, down, slab, first):
        given = normed_ref[side, cut]
        gate_value = dot(given, gate)
        up_value = dot(given, up)
        hidden_grad = dot_nt(grads, down)
        square = gate_value * gate_value
        curve = jnp.tanh(GELU_SCALE * gate_value * (1.0 + GELU_CUBE * square))
        half = 0.5 + 0.5 * curve
        gelu = gate_value * half
        slope = half + (0.5 * GELU_SCALE) * gate_value * (1.0 - curve * curve) * (
            1.0 + (3.0 * GELU_CUBE) * square
        )
        hidden = (gelu * up_value).astype(BF16)
        gate_back = (hidden_grad * up_value * slope).astype(BF16)
        up_back = (hidden_grad * gelu).astype(BF16)
        sums = [dot_tn(given, gate_back), dot_tn(given, up_back), dot_tn(hidden, grads)]
        for index in range(3):
            if side == 0:
                sums_ref[slab, index] = sums[index]
            else:
                sums_ref[slab, index] += sums[index]
        made = dot(hidden, down)
        back = dot_nt(gate_back, gate) + dot_nt(up_back, up)
        if first:
            made_ref[side, cut] = made
            back_ref[side, cut] = back
        else:
            made_ref[side, cut] += made
            back_ref[side, cut] += back

    slabs = ((1, (near_gate_ref, near_up_ref, near_down_ref)), (0, (gate_ref, up_ref, down_ref)))
    for slab, weights in slabs:
        work(0, slice(0, rows), grad_ref[...], *[ref[...] for ref in weights], slab, slab == 1)
    for part in range(2):
        cut = slice(part * half, (part + 1) * half)
        there[part].wait_recv()
        for slab, weights in slabs:
            work(1, cut, far_grad_ref[cut, :], *[ref[...] for ref in weights], slab, slab == 1)
            if part == 1 and slab == 1:
                near_out_ref[...] = sums_ref[1].astype(BF16)
                swap = remote(near_out_ref, near_in_ref, sems, 4, near)
                swap.start()
        far_out_ref[cut, :] = back_ref[1, cut].astype(BF16)
        returned[part].start()
    far_made_ref[...] = made_ref[1].astype(BF16)
    states_part_ref[...] = middle_ref[...] + made_ref[0]
    hand_on()
    swap.wait_recv()
    depth = weight_ref.shape[0] // 3
    for index in range(3):
        total = sums_ref[0, index] + near_in_ref[index].astype(F32)
        weight_ref[index * depth : (index + 1) * depth, :] = total.astype(BF16)
    size = weight_ref.shape[0] // 4
    halves = []
    for index, stride in enumerate(strides):
        begin = pl.multiple_of(2 * size * index + (1 - side_of(stride)) * size, 16)
        halves.append(
            remote(
                weight_ref.at[pl.ds(begin, size), :],
                half_in_ref.at[index],
                (half_sends_ref, half_receives_ref),
                index,
                partner(stride),
                axis="dp",
            )
        )
        halves[-1].start()
    for copy in returned:
        copy.wait_recv()
    normed_grad = back_ref[0] + far_in_ref[...].astype(F32)
    part, gain_grad = rms_back(normed_grad, middle_ref[...], gain_ref[...])
    gain_grad_ref[...] = jnp.broadcast_to(gain_grad, gain_grad_ref.shape)
    middle_grad = grad_ref[...].astype(F32) + part
    middle_grad_ref[...] = middle_grad
    low = middle_grad.astype(BF16)
    grad_stage_ref[...] = dot_nt(all_out_ref[...], low).astype(BF16).reshape(4, share, rows)
    out_part = dot(attended, low)
    for rank in range(4):
        out_part_ref[rank] = out_part[rank * share : (rank + 1) * share, :].T.astype(BF16)
    for index, stride in enumerate(strides):
        halves[index].wait_recv()
        begin = pl.multiple_of(2 * size * index + side_of(stride) * size, 16)
        total = weight_ref[pl.ds(begin, size), :].astype(F32) + half_in_ref[index].astype(F32)
        weight_half_ref[index * size : (index + 1) * size, :] = total.astype(BF16)
    for copy in halves:
        copy.wait_send()
    for copy in returned + there + [swap]:
        copy.wait_send()


def front_kernel(width, count, *refs):
    given, outs, landing, rest = refs[:18], refs[18:42], refs[42:48], refs[48:-4]
    out_ref, states_part_ref, far_made_ref, sems = refs[-4:]
    shipped = [
        pltpu.make_async_copy(source, target, sems.at[index])
        for index, (source, target) in enumerate(
            ((out_ref, outs[15]), (states_part_ref, outs[17]), (far_made_ref, outs[18]))
        )
    ]

    def hand_on():
        shipped[1].start()
        shipped[2].start()

    attended_ref, all_out_ref, near_gate_ref, near_up_ref, near_down_ref, far_grad_ref = landing
    forward_kernel(width, count, *given[:17], *outs[:15], out_ref, outs[16], *landing, *rest[:24])
    shipped[0].start()
    gate_ref, up_ref, down_ref, grad_ref, gain_ref = given[13:]
    ffn_kernel(
        count,
        hand_on,
        attended_ref,
        all_out_ref,
        rest[0],
        gain_ref,
        grad_ref,
        far_grad_ref,
        gate_ref,
        near_gate_ref,
        up_ref,
        near_up_ref,
        down_ref,
        near_down_ref,
        states_part_ref,
        far_made_ref,
        *outs[19:],
        *rest[24:],
    )
    for copy in shipped:
        copy.wait()


def back_kernel(
    width,
    count,
    buckets,
    grad_stage_ref,
    total_ref,
    joint_ref,
    bucket_ref,
    gain_ref,
    starts_ref,
    all_taps_ref,
    weight_half_ref,
    out_part_ref,
    far_made_ref,
    ffn_gain_grad_ref,
    query_t_hbm,
    query_hbm,
    twice_hbm,
    key_t_hbm,
    value_hbm,
    out_hbm,
    table_hbm,
    normed_hbm,
    residual_hbm,
    middle_grad_hbm,
    divisor_hbm,
    pooled_hbm,
    mix_hbm,
    all_join_hbm,
    states_part_hbm,
    input_grad_out,
    states_out_out,
    weight_total_out,
    joint_total_out,
    out_total_ref,
    join_total_ref,
    taps_total_ref,
    gains_total_ref,
    bias_total_ref,
    query_t_ref,
    query_ref,
    twice_ref,
    key_t_ref,
    value_ref,
    out_ref,
    table_ref,
    normed_ref,
    residual_ref,
    middle_grad_ref,
    divisor_ref,
    pooled_ref,
    mix_ref,
    all_join_ref,
    states_part_ref,
    load_ref,
    grad_t_ref,
    grad_ref,
    query_grad_ref,
    key_grad_ref,
    value_grad_ref,
    table_grad_ref,
    joint_grad_ref,
    core_out_ref,
    core_in_ref,
    chip_out_ref,
    chip_in_ref,
    made_in_ref,
    out_near_ref,
    out_sum_ref,
    out_far_ref,
    late_ref,
    ids_ref,
    summary_ref,
    join_part_ref,
    join_near_ref,
    join_sum_ref,
    join_far_ref,
    join_ref,
    small_near_ref,
    small_ref,
    small_in_ref,
    bias_ref,
    bias_in_ref,
    input_grad_ref,
    states_out_ref,
    weight_total_ref,
    joint_total_ref,
    ship_ref,
    sends_ref,
    receives_ref,
    chain_sends_ref,
    chain_receives_ref,
    *chain_refs,
):
    me, near, far, cross = ranks()
    peers = (near, far, cross)
    sems = (sends_ref, receives_ref)
    chain_sems = (chain_sends_ref, chain_receives_ref)
    heads, length = twice_ref.shape[0], twice_ref.shape[1]
    rows, model = residual_ref.shape
    share = join_part_ref.shape[1]
    inner = heads * width
    wide, deep = length // 4, length // 8
    strides = strides_of(count)
    turned_strides = [strides[1], strides[0]] + strides[2:]
    chains = []
    plan = [
        (None, 2 * weight_half_ref.shape[0], strides),
        (None, 2 * weight_half_ref.shape[0], turned_strides),
    ]
    for index, (ref, height, order) in enumerate(plan):
        half = height // 2
        chains.append(
            Chain(
                ref,
                (index % 2) * half,
                half,
                order,
                chain_refs[8 * index : 8 * index + 8],
                chain_sems,
                index * Chain.slots(strides),
            )
        )
    weight_chains, late_chains, join_chains = chains, [], []
    for index, chain in enumerate(weight_chains):
        chain.halved(weight_half_ref, index * (weight_half_ref.shape[0] // 2))
    for index, order in enumerate((strides, turned_strides)):
        join_chains.append(
            Exchange(
                join_ref,
                index * (join_ref.shape[0] // 2),
                join_ref.shape[0] // 2,
                order,
                chain_refs[30 + 2 * index : 32 + 2 * index],
                chain_sems,
                2 * Chain.slots(strides) + 2 * Quad.slots(strides) + index * len(strides),
            )
        )
        late_chains.append(
            Quad(
                late_ref,
                index * (late_ref.shape[0] // 2),
                late_ref.shape[0] // 2,
                order,
                chain_refs[16 + 7 * index : 23 + 7 * index],
                chain_sems,
                2 * Chain.slots(strides) + index * Quad.slots(strides),
            )
        )
    greet(peers, strides)
    loads = load_all(
        (
            (query_t_hbm, query_t_ref),
            (query_hbm, query_ref),
            (twice_hbm, twice_ref),
            (key_t_hbm, key_t_ref),
            (value_hbm, value_ref),
            (out_hbm, out_ref),
            (table_hbm, table_ref),
            (normed_hbm, normed_ref),
            (residual_hbm, residual_ref),
            (middle_grad_hbm, middle_grad_ref),
            (divisor_hbm, divisor_ref),
            (pooled_hbm, pooled_ref),
            (mix_hbm, mix_ref),
            (all_join_hbm, all_join_ref),
            (states_part_hbm, states_part_ref),
        ),
        load_ref,
    )
    greeted(peers, strides)
    gradient_copies = []
    for slot, peer in enumerate(peers):
        copy = remote(
            lambda peer=peer: grad_stage_ref.at[peer], lambda: grad_t_ref.at[me], sems, slot, peer
        )
        copy.start()
        gradient_copies.append(copy)
    out_copies = [
        remote(lambda: out_part_ref.at[near], lambda: out_near_ref.at[0], sems, 3, near),
        remote(lambda: out_part_ref.at[cross], lambda: out_near_ref.at[1], sems, 4, near),
    ]
    for copy in out_copies:
        copy.start()
    out_copy = remote(out_sum_ref, out_far_ref, sems, 5, far)
    made_copy = remote(far_made_ref, made_in_ref, sems, 6, far)
    core_copies = [
        remote(lambda: core_out_ref.at[0], lambda: core_in_ref.at[0], sems, 7, near),
        remote(lambda: core_out_ref.at[1], lambda: core_in_ref.at[1], sems, 8, near),
    ]
    chip_copy = remote(chip_out_ref, chip_in_ref, sems, 9, far)
    for chain in weight_chains:
        chain.step()
    made_copy.start()
    grad_t_ref[me] = grad_stage_ref[me]
    query_grad_ref[...] = jnp.zeros_like(query_grad_ref)
    key_grad_ref[...] = jnp.zeros_like(key_grad_ref)
    value_grad_ref[...] = jnp.zeros_like(value_grad_ref)
    table_grad_ref[...] = jnp.zeros_like(table_grad_ref)

    def gather_rows(rank):
        cut = pl.ds(pl.multiple_of(rank * wide, wide), wide)
        joint_grad_ref[cut, :inner] = query_grad_ref[:, cut].T.astype(BF16)
        joint_grad_ref[cut, inner : 2 * inner] = key_grad_ref[cut, :].astype(BF16)
        joint_grad_ref[cut, 2 * inner :] = value_grad_ref[cut, :].astype(BF16)
        return dot_nt(joint_grad_ref[cut, :], joint_ref[...])

    def block_of(relation):
        return 2 * ((me // 2 + relation // 2) % 2) + (me % 2 + relation % 2) % 2

    core = me % 2

    def step(index, carry):
        phase = index // 4
        middle = ((phase + 1) // 2) % 2
        away = middle * (2 + (core + phase - 1) % 2)
        block = block_of(away + (1 - middle) * ((index % 4) // 2))
        turn = (index + (2 + core) * (phase // 2)) % 4
        other = block_of(middle * turn + (1 - middle) * (index % 2 + 2 * (1 - phase // 3)))
        begin = pl.multiple_of(block * wide, wide)
        start = pl.multiple_of(other * wide, wide)
        span = pl.ds(begin, wide)
        @pl.when(index == 2)
        def _():
            gradient_copies[0].wait_recv()

        for first in range(2):

            @pl.when((index == 4 + 4 * first) & (core == first))
            def _():
                gradient_copies[1].wait_recv()

            @pl.when((index == 4 + 4 * first) & (core == 1 - first))
            def _():
                gradient_copies[2].wait_recv()

        @pl.when((index == 0) | (index == 2) | (index == 4) | (index == 8))
        def _():
            grad_ref[span, :] = turned(grad_t_ref[block])

        @pl.when(index == 3)
        def _():
            for copy in out_copies:
                copy.wait_recv()
            ours = out_part_ref[far].astype(F32) + out_near_ref[1].astype(F32)
            out_sum_ref[...] = ours.astype(BF16)
            out_copy.start()

        @pl.when(index == 4)
        def _():
            weight_chains[0].step()
            weight_chains[1].step()

        for first in range(2):

            @pl.when((index == 9 + 3 * first) & (core == first))
            def _():
                chip_out_ref[...] = gather_rows(far).astype(BF16)

            @pl.when((index == 9 + 3 * first) & (core == 1 - first))
            def _():
                core_out_ref[0] = gather_rows(cross).astype(BF16)
                core_copies[0].start()

            @pl.when((index == 10 + 3 * first) & (core == first))
            def _():
                core_copies[0].wait_recv()
                total = chip_out_ref[...].astype(F32) + core_in_ref[0].astype(F32)
                chip_out_ref[...] = total.astype(BF16)
                chip_copy.start()

        for head in range(heads):
            rows = slice(head * width, (head + 1) * width)
            scaled = query_t_ref[rows, span].astype(F32) * LOG2E
            queries = jnp.concatenate(split(scaled), axis=0)
            total = total_ref[head, :, span]
            grads = grad_t_ref[block, rows, :].astype(F32)
            dots = jnp.sum(grads * out_ref[rows, span], axis=0, keepdims=True)
            own_rows = lax.broadcasted_iota(jnp.int32, (inner, wide), 0) // width == head
            own_lanes = lax.broadcasted_iota(jnp.int32, (wide, inner), 1) // width == head
            grad_t_own = jnp.where(own_rows, grad_t_ref[block].astype(F32), 0.0).astype(BF16)
            query_own = jnp.where(own_lanes, query_ref[span, :].astype(F32), 0.0).astype(BF16)
            grad_own = jnp.where(own_lanes, grad_ref[span, :].astype(F32), 0.0).astype(BF16)
            query_grad = jnp.zeros((width, wide), F32)
            for part in range(wide // deep):
                cut = pl.ds(pl.multiple_of(start + part * deep, deep), deep)
                raw = dot(twice_ref[head, cut, :], queries)
                raw_grad = dot(value_ref[cut, :], grad_t_own)
                probs, score_grads = [], []
                for lane in range(0, wide, LANES):
                    piece = slice(lane, lane + LANES)
                    offset = start + part * deep - begin - lane + length - LANES
                    offset = pl.multiple_of(offset, LANES)
                    shift = table_ref[head, pl.ds(offset, deep), :]
                    prob = jnp.exp2(raw[:, piece] + shift - total[:, piece])
                    low = (prob * (raw_grad[:, piece] - dots[:, piece])).astype(BF16)
                    table_grad_ref[head, pl.ds(offset, deep), :] += low.astype(F32)
                    probs.append(prob.astype(BF16))
                    score_grads.append(low)
                probs = jnp.concatenate(probs, axis=1)
                score_grads = jnp.concatenate(score_grads, axis=1)
                value_grad_ref[cut, :] += dot(probs, grad_own)
                key_grad_ref[cut, :] += dot(score_grads, query_own)
                query_grad = query_grad + dot(key_t_ref[rows, cut], score_grads)
            query_grad_ref[rows, span] += query_grad
        return carry

    for copy in loads[:7]:
        copy.wait()
    lax.fori_loop(0, 16, step, 0)
    core_out_ref[1] = gather_rows(near).astype(BF16)
    core_copies[1].start()
    for chain in weight_chains:
        chain.step()
    normed_grad = gather_rows(me)
    for copy in loads[7:]:
        copy.wait()
    late_ref[:, : 3 * inner] = dot_tn(normed_ref[...], joint_grad_ref[...]).astype(BF16)
    out_copy.wait_recv()
    out_sum = (
        out_part_ref[me].astype(F32) + out_near_ref[0].astype(F32) + out_far_ref[...].astype(F32)
    )
    late_ref[:, 3 * inner :] = out_sum.astype(BF16)
    for chain in late_chains:
        chain.step()
    core_copies[1].wait_recv()
    normed_grad = normed_grad + core_in_ref[1].astype(F32)
    chip_copy.wait_recv()
    normed_grad = normed_grad + chip_in_ref[...].astype(F32)
    part, gain_grad = rms_back(normed_grad, residual_ref[...], gain_ref[...])
    residual_grad = middle_grad_ref[...] + part
    low = residual_grad.astype(BF16)
    join_part_ref[...] = dot_tn(mix_ref[...], low).astype(BF16).reshape(4, share, model)
    join_copies = [
        remote(join_part_ref.at[near], join_near_ref.at[0], sems, 16, near),
        remote(join_part_ref.at[cross], join_near_ref.at[1], sems, 17, near),
    ]
    for copy in join_copies:
        copy.start()
    words = Words(starts_ref, ids_ref, me, 4)
    picked = words.pick(back_target)
    high_mix, low_mix = split(dot_nt(low, all_join_ref[...]))
    summary_ref[me] = dot(picked, high_mix) + dot(picked, low_mix)
    copies = []
    for slot, peer in enumerate(peers):
        copies.append(remote(summary_ref.at[me], summary_ref.at[me], sems, 13 + slot, peer))
        copies[-1].start()
    for copy in join_copies:
        copy.wait_recv()
    join_sum_ref[...] = (
        join_part_ref[far].astype(F32) + join_near_ref[1].astype(F32)
    ).astype(BF16)
    join_copy = remote(join_sum_ref, join_far_ref, sems, 21, far)
    join_copy.start()
    for chain in weight_chains:
        chain.step()
    for chain in late_chains:
        chain.step()
    table = words.table()
    word_grad = dot(table, high_mix) + dot(table, low_mix)
    pooled = pooled_ref[...]
    tap_rows = [jnp.sum(pooled * word_grad, axis=0, keepdims=True)]
    for lag in range(1, 4):
        tap_rows.append(jnp.sum(pltpu.roll(pooled, lag, 0) * word_grad, axis=0, keepdims=True))
    tap_rows += [gain_grad, ffn_gain_grad_ref[0:1], jnp.zeros((2, model), F32)]
    small_near_ref[me] = jnp.concatenate(tap_rows, axis=0)
    for slot, peer in enumerate(peers):
        copies.append(remote(small_near_ref.at[me], small_near_ref.at[me], sems, 18 + slot, peer))
        copies[-1].start()
    shipped = []

    def ship(source, target):
        copy = pltpu.make_async_copy(source, target, ship_ref.at[len(shipped)])
        copy.start()
        shipped.append(copy)

    def write_weights(span, values):
        weight_total_ref[span, :] = values

    def write_late(span, values):
        joint_total_ref[span, :] = values

    def write_join(span, values):
        join_total_ref[span, :] = values

    bias_copies, small_copies = [], []

    def exchange(index, copies, ours, theirs, slot):
        stride = strides[index]
        copies.append(
            remote(
                ours.at[index],
                theirs.at[index],
                sems,
                slot + 2 * index,
                lambda: partner(stride),
                axis="dp",
            )
        )
        copies[-1].start()

    def pass_on(index, copies, ours, theirs, slot):
        copies[index].wait_recv()
        total = ours[index] + theirs[index]
        if index + 1 < len(strides):
            ours[index + 1] = total
            exchange(index + 1, copies, ours, theirs, slot)
        return total

    bias_parts = (bias_copies, bias_ref, bias_in_ref, 23)
    small_parts = (small_copies, small_ref, small_in_ref, 22)
    bias_ref[0] = bias_grad_rows(table_grad_ref, bucket_ref, buckets)
    exchange(0, *bias_parts)
    join_copy.wait_recv()
    join_ref[...] = (
        join_part_ref[me].astype(F32) + join_near_ref[0].astype(F32) + join_far_ref[...].astype(F32)
    ).astype(BF16)
    for chain in join_chains:
        chain.step(write_join)
    for copy in copies:
        copy.wait_recv()
    small = small_near_ref[0]
    for rank in range(1, 4):
        small = small + small_near_ref[rank]
    small_ref[0] = small
    exchange(0, *small_parts)
    for chain in late_chains:
        chain.step()
    word_grad = word_grad + dot(words.place(back_target, back_valid), stacked(summary_ref))
    taps = all_taps_ref[...]
    height = word_grad.shape[0]
    pooled_grad = word_grad * taps[0:1]
    for lag in range(1, 4):
        pooled_grad = pooled_grad + pltpu.roll(word_grad, height - lag, 0) * taps[lag : lag + 1]
    divisor = divisor_ref[...]
    pooled_grad = pooled_grad / jnp.concatenate([divisor] * (model // LANES), axis=1)
    high, low = split(pooled_grad)
    input_grad = residual_grad + (dot_tn(table, high) + dot_tn(table, low))
    input_grad_ref[...] = input_grad[:, None, :]
    ship(input_grad_ref, input_grad_out)
    bias = pass_on(0, *bias_parts)
    small = pass_on(0, *small_parts)
    for chain in join_chains:
        chain.step(write_join)
    made_copy.wait_recv()
    states_out_ref[...] = (states_part_ref[...] + made_in_ref[...].astype(F32))[:, None, :]
    ship(states_out_ref, states_out_out)
    for chain in weight_chains:
        while chain.at < chain.steps:
            chain.step(write_weights)
    ship(weight_total_ref, weight_total_out)
    for chain in late_chains:
        chain.step()
    bias = pass_on(1, *bias_parts)
    small = pass_on(1, *small_parts)
    for chain in join_chains:
        chain.step(write_join)
    for turn in range(1, len(strides) + 1):
        for group, finish in ((join_chains, write_join), (late_chains, write_late)):
            for chain in group:
                if chain.at < chain.steps:
                    chain.step(finish)
        if 1 < turn < len(strides):
            bias = pass_on(turn, *bias_parts)
            small = pass_on(turn, *small_parts)
    for chain in join_chains:
        while chain.at < chain.steps:
            chain.step(write_join)
    for chain in late_chains:
        while chain.at < chain.steps:
            chain.step(write_late)
    ship(joint_total_ref, joint_total_out)
    own = jnp.zeros((8, share), F32)
    for rank in range(4):
        own = jnp.where(me == rank, small[:, rank * share : (rank + 1) * share], own)
    taps_total_ref[...] = own
    gains_total_ref[...] = small
    bias_total_ref[...] = bias
    out_total_ref[...] = joint_total_ref[:, 3 * inner :].T
    for copy in shipped:
        copy.wait()
    finished = gradient_copies + out_copies + core_copies + [chip_copy, made_copy, out_copy]
    for copy in finished + copies + join_copies + [join_copy] + small_copies + bias_copies:
        copy.wait_send()


def place_kernel(
    joint_hbm,
    weight_hbm,
    states_hbm,
    input_hbm,
    out_hbm,
    join_hbm,
    taps_ref,
    gains_ref,
    bias_ref,
    states_out,
    input_out,
    two_out,
    three_out,
    four_out,
    join_out,
    norm_out,
    query_out,
    key_out,
    value_out,
    bias_out,
    out_out,
    ffn_out,
    gate_out,
    up_out,
    down_out,
    joint_ref,
    weight_ref,
    states_ref,
    input_ref,
    out_ref,
    join_ref,
    sems,
):
    loads = []
    for source, target in (
        (weight_hbm, weight_ref),
        (states_hbm, states_ref),
        (input_hbm, input_ref),
        (joint_hbm, joint_ref),
        (out_hbm, out_ref),
        (join_hbm, join_ref),
    ):
        loads.append(pltpu.make_async_copy(source, target, sems.at[10 + len(loads)]))
        loads[-1].start()
    inner, model = query_out.shape[1], gate_out.shape[0]
    pairs = [
        (weight_ref.at[pl.ds(index * model, model), :], target, 0)
        for index, target in enumerate((gate_out, up_out, down_out))
    ]
    pairs += [(states_ref, states_out, 1), (input_ref, input_out, 2)]
    pairs += [
        (joint_ref.at[:, pl.ds(index * inner, inner)], target, 3)
        for index, target in enumerate((query_out, key_out, value_out))
    ]
    pairs += [(out_ref, out_out, 4), (join_ref, join_out, 5)]
    copies, arrived = [], -1
    for index, (source, target, load) in enumerate(pairs):
        if load > arrived:
            loads[load].wait()
            arrived = load
        copies.append(pltpu.make_async_copy(source, target, sems.at[index]))
        copies[-1].start()
    two_out[...] = taps_ref[:2]
    three_out[...] = taps_ref[:3]
    four_out[...] = taps_ref[:4]
    norm_out[...] = gains_ref[4:5]
    ffn_out[...] = gains_ref[5:6]
    heads, buckets = bias_out.shape
    bias_out[...] = bias_ref[:heads, :buckets]
    for copy in copies:
        copy.wait()


def shards(
    byte_states,
    word_start,
    bucket_ids,
    conv_two,
    conv_three,
    conv_four,
    join_weight,
    norm_gain,
    query_weight,
    key_weight,
    value_weight,
    position_bias,
    out_weight,
    ffn_gain,
    gate_weight,
    up_weight,
    down_weight,
    out_grad,
):
    rows, batch, model = byte_states.shape
    length = word_start.shape[0]
    buckets, heads = position_bias.shape
    inner = query_weight.shape[1]
    width = inner // heads
    share = join_weight.shape[0]
    hidden = gate_weight.shape[1]
    count = rows + 16
    replicas = lax.axis_size("dp")
    strides = strides_of(replicas)
    states = byte_states.reshape(rows, model)
    grads = out_grad.reshape(rows, model)
    starts = word_start.reshape(length // LANES, LANES)
    span = bucket_ids.shape[0] + 1 - LANES
    made = (
        like((rows, model), F32),
        like((length, model), BF16),
        like((length, inner), BF16),
        like((inner, length), BF16),
        like((heads, length, 2 * width), BF16),
        like((inner, length), BF16),
        like((length, inner), BF16),
        like((heads, span, LANES), F32),
        like((count, LANES), F32),
        like((count, model), F32),
        like((rows, model), BF16),
        like((4 * share, model), BF16),
        like((model, 3 * inner), BF16),
        like((1, span + LANES), jnp.int32),
    )
    (
        residual,
        normed,
        queries,
        queries_t,
        twice_keys,
        keys_t,
        values,
        table,
        divisor,
        pooled,
        mix,
        all_taps,
        all_join,
        joint_weight,
        bucket_row,
        outs,
        totals,
        states_part,
        far_made,
        middle_grad,
        ffn_gain_grad,
        weight_half,
        out_part,
        grad_stage,
    ) = pl.pallas_call(
        functools.partial(front_kernel, width, replicas),
        out_shape=(
            *made[:11],
            like((8, model), F32),
            *made[11:],
            like((inner, length), F32),
            like((heads, 1, length), F32),
            like((rows, model), F32),
            like((rows, model), BF16),
            like((rows, model), F32),
            like((8, model), F32),
            like((3 * model // 2, hidden), BF16),
            like((4, model, inner), BF16),
            like((4, inner, rows), BF16),
        ),
        in_specs=whole(18),
        out_specs=anywhere(11) + whole(1) + anywhere(4) + whole(1) + anywhere(2) + whole(5),
        scratch_shapes=[
            pltpu.VMEM((4, inner, rows), BF16),
            pltpu.VMEM((4 * inner, model), BF16),
            pltpu.VMEM(gate_weight.shape, BF16),
            pltpu.VMEM(up_weight.shape, BF16),
            pltpu.VMEM(down_weight.shape, BF16),
            pltpu.VMEM((rows, model), BF16),
            *[pltpu.VMEM(part.shape, part.dtype) for part in made],
            pltpu.VMEM((inner, length), BF16),
            pltpu.VMEM((length // LANES, LANES), F32),
            pltpu.VMEM((4, 8, model + LANES), F32),
            pltpu.VMEM((4, 8, share), F32),
            pltpu.VMEM((length // 2, rows), F32),
            pltpu.VMEM((heads, 1, length), F32),
            pltpu.VMEM((4, inner, rows), BF16),
            pltpu.SemaphoreType.DMA((len(made),)),
            *semaphores(26),
            pltpu.VMEM((rows, model), F32),
            pltpu.VMEM((2, rows, model), BF16),
            pltpu.VMEM((2, rows, model), F32),
            pltpu.VMEM((2, rows, model), F32),
            pltpu.VMEM((2, 3, model, hidden), F32),
            pltpu.VMEM((rows, model), BF16),
            pltpu.VMEM((rows, model), BF16),
            pltpu.VMEM((3, model, hidden), BF16),
            pltpu.VMEM((3, model, hidden), BF16),
            pltpu.VMEM((3 * model, hidden), BF16),
            pltpu.VMEM((2, 3 * model // 4, hidden), BF16),
            *semaphores(5),
            *semaphores(2),
            pltpu.VMEM((inner, length), F32),
            pltpu.VMEM((rows, model), F32),
            pltpu.VMEM((rows, model), BF16),
            pltpu.SemaphoreType.DMA((3,)),
        ],
        compiler_params=params(0),
        name="front",
    )(
        states,
        starts,
        conv_two,
        conv_three,
        conv_four,
        join_weight,
        norm_gain[None],
        query_weight,
        key_weight,
        value_weight,
        bucket_ids[None],
        position_bias.T,
        out_weight,
        gate_weight,
        up_weight,
        down_weight,
        grads,
        ffn_gain[None],
    )
    chain_scratch = []
    for _ in range(2):
        chain_scratch += Chain.scratch(3 * model // 2, hidden, len(strides) - 2, True)
    for _ in range(2):
        chain_scratch += Quad.scratch(model // 2, 4 * inner, len(strides) - 3)
    for _ in range(2):
        chain_scratch += Exchange.scratch(share // 2, model, len(strides))
    loaded = (queries_t, queries, twice_keys, keys_t, values, outs, table)
    loaded += (normed, residual, middle_grad, divisor, pooled, mix, all_join, states_part)
    (
        input_grad,
        out_states,
        weight_total,
        joint_total,
        out_total,
        join_total,
        taps_total,
        gains_total,
        bias_total,
    ) = pl.pallas_call(
        functools.partial(back_kernel, width, replicas, buckets),
        out_shape=(
            like((rows, 1, model), F32),
            like((rows, 1, model), F32),
            like((3 * model, hidden), F32),
            like((model, 4 * inner), F32),
            like((inner, model), F32),
            like((share, model), F32),
            like((8, share), F32),
            like((8, model), F32),
            like((8, LANES), F32),
        ),
        in_specs=whole(11) + anywhere(len(loaded)),
        out_specs=anywhere(4) + whole(5),
        scratch_shapes=[
            *[pltpu.VMEM(part.shape, part.dtype) for part in loaded],
            pltpu.SemaphoreType.DMA((len(loaded),)),
            pltpu.VMEM((4, inner, rows), BF16),
            pltpu.VMEM((length, inner), BF16),
            pltpu.VMEM((inner, length), F32),
            pltpu.VMEM((length, inner), F32),
            pltpu.VMEM((length, inner), F32),
            pltpu.VMEM((heads, span, LANES), F32),
            pltpu.VMEM((length, 3 * inner), BF16),
            pltpu.VMEM((2, rows, model), BF16),
            pltpu.VMEM((2, rows, model), BF16),
            pltpu.VMEM((rows, model), BF16),
            pltpu.VMEM((rows, model), BF16),
            pltpu.VMEM((rows, model), BF16),
            pltpu.VMEM((2, model, inner), BF16),
            pltpu.VMEM((model, inner), BF16),
            pltpu.VMEM((model, inner), BF16),
            pltpu.VMEM((model, 4 * inner), BF16),
            pltpu.VMEM((length // LANES, LANES), F32),
            pltpu.VMEM((4, 8, model), F32),
            pltpu.VMEM((4, share, model), BF16),
            pltpu.VMEM((2, share, model), BF16),
            pltpu.VMEM((share, model), BF16),
            pltpu.VMEM((share, model), BF16),
            pltpu.VMEM((share, model), BF16),
            pltpu.VMEM((4, 8, model), F32),
            pltpu.VMEM((len(strides), 8, model), F32),
            pltpu.VMEM((len(strides), 8, model), F32),
            pltpu.VMEM((len(strides), 8, LANES), F32),
            pltpu.VMEM((len(strides), 8, LANES), F32),
            pltpu.VMEM((rows, 1, model), F32),
            pltpu.VMEM((rows, 1, model), F32),
            pltpu.VMEM((3 * model, hidden), F32),
            pltpu.VMEM((model, 4 * inner), F32),
            pltpu.SemaphoreType.DMA((4,)),
            *semaphores(22 + 2 * len(strides)),
            *semaphores(2 * Chain.slots(strides) + 2 * Quad.slots(strides) + 2 * len(strides)),
            *chain_scratch,
        ],
        compiler_params=params(3),
        name="back",
    )(
        grad_stage,
        totals,
        joint_weight,
        bucket_row,
        norm_gain[None],
        starts,
        all_taps,
        weight_half,
        out_part,
        far_made,
        ffn_gain_grad,
        *loaded,
    )
    placed = pl.pallas_call(
        place_kernel,
        out_shape=(
            like((rows, 1, model), F32),
            like((rows, 1, model), F32),
            like(conv_two.shape, F32),
            like(conv_three.shape, F32),
            like(conv_four.shape, F32),
            like((share, model), F32),
            like((1, model), F32),
            like((model, inner), F32),
            like((model, inner), F32),
            like((model, inner), F32),
            like((heads, buckets), F32),
            like((inner, model), F32),
            like((1, model), F32),
            like((model, hidden), F32),
            like((model, hidden), F32),
            like((hidden, model), F32),
        ),
        in_specs=anywhere(6) + whole(3),
        out_specs=anywhere(2)
        + whole(3)
        + anywhere(1)
        + whole(1)
        + anywhere(3)
        + whole(1)
        + anywhere(1)
        + whole(1)
        + anywhere(3),
        scratch_shapes=[
            *[
                pltpu.VMEM(part.shape, F32)
                for part in (joint_total, weight_total, out_states, input_grad, out_total, join_total)
            ],
            pltpu.SemaphoreType.DMA((16,)),
        ],
        compiler_params=params(),
        name="place",
    )(
        joint_total,
        weight_total,
        out_states,
        input_grad,
        out_total,
        join_total,
        taps_total,
        gains_total,
        bias_total,
    )
    placed = list(placed)
    placed[6], placed[10], placed[12] = placed[6][0], placed[10].T, placed[12][0]
    return tuple(placed)


def solution(mesh):
    return jax.shard_map(
        shards,
        mesh=mesh,
        in_specs=(
            P("mp", "dp", None),
            P(None, "dp"),
            P(),
            P(None, "mp"),
            P(None, "mp"),
            P(None, "mp"),
            P("mp", None),
            P(),
            P(None, "mp"),
            P(None, "mp"),
            P(None, "mp"),
            P(None, "mp"),
            P("mp", None),
            P(),
            P(None, "mp"),
            P(None, "mp"),
            P("mp", None),
            P("mp", "dp", None),
        ),
        out_specs=(
            P("mp", "dp", None),
            P("mp", "dp", None),
            P(None, "mp"),
            P(None, "mp"),
            P(None, "mp"),
            P("mp", None),
            P(),
            P(None, "mp"),
            P(None, "mp"),
            P(None, "mp"),
            P(None, "mp"),
            P("mp", None),
            P(),
            P(None, "mp"),
            P(None, "mp"),
            P("mp", None),
        ),
        check_vma=False,
    )
```
